32 devices in a mesh: ctx: 8 (over z, core), fsdp: 4 (over y, x).
Axes of the slice: x: 2, y: 2, z: 4, core: 2. Of those that a mesh axis runs over, the one named last changes fastest.
Arguments:
- tokens: bfloat16 [4, 1024, 2304], P('fsdp', 'ctx'), may hold values from -36 to 36, as said below
- w_query: bfloat16 [2304, 2048], P(('ctx', 'fsdp')), may hold values from -0.5 to 0.5
- w_key: bfloat16 [2304, 1024], P(('ctx', 'fsdp')), may hold values from -0.125 to 0.125
- w_value: bfloat16 [2304, 1024], P(('ctx', 'fsdp')), may hold values from -0.125 to 0.125
- w_out: bfloat16 [2048, 2304], P(('ctx', 'fsdp')), may hold values from -0.125 to 0.125
- w_gate: bfloat16 [2304, 9216], P(('ctx', 'fsdp')), may hold values from -0.125 to 0.125
- w_up: bfloat16 [2304, 9216], P(('ctx', 'fsdp')), may hold values from -0.125 to 0.125
- w_down: bfloat16 [9216, 2304], P(('ctx', 'fsdp')), may hold values from -0.0625 to 0.0625
- pre_gain: bfloat16 [2304], P(('ctx', 'fsdp')), may hold values from -0.5 to 0.5
- post_gain: bfloat16 [2304], P(('ctx', 'fsdp')), may hold values from -0.5 to 0.5
- pre_ffn_gain: bfloat16 [2304], P(('ctx', 'fsdp')), may hold values from -0.5 to 0.5
- post_ffn_gain: bfloat16 [2304], P(('ctx', 'fsdp')), may hold values from -0.5 to 0.5
- out_grad: bfloat16 [4, 1024, 2304], P('fsdp', 'ctx'), may hold values from -6 to 6
Outputs:
- output: bfloat16 [4, 1024, 2304], P('fsdp', 'ctx')
- token_grad: bfloat16 [4, 1024, 2304], P('fsdp', 'ctx')
- w_query_grad: float32 [2304, 2048], P(('ctx', 'fsdp'))
- w_key_grad: float32 [2304, 1024], P(('ctx', 'fsdp'))
- w_value_grad: float32 [2304, 1024], P(('ctx', 'fsdp'))
- w_out_grad: float32 [2048, 2304], P(('ctx', 'fsdp'))
- w_gate_grad: float32 [2304, 9216], P(('ctx', 'fsdp'))
- w_up_grad: float32 [2304, 9216], P(('ctx', 'fsdp'))
- w_down_grad: float32 [9216, 2304], P(('ctx', 'fsdp'))
- pre_gain_grad: float32 [2304], P(('ctx', 'fsdp'))
- post_gain_grad: float32 [2304], P(('ctx', 'fsdp'))
- pre_ffn_gain_grad: float32 [2304], P(('ctx', 'fsdp'))
- post_ffn_gain_grad: float32 [2304], P(('ctx', 'fsdp'))
The draws below stay inside these ranges and needn't reach their ends.
Inputs may be any that keep to these rules, and one draw needn't show every extreme that they name: `tokens`: token rows and feature columns carry scales of their own.
All inputs are finite; a program needn't handle non-finite values.
Results may differ from the reference program's by a relative error of at most 0.02.
The reference program's roundings to bfloat16 on the way count: a program that leaves them out, or rounds other values in their place, can miss the bound.
Values may be sent and summed in bfloat16 or wider, within the bound.
A program may use at most 640 MiB of HBM per device.

```python
import math
import jax
import jax.numpy as jnp
from jax import lax

D = 2304
H = 8
KVH = 4
HD = 256
CAP = 50
FF = 9216
LENGTH = 1024
SEQS = 4


def draw_tokens(key, part):
    key_rows, key_cols, key_base = jax.random.split(key, 3)
    shape = (SEQS, LENGTH, D)
    row_scale = jnp.exp(jax.random.uniform(key_rows, (SEQS, LENGTH, 1), jnp.float32, math.log(0.3), math.log(3.0)))
    col_scale = jnp.exp(jax.random.uniform(key_cols, (1, 1, D), jnp.float32, math.log(0.3), math.log(3.0)))
    base = jnp.clip(jax.random.normal(key_base, shape, jnp.float32), -4.0, 4.0)
    return (base * row_scale * col_scale).astype(jnp.bfloat16)


def levels(stream_key, dims, cuts, least, top_value):
    def one(axis_at, shards_of):
        draws = jax.random.uniform(jax.random.fold_in(jax.random.fold_in(stream_key, 6), axis_at), (shards_of,), jnp.float32, least / len(cuts), top_value / len(cuts))
        return jnp.repeat(jnp.exp(draws), dims[axis_at] // shards_of).reshape((-1,) + (1,) * (len(dims) - axis_at - 1))

    level = one(*cuts[0])
    for cut in cuts[1:]:
        level = level * one(*cut)
    return level


def noise(rng, shape, deviation, limit, shards=(), kind=jnp.bfloat16):
    values = jax.random.normal(rng, shape, jnp.float32) * deviation
    if len(shards) > 0:
        values = levels(rng, shape, shards, -0.22, 0.18) * values
    return jnp.clip(values, min=-limit, max=limit).astype(kind)


def setup_inputs(seed: int = 0) -> dict:
    seeds = jax.random.split(jax.random.key(seed), 14)
    tokens = draw_tokens(jax.random.fold_in(seeds[13], 71), 0)
    w_query = noise(seeds[1], (D, H * HD), (D // 16) ** -0.5, 0.5, ((0, 32),))
    w_key = noise(seeds[2], (D, KVH * HD), D ** -0.5, 0.125, ((0, 32),))
    w_value = noise(seeds[3], (D, KVH * HD), D ** -0.5, 0.125, ((0, 32),))
    w_out = noise(seeds[4], (H * HD, D), (H * HD) ** -0.5, 0.125, ((0, 32),))
    w_gate = noise(seeds[5], (D, FF), D ** -0.5, 0.125, ((0, 32),))
    w_up = noise(seeds[6], (D, FF), D ** -0.5, 0.125, ((0, 32),))
    w_down = noise(seeds[7], (FF, D), FF ** -0.5, 0.0625, ((0, 32),))
    pre_gain = jnp.clip(jax.random.uniform(seeds[8], (D,), jnp.float32, -0.5, 0.5) * levels(seeds[8], (D,), ((0, 32),), -0.4, 0.0), -0.5, 0.5).astype(jnp.bfloat16)
    post_gain = jnp.clip(jax.random.uniform(seeds[9], (D,), jnp.float32, -0.5, 0.5) * levels(seeds[9], (D,), ((0, 32),), -0.4, 0.0), -0.5, 0.5).astype(jnp.bfloat16)
    pre_ffn_gain = jnp.clip(jax.random.uniform(seeds[10], (D,), jnp.float32, -0.5, 0.5) * levels(seeds[10], (D,), ((0, 32),), -0.4, 0.0), -0.5, 0.5).astype(jnp.bfloat16)
    post_ffn_gain = jnp.clip(jax.random.uniform(seeds[11], (D,), jnp.float32, -0.5, 0.5) * levels(seeds[11], (D,), ((0, 32),), -0.4, 0.0), -0.5, 0.5).astype(jnp.bfloat16)
    out_grad = noise(seeds[12], (SEQS, LENGTH, D), 1.0, 6.0, ((0, 4), (1, 8)))
    return {"tokens": tokens, "w_query": w_query, "w_key": w_key, "w_value": w_value, "w_out": w_out, "w_gate": w_gate, "w_up": w_up, "w_down": w_down, "pre_gain": pre_gain, "post_gain": post_gain, "pre_ffn_gain": pre_ffn_gain, "post_ffn_gain": post_ffn_gain, "out_grad": out_grad}


@jax.custom_vjp
def low(v):
    return lax.optimization_barrier(v.astype(jnp.bfloat16)).astype(jnp.float32)

@jax.custom_vjp
def low_back(v):
    return v

def low_keep(v):
    return (low(v), None)

def low_pass(kept, grad):
    return (grad,)

def back_keep(v):
    return (v, None)

def back_low(kept, grad):
    return (low(grad),)
low.defvjp(low_keep, low_pass)
low_back.defvjp(back_keep, back_low)
EPSILON = 1e-06
ROPE_BASE = 10000.0

def rms_scale(values_in, gain):
    inverse = lax.rsqrt(lax.optimization_barrier(jnp.mean(values_in * values_in, axis=-1, keepdims=True)) + EPSILON)
    return values_in * inverse * (1.0 + gain)

def rotate(heads_in, positions):
    half_width = heads_in.shape[-1] // 2
    inv_freqs = ROPE_BASE ** (-jnp.arange(half_width, dtype=jnp.float32) * 2.0 / heads_in.shape[-1])
    angles = positions.astype(jnp.float32)[:, None] * inv_freqs[None, :]
    cos_tab = jnp.cos(angles)[:, None, :]
    sine_tab = jnp.sin(angles)[:, None, :]
    front_half = heads_in[..., :half_width]
    back_half = heads_in[..., half_width:]
    return jnp.concatenate([front_half * cos_tab - back_half * sine_tab, back_half * cos_tab + front_half * sine_tab], axis=-1)

def one_sequence(sequence_in, w_query, w_key, w_value, w_out, w_gate, w_up, w_down, pre_gain, post_gain, pre_ffn_gain, post_ffn_gain):
    top_prec = lax.Precision.HIGHEST
    positions = jnp.arange(LENGTH, dtype=jnp.int32)
    hidden = low(rms_scale(sequence_in, pre_gain))
    queries = low_back(jnp.dot(hidden, w_query, precision=top_prec)).reshape(LENGTH, H, HD)
    queries = low(rotate(queries, positions) * HD ** (-0.5))
    key_heads = low_back(jnp.dot(hidden, w_key, precision=top_prec)).reshape(LENGTH, KVH, HD)
    key_heads = low(rotate(key_heads, positions))
    value_heads = low(low_back(jnp.dot(hidden, w_value, precision=top_prec))).reshape(LENGTH, KVH, HD)
    q_group = H // KVH
    keys_wide = jnp.repeat(key_heads, q_group, axis=1)
    values_wide = jnp.repeat(value_heads, q_group, axis=1)
    block_rows = min(512, LENGTH)
    starts = jnp.arange(LENGTH // block_rows, dtype=jnp.int32) * block_rows

    @jax.checkpoint
    def attend(first_row):
        query_block = lax.dynamic_slice_in_dim(queries, first_row, block_rows, 0)
        raw_scores = low_back(jnp.einsum('qhd,khd->hqk', query_block, keys_wide, precision=top_prec))
        capped = CAP * jnp.tanh(raw_scores / CAP)
        query_pos = first_row + jnp.arange(block_rows, dtype=jnp.int32)
        allowed = positions[None, :] <= query_pos[:, None]
        weights = jnp.where(allowed[None], jnp.exp(capped), 0.0)
        row_total = lax.optimization_barrier(jnp.sum(weights, axis=-1))
        weighted = jnp.einsum('hqk,khd->qhd', low(weights), values_wide, precision=top_prec)
        return weighted / jnp.transpose(row_total)[:, :, None]
    attended = lax.map(attend, starts).reshape(LENGTH, H * HD)
    attended = low(low_back(attended))
    branch = low_back(jnp.dot(attended, w_out, precision=top_prec))
    middle = sequence_in + rms_scale(branch, post_gain)
    hidden_ffn = low(rms_scale(middle, pre_ffn_gain))
    gate_lin = low_back(jnp.dot(hidden_ffn, w_gate, precision=top_prec))
    up_lin = low_back(jnp.dot(hidden_ffn, w_up, precision=top_prec))
    active = low(jax.nn.gelu(gate_lin, approximate=True) * up_lin)
    ffn_branch = low_back(jnp.dot(active, w_down, precision=top_prec))
    return middle + rms_scale(ffn_branch, post_ffn_gain)

def forward(tokens_f, w_query, w_key, w_value, w_out, w_gate, w_up, w_down, pre_gain, post_gain, pre_ffn_gain, post_ffn_gain):

    def per_sequence(sequence_in):
        return one_sequence(sequence_in, w_query, w_key, w_value, w_out, w_gate, w_up, w_down, pre_gain, post_gain, pre_ffn_gain, post_ffn_gain)
    return lax.map(jax.checkpoint(per_sequence), tokens_f)

def reference(tokens, w_query, w_key, w_value, w_out, w_gate, w_up, w_down, pre_gain, post_gain, pre_ffn_gain, post_ffn_gain, out_grad):
    inputs = tuple((item.astype(jnp.float32) for item in (tokens, w_query, w_key, w_value, w_out, w_gate, w_up, w_down, pre_gain, post_gain, pre_ffn_gain, post_ffn_gain)))
    output, pullback = jax.vjp(forward, *inputs)
    grads = pullback(out_grad.astype(jnp.float32))
    return (output.astype(jnp.bfloat16), grads[0].astype(jnp.bfloat16), grads[1], grads[2], grads[3], grads[4], grads[5], grads[6], grads[7], grads[8], grads[9], grads[10], grads[11])
```

```python
import functools

import jax
import jax.numpy as jnp
from jax import lax
from jax.experimental import pallas as pl
from jax.experimental.pallas import tpu as pltpu
from jax.sharding import PartitionSpec as P

D = 2304
H = 8
KVH = 4
HD = 256
CAP = 50
FF = 9216

EPSILON = 1e-06
ROPE_BASE = 10000.0

MESH = pl.DeviceIdType.MESH
HBM = pl.BlockSpec(memory_space=pl.ANY)
VMEM = pl.BlockSpec(memory_space=pltpu.VMEM)
DMA = pltpu.SemaphoreType.DMA
BF = jnp.bfloat16
F32 = jnp.float32


def rope_tables(positions, width):
    half_width = width // 2
    inv_freqs = ROPE_BASE ** (-jnp.arange(half_width, dtype=F32) * 2.0 / width)
    angles = positions.astype(F32)[:, None] * inv_freqs[None, :]
    return (jnp.cos(angles), jnp.sin(angles))


def rotate(rows, cos_tab, sine_tab):
    half_width = rows.shape[-1] // 2
    front, back = rows[..., :half_width], rows[..., half_width:]
    return jnp.concatenate(
        [front * cos_tab - back * sine_tab, back * cos_tab + front * sine_tab], axis=-1
    )


def unrotate(rows, cos_tab, sine_tab):
    half_width = rows.shape[-1] // 2
    front, back = rows[..., :half_width], rows[..., half_width:]
    return jnp.concatenate(
        [front * cos_tab + back * sine_tab, back * cos_tab - front * sine_tab], axis=-1
    )


def rms_parts(values_in):
    inverse = lax.rsqrt(jnp.mean(values_in * values_in, axis=-1, keepdims=True) + EPSILON)
    return (inverse, values_in * inverse)


def norm_back(grad_normed, normed, inverse):
    return inverse * (grad_normed - normed * jnp.mean(grad_normed * normed, axis=-1, keepdims=True))


def contract_rows(left, right):
    return lax.dot_general(left, right, (((0,), (0,)), ((), ())), preferred_element_type=F32)


def contract_cols(left, right):
    return lax.dot_general(left, right, (((1,), (1,)), ((), ())), preferred_element_type=F32)


def fold_rows(left, right):
    return jnp.dot(left, right, preferred_element_type=F32)


def gated(gate_in, up_in):
    return jax.nn.gelu(gate_in, approximate=True) * up_in


NZ = 4
RING = 2 * NZ


def my_place():
    c, f = lax.axis_index("ctx"), lax.axis_index("fsdp")
    return c // 2, c % 2, f // 2, f % 2


def ring_index(y, z):
    return z + y * (RING - 1 - 2 * z)


def ring_yz(q):
    y = q // NZ
    return y, q + y * (RING - 1 - 2 * q)


def device(z, core, y, x):
    return (2 * z + core, 2 * y + x)


def ring_device(q, core, x):
    y, z = ring_yz(q)
    return device(z, core, y, x)


def remote(src, dst, send_sem, recv_sem, where):
    return pltpu.make_async_remote_copy(
        src_ref=src,
        dst_ref=dst,
        send_sem=send_sem,
        recv_sem=recv_sem,
        device_id=where,
        device_id_type=MESH,
    )


def greet(places):
    barrier = pltpu.get_barrier_semaphore()
    for place in places:
        pl.semaphore_signal(barrier, inc=1, device_id=place, device_id_type=MESH)
    pl.semaphore_wait(barrier, len(places))


def params(collective_id, vmem_mib=56):
    return pltpu.CompilerParams(
        collective_id=collective_id,
        has_side_effects=True,
        vmem_limit_bytes=vmem_mib * 2**20,
    )


SUB = 4


def ring_parts(direction, step, half_step):
    if step != half_step:
        return list(range(SUB))
    half = SUB // 2
    return list(range(half)) if direction == 0 else list(range(half, SUB))


def gather_kernel(paired, x_ref, *refs):
    if paired:
        ring_ref, seq_ref, loc_sem, ss, rs, sib_ss, sib_rs = refs
    else:
        ring_ref, loc_sem, ss, rs = refs
    z, core, y, x = my_place()
    p = ring_index(y, z)
    right, left = (p + 1) % RING, (p + RING - 1) % RING
    sibling = device(z, 1 - core, y, x)
    piece = x_ref.shape[0] // SUB
    greet(
        [ring_device(right, core, x), ring_device(left, core, x)] + ([sibling] if paired else [])
    )
    local = pltpu.make_async_copy(x_ref, ring_ref.at[p], loc_sem.at[RING])
    local.start()

    def copy(direction, step, k):
        q = (p + (RING - step if direction == 0 else step)) % RING
        rows = pl.ds(k * piece, piece)
        src = x_ref.at[rows] if step == 0 else ring_ref.at[q, rows]
        return remote(
            src,
            ring_ref.at[q, rows],
            ss.at[direction, step, k],
            rs.at[direction, step, k],
            ring_device(right if direction == 0 else left, core, x),
        )

    def place_block(q, act):
        if not paired:
            return
        yq, zq = ring_yz(q)

        @pl.when(yq == core)
        def _():
            act(pltpu.make_async_copy(ring_ref.at[q], seq_ref.at[2 * zq + core], loc_sem.at[q]))

        @pl.when(yq != core)
        def _():
            act(remote(ring_ref.at[q], seq_ref.at[2 * zq + core], sib_ss.at[zq], sib_rs.at[zq], sibling))

    pending = []
    for step in range(4):
        for k in range(SUB):
            for direction in (0, 1):
                if k not in ring_parts(direction, step, 3):
                    continue
                if step > 0:
                    copy(direction, step - 1, k).wait_recv()
                c = copy(direction, step, k)
                c.start()
                pending.append(c)
        if step == 0:
            local.wait()
            place_block(p, lambda c: c.start())
        elif step < 3:
            for direction in (0, 1):
                q = (p + (RING - step if direction == 0 else step)) % RING
                place_block(q, lambda c: c.start())
    for direction in (0, 1):
        for k in range(SUB):
            if k not in ring_parts(direction, 3, 3):
                copy(direction, 2, k).wait_recv()
    for direction in (0, 1):
        place_block((p + (RING - 3 if direction == 0 else 3)) % RING, lambda c: c.start())
    for direction in (0, 1):
        for k in ring_parts(direction, 3, 3):
            copy(direction, 3, k).wait_recv()
    place_block((p + 4) % RING, lambda c: c.start())
    for c in pending:
        c.wait_send()

    def finish(c):
        if c.is_remote:
            c.wait_send()
        else:
            c.wait()

    if paired:
        for q in range(RING):
            place_block((p + q) % RING, finish)
        for zq in range(NZ):
            remote(ring_ref.at[zq], seq_ref.at[2 * zq + 1 - core], sib_ss.at[zq], sib_rs.at[zq], sibling).wait_recv()


def ring_gather(block, collective_id, paired):
    rows, width = block.shape
    whole = jax.ShapeDtypeStruct((RING, rows, width), block.dtype)
    sems = [DMA((RING + 1,)), DMA((2, 4, SUB)), DMA((2, 4, SUB))]
    out = pl.pallas_call(
        functools.partial(gather_kernel, paired),
        out_shape=[whole, whole] if paired else [whole],
        in_specs=[HBM],
        out_specs=[HBM, HBM] if paired else [HBM],
        scratch_shapes=sems + ([DMA((NZ,)), DMA((NZ,))] if paired else []),
        compiler_params=params(collective_id),
    )(block)
    return out[-1].reshape(RING * rows, width)


def scatter_kernel(paired, part_ref, o_ref, *refs):
    if paired:
        mine_ref, buf, ss, rs, sib_ss, sib_rs, loc_sem = refs
    else:
        buf, ss, rs = refs
        mine_ref = part_ref
    z, core, y, x = my_place()
    p = ring_index(y, z)
    right, left = (p + 1) % RING, (p + RING - 1) % RING
    sibling = device(z, 1 - core, y, x)
    piece = o_ref.shape[0] // SUB
    greet(
        [ring_device(right, core, x), ring_device(left, core, x)] + ([sibling] if paired else [])
    )
    if paired:
        swaps, copies = [], []
        for zq in range(NZ):
            q = ring_index(core, zq)
            swaps.append(remote(part_ref.at[2 * zq + 1 - core], mine_ref.at[q], sib_ss.at[zq], sib_rs.at[zq], sibling))
            swaps[-1].start()
            copies.append(pltpu.make_async_copy(part_ref.at[2 * zq + core], mine_ref.at[q], loc_sem.at[zq]))
            copies[-1].start()
        for c in copies:
            c.wait()
        for zq in range(NZ):
            q = ring_index(1 - core, zq)
            remote(part_ref.at[zq], mine_ref.at[q], sib_ss.at[zq], sib_rs.at[zq], sibling).wait_recv()
        for c in swaps:
            c.wait_send()

    def copy(direction, step, k, src):
        rows = pl.ds(k * piece, piece)
        return remote(
            src,
            buf.at[direction, step, rows],
            ss.at[direction, step, k],
            rs.at[direction, step, k],
            ring_device(right if direction == 0 else left, core, x),
        )

    pending = []
    for step in range(4):
        for k in range(SUB):
            rows = pl.ds(k * piece, piece)
            for direction in (0, 1):
                if k not in ring_parts(direction, step, 0):
                    continue
                far = 4 - step
                q = (p + (far if direction == 0 else RING - far)) % RING
                src = mine_ref.at[q, rows]
                if step > 0 and k in ring_parts(direction, step - 1, 0):
                    src = buf.at[direction, step - 1, rows]
                    copy(direction, step - 1, k, src).wait_recv()
                    total = src[...].astype(F32) + mine_ref[q, rows].astype(F32)
                    src[...] = total.astype(BF)
                c = copy(direction, step, k, src)
                c.start()
                pending.append(c)
    for k in range(SUB):
        rows = pl.ds(k * piece, piece)
        total = mine_ref[p, rows].astype(F32)
        for direction in (0, 1):
            src = buf.at[direction, 3, rows]
            copy(direction, 3, k, src).wait_recv()
            total = total + src[...].astype(F32)
        o_ref[rows] = total
    for c in pending:
        c.wait_send()


def ring_scatter(part, collective_id, paired):
    rows, width = part.shape[0] // RING, part.shape[1]
    blocks = (RING, rows, width)
    sems = [DMA((2, 4, SUB)), DMA((2, 4, SUB))]
    return pl.pallas_call(
        functools.partial(scatter_kernel, paired),
        out_shape=jax.ShapeDtypeStruct((rows, width), F32),
        in_specs=[VMEM],
        out_specs=VMEM,
        scratch_shapes=([pltpu.VMEM(blocks, BF)] if paired else [])
        + [pltpu.VMEM((2, 4, rows, width), BF)]
        + sems
        + ([DMA((NZ,)), DMA((NZ,)), DMA((NZ,))] if paired else []),
        compiler_params=params(collective_id),
    )(part.astype(BF).reshape(blocks))


UNITS = FF // RING
WIDTHS = (UNITS, UNITS, HD, HD, HD)
STARTS = (0, UNITS, 2 * UNITS, 2 * UNITS + HD, 2 * UNITS + 2 * HD)
WIDE = 2 * UNITS + 3 * HD


def member_place(t, core, x):
    return device(t // 2, core, t % 2, x)


def column_start(which, t):
    if which < 2:
        return pl.multiple_of(t * UNITS, 128)
    return pl.multiple_of((t if which == 2 else t // 2) * HD, 128)


def weights_in_kernel(gate, up, query, key, value, down, out, gains, w_ref, d_ref, o_ref, g_ref,
                      loc, s1, r1, s2, r2, s3, r3, s4, r4, s5, r5):
    z, core, y, x = my_place()
    t = 2 * z + y
    sibling, across = device(z, 1 - core, y, x), device(z, core, y, 1 - x)

    def slot(tq, corq, xq):
        return (2 * (tq // 2) + corq) * 4 + 2 * (tq % 2) + xq

    me = slot(t, core, x)
    others = [(t + j) % RING for j in range(1, RING)]
    plane = []
    for dc in (0, 1):
        for dy in (0, 1):
            for dx in (0, 1):
                if (dc, dy, dx) != (0, 0, 0):
                    plane.append((dc, dy, dx))
    places = [member_place(tq, core, x) for tq in others] + [
        device(z, (core + dc) % 2, (y + dy) % 2, (x + dx) % 2)
        for dc, dy, dx in plane
        if (dc, dx) != (0, 0)
    ]
    greet(places)
    sources = (gate, up, query, key, value)

    def first(tq, a, wait=False):
        if a == 5:
            src, dst = gains, g_ref.at[slot(tq, core, x) if wait else me]
        else:
            src = sources[a].at[:, pl.ds(column_start(a, tq), WIDTHS[a])]
            dst = w_ref.at[slot(tq, core, x) if wait else me, :, pl.ds(STARTS[a], WIDTHS[a])]
        i = tq if wait else t
        return remote(src, dst, s1.at[tq, a], r1.at[i, a], member_place(tq, core, x))

    pending = []
    locals_ = [pltpu.make_async_copy(gains, g_ref.at[me], loc.at[5])]
    for a in range(5):
        locals_.append(
            pltpu.make_async_copy(
                sources[a].at[:, pl.ds(column_start(a, t), WIDTHS[a])],
                w_ref.at[me, :, pl.ds(STARTS[a], WIDTHS[a])],
                loc.at[a],
            )
        )
    for c in locals_:
        c.start()
    pair = ((down, d_ref), (out, o_ref))
    mine = 2 * y + x
    for xq in (0, 1):
        to_self = (x == core) & (y == core) & (xq == x)
        for a, (src, dst) in enumerate(pair):
            @pl.when(to_self)
            def _():
                pltpu.make_async_copy(src, dst.at[mine], s4.at[xq, a]).start()

            @pl.when(jnp.logical_not(to_self))
            def _():
                remote(src, dst.at[mine], s4.at[xq, a], r4.at[y, a], device(z, x, core, xq)).start()
    for a in (5, 2, 3, 4, 0, 1):
        for tq in others:
            c = first(tq, a)
            c.start()
            pending.append(c)

    def second(tq, wait=False):
        i = slot(tq, core, 1 - x if wait else x)
        return [
            remote(w_ref.at[i], w_ref.at[i], s2.at[tq, 0], r2.at[tq, 0], across),
            remote(g_ref.at[i], g_ref.at[i], s2.at[tq, 1], r2.at[tq, 1], across),
        ]

    def third(tq, flip, wait=False):
        i = slot(tq, 1 - core if wait else core, 1 - x if flip else x)
        return [
            remote(w_ref.at[i], w_ref.at[i], s3.at[tq, flip, 0], r3.at[tq, flip, 0], sibling),
            remote(g_ref.at[i], g_ref.at[i], s3.at[tq, flip, 1], r3.at[tq, flip, 1], sibling),
        ]

    for yq in (0, 1):
        from_self = (core == y) & (yq == y) & (core == x)
        for a, (src, dst) in enumerate(pair):
            @pl.when(from_self)
            def _():
                pltpu.make_async_copy(src, dst.at[mine], s4.at[x, a]).wait()

            @pl.when(jnp.logical_not(from_self))
            def _():
                remote(src, dst.at[2 * yq + core], s4.at[0, a], r4.at[yq, a], sibling).wait_recv()

            c = remote(dst.at[2 * yq + core], dst.at[2 * yq + core], s5.at[yq, a], r5.at[yq, a], sibling)
            c.start()
            pending.append(c)
    for c in locals_:
        c.wait()
    for tq in [t] + others:
        if tq is not t:
            for a in range(6):
                first(tq, a, True).wait_recv()
        for c in second(tq) + third(tq, 0):
            c.start()
            pending.append(c)
    for tq in [t] + others:
        for c in second(tq, True):
            c.wait_recv()
        for c in third(tq, 1):
            c.start()
            pending.append(c)
    for tq in [t] + others:
        for flip in (0, 1):
            for c in third(tq, flip, True):
                c.wait_recv()
    for yq in (0, 1):
        for a, (src, dst) in enumerate(pair):
            remote(src, dst.at[2 * yq + 1 - core], s5.at[yq, a], r5.at[yq, a], sibling).wait_recv()
    for c in pending:
        c.wait_send()
    for xq in (0, 1):
        to_self = (x == core) & (y == core) & (xq == x)
        for a, (src, dst) in enumerate(pair):
            @pl.when(jnp.logical_not(to_self))
            def _():
                remote(src, dst.at[mine], s4.at[xq, a], r4.at[y, a], device(z, x, core, xq)).wait_send()


def weights_in(gate, up, query, key, value, down, out, gains, collective_id):
    n = 4 * RING
    shapes = [
        jax.ShapeDtypeStruct((n, gate.shape[0], WIDE), BF),
        jax.ShapeDtypeStruct((4,) + down.shape, BF),
        jax.ShapeDtypeStruct((4,) + out.shape, BF),
        jax.ShapeDtypeStruct((n,) + gains.shape, gains.dtype),
    ]
    return pl.pallas_call(
        weights_in_kernel,
        out_shape=shapes,
        in_specs=[HBM] * 8,
        out_specs=[HBM] * 4,
        scratch_shapes=[
            DMA((6,)),
            DMA((RING, 6)), DMA((RING, 6)),
            DMA((RING, 2)), DMA((RING, 2)),
            DMA((RING, 2, 2)), DMA((RING, 2, 2)),
            DMA((2, 2)), DMA((2, 2)),
            DMA((2, 2)), DMA((2, 2)),
        ],
        compiler_params=params(collective_id, 16),
    )(gate, up, query, key, value, down, out, gains)


def add_into(dst, index, src, other):
    dst[index] = (dst[index].astype(F32) + src[other].astype(F32)).astype(BF)


def weights_out_kernel(gu_in, qkv_in, down_in, out_in, gain_in,
                       gate_o, up_o, query_o, key_o, value_o, down_o, out_o, gain_o,
                       a_buf, b_buf, c_buf, acc, da, db, dacc, dd, oa, ob, oacc, od, ga, gsum,
                       loc, sa, ra, sb, rb, sc, rc, sx, rx, sg, rg):
    z, core, y, x = my_place()
    t = 2 * z + y
    sibling, across = device(z, 1 - core, y, x), device(z, core, y, 1 - x)
    diagonal = device(z, 1 - core, 1 - y, x)
    others = [(t + j) % RING for j in range(1, RING)]
    greet([member_place(tq, core, x) for tq in others] + [sibling, across, diagonal])

    def slot(tq, corq, xq):
        return (2 * (tq // 2) + corq) * 4 + 2 * (tq % 2) + xq

    def load(tq, xq):
        i = slot(tq, core, xq)
        return [
            pltpu.make_async_copy(gu_in.at[i], acc.at[xq, tq, :, pl.ds(0, 2 * UNITS)], loc.at[xq, tq, 0]),
            pltpu.make_async_copy(qkv_in.at[i], acc.at[xq, tq, :, pl.ds(2 * UNITS, 3 * HD)], loc.at[xq, tq, 1]),
        ]

    def to_sibling(tq, xq):
        i = slot(tq, 1 - core, xq)
        return [
            remote(gu_in.at[i], a_buf.at[xq, tq, :, pl.ds(0, 2 * UNITS)], sa.at[xq, tq, 0], ra.at[xq, tq, 0], sibling),
            remote(qkv_in.at[i], a_buf.at[xq, tq, :, pl.ds(2 * UNITS, 3 * HD)], sa.at[xq, tq, 1], ra.at[xq, tq, 1], sibling),
        ]

    def to_across(tq):
        return remote(acc.at[1 - x, tq], b_buf.at[tq], sb.at[tq], rb.at[tq], across)

    def to_member(tq, wait=False):
        return remote(acc.at[x, tq], c_buf.at[tq if wait else t], sc.at[tq], rc.at[tq if wait else t], member_place(tq, core, x))

    def each(body):
        lax.fori_loop(0, RING, lambda j, carry: (body((t + 1 + j) % RING, j), carry)[1], 0)

    small = ((down_in, da, db, dacc, dd, down_o), (out_in, oa, ob, oacc, od, out_o))

    def small_a(a, xo):
        src, buf = small[a][0], small[a][1]
        return remote(src.at[2 * (1 - core) + xo], buf.at[xo], sx.at[a, xo], rx.at[a, xo], sibling)

    def small_b(a):
        return remote(small[a][3].at[1 - x], small[a][2], sx.at[a, 2], rx.at[a, 2], across)

    def small_c(a):
        return remote(small[a][3].at[x], small[a][4], sx.at[a, 3], rx.at[a, 3], diagonal)

    def small_load(a, xo):
        return pltpu.make_async_copy(small[a][0].at[2 * core + xo], small[a][3].at[xo], loc.at[a, xo, 2])

    def gain_a():
        return remote(gain_in, ga.at[RING], sg.at[RING], rg.at[RING], sibling)

    def gain_b():
        return remote(gsum.at[0], ga.at[RING + 1], sg.at[RING + 1], rg.at[RING + 1], across)

    def gain_c(tq, wait=False):
        return remote(gsum.at[1], ga.at[tq if wait else t], sg.at[tq], rg.at[tq if wait else t], member_place(tq, core, x))

    def start_a(xq):
        def body(tq, j):
            for c in load(tq, xq) + to_sibling(tq, xq):
                c.start()

        each(body)

    start_a(1 - x)
    gain_a().start()
    for a in (0, 1):
        for xo in (0, 1):
            small_a(a, xo).start()
            small_load(a, xo).start()
    start_a(x)

    def sum_a(xq, tq):
        for c in load(tq, xq):
            c.wait()
        for c in to_sibling(tq, xq):
            c.wait_recv()
        acc[xq, tq] = (acc[xq, tq].astype(F32) + a_buf[xq, tq].astype(F32)).astype(BF)

    def step_one(tq, j):
        sum_a(1 - x, tq)
        to_across(tq).start()

    each(step_one)
    gain_a().wait_recv()
    gsum[0] = gain_in[...] + ga[RING]
    gain_b().start()
    for a in (0, 1):
        buf, total = small[a][1], small[a][3]
        for xo in (0, 1):
            small_load(a, xo).wait()
            small_a(a, xo).wait_recv()
            total[xo] = (total[xo].astype(F32) + buf[xo].astype(F32)).astype(BF)
        small_b(a).start()
    each(lambda tq, j: sum_a(x, tq))
    gain_b().wait_recv()
    gsum[1] = gsum[0] + ga[RING + 1]
    for tq in others:
        gain_c(tq).start()

    def step_two(tq, j):
        to_across(tq).wait_recv()
        acc[x, tq] = (acc[x, tq].astype(F32) + b_buf[tq].astype(F32)).astype(BF)

        @pl.when(j < RING - 1)
        def _():
            to_member(tq).start()

    each(step_two)
    for a in (0, 1):
        other, total = small[a][2:4]
        small_b(a).wait_recv()
        total[x] = (total[x].astype(F32) + other[...].astype(F32)).astype(BF)
        for xo in (0, 1):
            small_a(a, xo).wait_send()

    @pl.when(core == y)
    def _():
        for a in (0, 1):
            small[a][5][...] = small[a][3][x].astype(F32)

    @pl.when(core != y)
    def _():
        for a in (0, 1):
            small_c(a).start()
        for a in (0, 1):
            small_c(a).wait_recv()
            small[a][5][...] = small[a][4][...].astype(F32)
        for a in (0, 1):
            small_c(a).wait_send()

    total = gsum[1]
    for tq in others:
        gain_c(tq, True).wait_recv()
        total = total + ga[tq]
    gain_o[...] = total
    c_buf[t] = acc[x, t]
    for tq in others:
        to_member(tq, True).wait_recv()
    for tq in range(RING):
        units = pl.ds(tq * UNITS, UNITS)
        gate_o[:, units] = c_buf[tq, :, pl.ds(0, UNITS)].astype(F32)
        up_o[:, units] = c_buf[tq, :, pl.ds(UNITS, UNITS)].astype(F32)
        query_o[:, pl.ds(tq * HD, HD)] = c_buf[tq, :, pl.ds(STARTS[2], HD)].astype(F32)
    for g in range(KVH):
        for start, result in ((STARTS[3], key_o), (STARTS[4], value_o)):
            columns = pl.ds(start, HD)
            result[:, pl.ds(g * HD, HD)] = c_buf[2 * g, :, columns].astype(F32) + c_buf[2 * g + 1, :, columns].astype(F32)

    def drain(tq, j):
        for xq in (0, 1):
            for c in to_sibling(tq, xq):
                c.wait_send()
        to_across(tq).wait_send()

        @pl.when(j < RING - 1)
        def _():
            to_member(tq).wait_send()

    each(drain)
    gain_a().wait_send()
    gain_b().wait_send()
    for tq in others:
        gain_c(tq).wait_send()
    for a in (0, 1):
        small_b(a).wait_send()


def weights_out(gu, qkv, down, out, gains, collective_id):
    n = 4 * RING
    rows, width = gu.shape[0] // n, gains.shape[1]
    gu, qkv = gu.reshape(n, rows, 2 * UNITS), qkv.reshape(n, rows, 3 * HD)
    down, out = down.reshape(4, -1, width), out.reshape(4, -1, width)
    down_rows, out_rows = down.shape[1], out.shape[1]
    wide = (RING, rows, WIDE)

    def full(*shape):
        return jax.ShapeDtypeStruct(shape, F32)

    return pl.pallas_call(
        weights_out_kernel,
        out_shape=[
            full(rows, FF), full(rows, FF), full(rows, H * HD), full(rows, KVH * HD), full(rows, KVH * HD),
            full(down_rows, width), full(out_rows, width), full(*gains.shape),
        ],
        in_specs=[HBM] * 4 + [VMEM],
        out_specs=[VMEM] * 8,
        scratch_shapes=[
            pltpu.VMEM((2,) + wide, BF), pltpu.VMEM(wide, BF), pltpu.VMEM(wide, BF), pltpu.VMEM((2,) + wide, BF),
            pltpu.VMEM((2, down_rows, width), BF), pltpu.VMEM((down_rows, width), BF), pltpu.VMEM((2, down_rows, width), BF), pltpu.VMEM((down_rows, width), BF),
            pltpu.VMEM((2, out_rows, width), BF), pltpu.VMEM((out_rows, width), BF), pltpu.VMEM((2, out_rows, width), BF), pltpu.VMEM((out_rows, width), BF),
            pltpu.VMEM((RING + 2,) + gains.shape, F32), pltpu.VMEM((2,) + gains.shape, F32),
            DMA((2, RING, 3)),
            DMA((2, RING, 2)), DMA((2, RING, 2)),
            DMA((RING,)), DMA((RING,)),
            DMA((RING,)), DMA((RING,)),
            DMA((2, 4)), DMA((2, 4)),
            DMA((RING + 2,)), DMA((RING + 2,)),
        ],
        compiler_params=params(collective_id),
    )(gu, qkv, down, out, gains)


def attend(queries, keys, values, positions):
    raw = contract_cols(queries, keys)
    capped = CAP * jnp.tanh(raw / CAP)
    allowed = positions[None, :] <= positions[:, None]
    weights = jnp.where(allowed, jnp.exp(capped), 0.0)
    inv_total = 1.0 / jnp.sum(weights, axis=-1, keepdims=True)
    attended = fold_rows(weights.astype(BF), values) * inv_total
    return attended, inv_total


def attend_back(queries, keys, values, positions, attended, inv_total, d_attended):
    raw = contract_cols(queries, keys)
    capped = CAP * jnp.tanh(raw / CAP)
    allowed = positions[None, :] <= positions[:, None]
    weights = jnp.where(allowed, jnp.exp(capped), 0.0)
    delta = jnp.sum(d_attended.astype(F32) * attended, axis=-1, keepdims=True)
    d_probs = contract_cols(d_attended, values)
    slope = 1.0 - capped / CAP * (capped / CAP)
    d_raw = (weights * inv_total * (d_probs - delta) * slope).astype(BF)
    d_query = fold_rows(d_raw, keys)
    d_key = contract_rows(d_raw, queries)
    weights_b = weights.astype(BF)
    d_scaled = d_attended.astype(F32) * inv_total
    scaled_high = d_scaled.astype(BF)
    scaled_rest = (d_scaled - scaled_high.astype(F32)).astype(BF)
    d_value = contract_rows(weights_b, scaled_high) + contract_rows(weights_b, scaled_rest)
    return d_query, d_key, d_value


def on_ring(
    tokens, w_query, w_key, w_value, w_out, w_gate, w_up, w_down,
    pre_gain, post_gain, pre_ffn_gain, post_ffn_gain, out_grad,
):
    ids = iter(range(32))
    n_shards = 4 * RING
    length = RING * tokens.shape[1]
    shard_gain = pre_gain.shape[0]
    gains = jnp.stack([pre_gain, post_gain, pre_ffn_gain, post_ffn_gain]).astype(F32)
    gains = jnp.pad(gains, ((0, 4), (0, 128 - shard_gain)))
    w_in, down_in, out_in, gains_in = weights_in(
        w_gate, w_up, w_query, w_key, w_value, w_down, w_out, gains, next(ids)
    )
    w_in = w_in.reshape(-1, WIDE)
    w_gu, w_qkv = w_in[:, : 2 * UNITS], w_in[:, 2 * UNITS :]
    w_dn = down_in.reshape(UNITS, D)
    w_ot = out_in.reshape(HD, D)
    factors = 1.0 + jnp.transpose(gains_in[:, :4, :shard_gain], (1, 0, 2)).reshape(4, D)
    pre_factor, post_factor, pre_ffn_factor, post_ffn_factor = (factors[i] for i in range(4))
    positions = jnp.arange(length, dtype=jnp.int32)
    cos_tab, sine_tab = rope_tables(positions, HD)
    q_scale = HD ** (-0.5)

    resid_in = tokens[0].astype(F32)
    inv_pre, normed_pre = rms_parts(resid_in)
    sequence = ring_gather(tokens[0], next(ids), True).astype(F32)
    hidden = (rms_parts(sequence)[1] * pre_factor).astype(BF)
    projected = fold_rows(hidden, w_qkv)
    queries = (rotate(projected[:, :HD], cos_tab, sine_tab) * q_scale).astype(BF)
    keys = rotate(projected[:, HD : 2 * HD], cos_tab, sine_tab).astype(BF)
    values = projected[:, 2 * HD :].astype(BF)
    attended, inv_total = attend(queries, keys, values, positions)
    attended_b = attended.astype(BF)
    branch = ring_scatter(fold_rows(attended_b, w_ot), next(ids), True)
    inv_post, normed_post = rms_parts(branch)
    middle = resid_in + normed_post * post_factor
    inv_mid, normed_mid = rms_parts(middle)
    hidden_ffn = ring_gather((normed_mid * pre_ffn_factor).astype(BF), next(ids), False)
    gate_up = fold_rows(hidden_ffn, w_gu)
    gate_lin, up_lin = gate_up[:, :UNITS], gate_up[:, UNITS:]
    active = gated(gate_lin, up_lin).astype(BF)
    ffn_branch = ring_scatter(fold_rows(active, w_dn), next(ids), False)
    inv_ffn, normed_ffn = rms_parts(ffn_branch)
    output = (middle + normed_ffn * post_ffn_factor).astype(BF)

    out_cot = out_grad[0].astype(F32)
    post_ffn_part = jnp.sum(out_cot * normed_ffn, axis=0)
    d_ffn = norm_back(out_cot * post_ffn_factor, normed_ffn, inv_ffn).astype(BF)
    d_ffn = ring_gather(d_ffn, next(ids), False)
    down_part = contract_rows(active, d_ffn)
    d_active = contract_cols(d_ffn, w_dn)
    unused_value, gate_pull = jax.vjp(gated, gate_lin, up_lin)
    d_gate, d_up = gate_pull(d_active)
    d_gu = jnp.concatenate([d_gate.astype(BF), d_up.astype(BF)], axis=1)
    d_hidden_ffn = ring_scatter(contract_cols(d_gu, w_gu), next(ids), False)
    gu_part = contract_rows(hidden_ffn, d_gu)
    pre_ffn_part = jnp.sum(d_hidden_ffn * normed_mid, axis=0)
    d_middle = out_cot + norm_back(d_hidden_ffn * pre_ffn_factor, normed_mid, inv_mid)
    post_part = jnp.sum(d_middle * normed_post, axis=0)
    d_branch = norm_back(d_middle * post_factor, normed_post, inv_post).astype(BF)
    d_branch = ring_gather(d_branch, next(ids), True)
    out_part = contract_rows(attended_b, d_branch)
    d_attended = contract_cols(d_branch, w_ot).astype(BF)
    d_query, d_key, d_value = attend_back(
        queries, keys, values, positions, attended, inv_total, d_attended
    )
    d_qkv = jnp.concatenate(
        [
            unrotate(d_query * q_scale, cos_tab, sine_tab).astype(BF),
            unrotate(d_key, cos_tab, sine_tab).astype(BF),
            d_value.astype(BF),
        ],
        axis=1,
    )
    d_hidden = ring_scatter(contract_cols(d_qkv, w_qkv), next(ids), True)
    qkv_part = contract_rows(hidden, d_qkv)
    pre_part = jnp.sum(d_hidden * normed_pre, axis=0)
    token_grad = d_middle + norm_back(d_hidden * pre_factor, normed_pre, inv_pre)
    gain_parts = jnp.pad(jnp.stack([pre_part, post_part, pre_ffn_part, post_ffn_part]), ((0, 4), (0, 0)))
    results = weights_out(
        gu_part.astype(BF), qkv_part.astype(BF), down_part.astype(BF), out_part.astype(BF),
        gain_parts, next(ids),
    )
    gate_g, up_g, query_g, key_g, value_g, down_g, out_g, gain_g = results
    mine = lax.axis_index("ctx") * 4 + lax.axis_index("fsdp")
    gain_g = lax.dynamic_slice(gain_g, (0, mine * shard_gain), (4, shard_gain))
    return (
        output[None], token_grad.astype(BF)[None],
        query_g, key_g, value_g, out_g, gate_g, up_g, down_g,
        gain_g[0], gain_g[1], gain_g[2], gain_g[3],
    )


ROW_FOLD = 4


def head_tables(positions, width):
    half_width = width // 2
    inv_freqs = ROPE_BASE ** (-jnp.arange(half_width, dtype=jnp.float32) * 2.0 / width)
    angles = positions.astype(jnp.float32)[:, None] * inv_freqs[None, :]
    return (jnp.cos(angles)[:, None, :], jnp.sin(angles)[:, None, :])


def rotate_heads(heads_in, cos_tab, sine_tab):
    half_width = heads_in.shape[-1] // 2
    front_half = heads_in[..., :half_width]
    back_half = heads_in[..., half_width:]
    return jnp.concatenate(
        [front_half * cos_tab - back_half * sine_tab, back_half * cos_tab + front_half * sine_tab],
        axis=-1,
    )


def unrotate_heads(grad_in, cos_tab, sine_tab):
    half_width = grad_in.shape[-1] // 2
    front_half = grad_in[..., :half_width]
    back_half = grad_in[..., half_width:]
    return jnp.concatenate(
        [front_half * cos_tab + back_half * sine_tab, back_half * cos_tab - front_half * sine_tab],
        axis=-1,
    )


def to_groups(flat_heads, tok_rows, q_group):
    shaped = flat_heads.reshape(tok_rows, KVH, q_group, HD)
    return jnp.transpose(shaped, (1, 2, 0, 3)).reshape(KVH, q_group * tok_rows, HD)


def from_groups(grouped, tok_rows, q_group):
    shaped = grouped.reshape(KVH, q_group, tok_rows, HD)
    return jnp.transpose(shaped, (2, 0, 1, 3)).reshape(tok_rows, KVH * q_group * HD)


def grad_rows(left, right, folding, count):
    block = contract_rows(left, right)
    return block.reshape(count, right.shape[1] // folding)


def blockwise(step_fn, carry, piece, width):
    key_count = piece[0].shape[0]
    n_steps = key_count // width
    stacked = tuple((member.reshape(n_steps, width, member.shape[1]) for member in piece))

    def one_step(partial_value, block_item):
        block_index, members = block_item
        return (step_fn(partial_value, members, block_index * width), None)

    carry, unused = lax.scan(one_step, carry, (jnp.arange(n_steps, dtype=jnp.int32), stacked))
    return carry


def block_grads(query_g, query_pos, d_att_g, delta, inv_tot, key_block, value_block, key_first):
    key_count = key_block.shape[0]
    key_grp = key_block.reshape(key_count, KVH, HD)
    value_grp = value_block.reshape(key_count, KVH, HD)
    raw_scores = jnp.einsum("grd,ngd->grn", query_g, key_grp, preferred_element_type=jnp.float32)
    capped = CAP * jnp.tanh(raw_scores / CAP)
    key_pos = key_first + jnp.arange(key_count, dtype=jnp.int32)
    allowed = key_pos[None, None, :] <= query_pos[None, :, None]
    weights = jnp.where(allowed, jnp.exp(capped), 0.0)
    prob_rows = weights * inv_tot[..., None]
    d_probs = jnp.einsum("grd,ngd->grn", d_att_g, value_grp, preferred_element_type=jnp.float32)
    slope = 1.0 - capped / CAP * (capped / CAP)
    d_raw = (prob_rows * (d_probs - delta[..., None]) * slope).astype(jnp.bfloat16)
    d_query = jnp.einsum("grn,ngd->grd", d_raw, key_grp, preferred_element_type=jnp.float32)
    d_key = jnp.einsum("grn,grd->ngd", d_raw, query_g, preferred_element_type=jnp.float32)
    weights_b = weights.astype(jnp.bfloat16)
    d_scaled = d_att_g.astype(jnp.float32) * inv_tot[..., None]
    scaled_high = d_scaled.astype(jnp.bfloat16)
    scaled_rest = (d_scaled - scaled_high.astype(jnp.float32)).astype(jnp.bfloat16)
    d_value = jnp.einsum("grn,grd->ngd", weights_b, scaled_high, preferred_element_type=jnp.float32)
    d_value = d_value + jnp.einsum(
        "grn,grd->ngd", weights_b, scaled_rest, preferred_element_type=jnp.float32
    )
    return (d_query, d_key.reshape(key_count, KVH * HD), d_value.reshape(key_count, KVH * HD))


def on_any_mesh(
    tokens,
    w_query,
    w_key,
    w_value,
    w_out,
    w_gate,
    w_up,
    w_down,
    pre_gain,
    post_gain,
    pre_ffn_gain,
    post_ffn_gain,
    out_grad,
):
    tok_rows = tokens.shape[1]
    q_group = H // KVH
    q_scale = HD ** (-0.5)
    width_q = H * HD
    width_kv = KVH * HD
    width_qkv = width_q + 2 * width_kv
    n_ctx = lax.axis_size("ctx")
    my_block = lax.axis_index("ctx")
    my_start = my_block * tok_rows
    positions = my_start + jnp.arange(tok_rows, dtype=jnp.int32)
    cos_tab, sine_tab = head_tables(positions, HD)
    row_pos = jnp.tile(positions, q_group)
    last_pos = my_start + tok_rows - 1
    resid_in = tokens[0].astype(jnp.float32)
    qkv_shard = jnp.concatenate([w_query, w_key, w_value], axis=1)
    gateup_shard = jnp.concatenate([w_gate, w_up], axis=1)
    shard_rows = qkv_shard.shape[0]
    gains_shard = jnp.stack([pre_gain, post_gain, pre_ffn_gain, post_ffn_gain])
    full_gains, full_qkv, full_out = (
        lax.all_gather(gains_shard, ("ctx", "fsdp"), axis=1, tiled=True),
        lax.all_gather(qkv_shard, ("ctx", "fsdp"), axis=0, tiled=True),
        lax.all_gather(w_out, ("ctx", "fsdp"), axis=0, tiled=True),
    )
    factors = 1.0 + full_gains.astype(jnp.float32)
    pre_factor, post_factor, pre_ffn_factor, post_ffn_factor = (
        factors[0],
        factors[1],
        factors[2],
        factors[3],
    )
    inv_pre, normed_pre = rms_parts(resid_in)
    hidden = (normed_pre * pre_factor).astype(jnp.bfloat16)
    projected = jnp.dot(hidden, full_qkv, preferred_element_type=jnp.float32)
    query_lin = projected[:, :width_q].reshape(tok_rows, H, HD)
    queries = (
        (rotate_heads(query_lin, cos_tab, sine_tab) * q_scale)
        .astype(jnp.bfloat16)
        .reshape(tok_rows, width_q)
    )
    query_grp = to_groups(queries, tok_rows, q_group)
    key_lin = projected[:, width_q : width_q + width_kv].reshape(tok_rows, KVH, HD)
    key_rows = rotate_heads(key_lin, cos_tab, sine_tab).astype(jnp.bfloat16).reshape(tok_rows, width_kv)
    value_rows = projected[:, width_q + width_kv :].astype(jnp.bfloat16)

    def add_block(partial_value, piece, first_row):
        key_block, value_block = piece

        def add_compute_block(state):
            row_total, weighted = state
            key_count = key_block.shape[0]
            key_grp = key_block.reshape(key_count, KVH, HD)
            raw_scores = jnp.einsum(
                "grd,ngd->grn", query_grp, key_grp, preferred_element_type=jnp.float32
            )
            capped = CAP * jnp.tanh(raw_scores / CAP)
            key_pos = first_row + jnp.arange(key_count, dtype=jnp.int32)
            allowed = key_pos[None, None, :] <= row_pos[None, :, None]
            weights = jnp.where(allowed, jnp.exp(capped), 0.0)
            value_grp = value_block.reshape(key_count, KVH, HD)
            weighted = weighted + jnp.einsum(
                "grn,ngd->grd",
                weights.astype(jnp.bfloat16),
                value_grp,
                preferred_element_type=jnp.float32,
            )
            return (row_total + jnp.sum(weights, axis=-1), weighted)

        def add_skip_block(state):
            return state

        return lax.cond(first_row <= last_pos, add_compute_block, add_skip_block, partial_value)

    start_state = (
        jnp.zeros((KVH, q_group * tok_rows), jnp.float32),
        jnp.zeros((KVH, q_group * tok_rows, HD), jnp.float32),
    )
    row_total, weighted = blockwise(
        add_block,
        start_state,
        (
            lax.all_gather(key_rows, "ctx", axis=0, tiled=True),
            lax.all_gather(value_rows, "ctx", axis=0, tiled=True),
        ),
        512,
    )
    inv_total = 1.0 / row_total
    attended_grp = weighted * inv_total[..., None]
    attended_b = from_groups(attended_grp, tok_rows, q_group).astype(jnp.bfloat16)
    branch = jnp.dot(attended_b, full_out, preferred_element_type=jnp.float32)
    inv_post, normed_post = rms_parts(branch)
    middle = resid_in + normed_post * post_factor
    inv_mid, normed_mid = rms_parts(middle)
    hidden_ffn = (normed_mid * pre_ffn_factor).astype(jnp.bfloat16)
    gate_up = fold_rows(
        hidden_ffn, lax.all_gather(gateup_shard, ("ctx", "fsdp"), axis=0, tiled=True)
    )
    gate_lin = gate_up[:, :FF]
    up_lin = gate_up[:, FF:]
    active = gated(gate_lin, up_lin).astype(jnp.bfloat16)
    ffn_branch = fold_rows(active, lax.all_gather(w_down, ("ctx", "fsdp"), axis=0, tiled=True))
    inv_ffn, normed_ffn = rms_parts(ffn_branch)
    output = (middle + normed_ffn * post_ffn_factor).astype(jnp.bfloat16)
    out_cot = out_grad[0].astype(jnp.float32)
    post_ffn_part = jnp.sum(out_cot * normed_ffn, axis=0)
    d_ffn_b = norm_back(out_cot * post_ffn_factor, normed_ffn, inv_ffn).astype(jnp.bfloat16)
    down_total = lax.psum_scatter(
        grad_rows(active, d_ffn_b, 1, lax.axis_size(("ctx", "fsdp")) * w_down.shape[0]),
        ("ctx", "fsdp"),
        scatter_dimension=0,
        tiled=True,
    )
    d_active = contract_cols(d_ffn_b, lax.all_gather(w_down, ("ctx", "fsdp"), axis=0, tiled=True))
    unused_value, gate_pull = jax.vjp(gated, gate_lin, up_lin)
    d_gate, d_up = gate_pull(d_active)
    d_gateup_b = jnp.concatenate([d_gate.astype(jnp.bfloat16), d_up.astype(jnp.bfloat16)], axis=1)
    gateup_folded = lax.psum_scatter(
        grad_rows(
            hidden_ffn,
            d_gateup_b,
            ROW_FOLD,
            lax.axis_size(("ctx", "fsdp")) * (ROW_FOLD * shard_rows),
        ),
        ("ctx", "fsdp"),
        scatter_dimension=0,
        tiled=True,
    )
    gateup_total = gateup_folded.reshape(shard_rows, 2 * FF)
    d_hidden_ffn = contract_cols(
        d_gateup_b, lax.all_gather(gateup_shard, ("ctx", "fsdp"), axis=0, tiled=True)
    )
    pre_ffn_part = jnp.sum(d_hidden_ffn * normed_mid, axis=0)
    d_middle = out_cot + norm_back(d_hidden_ffn * pre_ffn_factor, normed_mid, inv_mid)
    back_qkv, back_out = (
        lax.all_gather(qkv_shard, ("ctx", "fsdp"), axis=0, tiled=True),
        lax.all_gather(w_out, ("ctx", "fsdp"), axis=0, tiled=True),
    )
    post_gain_part = jnp.sum(d_middle * normed_post, axis=0)
    d_branch_b = norm_back(d_middle * post_factor, normed_post, inv_post).astype(jnp.bfloat16)
    w_out_part = contract_rows(attended_b, d_branch_b)
    d_attended = contract_cols(d_branch_b, back_out).astype(jnp.bfloat16)
    d_att_grp = to_groups(d_attended, tok_rows, q_group)
    row_delta = jnp.sum(d_att_grp.astype(jnp.float32) * attended_grp, axis=-1)
    zero_rows = jnp.zeros((tok_rows, width_kv), jnp.float32)
    zero_query = jnp.zeros((KVH, q_group * tok_rows, HD), jnp.float32)
    block_ids = jnp.arange(n_ctx, dtype=jnp.int32)
    all_keys, all_values = (
        lax.all_gather(key_rows, "ctx", axis=0, tiled=True),
        lax.all_gather(value_rows, "ctx", axis=0, tiled=True),
    )

    def returned_step(acc_query, block_item):
        block_index, key_block, value_block = block_item
        first_row = block_index * tok_rows

        def returned_compute_block(acc_in):
            d_query, d_key, d_value = block_grads(
                query_grp,
                row_pos,
                d_att_grp,
                row_delta,
                inv_total,
                key_block,
                value_block,
                first_row,
            )
            return (acc_in + d_query, (d_key, d_value))

        def returned_skip_block(acc_in):
            return (acc_in, (zero_rows, zero_rows))

        return lax.cond(
            first_row <= last_pos, returned_compute_block, returned_skip_block, acc_query
        )

    key_blocks = all_keys.reshape(n_ctx, tok_rows, width_kv)
    value_blocks = all_values.reshape(n_ctx, tok_rows, width_kv)
    d_query_grp, key_terms = lax.scan(
        returned_step, zero_query, (block_ids, key_blocks, value_blocks)
    )
    key_term_rows = key_terms[0].reshape(n_ctx * tok_rows, width_kv)
    value_term_rows = key_terms[1].reshape(n_ctx * tok_rows, width_kv)
    d_keys, d_values = (
        lax.psum_scatter(
            key_term_rows.astype(jnp.bfloat16), "ctx", scatter_dimension=0, tiled=True
        ).astype(jnp.float32),
        lax.psum_scatter(
            value_term_rows.astype(jnp.bfloat16), "ctx", scatter_dimension=0, tiled=True
        ).astype(jnp.float32),
    )
    d_query_flat = from_groups(d_query_grp, tok_rows, q_group).reshape(tok_rows, H, HD) * q_scale
    dq_lin = (
        unrotate_heads(d_query_flat, cos_tab, sine_tab).astype(jnp.bfloat16).reshape(tok_rows, width_q)
    )
    dk_lin = (
        unrotate_heads(d_keys.reshape(tok_rows, KVH, HD), cos_tab, sine_tab)
        .astype(jnp.bfloat16)
        .reshape(tok_rows, width_kv)
    )
    dv_lin = d_values.astype(jnp.bfloat16)
    dqkv_b = jnp.concatenate([dq_lin, dk_lin, dv_lin], axis=1)
    d_hidden = contract_cols(dqkv_b, back_qkv)
    qkv_part = contract_rows(hidden, dqkv_b).reshape(ROW_FOLD * D, width_qkv // ROW_FOLD)
    pre_gain_part = jnp.sum(d_hidden * normed_pre, axis=0)
    token_grad = d_middle + norm_back(d_hidden * pre_factor, normed_pre, inv_pre)
    gain_parts = jnp.stack([pre_gain_part, post_gain_part, pre_ffn_part, post_ffn_part])
    qkv_folded, out_total, gain_totals = (
        lax.psum_scatter(qkv_part, ("ctx", "fsdp"), scatter_dimension=0, tiled=True),
        lax.psum_scatter(w_out_part, ("ctx", "fsdp"), scatter_dimension=0, tiled=True),
        lax.psum_scatter(gain_parts, ("ctx", "fsdp"), scatter_dimension=1, tiled=True),
    )
    qkv_total = qkv_folded.reshape(shard_rows, width_qkv)
    return (
        output[None],
        token_grad.astype(jnp.bfloat16)[None],
        qkv_total[:, :width_q],
        qkv_total[:, width_q : width_q + width_kv],
        qkv_total[:, width_q + width_kv :],
        out_total,
        gateup_total[:, :FF],
        gateup_total[:, FF:],
        down_total,
        gain_totals[0],
        gain_totals[1],
        gain_totals[2],
        gain_totals[3],
    )


def solution(mesh):
    ring = mesh.shape["ctx"] == RING and mesh.shape["fsdp"] == 4
    tokens, rows, gains = P("fsdp", "ctx", None), P(("ctx", "fsdp"), None), P(("ctx", "fsdp"))
    return jax.shard_map(
        on_ring if ring else on_any_mesh,
        mesh=mesh,
        in_specs=(tokens,) + (rows,) * 7 + (gains,) * 4 + (tokens,),
        out_specs=(tokens, tokens) + (rows,) * 7 + (gains,) * 4,
        check_vma=False,
    )
```

```python
import functools

import jax
import jax.numpy as jnp
from jax import lax
from jax.experimental import pallas as pl
from jax.experimental.pallas import tpu as pltpu
from jax.sharding import PartitionSpec as P

D = 2304
H = 8
KVH = 4
HD = 256
CAP = 50
FF = 9216

EPSILON = 1e-06
ROPE_BASE = 10000.0

MESH = pl.DeviceIdType.MESH
HBM = pl.BlockSpec(memory_space=pl.ANY)
VMEM = pl.BlockSpec(memory_space=pltpu.VMEM)
DMA = pltpu.SemaphoreType.DMA
BF = jnp.bfloat16
F32 = jnp.float32


def rope_tables(positions, width):
    half_width = width // 2
    inv_freqs = ROPE_BASE ** (-jnp.arange(half_width, dtype=F32) * 2.0 / width)
    angles = positions.astype(F32)[:, None] * inv_freqs[None, :]
    return (jnp.cos(angles), jnp.sin(angles))


def rotate(rows, cos_tab, sine_tab):
    half_width = rows.shape[-1] // 2
    front, back = rows[..., :half_width], rows[..., half_width:]
    return jnp.concatenate(
        [front * cos_tab - back * sine_tab, back * cos_tab + front * sine_tab], axis=-1
    )


def unrotate(rows, cos_tab, sine_tab):
    half_width = rows.shape[-1] // 2
    front, back = rows[..., :half_width], rows[..., half_width:]
    return jnp.concatenate(
        [front * cos_tab + back * sine_tab, back * cos_tab - front * sine_tab], axis=-1
    )


def rms_parts(values_in):
    inverse = lax.rsqrt(jnp.mean(values_in * values_in, axis=-1, keepdims=True) + EPSILON)
    return (inverse, values_in * inverse)


def norm_back(grad_normed, normed, inverse):
    return inverse * (grad_normed - normed * jnp.mean(grad_normed * normed, axis=-1, keepdims=True))


def contract_rows(left, right):
    return lax.dot_general(left, right, (((0,), (0,)), ((), ())), preferred_element_type=F32)


def contract_cols(left, right):
    return lax.dot_general(left, right, (((1,), (1,)), ((), ())), preferred_element_type=F32)


def fold_rows(left, right):
    return jnp.dot(left, right, preferred_element_type=F32)


def gated(gate_in, up_in):
    return jax.nn.gelu(gate_in, approximate=True) * up_in


NZ = 4
RING = 2 * NZ


def my_place():
    c, f = lax.axis_index("ctx"), lax.axis_index("fsdp")
    return c // 2, c % 2, f // 2, f % 2


def ring_index(y, z):
    return z + y * (RING - 1 - 2 * z)


def ring_yz(q):
    y = q // NZ
    return y, q + y * (RING - 1 - 2 * q)


def device(z, core, y, x):
    return (2 * z + core, 2 * y + x)


def ring_device(q, core, x):
    y, z = ring_yz(q)
    return device(z, core, y, x)


def remote(src, dst, send_sem, recv_sem, where):
    return pltpu.make_async_remote_copy(
        src_ref=src,
        dst_ref=dst,
        send_sem=send_sem,
        recv_sem=recv_sem,
        device_id=where,
        device_id_type=MESH,
    )


def greet(places):
    barrier = pltpu.get_barrier_semaphore()
    for place in places:
        pl.semaphore_signal(barrier, inc=1, device_id=place, device_id_type=MESH)
    pl.semaphore_wait(barrier, len(places))


def params(collective_id, vmem_mib=56):
    return pltpu.CompilerParams(
        collective_id=collective_id,
        has_side_effects=True,
        vmem_limit_bytes=vmem_mib * 2**20,
    )


SUB = 4


def ring_parts(direction, step, half_step):
    if step != half_step:
        return list(range(SUB))
    half = SUB // 2
    return list(range(half)) if direction == 0 else list(range(half, SUB))


class RingGather:
    def __init__(self, x_ref, ring_ref, seq_ref, loc_sem, ss, rs, sib_ss=None, sib_rs=None):
        self.x_ref, self.ring_ref, self.seq_ref, self.loc_sem = x_ref, ring_ref, seq_ref, loc_sem
        self.ss, self.rs, self.sib_ss, self.sib_rs = ss, rs, sib_ss, sib_rs
        self.z, self.core, self.y, self.x = my_place()
        self.p = ring_index(self.y, self.z)
        self.right, self.left = (self.p + 1) % RING, (self.p + RING - 1) % RING
        self.sibling = device(self.z, 1 - self.core, self.y, self.x)
        self.piece = x_ref.shape[0] // SUB
        self.pending = []
        self.local = pltpu.make_async_copy(x_ref, ring_ref.at[self.p], loc_sem.at[RING])

    def places(self):
        near = [ring_device(self.right, self.core, self.x), ring_device(self.left, self.core, self.x)]
        return near + ([self.sibling] if self.seq_ref is not None else [])

    def origin(self, direction, step):
        return (self.p + (RING - step if direction == 0 else step)) % RING

    def copy(self, direction, step, k):
        q = self.origin(direction, step)
        rows = pl.ds(k * self.piece, self.piece)
        src = self.x_ref.at[rows] if step == 0 else self.ring_ref.at[q, rows]
        return remote(
            src,
            self.ring_ref.at[q, rows],
            self.ss.at[direction, step, k],
            self.rs.at[direction, step, k],
            ring_device(self.right if direction == 0 else self.left, self.core, self.x),
        )

    def place(self, q, act):
        if self.seq_ref is None:
            return
        yq, zq = ring_yz(q)
        src, dst = self.ring_ref.at[q], self.seq_ref.at[2 * zq + self.core]

        @pl.when(yq == self.core)
        def _():
            act(pltpu.make_async_copy(src, dst, self.loc_sem.at[q]))

        @pl.when(yq != self.core)
        def _():
            act(remote(src, dst, self.sib_ss.at[zq], self.sib_rs.at[zq], self.sibling))

    def step(self, step):
        if step == 0:
            self.local.start()
        for k in range(SUB):
            for direction in (0, 1):
                if step > 0 and (step < 3 or k in ring_parts(direction, 3, 3)):
                    self.copy(direction, step - 1, k).wait_recv()
                if k in ring_parts(direction, step, 3):
                    c = self.copy(direction, step, k)
                    c.start()
                    self.pending.append(c)
        if step == 1:
            self.local.wait()
            self.place(self.p, lambda c: c.start())
        if step == 3:
            for direction in (0, 1):
                for k in range(SUB):
                    if k not in ring_parts(direction, 3, 3):
                        self.copy(direction, 2, k).wait_recv()
        if step > 0:
            for direction in (0, 1):
                self.place(self.origin(direction, step), lambda c: c.start())

    def finish(self):
        for direction in (0, 1):
            for k in ring_parts(direction, 3, 3):
                self.copy(direction, 3, k).wait_recv()
        self.place((self.p + 4) % RING, lambda c: c.start())
        for c in self.pending:
            c.wait_send()
        if self.seq_ref is None:
            return
        for q in range(RING):
            self.place((self.p + q) % RING, lambda c: c.wait_send() if c.is_remote else c.wait())
        for zq in range(NZ):
            dst = self.seq_ref.at[2 * zq + 1 - self.core]
            remote(self.ring_ref.at[zq], dst, self.sib_ss.at[zq], self.sib_rs.at[zq], self.sibling).wait_recv()


def gather_kernel(paired, x_ref, *refs):
    if paired:
        seq_ref, ring_ref, *sems = refs
    else:
        ring_ref, *sems = refs
        seq_ref = None
    ring = RingGather(x_ref, ring_ref, seq_ref, *sems)
    greet(ring.places())
    for step in range(4):
        ring.step(step)
    ring.finish()


def ring_gather(block, collective_id, paired):
    rows, width = block.shape
    whole = jax.ShapeDtypeStruct((RING, rows, width), block.dtype)
    sems = [DMA((RING + 1,)), DMA((2, 4, SUB)), DMA((2, 4, SUB))]
    if paired:
        sems = [pltpu.VMEM(whole.shape, whole.dtype)] + sems + [DMA((NZ,)), DMA((NZ,))]
    out = pl.pallas_call(
        functools.partial(gather_kernel, paired),
        out_shape=whole,
        in_specs=[VMEM],
        out_specs=VMEM if paired else HBM,
        scratch_shapes=sems,
        compiler_params=params(collective_id),
    )(block)
    return out.reshape(RING * rows, width)


def scatter_kernel(paired, part_ref, o_ref, *refs):
    if paired:
        mine_ref, buf, ss, rs, sib_ss, sib_rs, loc_sem = refs
    else:
        buf, ss, rs = refs
        mine_ref = part_ref
    z, core, y, x = my_place()
    p = ring_index(y, z)
    right, left = (p + 1) % RING, (p + RING - 1) % RING
    sibling = device(z, 1 - core, y, x)
    piece = o_ref.shape[0] // SUB
    greet(
        [ring_device(right, core, x), ring_device(left, core, x)] + ([sibling] if paired else [])
    )
    if paired:
        swaps, copies = [], []
        for zq in range(NZ):
            q = ring_index(core, zq)
            swaps.append(remote(part_ref.at[2 * zq + 1 - core], mine_ref.at[q], sib_ss.at[zq], sib_rs.at[zq], sibling))
            swaps[-1].start()
            copies.append(pltpu.make_async_copy(part_ref.at[2 * zq + core], mine_ref.at[q], loc_sem.at[zq]))
            copies[-1].start()
        for c in copies:
            c.wait()
        for zq in range(NZ):
            q = ring_index(1 - core, zq)
            remote(part_ref.at[zq], mine_ref.at[q], sib_ss.at[zq], sib_rs.at[zq], sibling).wait_recv()
        for c in swaps:
            c.wait_send()

    def copy(direction, step, k, src):
        rows = pl.ds(k * piece, piece)
        return remote(
            src,
            buf.at[direction, step, rows],
            ss.at[direction, step, k],
            rs.at[direction, step, k],
            ring_device(right if direction == 0 else left, core, x),
        )

    pending = []
    for step in range(4):
        for k in range(SUB):
            rows = pl.ds(k * piece, piece)
            for direction in (0, 1):
                if k not in ring_parts(direction, step, 0):
                    continue
                far = 4 - step
                q = (p + (far if direction == 0 else RING - far)) % RING
                src = mine_ref.at[q, rows]
                if step > 0 and k in ring_parts(direction, step - 1, 0):
                    src = buf.at[direction, step - 1, rows]
                    copy(direction, step - 1, k, src).wait_recv()
                    total = src[...].astype(F32) + mine_ref[q, rows].astype(F32)
                    src[...] = total.astype(BF)
                c = copy(direction, step, k, src)
                c.start()
                pending.append(c)
    for k in range(SUB):
        rows = pl.ds(k * piece, piece)
        total = mine_ref[p, rows].astype(F32)
        for direction in (0, 1):
            src = buf.at[direction, 3, rows]
            copy(direction, 3, k, src).wait_recv()
            total = total + src[...].astype(F32)
        o_ref[rows] = total
    for c in pending:
        c.wait_send()


def ring_scatter(part, collective_id, paired):
    rows, width = part.shape[0] // RING, part.shape[1]
    blocks = (RING, rows, width)
    sems = [DMA((2, 4, SUB)), DMA((2, 4, SUB))]
    return pl.pallas_call(
        functools.partial(scatter_kernel, paired),
        out_shape=jax.ShapeDtypeStruct((rows, width), F32),
        in_specs=[VMEM],
        out_specs=VMEM,
        scratch_shapes=([pltpu.VMEM(blocks, BF)] if paired else [])
        + [pltpu.VMEM((2, 4, rows, width), BF)]
        + sems
        + ([DMA((NZ,)), DMA((NZ,)), DMA((NZ,))] if paired else []),
        compiler_params=params(collective_id),
    )(part.astype(BF).reshape(blocks))


UNITS = FF // RING
WIDTHS = (UNITS, UNITS, HD, HD, HD)
STARTS = (0, UNITS, 2 * UNITS, 2 * UNITS + HD, 2 * UNITS + 2 * HD)
WIDE = 2 * UNITS + 3 * HD


def member_place(t, core, x):
    return device(t // 2, core, t % 2, x)


def partner(t, j):
    out = 0
    for bit in (1, 2, 4):
        on = (t // bit) % 2
        out = out + bit * (1 - on if j & bit else on)
    return out


def column_start(which, t):
    if which < 2:
        return pl.multiple_of(t * UNITS, 128)
    return pl.multiple_of((t if which == 2 else t // 2) * HD, 128)


def weights_in_kernel(gate, up, query, key, value, down, out, gains, x_ref, w_ref, d_ref, o_ref, g_ref, seq_ref,
                      ring_ref, loc, s1, r1, s2, r2, s3, r3, s4, r4, s5, r5, ring_loc, ss, rs, sib_ss, sib_rs):
    z, core, y, x = my_place()
    t = 2 * z + y
    sibling, across = device(z, 1 - core, y, x), device(z, core, y, 1 - x)

    def slot(tq, corq, xq):
        return (2 * (tq // 2) + corq) * 4 + 2 * (tq % 2) + xq

    me = slot(t, core, x)
    member = [partner(t, j) for j in range(RING)]
    plane = []
    for dc in (0, 1):
        for dy in (0, 1):
            for dx in (0, 1):
                if (dc, dx) != (0, 0):
                    plane.append(device(z, (core + dc) % 2, (y + dy) % 2, (x + dx) % 2))
    greet([member_place(member[j], core, x) for j in range(1, RING)] + plane)
    sources = (gate, up, query, key, value)
    ring = RingGather(x_ref, ring_ref, seq_ref, ring_loc, ss, rs, sib_ss, sib_rs)

    def first(j, a, wait=False):
        tq = member[j]
        if a == 5:
            src, dst = gains, g_ref.at[slot(tq, core, x) if wait else me]
        else:
            src = sources[a].at[:, pl.ds(column_start(a, tq), WIDTHS[a])]
            dst = w_ref.at[slot(tq, core, x) if wait else me, :, pl.ds(STARTS[a], WIDTHS[a])]
        return remote(src, dst, s1.at[j, a], r1.at[j, a], member_place(tq, core, x))

    pending = []

    def go(copies):
        for c in copies:
            c.start()
            pending.append(c)

    def second(j, wait=False):
        i = slot(member[j], core, 1 - x if wait else x)
        return [
            remote(w_ref.at[i], w_ref.at[i], s2.at[j, 0], r2.at[j, 0], across),
            remote(g_ref.at[i], g_ref.at[i], s2.at[j, 1], r2.at[j, 1], across),
        ]

    def third(j, flip, wait=False):
        i = slot(member[j], 1 - core if wait else core, 1 - x if flip else x)
        return [
            remote(w_ref.at[i], w_ref.at[i], s3.at[j, flip, 0], r3.at[j, flip, 0], sibling),
            remote(g_ref.at[i], g_ref.at[i], s3.at[j, flip, 1], r3.at[j, flip, 1], sibling),
        ]

    def start_round(j):
        go([first(j, a) for a in (5, 2, 3, 4, 0, 1)])

    def end_round(j):
        for a in range(6):
            first(j, a, True).wait_recv()
        go(second(j) + third(j, 0))

    def end_across(j):
        for c in second(j, True):
            c.wait_recv()
        go(third(j, 1))

    ring.step(0)
    start_round(4)
    start_round(1)
    locals_ = [pltpu.make_async_copy(gains, g_ref.at[me], loc.at[5])]
    for a in range(5):
        locals_.append(
            pltpu.make_async_copy(
                sources[a].at[:, pl.ds(column_start(a, t), WIDTHS[a])],
                w_ref.at[me, :, pl.ds(STARTS[a], WIDTHS[a])],
                loc.at[a],
            )
        )
    for c in locals_:
        c.start()
    pair = ((down, d_ref), (out, o_ref))
    mine = 2 * y + x
    for xq in (0, 1):
        to_self = (x == core) & (y == core) & (xq == x)
        for a, (src, dst) in enumerate(pair):
            @pl.when(to_self)
            def _():
                pltpu.make_async_copy(src, dst.at[mine], s4.at[xq, a]).start()

            @pl.when(jnp.logical_not(to_self))
            def _():
                remote(src, dst.at[mine], s4.at[xq, a], r4.at[y, a], device(z, x, core, xq)).start()
    for c in locals_:
        c.wait()
    go(second(0) + third(0, 0))
    ring.step(1)
    end_round(1)
    start_round(2)
    end_round(4)
    start_round(5)
    ring.step(2)
    end_round(2)
    start_round(3)
    end_across(0)
    end_across(1)
    end_round(5)
    start_round(6)
    ring.step(3)
    end_round(3)
    start_round(7)
    end_across(4)
    for yq in (0, 1):
        from_self = (core == y) & (yq == y) & (core == x)
        for a, (src, dst) in enumerate(pair):
            @pl.when(from_self)
            def _():
                pltpu.make_async_copy(src, dst.at[mine], s4.at[x, a]).wait()

            @pl.when(jnp.logical_not(from_self))
            def _():
                remote(src, dst.at[2 * yq + core], s4.at[0, a], r4.at[yq, a], sibling).wait_recv()

            go([remote(dst.at[2 * yq + core], dst.at[2 * yq + core], s5.at[yq, a], r5.at[yq, a], sibling)])
    end_across(2)
    end_across(5)
    ring.finish()
    end_round(6)
    end_across(3)
    end_round(7)
    end_across(6)
    end_across(7)
    for j in range(RING):
        for flip in (0, 1):
            for c in third(j, flip, True):
                c.wait_recv()
    for yq in (0, 1):
        for a, (src, dst) in enumerate(pair):
            remote(src, dst.at[2 * yq + 1 - core], s5.at[yq, a], r5.at[yq, a], sibling).wait_recv()
    for c in pending:
        c.wait_send()
    for xq in (0, 1):
        to_self = (x == core) & (y == core) & (xq == x)
        for a, (src, dst) in enumerate(pair):
            @pl.when(jnp.logical_not(to_self))
            def _():
                remote(src, dst.at[mine], s4.at[xq, a], r4.at[y, a], device(z, x, core, xq)).wait_send()


def weights_in(gate, up, query, key, value, down, out, gains, block, collective_id):
    n = 4 * RING
    whole = (RING,) + block.shape
    shapes = [
        jax.ShapeDtypeStruct((n, gate.shape[0], WIDE), BF),
        jax.ShapeDtypeStruct((4,) + down.shape, BF),
        jax.ShapeDtypeStruct((4,) + out.shape, BF),
        jax.ShapeDtypeStruct((n,) + gains.shape, gains.dtype),
        jax.ShapeDtypeStruct(whole, BF),
    ]
    results = pl.pallas_call(
        weights_in_kernel,
        out_shape=shapes,
        in_specs=[VMEM] * 9,
        out_specs=[HBM] * 4 + [VMEM],
        scratch_shapes=[
            pltpu.VMEM(whole, BF),
            DMA((6,)),
            DMA((RING, 6)), DMA((RING, 6)),
            DMA((RING, 2)), DMA((RING, 2)),
            DMA((RING, 2, 2)), DMA((RING, 2, 2)),
            DMA((2, 2)), DMA((2, 2)),
            DMA((2, 2)), DMA((2, 2)),
            DMA((RING + 1,)), DMA((2, 4, SUB)), DMA((2, 4, SUB)), DMA((NZ,)), DMA((NZ,)),
        ],
        compiler_params=params(collective_id, 32),
    )(gate, up, query, key, value, down, out, gains, block)
    return list(results[:4]) + [results[4].reshape(RING * block.shape[0], block.shape[1])]


def add_into(dst, index, src, other):
    dst[index] = (dst[index].astype(F32) + src[other].astype(F32)).astype(BF)


def weights_out_kernel(gu_in, qkv_in, down_in, out_in, gain_in,
                       gate_o, up_o, query_o, key_o, value_o, down_o, out_o, gain_o,
                       a_buf, b_buf, c_buf, acc, da, db, dacc, dd, oa, ob, oacc, od, ga, gsum,
                       loc, sa, ra, sb, rb, sc, rc, sx, rx, sg, rg):
    z, core, y, x = my_place()
    t = 2 * z + y
    sibling, across = device(z, 1 - core, y, x), device(z, core, y, 1 - x)
    diagonal = device(z, 1 - core, 1 - y, x)
    others = [(t + j) % RING for j in range(1, RING)]
    greet([member_place(tq, core, x) for tq in others] + [sibling, across, diagonal])

    def slot(tq, corq, xq):
        return (2 * (tq // 2) + corq) * 4 + 2 * (tq % 2) + xq

    def load(tq, xq):
        i = slot(tq, core, xq)
        return [
            pltpu.make_async_copy(gu_in.at[i], acc.at[xq, tq, :, pl.ds(0, 2 * UNITS)], loc.at[xq, tq, 0]),
            pltpu.make_async_copy(qkv_in.at[i], acc.at[xq, tq, :, pl.ds(2 * UNITS, 3 * HD)], loc.at[xq, tq, 1]),
        ]

    def to_sibling(tq, xq):
        i = slot(tq, 1 - core, xq)
        return [
            remote(gu_in.at[i], a_buf.at[xq, tq, :, pl.ds(0, 2 * UNITS)], sa.at[xq, tq, 0], ra.at[xq, tq, 0], sibling),
            remote(qkv_in.at[i], a_buf.at[xq, tq, :, pl.ds(2 * UNITS, 3 * HD)], sa.at[xq, tq, 1], ra.at[xq, tq, 1], sibling),
        ]

    def to_across(tq):
        return remote(acc.at[1 - x, tq], b_buf.at[tq], sb.at[tq], rb.at[tq], across)

    def to_member(tq, wait=False):
        return remote(acc.at[x, tq], c_buf.at[tq if wait else t], sc.at[tq], rc.at[tq if wait else t], member_place(tq, core, x))

    order = [partner(t, j) for j in (4, 5, 6, 7, 2, 3, 1, 0)]

    small = ((down_in, da, db, dacc, dd, down_o), (out_in, oa, ob, oacc, od, out_o))

    def small_a(a, xo):
        src, buf = small[a][0], small[a][1]
        return remote(src.at[2 * (1 - core) + xo], buf.at[xo], sx.at[a, xo], rx.at[a, xo], sibling)

    def small_b(a):
        return remote(small[a][3].at[1 - x], small[a][2], sx.at[a, 2], rx.at[a, 2], across)

    def small_c(a):
        return remote(small[a][3].at[x], small[a][4], sx.at[a, 3], rx.at[a, 3], diagonal)

    def small_load(a, xo):
        return pltpu.make_async_copy(small[a][0].at[2 * core + xo], small[a][3].at[xo], loc.at[a, xo, 2])

    def gain_a():
        return remote(gain_in, ga.at[RING], sg.at[RING], rg.at[RING], sibling)

    def gain_b():
        return remote(gsum.at[0], ga.at[RING + 1], sg.at[RING + 1], rg.at[RING + 1], across)

    def gain_c(tq, wait=False):
        return remote(gsum.at[1], ga.at[tq if wait else t], sg.at[tq], rg.at[tq if wait else t], member_place(tq, core, x))

    def start_a(tq, xq):
        for c in load(tq, xq) + to_sibling(tq, xq):
            c.start()

    def sum_a(tq, xq):
        for c in load(tq, xq):
            c.wait()
        for c in to_sibling(tq, xq):
            c.wait_recv()
        acc[xq, tq] = (acc[xq, tq].astype(F32) + a_buf[xq, tq].astype(F32)).astype(BF)

    def small_start(a):
        buf, total = small[a][1], small[a][3]
        for xo in (0, 1):
            small_load(a, xo).wait()
            small_a(a, xo).wait_recv()
            total[xo] = (total[xo].astype(F32) + buf[xo].astype(F32)).astype(BF)
        small_b(a).start()

    for tq in order:
        start_a(tq, 1 - x)
    gain_a().start()
    for a in (1, 0):
        for xo in (0, 1):
            small_a(a, xo).start()
            small_load(a, xo).start()
    for tq in order:
        start_a(tq, x)
    ahead = 2
    for tq in order[:ahead]:
        sum_a(tq, 1 - x)
        to_across(tq).start()
    gain_a().wait_recv()
    gsum[0] = gain_in[...] + ga[RING]
    gain_b().start()
    small_start(1)
    for tq in order[ahead:]:
        sum_a(tq, 1 - x)
    for j, tq in enumerate(order):
        sum_a(tq, x)
        to_across(tq).wait_recv()
        if j + ahead < RING:
            to_across(order[j + ahead]).start()
        elif j + ahead == RING:
            small_start(0)
        if j == 0:
            gain_b().wait_recv()
            gsum[1] = gsum[0] + ga[RING + 1]
            for other in others:
                gain_c(other).start()
        acc[x, tq] = (acc[x, tq].astype(F32) + b_buf[tq].astype(F32)).astype(BF)
        if j < RING - 1:
            to_member(tq).start()
    for a in (1, 0):
        other, total = small[a][2:4]
        small_b(a).wait_recv()
        total[x] = (total[x].astype(F32) + other[...].astype(F32)).astype(BF)
        for xo in (0, 1):
            small_a(a, xo).wait_send()

    @pl.when(core == y)
    def _():
        for a in (0, 1):
            small[a][5][...] = small[a][3][x].astype(F32)

    @pl.when(core != y)
    def _():
        for a in (0, 1):
            small_c(a).start()
        for a in (0, 1):
            small_c(a).wait_recv()
            small[a][5][...] = small[a][4][...].astype(F32)
        for a in (0, 1):
            small_c(a).wait_send()

    total = gsum[1]
    for tq in others:
        gain_c(tq, True).wait_recv()
        total = total + ga[tq]
    gain_o[...] = total
    c_buf[t] = acc[x, t]
    for tq in others:
        to_member(tq, True).wait_recv()
    for tq in range(RING):
        units = pl.ds(tq * UNITS, UNITS)
        gate_o[:, units] = c_buf[tq, :, pl.ds(0, UNITS)].astype(F32)
        up_o[:, units] = c_buf[tq, :, pl.ds(UNITS, UNITS)].astype(F32)
        query_o[:, pl.ds(tq * HD, HD)] = c_buf[tq, :, pl.ds(STARTS[2], HD)].astype(F32)
    for g in range(KVH):
        for start, result in ((STARTS[3], key_o), (STARTS[4], value_o)):
            columns = pl.ds(start, HD)
            result[:, pl.ds(g * HD, HD)] = c_buf[2 * g, :, columns].astype(F32) + c_buf[2 * g + 1, :, columns].astype(F32)

    for j, tq in enumerate(order):
        for xq in (0, 1):
            for c in to_sibling(tq, xq):
                c.wait_send()
        to_across(tq).wait_send()
        if j < RING - 1:
            to_member(tq).wait_send()
    gain_a().wait_send()
    gain_b().wait_send()
    for tq in others:
        gain_c(tq).wait_send()
    for a in (0, 1):
        small_b(a).wait_send()


def weights_out(gu, qkv, down, out, gains, collective_id):
    n = 4 * RING
    rows, width = gu.shape[0] // n, gains.shape[1]
    gu, qkv = gu.reshape(n, rows, 2 * UNITS), qkv.reshape(n, rows, 3 * HD)
    down, out = down.reshape(4, -1, width), out.reshape(4, -1, width)
    down_rows, out_rows = down.shape[1], out.shape[1]
    wide = (RING, rows, WIDE)

    def full(*shape):
        return jax.ShapeDtypeStruct(shape, F32)

    return pl.pallas_call(
        weights_out_kernel,
        out_shape=[
            full(rows, FF), full(rows, FF), full(rows, H * HD), full(rows, KVH * HD), full(rows, KVH * HD),
            full(down_rows, width), full(out_rows, width), full(*gains.shape),
        ],
        in_specs=[HBM] * 4 + [VMEM],
        out_specs=[VMEM] * 8,
        scratch_shapes=[
            pltpu.VMEM((2,) + wide, BF), pltpu.VMEM(wide, BF), pltpu.VMEM(wide, BF), pltpu.VMEM((2,) + wide, BF),
            pltpu.VMEM((2, down_rows, width), BF), pltpu.VMEM((down_rows, width), BF), pltpu.VMEM((2, down_rows, width), BF), pltpu.VMEM((down_rows, width), BF),
            pltpu.VMEM((2, out_rows, width), BF), pltpu.VMEM((out_rows, width), BF), pltpu.VMEM((2, out_rows, width), BF), pltpu.VMEM((out_rows, width), BF),
            pltpu.VMEM((RING + 2,) + gains.shape, F32), pltpu.VMEM((2,) + gains.shape, F32),
            DMA((2, RING, 3)),
            DMA((2, RING, 2)), DMA((2, RING, 2)),
            DMA((RING,)), DMA((RING,)),
            DMA((RING,)), DMA((RING,)),
            DMA((2, 4)), DMA((2, 4)),
            DMA((RING + 2,)), DMA((RING + 2,)),
        ],
        compiler_params=params(collective_id),
    )(gu, qkv, down, out, gains)


def attend(queries, keys, values, positions):
    raw = contract_cols(queries, keys)
    capped = CAP * jnp.tanh(raw / CAP)
    allowed = positions[None, :] <= positions[:, None]
    weights = jnp.where(allowed, jnp.exp(capped), 0.0)
    inv_total = 1.0 / jnp.sum(weights, axis=-1, keepdims=True)
    attended = fold_rows(weights.astype(BF), values) * inv_total
    return attended, inv_total


def attend_back(queries, keys, values, positions, attended, inv_total, d_attended):
    raw = contract_cols(queries, keys)
    capped = CAP * jnp.tanh(raw / CAP)
    allowed = positions[None, :] <= positions[:, None]
    weights = jnp.where(allowed, jnp.exp(capped), 0.0)
    delta = jnp.sum(d_attended.astype(F32) * attended, axis=-1, keepdims=True)
    d_probs = contract_cols(d_attended, values)
    slope = 1.0 - capped / CAP * (capped / CAP)
    d_raw = (weights * inv_total * (d_probs - delta) * slope).astype(BF)
    d_query = fold_rows(d_raw, keys)
    d_key = contract_rows(d_raw, queries)
    weights_b = weights.astype(BF)
    d_scaled = d_attended.astype(F32) * inv_total
    scaled_high = d_scaled.astype(BF)
    scaled_rest = (d_scaled - scaled_high.astype(F32)).astype(BF)
    d_value = contract_rows(weights_b, scaled_high) + contract_rows(weights_b, scaled_rest)
    return d_query, d_key, d_value


def on_ring(
    tokens, w_query, w_key, w_value, w_out, w_gate, w_up, w_down,
    pre_gain, post_gain, pre_ffn_gain, post_ffn_gain, out_grad,
):
    ids = iter(range(32))
    n_shards = 4 * RING
    length = RING * tokens.shape[1]
    shard_gain = pre_gain.shape[0]
    gains = jnp.stack([pre_gain, post_gain, pre_ffn_gain, post_ffn_gain]).astype(F32)
    gains = jnp.pad(gains, ((0, 4), (0, 128 - shard_gain)))
    w_in, down_in, out_in, gains_in, sequence = weights_in(
        w_gate, w_up, w_query, w_key, w_value, w_down, w_out, gains, tokens[0], next(ids)
    )
    w_in = w_in.reshape(-1, WIDE)
    w_gu, w_qkv = w_in[:, : 2 * UNITS], w_in[:, 2 * UNITS :]
    w_dn = down_in.reshape(UNITS, D)
    w_ot = out_in.reshape(HD, D)
    factors = 1.0 + jnp.transpose(gains_in[:, :4, :shard_gain], (1, 0, 2)).reshape(4, D)
    pre_factor, post_factor, pre_ffn_factor, post_ffn_factor = (factors[i] for i in range(4))
    positions = jnp.arange(length, dtype=jnp.int32)
    cos_tab, sine_tab = rope_tables(positions, HD)
    q_scale = HD ** (-0.5)

    resid_in = tokens[0].astype(F32)
    inv_pre, normed_pre = rms_parts(resid_in)
    hidden = (rms_parts(sequence.astype(F32))[1] * pre_factor).astype(BF)
    projected = fold_rows(hidden, w_qkv)
    queries = (rotate(projected[:, :HD], cos_tab, sine_tab) * q_scale).astype(BF)
    keys = rotate(projected[:, HD : 2 * HD], cos_tab, sine_tab).astype(BF)
    values = projected[:, 2 * HD :].astype(BF)
    attended, inv_total = attend(queries, keys, values, positions)
    attended_b = attended.astype(BF)
    branch = ring_scatter(fold_rows(attended_b, w_ot), next(ids), True)
    inv_post, normed_post = rms_parts(branch)
    middle = resid_in + normed_post * post_factor
    inv_mid, normed_mid = rms_parts(middle)
    hidden_ffn = ring_gather((normed_mid * pre_ffn_factor).astype(BF), next(ids), False)
    gate_up = fold_rows(hidden_ffn, w_gu)
    gate_lin, up_lin = gate_up[:, :UNITS], gate_up[:, UNITS:]
    active = gated(gate_lin, up_lin).astype(BF)
    ffn_branch = ring_scatter(fold_rows(active, w_dn), next(ids), False)
    inv_ffn, normed_ffn = rms_parts(ffn_branch)
    output = (middle + normed_ffn * post_ffn_factor).astype(BF)

    out_cot = out_grad[0].astype(F32)
    post_ffn_part = jnp.sum(out_cot * normed_ffn, axis=0)
    d_ffn = norm_back(out_cot * post_ffn_factor, normed_ffn, inv_ffn).astype(BF)
    d_ffn = ring_gather(d_ffn, next(ids), False)
    down_part = contract_rows(active, d_ffn)
    d_active = contract_cols(d_ffn, w_dn)
    unused_value, gate_pull = jax.vjp(gated, gate_lin, up_lin)
    d_gate, d_up = gate_pull(d_active)
    d_gu = jnp.concatenate([d_gate.astype(BF), d_up.astype(BF)], axis=1)
    d_hidden_ffn = ring_scatter(contract_cols(d_gu, w_gu), next(ids), False)
    gu_part = contract_rows(hidden_ffn, d_gu)
    pre_ffn_part = jnp.sum(d_hidden_ffn * normed_mid, axis=0)
    d_middle = out_cot + norm_back(d_hidden_ffn * pre_ffn_factor, normed_mid, inv_mid)
    post_part = jnp.sum(d_middle * normed_post, axis=0)
    d_branch = norm_back(d_middle * post_factor, normed_post, inv_post).astype(BF)
    d_branch = ring_gather(d_branch, next(ids), True)
    out_part = contract_rows(attended_b, d_branch)
    d_attended = contract_cols(d_branch, w_ot).astype(BF)
    d_query, d_key, d_value = attend_back(
        queries, keys, values, positions, attended, inv_total, d_attended
    )
    d_qkv = jnp.concatenate(
        [
            unrotate(d_query * q_scale, cos_tab, sine_tab).astype(BF),
            unrotate(d_key, cos_tab, sine_tab).astype(BF),
            d_value.astype(BF),
        ],
        axis=1,
    )
    d_hidden = ring_scatter(contract_cols(d_qkv, w_qkv), next(ids), True)
    qkv_part = contract_rows(hidden, d_qkv)
    pre_part = jnp.sum(d_hidden * normed_pre, axis=0)
    token_grad = d_middle + norm_back(d_hidden * pre_factor, normed_pre, inv_pre)
    gain_parts = jnp.pad(jnp.stack([pre_part, post_part, pre_ffn_part, post_ffn_part]), ((0, 4), (0, 0)))
    results = weights_out(
        gu_part.astype(BF), qkv_part.astype(BF), down_part.astype(BF), out_part.astype(BF),
        gain_parts, next(ids),
    )
    gate_g, up_g, query_g, key_g, value_g, down_g, out_g, gain_g = results
    mine = lax.axis_index("ctx") * 4 + lax.axis_index("fsdp")
    gain_g = lax.dynamic_slice(gain_g, (0, mine * shard_gain), (4, shard_gain))
    return (
        output[None], token_grad.astype(BF)[None],
        query_g, key_g, value_g, out_g, gate_g, up_g, down_g,
        gain_g[0], gain_g[1], gain_g[2], gain_g[3],
    )


ROW_FOLD = 4


def head_tables(positions, width):
    half_width = width // 2
    inv_freqs = ROPE_BASE ** (-jnp.arange(half_width, dtype=jnp.float32) * 2.0 / width)
    angles = positions.astype(jnp.float32)[:, None] * inv_freqs[None, :]
    return (jnp.cos(angles)[:, None, :], jnp.sin(angles)[:, None, :])


def rotate_heads(heads_in, cos_tab, sine_tab):
    half_width = heads_in.shape[-1] // 2
    front_half = heads_in[..., :half_width]
    back_half = heads_in[..., half_width:]
    return jnp.concatenate(
        [front_half * cos_tab - back_half * sine_tab, back_half * cos_tab + front_half * sine_tab],
        axis=-1,
    )


def unrotate_heads(grad_in, cos_tab, sine_tab):
    half_width = grad_in.shape[-1] // 2
    front_half = grad_in[..., :half_width]
    back_half = grad_in[..., half_width:]
    return jnp.concatenate(
        [front_half * cos_tab + back_half * sine_tab, back_half * cos_tab - front_half * sine_tab],
        axis=-1,
    )


def to_groups(flat_heads, tok_rows, q_group):
    shaped = flat_heads.reshape(tok_rows, KVH, q_group, HD)
    return jnp.transpose(shaped, (1, 2, 0, 3)).reshape(KVH, q_group * tok_rows, HD)


def from_groups(grouped, tok_rows, q_group):
    shaped = grouped.reshape(KVH, q_group, tok_rows, HD)
    return jnp.transpose(shaped, (2, 0, 1, 3)).reshape(tok_rows, KVH * q_group * HD)


def grad_rows(left, right, folding, count):
    block = contract_rows(left, right)
    return block.reshape(count, right.shape[1] // folding)


def blockwise(step_fn, carry, piece, width):
    key_count = piece[0].shape[0]
    n_steps = key_count // width
    stacked = tuple((member.reshape(n_steps, width, member.shape[1]) for member in piece))

    def one_step(partial_value, block_item):
        block_index, members = block_item
        return (step_fn(partial_value, members, block_index * width), None)

    carry, unused = lax.scan(one_step, carry, (jnp.arange(n_steps, dtype=jnp.int32), stacked))
    return carry


def block_grads(query_g, query_pos, d_att_g, delta, inv_tot, key_block, value_block, key_first):
    key_count = key_block.shape[0]
    key_grp = key_block.reshape(key_count, KVH, HD)
    value_grp = value_block.reshape(key_count, KVH, HD)
    raw_scores = jnp.einsum("grd,ngd->grn", query_g, key_grp, preferred_element_type=jnp.float32)
    capped = CAP * jnp.tanh(raw_scores / CAP)
    key_pos = key_first + jnp.arange(key_count, dtype=jnp.int32)
    allowed = key_pos[None, None, :] <= query_pos[None, :, None]
    weights = jnp.where(allowed, jnp.exp(capped), 0.0)
    prob_rows = weights * inv_tot[..., None]
    d_probs = jnp.einsum("grd,ngd->grn", d_att_g, value_grp, preferred_element_type=jnp.float32)
    slope = 1.0 - capped / CAP * (capped / CAP)
    d_raw = (prob_rows * (d_probs - delta[..., None]) * slope).astype(jnp.bfloat16)
    d_query = jnp.einsum("grn,ngd->grd", d_raw, key_grp, preferred_element_type=jnp.float32)
    d_key = jnp.einsum("grn,grd->ngd", d_raw, query_g, preferred_element_type=jnp.float32)
    weights_b = weights.astype(jnp.bfloat16)
    d_scaled = d_att_g.astype(jnp.float32) * inv_tot[..., None]
    scaled_high = d_scaled.astype(jnp.bfloat16)
    scaled_rest = (d_scaled - scaled_high.astype(jnp.float32)).astype(jnp.bfloat16)
    d_value = jnp.einsum("grn,grd->ngd", weights_b, scaled_high, preferred_element_type=jnp.float32)
    d_value = d_value + jnp.einsum(
        "grn,grd->ngd", weights_b, scaled_rest, preferred_element_type=jnp.float32
    )
    return (d_query, d_key.reshape(key_count, KVH * HD), d_value.reshape(key_count, KVH * HD))


def on_any_mesh(
    tokens,
    w_query,
    w_key,
    w_value,
    w_out,
    w_gate,
    w_up,
    w_down,
    pre_gain,
    post_gain,
    pre_ffn_gain,
    post_ffn_gain,
    out_grad,
):
    tok_rows = tokens.shape[1]
    q_group = H // KVH
    q_scale = HD ** (-0.5)
    width_q = H * HD
    width_kv = KVH * HD
    width_qkv = width_q + 2 * width_kv
    n_ctx = lax.axis_size("ctx")
    my_block = lax.axis_index("ctx")
    my_start = my_block * tok_rows
    positions = my_start + jnp.arange(tok_rows, dtype=jnp.int32)
    cos_tab, sine_tab = head_tables(positions, HD)
    row_pos = jnp.tile(positions, q_group)
    last_pos = my_start + tok_rows - 1
    resid_in = tokens[0].astype(jnp.float32)
    qkv_shard = jnp.concatenate([w_query, w_key, w_value], axis=1)
    gateup_shard = jnp.concatenate([w_gate, w_up], axis=1)
    shard_rows = qkv_shard.shape[0]
    gains_shard = jnp.stack([pre_gain, post_gain, pre_ffn_gain, post_ffn_gain])
    full_gains, full_qkv, full_out = (
        lax.all_gather(gains_shard, ("ctx", "fsdp"), axis=1, tiled=True),
        lax.all_gather(qkv_shard, ("ctx", "fsdp"), axis=0, tiled=True),
        lax.all_gather(w_out, ("ctx", "fsdp"), axis=0, tiled=True),
    )
    factors = 1.0 + full_gains.astype(jnp.float32)
    pre_factor, post_factor, pre_ffn_factor, post_ffn_factor = (
        factors[0],
        factors[1],
        factors[2],
        factors[3],
    )
    inv_pre, normed_pre = rms_parts(resid_in)
    hidden = (normed_pre * pre_factor).astype(jnp.bfloat16)
    projected = jnp.dot(hidden, full_qkv, preferred_element_type=jnp.float32)
    query_lin = projected[:, :width_q].reshape(tok_rows, H, HD)
    queries = (
        (rotate_heads(query_lin, cos_tab, sine_tab) * q_scale)
        .astype(jnp.bfloat16)
        .reshape(tok_rows, width_q)
    )
    query_grp = to_groups(queries, tok_rows, q_group)
    key_lin = projected[:, width_q : width_q + width_kv].reshape(tok_rows, KVH, HD)
    key_rows = rotate_heads(key_lin, cos_tab, sine_tab).astype(jnp.bfloat16).reshape(tok_rows, width_kv)
    value_rows = projected[:, width_q + width_kv :].astype(jnp.bfloat16)

    def add_block(partial_value, piece, first_row):
        key_block, value_block = piece

        def add_compute_block(state):
            row_total, weighted = state
            key_count = key_block.shape[0]
            key_grp = key_block.reshape(key_count, KVH, HD)
            raw_scores = jnp.einsum(
                "grd,ngd->grn", query_grp, key_grp, preferred_element_type=jnp.float32
            )
            capped = CAP * jnp.tanh(raw_scores / CAP)
            key_pos = first_row + jnp.arange(key_count, dtype=jnp.int32)
            allowed = key_pos[None, None, :] <= row_pos[None, :, None]
            weights = jnp.where(allowed, jnp.exp(capped), 0.0)
            value_grp = value_block.reshape(key_count, KVH, HD)
            weighted = weighted + jnp.einsum(
                "grn,ngd->grd",
                weights.astype(jnp.bfloat16),
                value_grp,
                preferred_element_type=jnp.float32,
            )
            return (row_total + jnp.sum(weights, axis=-1), weighted)

        def add_skip_block(state):
            return state

        return lax.cond(first_row <= last_pos, add_compute_block, add_skip_block, partial_value)

    start_state = (
        jnp.zeros((KVH, q_group * tok_rows), jnp.float32),
        jnp.zeros((KVH, q_group * tok_rows, HD), jnp.float32),
    )
    row_total, weighted = blockwise(
        add_block,
        start_state,
        (
            lax.all_gather(key_rows, "ctx", axis=0, tiled=True),
            lax.all_gather(value_rows, "ctx", axis=0, tiled=True),
        ),
        512,
    )
    inv_total = 1.0 / row_total
    attended_grp = weighted * inv_total[..., None]
    attended_b = from_groups(attended_grp, tok_rows, q_group).astype(jnp.bfloat16)
    branch = jnp.dot(attended_b, full_out, preferred_element_type=jnp.float32)
    inv_post, normed_post = rms_parts(branch)
    middle = resid_in + normed_post * post_factor
    inv_mid, normed_mid = rms_parts(middle)
    hidden_ffn = (normed_mid * pre_ffn_factor).astype(jnp.bfloat16)
    gate_up = fold_rows(
        hidden_ffn, lax.all_gather(gateup_shard, ("ctx", "fsdp"), axis=0, tiled=True)
    )
    gate_lin = gate_up[:, :FF]
    up_lin = gate_up[:, FF:]
    active = gated(gate_lin, up_lin).astype(jnp.bfloat16)
    ffn_branch = fold_rows(active, lax.all_gather(w_down, ("ctx", "fsdp"), axis=0, tiled=True))
    inv_ffn, normed_ffn = rms_parts(ffn_branch)
    output = (middle + normed_ffn * post_ffn_factor).astype(jnp.bfloat16)
    out_cot = out_grad[0].astype(jnp.float32)
    post_ffn_part = jnp.sum(out_cot * normed_ffn, axis=0)
    d_ffn_b = norm_back(out_cot * post_ffn_factor, normed_ffn, inv_ffn).astype(jnp.bfloat16)
    down_total = lax.psum_scatter(
        grad_rows(active, d_ffn_b, 1, lax.axis_size(("ctx", "fsdp")) * w_down.shape[0]),
        ("ctx", "fsdp"),
        scatter_dimension=0,
        tiled=True,
    )
    d_active = contract_cols(d_ffn_b, lax.all_gather(w_down, ("ctx", "fsdp"), axis=0, tiled=True))
    unused_value, gate_pull = jax.vjp(gated, gate_lin, up_lin)
    d_gate, d_up = gate_pull(d_active)
    d_gateup_b = jnp.concatenate([d_gate.astype(jnp.bfloat16), d_up.astype(jnp.bfloat16)], axis=1)
    gateup_folded = lax.psum_scatter(
        grad_rows(
            hidden_ffn,
            d_gateup_b,
            ROW_FOLD,
            lax.axis_size(("ctx", "fsdp")) * (ROW_FOLD * shard_rows),
        ),
        ("ctx", "fsdp"),
        scatter_dimension=0,
        tiled=True,
    )
    gateup_total = gateup_folded.reshape(shard_rows, 2 * FF)
    d_hidden_ffn = contract_cols(
        d_gateup_b, lax.all_gather(gateup_shard, ("ctx", "fsdp"), axis=0, tiled=True)
    )
    pre_ffn_part = jnp.sum(d_hidden_ffn * normed_mid, axis=0)
    d_middle = out_cot + norm_back(d_hidden_ffn * pre_ffn_factor, normed_mid, inv_mid)
    back_qkv, back_out = (
        lax.all_gather(qkv_shard, ("ctx", "fsdp"), axis=0, tiled=True),
        lax.all_gather(w_out, ("ctx", "fsdp"), axis=0, tiled=True),
    )
    post_gain_part = jnp.sum(d_middle * normed_post, axis=0)
    d_branch_b = norm_back(d_middle * post_factor, normed_post, inv_post).astype(jnp.bfloat16)
    w_out_part = contract_rows(attended_b, d_branch_b)
    d_attended = contract_cols(d_branch_b, back_out).astype(jnp.bfloat16)
    d_att_grp = to_groups(d_attended, tok_rows, q_group)
    row_delta = jnp.sum(d_att_grp.astype(jnp.float32) * attended_grp, axis=-1)
    zero_rows = jnp.zeros((tok_rows, width_kv), jnp.float32)
    zero_query = jnp.zeros((KVH, q_group * tok_rows, HD), jnp.float32)
    block_ids = jnp.arange(n_ctx, dtype=jnp.int32)
    all_keys, all_values = (
        lax.all_gather(key_rows, "ctx", axis=0, tiled=True),
        lax.all_gather(value_rows, "ctx", axis=0, tiled=True),
    )

    def returned_step(acc_query, block_item):
        block_index, key_block, value_block = block_item
        first_row = block_index * tok_rows

        def returned_compute_block(acc_in):
            d_query, d_key, d_value = block_grads(
                query_grp,
                row_pos,
                d_att_grp,
                row_delta,
                inv_total,
                key_block,
                value_block,
                first_row,
            )
            return (acc_in + d_query, (d_key, d_value))

        def returned_skip_block(acc_in):
            return (acc_in, (zero_rows, zero_rows))

        return lax.cond(
            first_row <= last_pos, returned_compute_block, returned_skip_block, acc_query
        )

    key_blocks = all_keys.reshape(n_ctx, tok_rows, width_kv)
    value_blocks = all_values.reshape(n_ctx, tok_rows, width_kv)
    d_query_grp, key_terms = lax.scan(
        returned_step, zero_query, (block_ids, key_blocks, value_blocks)
    )
    key_term_rows = key_terms[0].reshape(n_ctx * tok_rows, width_kv)
    value_term_rows = key_terms[1].reshape(n_ctx * tok_rows, width_kv)
    d_keys, d_values = (
        lax.psum_scatter(
            key_term_rows.astype(jnp.bfloat16), "ctx", scatter_dimension=0, tiled=True
        ).astype(jnp.float32),
        lax.psum_scatter(
            value_term_rows.astype(jnp.bfloat16), "ctx", scatter_dimension=0, tiled=True
        ).astype(jnp.float32),
    )
    d_query_flat = from_groups(d_query_grp, tok_rows, q_group).reshape(tok_rows, H, HD) * q_scale
    dq_lin = (
        unrotate_heads(d_query_flat, cos_tab, sine_tab).astype(jnp.bfloat16).reshape(tok_rows, width_q)
    )
    dk_lin = (
        unrotate_heads(d_keys.reshape(tok_rows, KVH, HD), cos_tab, sine_tab)
        .astype(jnp.bfloat16)
        .reshape(tok_rows, width_kv)
    )
    dv_lin = d_values.astype(jnp.bfloat16)
    dqkv_b = jnp.concatenate([dq_lin, dk_lin, dv_lin], axis=1)
    d_hidden = contract_cols(dqkv_b, back_qkv)
    qkv_part = contract_rows(hidden, dqkv_b).reshape(ROW_FOLD * D, width_qkv // ROW_FOLD)
    pre_gain_part = jnp.sum(d_hidden * normed_pre, axis=0)
    token_grad = d_middle + norm_back(d_hidden * pre_factor, normed_pre, inv_pre)
    gain_parts = jnp.stack([pre_gain_part, post_gain_part, pre_ffn_part, post_ffn_part])
    qkv_folded, out_total, gain_totals = (
        lax.psum_scatter(qkv_part, ("ctx", "fsdp"), scatter_dimension=0, tiled=True),
        lax.psum_scatter(w_out_part, ("ctx", "fsdp"), scatter_dimension=0, tiled=True),
        lax.psum_scatter(gain_parts, ("ctx", "fsdp"), scatter_dimension=1, tiled=True),
    )
    qkv_total = qkv_folded.reshape(shard_rows, width_qkv)
    return (
        output[None],
        token_grad.astype(jnp.bfloat16)[None],
        qkv_total[:, :width_q],
        qkv_total[:, width_q : width_q + width_kv],
        qkv_total[:, width_q + width_kv :],
        out_total,
        gateup_total[:, :FF],
        gateup_total[:, FF:],
        down_total,
        gain_totals[0],
        gain_totals[1],
        gain_totals[2],
        gain_totals[3],
    )


def solution(mesh):
    ring = mesh.shape["ctx"] == RING and mesh.shape["fsdp"] == 4
    tokens, rows, gains = P("fsdp", "ctx", None), P(("ctx", "fsdp"), None), P(("ctx", "fsdp"))
    return jax.shard_map(
        on_ring if ring else on_any_mesh,
        mesh=mesh,
        in_specs=(tokens,) + (rows,) * 7 + (gains,) * 4 + (tokens,),
        out_specs=(tokens, tokens) + (rows,) * 7 + (gains,) * 4,
        check_vma=False,
    )
```

```python
import functools

import jax
import jax.numpy as jnp
from jax import lax
from jax.experimental import pallas as pl
from jax.experimental.pallas import tpu as pltpu
from jax.sharding import PartitionSpec as P

D = 2304
H = 8
KVH = 4
HD = 256
CAP = 50
FF = 9216

EPSILON = 1e-06
ROPE_BASE = 10000.0

MESH = pl.DeviceIdType.MESH
HBM = pl.BlockSpec(memory_space=pl.ANY)
VMEM = pl.BlockSpec(memory_space=pltpu.VMEM)
DMA = pltpu.SemaphoreType.DMA
BF = jnp.bfloat16
F32 = jnp.float32


def rope_tables(positions, width):
    half_width = width // 2
    inv_freqs = ROPE_BASE ** (-jnp.arange(half_width, dtype=F32) * 2.0 / width)
    angles = positions.astype(F32)[:, None] * inv_freqs[None, :]
    return (jnp.cos(angles), jnp.sin(angles))


def rotate(rows, cos_tab, sine_tab):
    half_width = rows.shape[-1] // 2
    front, back = rows[..., :half_width], rows[..., half_width:]
    return jnp.concatenate(
        [front * cos_tab - back * sine_tab, back * cos_tab + front * sine_tab], axis=-1
    )


def unrotate(rows, cos_tab, sine_tab):
    half_width = rows.shape[-1] // 2
    front, back = rows[..., :half_width], rows[..., half_width:]
    return jnp.concatenate(
        [front * cos_tab + back * sine_tab, back * cos_tab - front * sine_tab], axis=-1
    )


def rms_parts(values_in):
    inverse = lax.rsqrt(jnp.mean(values_in * values_in, axis=-1, keepdims=True) + EPSILON)
    return (inverse, values_in * inverse)


def norm_back(grad_normed, normed, inverse):
    return inverse * (grad_normed - normed * jnp.mean(grad_normed * normed, axis=-1, keepdims=True))


def contract_rows(left, right):
    return lax.dot_general(left, right, (((0,), (0,)), ((), ())), preferred_element_type=F32)


def contract_cols(left, right):
    return lax.dot_general(left, right, (((1,), (1,)), ((), ())), preferred_element_type=F32)


def fold_rows(left, right):
    return jnp.dot(left, right, preferred_element_type=F32)


def gated(gate_in, up_in):
    return jax.nn.gelu(gate_in, approximate=True) * up_in


NZ = 4
RING = 2 * NZ


def my_place():
    c, f = lax.axis_index("ctx"), lax.axis_index("fsdp")
    return c // 2, c % 2, f // 2, f % 2


def ring_index(y, z):
    return z + y * (RING - 1 - 2 * z)


def ring_yz(q):
    y = q // NZ
    return y, q + y * (RING - 1 - 2 * q)


def device(z, core, y, x):
    return (2 * z + core, 2 * y + x)


def ring_device(q, core, x):
    y, z = ring_yz(q)
    return device(z, core, y, x)


def remote(src, dst, send_sem, recv_sem, where):
    return pltpu.make_async_remote_copy(
        src_ref=src,
        dst_ref=dst,
        send_sem=send_sem,
        recv_sem=recv_sem,
        device_id=where,
        device_id_type=MESH,
    )


def greet(places):
    barrier = pltpu.get_barrier_semaphore()
    for place in places:
        pl.semaphore_signal(barrier, inc=1, device_id=place, device_id_type=MESH)
    pl.semaphore_wait(barrier, len(places))


def params(collective_id, vmem_mib=56):
    return pltpu.CompilerParams(
        collective_id=collective_id,
        has_side_effects=True,
        vmem_limit_bytes=vmem_mib * 2**20,
    )


SUB = 4


def ring_parts(direction, step, half_step):
    if step != half_step:
        return list(range(SUB))
    half = SUB // 2
    return list(range(half)) if direction == 0 else list(range(half, SUB))


class RingGather:
    def __init__(self, x_ref, ring_ref, seq_ref, loc_sem, ss, rs, sib_ss=None, sib_rs=None):
        self.x_ref, self.ring_ref, self.seq_ref, self.loc_sem = x_ref, ring_ref, seq_ref, loc_sem
        self.ss, self.rs, self.sib_ss, self.sib_rs = ss, rs, sib_ss, sib_rs
        self.z, self.core, self.y, self.x = my_place()
        self.p = ring_index(self.y, self.z)
        self.right, self.left = (self.p + 1) % RING, (self.p + RING - 1) % RING
        self.sibling = device(self.z, 1 - self.core, self.y, self.x)
        self.piece = x_ref.shape[0] // SUB
        self.pending = []
        self.local = pltpu.make_async_copy(x_ref, ring_ref.at[self.p], loc_sem.at[RING])

    def places(self):
        near = [ring_device(self.right, self.core, self.x), ring_device(self.left, self.core, self.x)]
        return near + ([self.sibling] if self.seq_ref is not None else [])

    def origin(self, direction, step):
        return (self.p + (RING - step if direction == 0 else step)) % RING

    def copy(self, direction, step, k):
        q = self.origin(direction, step)
        rows = pl.ds(k * self.piece, self.piece)
        src = self.x_ref.at[rows] if step == 0 else self.ring_ref.at[q, rows]
        return remote(
            src,
            self.ring_ref.at[q, rows],
            self.ss.at[direction, step, k],
            self.rs.at[direction, step, k],
            ring_device(self.right if direction == 0 else self.left, self.core, self.x),
        )

    def place(self, q, act):
        if self.seq_ref is None:
            return
        yq, zq = ring_yz(q)
        src, dst = self.ring_ref.at[q], self.seq_ref.at[2 * zq + self.core]

        @pl.when(yq == self.core)
        def _():
            act(pltpu.make_async_copy(src, dst, self.loc_sem.at[q]))

        @pl.when(yq != self.core)
        def _():
            act(remote(src, dst, self.sib_ss.at[zq], self.sib_rs.at[zq], self.sibling))

    def step(self, step):
        if step == 0:
            self.local.start()
        for k in range(SUB):
            for direction in (0, 1):
                if step > 0 and (step < 3 or k in ring_parts(direction, 3, 3)):
                    self.copy(direction, step - 1, k).wait_recv()
                if k in ring_parts(direction, step, 3):
                    c = self.copy(direction, step, k)
                    c.start()
                    self.pending.append(c)
        if step == 1:
            self.local.wait()
            self.place(self.p, lambda c: c.start())
        if step == 3:
            for direction in (0, 1):
                for k in range(SUB):
                    if k not in ring_parts(direction, 3, 3):
                        self.copy(direction, 2, k).wait_recv()
        if step > 0:
            for direction in (0, 1):
                self.place(self.origin(direction, step), lambda c: c.start())

    def finish(self):
        for direction in (0, 1):
            for k in ring_parts(direction, 3, 3):
                self.copy(direction, 3, k).wait_recv()
        self.place((self.p + 4) % RING, lambda c: c.start())
        for c in self.pending:
            c.wait_send()
        if self.seq_ref is None:
            return
        for q in range(RING):
            self.place((self.p + q) % RING, lambda c: c.wait_send() if c.is_remote else c.wait())
        for zq in range(NZ):
            dst = self.seq_ref.at[2 * zq + 1 - self.core]
            remote(self.ring_ref.at[zq], dst, self.sib_ss.at[zq], self.sib_rs.at[zq], self.sibling).wait_recv()


def gather_kernel(paired, x_ref, *refs):
    if paired:
        seq_ref, ring_ref, *sems = refs
    else:
        ring_ref, *sems = refs
        seq_ref = None
    ring = RingGather(x_ref, ring_ref, seq_ref, *sems)
    greet(ring.places())
    for step in range(4):
        ring.step(step)
    ring.finish()


def ring_gather(block, collective_id, paired):
    rows, width = block.shape
    whole = jax.ShapeDtypeStruct((RING, rows, width), block.dtype)
    sems = [DMA((RING + 1,)), DMA((2, 4, SUB)), DMA((2, 4, SUB))]
    if paired:
        sems = [pltpu.VMEM(whole.shape, whole.dtype)] + sems + [DMA((NZ,)), DMA((NZ,))]
    out = pl.pallas_call(
        functools.partial(gather_kernel, paired),
        out_shape=whole,
        in_specs=[VMEM],
        out_specs=VMEM if paired else HBM,
        scratch_shapes=sems,
        compiler_params=params(collective_id),
    )(block)
    return out.reshape(RING * rows, width)


def scatter_kernel(paired, part_ref, o_ref, *refs):
    if paired:
        mine_ref, buf, ss, rs, sib_ss, sib_rs, loc_sem = refs
    else:
        buf, ss, rs = refs
        mine_ref = part_ref
    z, core, y, x = my_place()
    p = ring_index(y, z)
    right, left = (p + 1) % RING, (p + RING - 1) % RING
    sibling = device(z, 1 - core, y, x)
    piece = o_ref.shape[0] // SUB
    greet(
        [ring_device(right, core, x), ring_device(left, core, x)] + ([sibling] if paired else [])
    )
    if paired:
        swaps, copies = [], []
        for zq in range(NZ):
            q = ring_index(core, zq)
            swaps.append(remote(part_ref.at[2 * zq + 1 - core], mine_ref.at[q], sib_ss.at[zq], sib_rs.at[zq], sibling))
            swaps[-1].start()
            copies.append(pltpu.make_async_copy(part_ref.at[2 * zq + core], mine_ref.at[q], loc_sem.at[zq]))
            copies[-1].start()
        for c in copies:
            c.wait()
        for zq in range(NZ):
            q = ring_index(1 - core, zq)
            remote(part_ref.at[zq], mine_ref.at[q], sib_ss.at[zq], sib_rs.at[zq], sibling).wait_recv()
        for c in swaps:
            c.wait_send()

    def copy(direction, step, k, src):
        rows = pl.ds(k * piece, piece)
        return remote(
            src,
            buf.at[direction, step, rows],
            ss.at[direction, step, k],
            rs.at[direction, step, k],
            ring_device(right if direction == 0 else left, core, x),
        )

    pending = []
    for step in range(4):
        for k in range(SUB):
            rows = pl.ds(k * piece, piece)
            for direction in (0, 1):
                if k not in ring_parts(direction, step, 0):
                    continue
                far = 4 - step
                q = (p + (far if direction == 0 else RING - far)) % RING
                src = mine_ref.at[q, rows]
                if step > 0 and k in ring_parts(direction, step - 1, 0):
                    src = buf.at[direction, step - 1, rows]
                    copy(direction, step - 1, k, src).wait_recv()
                    total = src[...].astype(F32) + mine_ref[q, rows].astype(F32)
                    src[...] = total.astype(BF)
                c = copy(direction, step, k, src)
                c.start()
                pending.append(c)
    for k in range(SUB):
        rows = pl.ds(k * piece, piece)
        total = mine_ref[p, rows].astype(F32)
        for direction in (0, 1):
            src = buf.at[direction, 3, rows]
            copy(direction, 3, k, src).wait_recv()
            total = total + src[...].astype(F32)
        o_ref[rows] = total
    for c in pending:
        c.wait_send()


def ring_scatter(part, collective_id, paired):
    rows, width = part.shape[0] // RING, part.shape[1]
    blocks = (RING, rows, width)
    sems = [DMA((2, 4, SUB)), DMA((2, 4, SUB))]
    return pl.pallas_call(
        functools.partial(scatter_kernel, paired),
        out_shape=jax.ShapeDtypeStruct((rows, width), F32),
        in_specs=[VMEM],
        out_specs=VMEM,
        scratch_shapes=([pltpu.VMEM(blocks, BF)] if paired else [])
        + [pltpu.VMEM((2, 4, rows, width), BF)]
        + sems
        + ([DMA((NZ,)), DMA((NZ,)), DMA((NZ,))] if paired else []),
        compiler_params=params(collective_id),
    )(part.astype(BF).reshape(blocks))


TOK = 128
UNITS = FF // RING
TILE = 128
GELU_K = 0.7978845608028654
GELU_A = 0.044715


class SlotGather:
    def __init__(self, buf, ss, rs):
        z, core, y, x = my_place()
        p = ring_index(y, z)
        self.buf, self.ss, self.rs = buf, ss, rs
        self.near = (ring_device((p + 1) % RING, core, x), ring_device((p + RING - 1) % RING, core, x))
        self.pending = []

    def copy(self, direction, step, k):
        piece = TOK // SUB
        src = 0 if step == 0 else 2 * step - 1 + direction
        dst = 7 if step == 3 else 2 * step + 1 + direction
        return remote(
            self.buf.at[pl.ds(src * TOK + k * piece, piece)],
            self.buf.at[pl.ds(dst * TOK + k * piece, piece)],
            self.ss.at[direction, step, k],
            self.rs.at[direction, step, k],
            self.near[direction],
        )

    def step(self, step):
        for k in range(SUB):
            for direction in (0, 1):
                if step > 0:
                    self.copy(direction, step - 1, k).wait_recv()
                if k in ring_parts(direction, step, 3):
                    c = self.copy(direction, step, k)
                    c.start()
                    self.pending.append(c)

    def finish(self):
        for direction in (0, 1):
            for k in ring_parts(direction, 3, 3):
                self.copy(direction, 3, k).wait_recv()

    def drain(self):
        for c in self.pending:
            c.wait_send()


class SlotScatter:
    def __init__(self, part, buf, ss, rs):
        z, core, y, x = my_place()
        p = ring_index(y, z)
        self.part, self.buf, self.ss, self.rs = part, buf, ss, rs
        self.near = (ring_device((p + 1) % RING, core, x), ring_device((p + RING - 1) % RING, core, x))
        self.pending = []

    def copy(self, direction, step, k, src):
        rows = pl.ds(k * (TOK // SUB), TOK // SUB)
        return remote(
            src,
            self.buf.at[direction, step, rows],
            self.ss.at[direction, step, k],
            self.rs.at[direction, step, k],
            self.near[direction],
        )

    def step(self, step):
        piece = TOK // SUB
        for k in range(SUB):
            rows = pl.ds(k * piece, piece)
            for direction in (0, 1):
                if k not in ring_parts(direction, step, 0):
                    continue
                slot = 7 if step == 0 else 2 * (4 - step) - direction
                mine = pl.ds(slot * TOK + k * piece, piece)
                src = self.part.at[mine]
                if step > 0 and k in ring_parts(direction, step - 1, 0):
                    src = self.buf.at[direction, step - 1, rows]
                    self.copy(direction, step - 1, k, src).wait_recv()
                    src[...] = (src[...].astype(F32) + self.part[mine].astype(F32)).astype(BF)
                c = self.copy(direction, step, k, src)
                c.start()
                self.pending.append(c)

    def finish(self, total):
        for k in range(SUB):
            rows = pl.ds(k * (TOK // SUB), TOK // SUB)
            for direction in (0, 1):
                src = self.buf.at[direction, 3, rows]
                self.copy(direction, 3, k, src).wait_recv()
                total[rows] = total[rows] + src[...].astype(F32)

    def drain(self):
        for c in self.pending:
            c.wait_send()


def tiles(count, width, body):
    def step(i, carry):
        body(pl.ds(pl.multiple_of(i * width, width), width))
        return carry

    lax.fori_loop(0, count, step, 0)


def gelu_parts(v):
    bent = jnp.tanh(GELU_K * (v + GELU_A * (v * v * v)))
    value = 0.5 * v * (1.0 + bent)
    slope = 0.5 * (1.0 + bent) + 0.5 * v * (1.0 - bent * bent) * (GELU_K * (1.0 + 3.0 * GELU_A * (v * v)))
    return value, slope


PAIRS = ((128, 256), (384, 256), (640, 256))
LAST = (896, 128)
OWN = (0, 128)


def feed_forward_kernel(hid, middle, factor, cot, w_hbm, wd_hbm,
                        out_o, d_hid_o, gain_o, wd_grad, gu_grad,
                        wgu, wd, ha, gu, act, part, buf, df, dgu, total, stage,
                        w_sem, ags, agr, rss, rsr, out_sem):
    gather = [SlotGather(b, ags.at[i], agr.at[i]) for i, b in enumerate((ha, df))]
    scatter = [SlotScatter(part, buf, rss.at[i], rsr.at[i]) for i in range(2)]
    greet(gather[0].near)
    loads = [
        pltpu.make_async_copy(w_hbm.at[:, pl.ds(0, 2 * UNITS)], wgu, w_sem.at[0]),
        pltpu.make_async_copy(wd_hbm, wd, w_sem.at[1]),
    ]
    ha[0:TOK] = hid[...]
    gather[0].step(0)
    for c in loads:
        c.start()
    loads[0].wait()

    def gate_up(first, count):
        rows = pl.ds(first, count)

        def column(cols):
            gu[rows, cols] = fold_rows(ha[rows], wgu[:, cols])

        tiles(3, 768, column)

        def finish(i, carry):
            r = pl.ds(pl.multiple_of(first + i * 32, 32), 32)
            act[r] = (gelu_parts(gu[r, 0:UNITS])[0] * gu[r, UNITS : 2 * UNITS]).astype(BF)
            return carry

        lax.fori_loop(0, count // 32, finish, 0)

    def down_part(first, count, dst):
        def column(cols):
            value = fold_rows(act[pl.ds(first, count)], wd[:, cols])
            dst[pl.ds(first, count), cols] = value.astype(dst.dtype)

        tiles(3, 768, column)

    def active_back(first, count):
        rows = pl.ds(first, count)
        for n in range(3):
            cols, up_cols = pl.ds(n * 384, 384), pl.ds(UNITS + n * 384, 384)
            d_active = contract_cols(df[rows], wd[cols])
            value, slope = gelu_parts(gu[rows, cols])
            dgu[rows, cols] = (d_active * gu[rows, up_cols] * slope).astype(BF)
            dgu[rows, up_cols] = (d_active * value).astype(BF)

    def hidden_part(first, count, dst):
        def column(cols):
            value = contract_cols(dgu[pl.ds(first, count)], wgu[cols])
            dst[pl.ds(first, count), cols] = value.astype(dst.dtype)

        tiles(9, 256, column)

    n_down = UNITS // TILE

    def grad_out(i):
        slot = i % 2
        if i < n_down:
            return pltpu.make_async_copy(stage.at[slot], wd_grad.at[pl.ds(i * TILE, TILE)], out_sem.at[slot])
        return pltpu.make_async_copy(stage.at[slot], gu_grad.at[pl.ds((i - n_down) * TILE, TILE)], out_sem.at[slot])

    def grad_tiles(first, last):
        for i in range(first, last):
            if i >= 2:
                grad_out(i - 2).wait()
            if i < n_down:
                value = contract_rows(act[:, pl.ds(i * TILE, TILE)], df[...])
            else:
                value = contract_rows(ha[:, pl.ds((i - n_down) * TILE, TILE)], dgu[...])
            stage[i % 2] = value.astype(BF)
            grad_out(i).start()

    gate_up(*OWN)
    for step, pair in enumerate(PAIRS):
        gather[0].step(step + 1)
        if step == 0:
            loads[1].wait()
        gate_up(*pair)
    gather[0].finish()
    gate_up(*LAST)
    down_part(*LAST, part)
    scatter[0].step(0)
    for step, pair in enumerate(PAIRS[::-1]):
        down_part(*pair, part)
        scatter[0].step(step + 1)
    down_part(*OWN, total)
    scatter[0].finish(total)
    gather[0].drain()
    scatter[0].drain()

    branch = total[...]
    inverse, normed = rms_parts(branch)
    out_cot = cot[...].astype(F32)
    scale = factor[...]
    df[0:TOK] = norm_back(out_cot * scale, normed, inverse).astype(BF)
    gather[1].step(0)
    out_o[...] = (middle[...] + normed * scale).astype(BF)
    gain_o[...] = jnp.sum(out_cot * normed, axis=0, keepdims=True)
    active_back(*OWN)
    for step, pair in enumerate(PAIRS):
        gather[1].step(step + 1)
        active_back(*pair)
    gather[1].finish()
    active_back(*LAST)
    hidden_part(*LAST, part)
    scatter[1].step(0)
    done = 0
    for step, pair in enumerate(PAIRS[::-1]):
        hidden_part(*pair, part)
        scatter[1].step(step + 1)
        grad_tiles(done, done + 6)
        done += 6
    hidden_part(*OWN, d_hid_o)
    scatter[1].finish(d_hid_o)
    n_tiles = n_down + ha.shape[1] // TILE
    grad_tiles(done, n_tiles)
    for i in (n_tiles - 2, n_tiles - 1):
        grad_out(i).wait()
    gather[1].drain()
    scatter[1].drain()


def feed_forward(hidden_ffn, middle, factor, out_grad, w_in, w_down, collective_id):
    rows, width = hidden_ffn.shape
    total = RING * rows

    def full(*shape, dtype=F32):
        return jax.ShapeDtypeStruct(shape, dtype)

    return pl.pallas_call(
        feed_forward_kernel,
        out_shape=[
            full(rows, width, dtype=BF), full(rows, width), full(1, width),
            full(UNITS, width, dtype=BF), full(width, 2 * UNITS, dtype=BF),
        ],
        in_specs=[VMEM] * 4 + [HBM] * 2,
        out_specs=[VMEM] * 3 + [HBM] * 2,
        scratch_shapes=[
            pltpu.VMEM((width, 2 * UNITS), BF), pltpu.VMEM((UNITS, width), BF),
            pltpu.VMEM((total, width), BF), pltpu.VMEM((total, 2 * UNITS), F32), pltpu.VMEM((total, UNITS), BF),
            pltpu.VMEM((total, width), BF), pltpu.VMEM((2, 4, rows, width), BF),
            pltpu.VMEM((total, width), BF), pltpu.VMEM((total, 2 * UNITS), BF),
            pltpu.VMEM((rows, width), F32), pltpu.VMEM((2, TILE, width), BF),
            DMA((2,)),
            DMA((2, 2, 4, SUB)), DMA((2, 2, 4, SUB)), DMA((2, 2, 4, SUB)), DMA((2, 2, 4, SUB)),
            DMA((2,)),
        ],
        compiler_params=params(collective_id, 60),
    )(hidden_ffn, middle, factor, out_grad, w_in, w_down)


WIDTHS = (UNITS, UNITS, HD, HD, HD)
STARTS = (0, UNITS, 2 * UNITS, 2 * UNITS + HD, 2 * UNITS + 2 * HD)
WIDE = 2 * UNITS + 3 * HD


def member_place(t, core, x):
    return device(t // 2, core, t % 2, x)


def partner(t, j):
    out = 0
    for bit in (1, 2, 4):
        on = (t // bit) % 2
        out = out + bit * (1 - on if j & bit else on)
    return out


def column_start(which, t):
    if which < 2:
        return pl.multiple_of(t * UNITS, 128)
    return pl.multiple_of((t if which == 2 else t // 2) * HD, 128)


def weights_in_kernel(gate, up, query, key, value, down, out, gains, x_ref, w_ref, d_ref, o_ref, g_ref, seq_ref,
                      ring_ref, loc, s1, r1, s2, r2, s3, r3, s4, r4, s5, r5, ring_loc, ss, rs, sib_ss, sib_rs):
    z, core, y, x = my_place()
    t = 2 * z + y
    sibling, across = device(z, 1 - core, y, x), device(z, core, y, 1 - x)

    def slot(tq, corq, xq):
        return (2 * (tq // 2) + corq) * 4 + 2 * (tq % 2) + xq

    me = slot(t, core, x)
    member = [partner(t, j) for j in range(RING)]
    plane = []
    for dc in (0, 1):
        for dy in (0, 1):
            for dx in (0, 1):
                if (dc, dx) != (0, 0):
                    plane.append(device(z, (core + dc) % 2, (y + dy) % 2, (x + dx) % 2))
    greet([member_place(member[j], core, x) for j in range(1, RING)] + plane)
    sources = (gate, up, query, key, value)
    ring = RingGather(x_ref, ring_ref, seq_ref, ring_loc, ss, rs, sib_ss, sib_rs)

    def first(j, a, wait=False):
        tq = member[j]
        if a == 5:
            src, dst = gains, g_ref.at[slot(tq, core, x) if wait else me]
        else:
            src = sources[a].at[:, pl.ds(column_start(a, tq), WIDTHS[a])]
            dst = w_ref.at[slot(tq, core, x) if wait else me, :, pl.ds(STARTS[a], WIDTHS[a])]
        return remote(src, dst, s1.at[j, a], r1.at[j, a], member_place(tq, core, x))

    pending = []

    def go(copies):
        for c in copies:
            c.start()
            pending.append(c)

    def second(j, wait=False):
        i = slot(member[j], core, 1 - x if wait else x)
        return [
            remote(w_ref.at[i], w_ref.at[i], s2.at[j, 0], r2.at[j, 0], across),
            remote(g_ref.at[i], g_ref.at[i], s2.at[j, 1], r2.at[j, 1], across),
        ]

    def third(j, flip, wait=False):
        i = slot(member[j], 1 - core if wait else core, 1 - x if flip else x)
        return [
            remote(w_ref.at[i], w_ref.at[i], s3.at[j, flip, 0], r3.at[j, flip, 0], sibling),
            remote(g_ref.at[i], g_ref.at[i], s3.at[j, flip, 1], r3.at[j, flip, 1], sibling),
        ]

    def start_round(j):
        go([first(j, a) for a in (5, 2, 3, 4, 0, 1)])

    def end_round(j):
        for a in range(6):
            first(j, a, True).wait_recv()
        go(second(j) + third(j, 0))

    def end_across(j):
        for c in second(j, True):
            c.wait_recv()
        go(third(j, 1))

    ring.step(0)
    start_round(4)
    start_round(1)
    locals_ = [pltpu.make_async_copy(gains, g_ref.at[me], loc.at[5])]
    for a in range(5):
        locals_.append(
            pltpu.make_async_copy(
                sources[a].at[:, pl.ds(column_start(a, t), WIDTHS[a])],
                w_ref.at[me, :, pl.ds(STARTS[a], WIDTHS[a])],
                loc.at[a],
            )
        )
    for c in locals_:
        c.start()
    pair = ((down, d_ref), (out, o_ref))
    mine = 2 * y + x
    for xq in (0, 1):
        to_self = (x == core) & (y == core) & (xq == x)
        for a, (src, dst) in enumerate(pair):
            @pl.when(to_self)
            def _():
                pltpu.make_async_copy(src, dst.at[mine], s4.at[xq, a]).start()

            @pl.when(jnp.logical_not(to_self))
            def _():
                remote(src, dst.at[mine], s4.at[xq, a], r4.at[y, a], device(z, x, core, xq)).start()
    for c in locals_:
        c.wait()
    go(second(0) + third(0, 0))
    ring.step(1)
    end_round(1)
    start_round(2)
    end_round(4)
    start_round(5)
    ring.step(2)
    end_round(2)
    start_round(3)
    end_across(0)
    end_across(1)
    end_round(5)
    start_round(6)
    ring.step(3)
    end_round(3)
    start_round(7)
    end_across(4)
    for yq in (0, 1):
        from_self = (core == y) & (yq == y) & (core == x)
        for a, (src, dst) in enumerate(pair):
            @pl.when(from_self)
            def _():
                pltpu.make_async_copy(src, dst.at[mine], s4.at[x, a]).wait()

            @pl.when(jnp.logical_not(from_self))
            def _():
                remote(src, dst.at[2 * yq + core], s4.at[0, a], r4.at[yq, a], sibling).wait_recv()

            go([remote(dst.at[2 * yq + core], dst.at[2 * yq + core], s5.at[yq, a], r5.at[yq, a], sibling)])
    end_across(2)
    end_across(5)
    ring.finish()
    end_round(6)
    end_across(3)
    end_round(7)
    end_across(6)
    end_across(7)
    for j in range(RING):
        for flip in (0, 1):
            for c in third(j, flip, True):
                c.wait_recv()
    for yq in (0, 1):
        for a, (src, dst) in enumerate(pair):
            remote(src, dst.at[2 * yq + 1 - core], s5.at[yq, a], r5.at[yq, a], sibling).wait_recv()
    for c in pending:
        c.wait_send()
    for xq in (0, 1):
        to_self = (x == core) & (y == core) & (xq == x)
        for a, (src, dst) in enumerate(pair):
            @pl.when(jnp.logical_not(to_self))
            def _():
                remote(src, dst.at[mine], s4.at[xq, a], r4.at[y, a], device(z, x, core, xq)).wait_send()


def weights_in(gate, up, query, key, value, down, out, gains, block, collective_id):
    n = 4 * RING
    whole = (RING,) + block.shape
    shapes = [
        jax.ShapeDtypeStruct((n, gate.shape[0], WIDE), BF),
        jax.ShapeDtypeStruct((4,) + down.shape, BF),
        jax.ShapeDtypeStruct((4,) + out.shape, BF),
        jax.ShapeDtypeStruct((n,) + gains.shape, gains.dtype),
        jax.ShapeDtypeStruct(whole, BF),
    ]
    results = pl.pallas_call(
        weights_in_kernel,
        out_shape=shapes,
        in_specs=[VMEM] * 9,
        out_specs=[HBM] * 4 + [VMEM],
        scratch_shapes=[
            pltpu.VMEM(whole, BF),
            DMA((6,)),
            DMA((RING, 6)), DMA((RING, 6)),
            DMA((RING, 2)), DMA((RING, 2)),
            DMA((RING, 2, 2)), DMA((RING, 2, 2)),
            DMA((2, 2)), DMA((2, 2)),
            DMA((2, 2)), DMA((2, 2)),
            DMA((RING + 1,)), DMA((2, 4, SUB)), DMA((2, 4, SUB)), DMA((NZ,)), DMA((NZ,)),
        ],
        compiler_params=params(collective_id, 32),
    )(gate, up, query, key, value, down, out, gains, block)
    return list(results[:4]) + [results[4].reshape(RING * block.shape[0], block.shape[1])]


def add_into(dst, index, src, other):
    dst[index] = (dst[index].astype(F32) + src[other].astype(F32)).astype(BF)


def weights_out_kernel(gu_in, qkv_in, down_in, out_in, gain_in,
                       gate_o, up_o, query_o, key_o, value_o, down_o, out_o, gain_o,
                       a_buf, b_buf, c_buf, acc, da, db, dacc, dd, oa, ob, oacc, od, ga, gsum,
                       loc, sa, ra, sb, rb, sc, rc, sx, rx, sg, rg):
    z, core, y, x = my_place()
    t = 2 * z + y
    sibling, across = device(z, 1 - core, y, x), device(z, core, y, 1 - x)
    diagonal = device(z, 1 - core, 1 - y, x)
    others = [(t + j) % RING for j in range(1, RING)]
    greet([member_place(tq, core, x) for tq in others] + [sibling, across, diagonal])

    def slot(tq, corq, xq):
        return (2 * (tq // 2) + corq) * 4 + 2 * (tq % 2) + xq

    def load(tq, xq):
        i = slot(tq, core, xq)
        return [
            pltpu.make_async_copy(gu_in.at[i], acc.at[xq, tq, :, pl.ds(0, 2 * UNITS)], loc.at[xq, tq, 0]),
            pltpu.make_async_copy(qkv_in.at[i], acc.at[xq, tq, :, pl.ds(2 * UNITS, 3 * HD)], loc.at[xq, tq, 1]),
        ]

    def to_sibling(tq, xq):
        i = slot(tq, 1 - core, xq)
        return [
            remote(gu_in.at[i], a_buf.at[xq, tq, :, pl.ds(0, 2 * UNITS)], sa.at[xq, tq, 0], ra.at[xq, tq, 0], sibling),
            remote(qkv_in.at[i], a_buf.at[xq, tq, :, pl.ds(2 * UNITS, 3 * HD)], sa.at[xq, tq, 1], ra.at[xq, tq, 1], sibling),
        ]

    def to_across(tq):
        return remote(acc.at[1 - x, tq], b_buf.at[tq], sb.at[tq], rb.at[tq], across)

    def to_member(tq, wait=False):
        return remote(acc.at[x, tq], c_buf.at[tq if wait else t], sc.at[tq], rc.at[tq if wait else t], member_place(tq, core, x))

    order = [partner(t, j) for j in (4, 5, 6, 7, 2, 3, 1, 0)]

    small = ((down_in, da, db, dacc, dd, down_o), (out_in, oa, ob, oacc, od, out_o))

    def small_a(a, xo):
        src, buf = small[a][0], small[a][1]
        return remote(src.at[2 * (1 - core) + xo], buf.at[xo], sx.at[a, xo], rx.at[a, xo], sibling)

    def small_b(a):
        return remote(small[a][3].at[1 - x], small[a][2], sx.at[a, 2], rx.at[a, 2], across)

    def small_c(a):
        return remote(small[a][3].at[x], small[a][4], sx.at[a, 3], rx.at[a, 3], diagonal)

    def small_load(a, xo):
        return pltpu.make_async_copy(small[a][0].at[2 * core + xo], small[a][3].at[xo], loc.at[a, xo, 2])

    def gain_a():
        return remote(gain_in, ga.at[RING], sg.at[RING], rg.at[RING], sibling)

    def gain_b():
        return remote(gsum.at[0], ga.at[RING + 1], sg.at[RING + 1], rg.at[RING + 1], across)

    def gain_c(tq, wait=False):
        return remote(gsum.at[1], ga.at[tq if wait else t], sg.at[tq], rg.at[tq if wait else t], member_place(tq, core, x))

    def start_a(tq, xq):
        for c in load(tq, xq) + to_sibling(tq, xq):
            c.start()

    def sum_a(tq, xq):
        for c in load(tq, xq):
            c.wait()
        for c in to_sibling(tq, xq):
            c.wait_recv()
        acc[xq, tq] = (acc[xq, tq].astype(F32) + a_buf[xq, tq].astype(F32)).astype(BF)

    def small_start(a):
        buf, total = small[a][1], small[a][3]
        for xo in (0, 1):
            small_load(a, xo).wait()
            small_a(a, xo).wait_recv()
            total[xo] = (total[xo].astype(F32) + buf[xo].astype(F32)).astype(BF)
        small_b(a).start()

    for tq in order:
        start_a(tq, 1 - x)
    gain_a().start()
    for a in (1, 0):
        for xo in (0, 1):
            small_a(a, xo).start()
            small_load(a, xo).start()
    for tq in order:
        start_a(tq, x)
    ahead = 2
    for tq in order[:ahead]:
        sum_a(tq, 1 - x)
        to_across(tq).start()
    gain_a().wait_recv()
    gsum[0] = gain_in[...] + ga[RING]
    gain_b().start()
    small_start(1)
    for tq in order[ahead:]:
        sum_a(tq, 1 - x)
    for j, tq in enumerate(order):
        sum_a(tq, x)
        to_across(tq).wait_recv()
        if j + ahead < RING:
            to_across(order[j + ahead]).start()
        elif j + ahead == RING:
            small_start(0)
        if j == 0:
            gain_b().wait_recv()
            gsum[1] = gsum[0] + ga[RING + 1]
            for other in others:
                gain_c(other).start()
        acc[x, tq] = (acc[x, tq].astype(F32) + b_buf[tq].astype(F32)).astype(BF)
        if j < RING - 1:
            to_member(tq).start()
    for a in (1, 0):
        other, total = small[a][2:4]
        small_b(a).wait_recv()
        total[x] = (total[x].astype(F32) + other[...].astype(F32)).astype(BF)
        for xo in (0, 1):
            small_a(a, xo).wait_send()

    @pl.when(core == y)
    def _():
        for a in (0, 1):
            small[a][5][...] = small[a][3][x].astype(F32)

    @pl.when(core != y)
    def _():
        for a in (0, 1):
            small_c(a).start()
        for a in (0, 1):
            small_c(a).wait_recv()
            small[a][5][...] = small[a][4][...].astype(F32)
        for a in (0, 1):
            small_c(a).wait_send()

    total = gsum[1]
    for tq in others:
        gain_c(tq, True).wait_recv()
        total = total + ga[tq]
    gain_o[...] = total
    c_buf[t] = acc[x, t]
    for tq in others:
        to_member(tq, True).wait_recv()
    for tq in range(RING):
        units = pl.ds(tq * UNITS, UNITS)
        gate_o[:, units] = c_buf[tq, :, pl.ds(0, UNITS)].astype(F32)
        up_o[:, units] = c_buf[tq, :, pl.ds(UNITS, UNITS)].astype(F32)
        query_o[:, pl.ds(tq * HD, HD)] = c_buf[tq, :, pl.ds(STARTS[2], HD)].astype(F32)
    for g in range(KVH):
        for start, result in ((STARTS[3], key_o), (STARTS[4], value_o)):
            columns = pl.ds(start, HD)
            result[:, pl.ds(g * HD, HD)] = c_buf[2 * g, :, columns].astype(F32) + c_buf[2 * g + 1, :, columns].astype(F32)

    for j, tq in enumerate(order):
        for xq in (0, 1):
            for c in to_sibling(tq, xq):
                c.wait_send()
        to_across(tq).wait_send()
        if j < RING - 1:
            to_member(tq).wait_send()
    gain_a().wait_send()
    gain_b().wait_send()
    for tq in others:
        gain_c(tq).wait_send()
    for a in (0, 1):
        small_b(a).wait_send()


def weights_out(gu, qkv, down, out, gains, collective_id):
    n = 4 * RING
    rows, width = gu.shape[0] // n, gains.shape[1]
    gu, qkv = gu.reshape(n, rows, 2 * UNITS), qkv.reshape(n, rows, 3 * HD)
    down, out = down.reshape(4, -1, width), out.reshape(4, -1, width)
    down_rows, out_rows = down.shape[1], out.shape[1]
    wide = (RING, rows, WIDE)

    def full(*shape):
        return jax.ShapeDtypeStruct(shape, F32)

    return pl.pallas_call(
        weights_out_kernel,
        out_shape=[
            full(rows, FF), full(rows, FF), full(rows, H * HD), full(rows, KVH * HD), full(rows, KVH * HD),
            full(down_rows, width), full(out_rows, width), full(*gains.shape),
        ],
        in_specs=[HBM] * 4 + [VMEM],
        out_specs=[VMEM] * 8,
        scratch_shapes=[
            pltpu.VMEM((2,) + wide, BF), pltpu.VMEM(wide, BF), pltpu.VMEM(wide, BF), pltpu.VMEM((2,) + wide, BF),
            pltpu.VMEM((2, down_rows, width), BF), pltpu.VMEM((down_rows, width), BF), pltpu.VMEM((2, down_rows, width), BF), pltpu.VMEM((down_rows, width), BF),
            pltpu.VMEM((2, out_rows, width), BF), pltpu.VMEM((out_rows, width), BF), pltpu.VMEM((2, out_rows, width), BF), pltpu.VMEM((out_rows, width), BF),
            pltpu.VMEM((RING + 2,) + gains.shape, F32), pltpu.VMEM((2,) + gains.shape, F32),
            DMA((2, RING, 3)),
            DMA((2, RING, 2)), DMA((2, RING, 2)),
            DMA((RING,)), DMA((RING,)),
            DMA((RING,)), DMA((RING,)),
            DMA((2, 4)), DMA((2, 4)),
            DMA((RING + 2,)), DMA((RING + 2,)),
        ],
        compiler_params=params(collective_id),
    )(gu, qkv, down, out, gains)


def attend(queries, keys, values, positions):
    raw = contract_cols(queries, keys)
    capped = CAP * jnp.tanh(raw / CAP)
    allowed = positions[None, :] <= positions[:, None]
    weights = jnp.where(allowed, jnp.exp(capped), 0.0)
    inv_total = 1.0 / jnp.sum(weights, axis=-1, keepdims=True)
    attended = fold_rows(weights.astype(BF), values) * inv_total
    return attended, inv_total


def attend_back(queries, keys, values, positions, attended, inv_total, d_attended):
    raw = contract_cols(queries, keys)
    capped = CAP * jnp.tanh(raw / CAP)
    allowed = positions[None, :] <= positions[:, None]
    weights = jnp.where(allowed, jnp.exp(capped), 0.0)
    delta = jnp.sum(d_attended.astype(F32) * attended, axis=-1, keepdims=True)
    d_probs = contract_cols(d_attended, values)
    slope = 1.0 - capped / CAP * (capped / CAP)
    d_raw = (weights * inv_total * (d_probs - delta) * slope).astype(BF)
    d_query = fold_rows(d_raw, keys)
    d_key = contract_rows(d_raw, queries)
    weights_b = weights.astype(BF)
    d_scaled = d_attended.astype(F32) * inv_total
    scaled_high = d_scaled.astype(BF)
    scaled_rest = (d_scaled - scaled_high.astype(F32)).astype(BF)
    d_value = contract_rows(weights_b, scaled_high) + contract_rows(weights_b, scaled_rest)
    return d_query, d_key, d_value


def on_ring(
    tokens, w_query, w_key, w_value, w_out, w_gate, w_up, w_down,
    pre_gain, post_gain, pre_ffn_gain, post_ffn_gain, out_grad,
):
    ids = iter(range(32))
    n_shards = 4 * RING
    length = RING * tokens.shape[1]
    shard_gain = pre_gain.shape[0]
    gains = jnp.stack([pre_gain, post_gain, pre_ffn_gain, post_ffn_gain]).astype(F32)
    gains = jnp.pad(gains, ((0, 4), (0, 128 - shard_gain)))
    w_in, down_in, out_in, gains_in, sequence = weights_in(
        w_gate, w_up, w_query, w_key, w_value, w_down, w_out, gains, tokens[0], next(ids)
    )
    w_in = w_in.reshape(-1, WIDE)
    w_qkv = w_in[:, 2 * UNITS :]
    w_dn = down_in.reshape(UNITS, D)
    w_ot = out_in.reshape(HD, D)
    factors = 1.0 + jnp.transpose(gains_in[:, :4, :shard_gain], (1, 0, 2)).reshape(4, D)
    pre_factor, post_factor, pre_ffn_factor, post_ffn_factor = (factors[i] for i in range(4))
    positions = jnp.arange(length, dtype=jnp.int32)
    cos_tab, sine_tab = rope_tables(positions, HD)
    q_scale = HD ** (-0.5)

    resid_in = tokens[0].astype(F32)
    inv_pre, normed_pre = rms_parts(resid_in)
    hidden = (rms_parts(sequence.astype(F32))[1] * pre_factor).astype(BF)
    projected = fold_rows(hidden, w_qkv)
    queries = (rotate(projected[:, :HD], cos_tab, sine_tab) * q_scale).astype(BF)
    keys = rotate(projected[:, HD : 2 * HD], cos_tab, sine_tab).astype(BF)
    values = projected[:, 2 * HD :].astype(BF)
    attended, inv_total = attend(queries, keys, values, positions)
    attended_b = attended.astype(BF)
    branch = ring_scatter(fold_rows(attended_b, w_ot), next(ids), True)
    inv_post, normed_post = rms_parts(branch)
    middle = resid_in + normed_post * post_factor
    inv_mid, normed_mid = rms_parts(middle)
    hidden_ffn = (normed_mid * pre_ffn_factor).astype(BF)
    output, d_hidden_ffn, post_ffn_part, down_part, gu_part = feed_forward(
        hidden_ffn, middle, post_ffn_factor[None], out_grad[0], w_in, w_dn, next(ids)
    )
    post_ffn_part = post_ffn_part[0]
    out_cot = out_grad[0].astype(F32)
    pre_ffn_part = jnp.sum(d_hidden_ffn * normed_mid, axis=0)
    d_middle = out_cot + norm_back(d_hidden_ffn * pre_ffn_factor, normed_mid, inv_mid)
    post_part = jnp.sum(d_middle * normed_post, axis=0)
    d_branch = norm_back(d_middle * post_factor, normed_post, inv_post).astype(BF)
    d_branch = ring_gather(d_branch, next(ids), True)
    out_part = contract_rows(attended_b, d_branch)
    d_attended = contract_cols(d_branch, w_ot).astype(BF)
    d_query, d_key, d_value = attend_back(
        queries, keys, values, positions, attended, inv_total, d_attended
    )
    d_qkv = jnp.concatenate(
        [
            unrotate(d_query * q_scale, cos_tab, sine_tab).astype(BF),
            unrotate(d_key, cos_tab, sine_tab).astype(BF),
            d_value.astype(BF),
        ],
        axis=1,
    )
    d_hidden = ring_scatter(contract_cols(d_qkv, w_qkv), next(ids), True)
    qkv_part = contract_rows(hidden, d_qkv)
    pre_part = jnp.sum(d_hidden * normed_pre, axis=0)
    token_grad = d_middle + norm_back(d_hidden * pre_factor, normed_pre, inv_pre)
    gain_parts = jnp.pad(jnp.stack([pre_part, post_part, pre_ffn_part, post_ffn_part]), ((0, 4), (0, 0)))
    results = weights_out(
        gu_part, qkv_part.astype(BF), down_part, out_part.astype(BF),
        gain_parts, next(ids),
    )
    gate_g, up_g, query_g, key_g, value_g, down_g, out_g, gain_g = results
    mine = lax.axis_index("ctx") * 4 + lax.axis_index("fsdp")
    gain_g = lax.dynamic_slice(gain_g, (0, mine * shard_gain), (4, shard_gain))
    return (
        output[None], token_grad.astype(BF)[None],
        query_g, key_g, value_g, out_g, gate_g, up_g, down_g,
        gain_g[0], gain_g[1], gain_g[2], gain_g[3],
    )


ROW_FOLD = 4


def head_tables(positions, width):
    half_width = width // 2
    inv_freqs = ROPE_BASE ** (-jnp.arange(half_width, dtype=jnp.float32) * 2.0 / width)
    angles = positions.astype(jnp.float32)[:, None] * inv_freqs[None, :]
    return (jnp.cos(angles)[:, None, :], jnp.sin(angles)[:, None, :])


def rotate_heads(heads_in, cos_tab, sine_tab):
    half_width = heads_in.shape[-1] // 2
    front_half = heads_in[..., :half_width]
    back_half = heads_in[..., half_width:]
    return jnp.concatenate(
        [front_half * cos_tab - back_half * sine_tab, back_half * cos_tab + front_half * sine_tab],
        axis=-1,
    )


def unrotate_heads(grad_in, cos_tab, sine_tab):
    half_width = grad_in.shape[-1] // 2
    front_half = grad_in[..., :half_width]
    back_half = grad_in[..., half_width:]
    return jnp.concatenate(
        [front_half * cos_tab + back_half * sine_tab, back_half * cos_tab - front_half * sine_tab],
        axis=-1,
    )


def to_groups(flat_heads, tok_rows, q_group):
    shaped = flat_heads.reshape(tok_rows, KVH, q_group, HD)
    return jnp.transpose(shaped, (1, 2, 0, 3)).reshape(KVH, q_group * tok_rows, HD)


def from_groups(grouped, tok_rows, q_group):
    shaped = grouped.reshape(KVH, q_group, tok_rows, HD)
    return jnp.transpose(shaped, (2, 0, 1, 3)).reshape(tok_rows, KVH * q_group * HD)


def grad_rows(left, right, folding, count):
    block = contract_rows(left, right)
    return block.reshape(count, right.shape[1] // folding)


def blockwise(step_fn, carry, piece, width):
    key_count = piece[0].shape[0]
    n_steps = key_count // width
    stacked = tuple((member.reshape(n_steps, width, member.shape[1]) for member in piece))

    def one_step(partial_value, block_item):
        block_index, members = block_item
        return (step_fn(partial_value, members, block_index * width), None)

    carry, unused = lax.scan(one_step, carry, (jnp.arange(n_steps, dtype=jnp.int32), stacked))
    return carry


def block_grads(query_g, query_pos, d_att_g, delta, inv_tot, key_block, value_block, key_first):
    key_count = key_block.shape[0]
    key_grp = key_block.reshape(key_count, KVH, HD)
    value_grp = value_block.reshape(key_count, KVH, HD)
    raw_scores = jnp.einsum("grd,ngd->grn", query_g, key_grp, preferred_element_type=jnp.float32)
    capped = CAP * jnp.tanh(raw_scores / CAP)
    key_pos = key_first + jnp.arange(key_count, dtype=jnp.int32)
    allowed = key_pos[None, None, :] <= query_pos[None, :, None]
    weights = jnp.where(allowed, jnp.exp(capped), 0.0)
    prob_rows = weights * inv_tot[..., None]
    d_probs = jnp.einsum("grd,ngd->grn", d_att_g, value_grp, preferred_element_type=jnp.float32)
    slope = 1.0 - capped / CAP * (capped / CAP)
    d_raw = (prob_rows * (d_probs - delta[..., None]) * slope).astype(jnp.bfloat16)
    d_query = jnp.einsum("grn,ngd->grd", d_raw, key_grp, preferred_element_type=jnp.float32)
    d_key = jnp.einsum("grn,grd->ngd", d_raw, query_g, preferred_element_type=jnp.float32)
    weights_b = weights.astype(jnp.bfloat16)
    d_scaled = d_att_g.astype(jnp.float32) * inv_tot[..., None]
    scaled_high = d_scaled.astype(jnp.bfloat16)
    scaled_rest = (d_scaled - scaled_high.astype(jnp.float32)).astype(jnp.bfloat16)
    d_value = jnp.einsum("grn,grd->ngd", weights_b, scaled_high, preferred_element_type=jnp.float32)
    d_value = d_value + jnp.einsum(
        "grn,grd->ngd", weights_b, scaled_rest, preferred_element_type=jnp.float32
    )
    return (d_query, d_key.reshape(key_count, KVH * HD), d_value.reshape(key_count, KVH * HD))


def on_any_mesh(
    tokens,
    w_query,
    w_key,
    w_value,
    w_out,
    w_gate,
    w_up,
    w_down,
    pre_gain,
    post_gain,
    pre_ffn_gain,
    post_ffn_gain,
    out_grad,
):
    tok_rows = tokens.shape[1]
    q_group = H // KVH
    q_scale = HD ** (-0.5)
    width_q = H * HD
    width_kv = KVH * HD
    width_qkv = width_q + 2 * width_kv
    n_ctx = lax.axis_size("ctx")
    my_block = lax.axis_index("ctx")
    my_start = my_block * tok_rows
    positions = my_start + jnp.arange(tok_rows, dtype=jnp.int32)
    cos_tab, sine_tab = head_tables(positions, HD)
    row_pos = jnp.tile(positions, q_group)
    last_pos = my_start + tok_rows - 1
    resid_in = tokens[0].astype(jnp.float32)
    qkv_shard = jnp.concatenate([w_query, w_key, w_value], axis=1)
    gateup_shard = jnp.concatenate([w_gate, w_up], axis=1)
    shard_rows = qkv_shard.shape[0]
    gains_shard = jnp.stack([pre_gain, post_gain, pre_ffn_gain, post_ffn_gain])
    full_gains, full_qkv, full_out = (
        lax.all_gather(gains_shard, ("ctx", "fsdp"), axis=1, tiled=True),
        lax.all_gather(qkv_shard, ("ctx", "fsdp"), axis=0, tiled=True),
        lax.all_gather(w_out, ("ctx", "fsdp"), axis=0, tiled=True),
    )
    factors = 1.0 + full_gains.astype(jnp.float32)
    pre_factor, post_factor, pre_ffn_factor, post_ffn_factor = (
        factors[0],
        factors[1],
        factors[2],
        factors[3],
    )
    inv_pre, normed_pre = rms_parts(resid_in)
    hidden = (normed_pre * pre_factor).astype(jnp.bfloat16)
    projected = jnp.dot(hidden, full_qkv, preferred_element_type=jnp.float32)
    query_lin = projected[:, :width_q].reshape(tok_rows, H, HD)
    queries = (
        (rotate_heads(query_lin, cos_tab, sine_tab) * q_scale)
        .astype(jnp.bfloat16)
        .reshape(tok_rows, width_q)
    )
    query_grp = to_groups(queries, tok_rows, q_group)
    key_lin = projected[:, width_q : width_q + width_kv].reshape(tok_rows, KVH, HD)
    key_rows = rotate_heads(key_lin, cos_tab, sine_tab).astype(jnp.bfloat16).reshape(tok_rows, width_kv)
    value_rows = projected[:, width_q + width_kv :].astype(jnp.bfloat16)

    def add_block(partial_value, piece, first_row):
        key_block, value_block = piece

        def add_compute_block(state):
            row_total, weighted = state
            key_count = key_block.shape[0]
            key_grp = key_block.reshape(key_count, KVH, HD)
            raw_scores = jnp.einsum(
                "grd,ngd->grn", query_grp, key_grp, preferred_element_type=jnp.float32
            )
            capped = CAP * jnp.tanh(raw_scores / CAP)
            key_pos = first_row + jnp.arange(key_count, dtype=jnp.int32)
            allowed = key_pos[None, None, :] <= row_pos[None, :, None]
            weights = jnp.where(allowed, jnp.exp(capped), 0.0)
            value_grp = value_block.reshape(key_count, KVH, HD)
            weighted = weighted + jnp.einsum(
                "grn,ngd->grd",
                weights.astype(jnp.bfloat16),
                value_grp,
                preferred_element_type=jnp.float32,
            )
            return (row_total + jnp.sum(weights, axis=-1), weighted)

        def add_skip_block(state):
            return state

        return lax.cond(first_row <= last_pos, add_compute_block, add_skip_block, partial_value)

    start_state = (
        jnp.zeros((KVH, q_group * tok_rows), jnp.float32),
        jnp.zeros((KVH, q_group * tok_rows, HD), jnp.float32),
    )
    row_total, weighted = blockwise(
        add_block,
        start_state,
        (
            lax.all_gather(key_rows, "ctx", axis=0, tiled=True),
            lax.all_gather(value_rows, "ctx", axis=0, tiled=True),
        ),
        512,
    )
    inv_total = 1.0 / row_total
    attended_grp = weighted * inv_total[..., None]
    attended_b = from_groups(attended_grp, tok_rows, q_group).astype(jnp.bfloat16)
    branch = jnp.dot(attended_b, full_out, preferred_element_type=jnp.float32)
    inv_post, normed_post = rms_parts(branch)
    middle = resid_in + normed_post * post_factor
    inv_mid, normed_mid = rms_parts(middle)
    hidden_ffn = (normed_mid * pre_ffn_factor).astype(jnp.bfloat16)
    gate_up = fold_rows(
        hidden_ffn, lax.all_gather(gateup_shard, ("ctx", "fsdp"), axis=0, tiled=True)
    )
    gate_lin = gate_up[:, :FF]
    up_lin = gate_up[:, FF:]
    active = gated(gate_lin, up_lin).astype(jnp.bfloat16)
    ffn_branch = fold_rows(active, lax.all_gather(w_down, ("ctx", "fsdp"), axis=0, tiled=True))
    inv_ffn, normed_ffn = rms_parts(ffn_branch)
    output = (middle + normed_ffn * post_ffn_factor).astype(jnp.bfloat16)
    out_cot = out_grad[0].astype(jnp.float32)
    post_ffn_part = jnp.sum(out_cot * normed_ffn, axis=0)
    d_ffn_b = norm_back(out_cot * post_ffn_factor, normed_ffn, inv_ffn).astype(jnp.bfloat16)
    down_total = lax.psum_scatter(
        grad_rows(active, d_ffn_b, 1, lax.axis_size(("ctx", "fsdp")) * w_down.shape[0]),
        ("ctx", "fsdp"),
        scatter_dimension=0,
        tiled=True,
    )
    d_active = contract_cols(d_ffn_b, lax.all_gather(w_down, ("ctx", "fsdp"), axis=0, tiled=True))
    unused_value, gate_pull = jax.vjp(gated, gate_lin, up_lin)
    d_gate, d_up = gate_pull(d_active)
    d_gateup_b = jnp.concatenate([d_gate.astype(jnp.bfloat16), d_up.astype(jnp.bfloat16)], axis=1)
    gateup_folded = lax.psum_scatter(
        grad_rows(
            hidden_ffn,
            d_gateup_b,
            ROW_FOLD,
            lax.axis_size(("ctx", "fsdp")) * (ROW_FOLD * shard_rows),
        ),
        ("ctx", "fsdp"),
        scatter_dimension=0,
        tiled=True,
    )
    gateup_total = gateup_folded.reshape(shard_rows, 2 * FF)
    d_hidden_ffn = contract_cols(
        d_gateup_b, lax.all_gather(gateup_shard, ("ctx", "fsdp"), axis=0, tiled=True)
    )
    pre_ffn_part = jnp.sum(d_hidden_ffn * normed_mid, axis=0)
    d_middle = out_cot + norm_back(d_hidden_ffn * pre_ffn_factor, normed_mid, inv_mid)
    back_qkv, back_out = (
        lax.all_gather(qkv_shard, ("ctx", "fsdp"), axis=0, tiled=True),
        lax.all_gather(w_out, ("ctx", "fsdp"), axis=0, tiled=True),
    )
    post_gain_part = jnp.sum(d_middle * normed_post, axis=0)
    d_branch_b = norm_back(d_middle * post_factor, normed_post, inv_post).astype(jnp.bfloat16)
    w_out_part = contract_rows(attended_b, d_branch_b)
    d_attended = contract_cols(d_branch_b, back_out).astype(jnp.bfloat16)
    d_att_grp = to_groups(d_attended, tok_rows, q_group)
    row_delta = jnp.sum(d_att_grp.astype(jnp.float32) * attended_grp, axis=-1)
    zero_rows = jnp.zeros((tok_rows, width_kv), jnp.float32)
    zero_query = jnp.zeros((KVH, q_group * tok_rows, HD), jnp.float32)
    block_ids = jnp.arange(n_ctx, dtype=jnp.int32)
    all_keys, all_values = (
        lax.all_gather(key_rows, "ctx", axis=0, tiled=True),
        lax.all_gather(value_rows, "ctx", axis=0, tiled=True),
    )

    def returned_step(acc_query, block_item):
        block_index, key_block, value_block = block_item
        first_row = block_index * tok_rows

        def returned_compute_block(acc_in):
            d_query, d_key, d_value = block_grads(
                query_grp,
                row_pos,
                d_att_grp,
                row_delta,
                inv_total,
                key_block,
                value_block,
                first_row,
            )
            return (acc_in + d_query, (d_key, d_value))

        def returned_skip_block(acc_in):
            return (acc_in, (zero_rows, zero_rows))

        return lax.cond(
            first_row <= last_pos, returned_compute_block, returned_skip_block, acc_query
        )

    key_blocks = all_keys.reshape(n_ctx, tok_rows, width_kv)
    value_blocks = all_values.reshape(n_ctx, tok_rows, width_kv)
    d_query_grp, key_terms = lax.scan(
        returned_step, zero_query, (block_ids, key_blocks, value_blocks)
    )
    key_term_rows = key_terms[0].reshape(n_ctx * tok_rows, width_kv)
    value_term_rows = key_terms[1].reshape(n_ctx * tok_rows, width_kv)
    d_keys, d_values = (
        lax.psum_scatter(
            key_term_rows.astype(jnp.bfloat16), "ctx", scatter_dimension=0, tiled=True
        ).astype(jnp.float32),
        lax.psum_scatter(
            value_term_rows.astype(jnp.bfloat16), "ctx", scatter_dimension=0, tiled=True
        ).astype(jnp.float32),
    )
    d_query_flat = from_groups(d_query_grp, tok_rows, q_group).reshape(tok_rows, H, HD) * q_scale
    dq_lin = (
        unrotate_heads(d_query_flat, cos_tab, sine_tab).astype(jnp.bfloat16).reshape(tok_rows, width_q)
    )
    dk_lin = (
        unrotate_heads(d_keys.reshape(tok_rows, KVH, HD), cos_tab, sine_tab)
        .astype(jnp.bfloat16)
        .reshape(tok_rows, width_kv)
    )
    dv_lin = d_values.astype(jnp.bfloat16)
    dqkv_b = jnp.concatenate([dq_lin, dk_lin, dv_lin], axis=1)
    d_hidden = contract_cols(dqkv_b, back_qkv)
    qkv_part = contract_rows(hidden, dqkv_b).reshape(ROW_FOLD * D, width_qkv // ROW_FOLD)
    pre_gain_part = jnp.sum(d_hidden * normed_pre, axis=0)
    token_grad = d_middle + norm_back(d_hidden * pre_factor, normed_pre, inv_pre)
    gain_parts = jnp.stack([pre_gain_part, post_gain_part, pre_ffn_part, post_ffn_part])
    qkv_folded, out_total, gain_totals = (
        lax.psum_scatter(qkv_part, ("ctx", "fsdp"), scatter_dimension=0, tiled=True),
        lax.psum_scatter(w_out_part, ("ctx", "fsdp"), scatter_dimension=0, tiled=True),
        lax.psum_scatter(gain_parts, ("ctx", "fsdp"), scatter_dimension=1, tiled=True),
    )
    qkv_total = qkv_folded.reshape(shard_rows, width_qkv)
    return (
        output[None],
        token_grad.astype(jnp.bfloat16)[None],
        qkv_total[:, :width_q],
        qkv_total[:, width_q : width_q + width_kv],
        qkv_total[:, width_q + width_kv :],
        out_total,
        gateup_total[:, :FF],
        gateup_total[:, FF:],
        down_total,
        gain_totals[0],
        gain_totals[1],
        gain_totals[2],
        gain_totals[3],
    )


def solution(mesh):
    ring = mesh.shape["ctx"] == RING and mesh.shape["fsdp"] == 4
    tokens, rows, gains = P("fsdp", "ctx", None), P(("ctx", "fsdp"), None), P(("ctx", "fsdp"))
    return jax.shard_map(
        on_ring if ring else on_any_mesh,
        mesh=mesh,
        in_specs=(tokens,) + (rows,) * 7 + (gains,) * 4 + (tokens,),
        out_specs=(tokens, tokens) + (rows,) * 7 + (gains,) * 4,
        check_vma=False,
    )
```

```python
import functools

import jax
import jax.numpy as jnp
from jax import lax
from jax.experimental import pallas as pl
from jax.experimental.pallas import tpu as pltpu
from jax.sharding import PartitionSpec as P

D = 2304
H = 8
KVH = 4
HD = 256
CAP = 50
FF = 9216

EPSILON = 1e-06
ROPE_BASE = 10000.0

MESH = pl.DeviceIdType.MESH
HBM = pl.BlockSpec(memory_space=pl.ANY)
VMEM = pl.BlockSpec(memory_space=pltpu.VMEM)
DMA = pltpu.SemaphoreType.DMA
BF = jnp.bfloat16
F32 = jnp.float32


def rope_tables(positions, width):
    half_width = width // 2
    inv_freqs = ROPE_BASE ** (-jnp.arange(half_width, dtype=F32) * 2.0 / width)
    angles = positions.astype(F32)[:, None] * inv_freqs[None, :]
    return (jnp.cos(angles), jnp.sin(angles))


def rotate(rows, cos_tab, sine_tab):
    half_width = rows.shape[-1] // 2
    front, back = rows[..., :half_width], rows[..., half_width:]
    return jnp.concatenate(
        [front * cos_tab - back * sine_tab, back * cos_tab + front * sine_tab], axis=-1
    )


def unrotate(rows, cos_tab, sine_tab):
    half_width = rows.shape[-1] // 2
    front, back = rows[..., :half_width], rows[..., half_width:]
    return jnp.concatenate(
        [front * cos_tab + back * sine_tab, back * cos_tab - front * sine_tab], axis=-1
    )


def rms_parts(values_in):
    inverse = lax.rsqrt(jnp.mean(values_in * values_in, axis=-1, keepdims=True) + EPSILON)
    return (inverse, values_in * inverse)


def norm_back(grad_normed, normed, inverse):
    return inverse * (grad_normed - normed * jnp.mean(grad_normed * normed, axis=-1, keepdims=True))


def contract_rows(left, right):
    return lax.dot_general(left, right, (((0,), (0,)), ((), ())), preferred_element_type=F32)


def contract_cols(left, right):
    return lax.dot_general(left, right, (((1,), (1,)), ((), ())), preferred_element_type=F32)


def fold_rows(left, right):
    return jnp.dot(left, right, preferred_element_type=F32)


def gated(gate_in, up_in):
    return jax.nn.gelu(gate_in, approximate=True) * up_in


NZ = 4
RING = 2 * NZ


def my_place():
    c, f = lax.axis_index("ctx"), lax.axis_index("fsdp")
    return c // 2, c % 2, f // 2, f % 2


def ring_index(y, z):
    return z + y * (RING - 1 - 2 * z)


def ring_yz(q):
    y = q // NZ
    return y, q + y * (RING - 1 - 2 * q)


def device(z, core, y, x):
    return (2 * z + core, 2 * y + x)


def ring_device(q, core, x):
    y, z = ring_yz(q)
    return device(z, core, y, x)


def remote(src, dst, send_sem, recv_sem, where):
    return pltpu.make_async_remote_copy(
        src_ref=src,
        dst_ref=dst,
        send_sem=send_sem,
        recv_sem=recv_sem,
        device_id=where,
        device_id_type=MESH,
    )


def greet(places):
    barrier = pltpu.get_barrier_semaphore()
    for place in places:
        pl.semaphore_signal(barrier, inc=1, device_id=place, device_id_type=MESH)
    pl.semaphore_wait(barrier, len(places))


def params(collective_id, vmem_mib=56):
    return pltpu.CompilerParams(
        collective_id=collective_id,
        has_side_effects=True,
        vmem_limit_bytes=vmem_mib * 2**20,
    )


SUB = 4


def ring_parts(direction, step, half_step):
    if step != half_step:
        return list(range(SUB))
    half = SUB // 2
    return list(range(half)) if direction == 0 else list(range(half, SUB))


class RingGather:
    def __init__(self, x_ref, ring_ref, seq_ref, loc_sem, ss, rs, sib_ss=None, sib_rs=None):
        self.x_ref, self.ring_ref, self.seq_ref, self.loc_sem = x_ref, ring_ref, seq_ref, loc_sem
        self.ss, self.rs, self.sib_ss, self.sib_rs = ss, rs, sib_ss, sib_rs
        self.z, self.core, self.y, self.x = my_place()
        self.p = ring_index(self.y, self.z)
        self.right, self.left = (self.p + 1) % RING, (self.p + RING - 1) % RING
        self.sibling = device(self.z, 1 - self.core, self.y, self.x)
        self.piece = x_ref.shape[0] // SUB
        self.pending = []
        self.local = pltpu.make_async_copy(x_ref, ring_ref.at[self.p], loc_sem.at[RING])

    def places(self):
        near = [ring_device(self.right, self.core, self.x), ring_device(self.left, self.core, self.x)]
        return near + ([self.sibling] if self.seq_ref is not None else [])

    def origin(self, direction, step):
        return (self.p + (RING - step if direction == 0 else step)) % RING

    def copy(self, direction, step, k):
        q = self.origin(direction, step)
        rows = pl.ds(k * self.piece, self.piece)
        src = self.x_ref.at[rows] if step == 0 else self.ring_ref.at[q, rows]
        return remote(
            src,
            self.ring_ref.at[q, rows],
            self.ss.at[direction, step, k],
            self.rs.at[direction, step, k],
            ring_device(self.right if direction == 0 else self.left, self.core, self.x),
        )

    def place(self, q, act):
        if self.seq_ref is None:
            return
        yq, zq = ring_yz(q)
        src, dst = self.ring_ref.at[q], self.seq_ref.at[2 * zq + self.core]

        @pl.when(yq == self.core)
        def _():
            act(pltpu.make_async_copy(src, dst, self.loc_sem.at[q]))

        @pl.when(yq != self.core)
        def _():
            act(remote(src, dst, self.sib_ss.at[zq], self.sib_rs.at[zq], self.sibling))

    def step(self, step):
        if step == 0:
            self.local.start()
        for k in range(SUB):
            for direction in (0, 1):
                if step > 0 and (step < 3 or k in ring_parts(direction, 3, 3)):
                    self.copy(direction, step - 1, k).wait_recv()
                if k in ring_parts(direction, step, 3):
                    c = self.copy(direction, step, k)
                    c.start()
                    self.pending.append(c)
        if step == 1:
            self.local.wait()
            self.place(self.p, lambda c: c.start())
        if step == 3:
            for direction in (0, 1):
                for k in range(SUB):
                    if k not in ring_parts(direction, 3, 3):
                        self.copy(direction, 2, k).wait_recv()
        if step > 0:
            for direction in (0, 1):
                self.place(self.origin(direction, step), lambda c: c.start())

    def finish(self):
        for direction in (0, 1):
            for k in ring_parts(direction, 3, 3):
                self.copy(direction, 3, k).wait_recv()
        self.place((self.p + 4) % RING, lambda c: c.start())
        for c in self.pending:
            c.wait_send()
        if self.seq_ref is None:
            return
        for q in range(RING):
            self.place((self.p + q) % RING, lambda c: c.wait_send() if c.is_remote else c.wait())
        for zq in range(NZ):
            dst = self.seq_ref.at[2 * zq + 1 - self.core]
            remote(self.ring_ref.at[zq], dst, self.sib_ss.at[zq], self.sib_rs.at[zq], self.sibling).wait_recv()


def gather_kernel(paired, x_ref, *refs):
    if paired:
        seq_ref, ring_ref, *sems = refs
    else:
        ring_ref, *sems = refs
        seq_ref = None
    ring = RingGather(x_ref, ring_ref, seq_ref, *sems)
    greet(ring.places())
    for step in range(4):
        ring.step(step)
    ring.finish()


def ring_gather(block, collective_id, paired):
    rows, width = block.shape
    whole = jax.ShapeDtypeStruct((RING, rows, width), block.dtype)
    sems = [DMA((RING + 1,)), DMA((2, 4, SUB)), DMA((2, 4, SUB))]
    if paired:
        sems = [pltpu.VMEM(whole.shape, whole.dtype)] + sems + [DMA((NZ,)), DMA((NZ,))]
    out = pl.pallas_call(
        functools.partial(gather_kernel, paired),
        out_shape=whole,
        in_specs=[VMEM],
        out_specs=VMEM if paired else HBM,
        scratch_shapes=sems,
        compiler_params=params(collective_id),
    )(block)
    return out.reshape(RING * rows, width)


def scatter_kernel(paired, part_ref, o_ref, *refs):
    if paired:
        mine_ref, buf, ss, rs, sib_ss, sib_rs, loc_sem = refs
    else:
        buf, ss, rs = refs
        mine_ref = part_ref
    z, core, y, x = my_place()
    p = ring_index(y, z)
    right, left = (p + 1) % RING, (p + RING - 1) % RING
    sibling = device(z, 1 - core, y, x)
    piece = o_ref.shape[0] // SUB
    greet(
        [ring_device(right, core, x), ring_device(left, core, x)] + ([sibling] if paired else [])
    )
    if paired:
        swaps, copies = [], []
        for zq in range(NZ):
            q = ring_index(core, zq)
            swaps.append(remote(part_ref.at[2 * zq + 1 - core], mine_ref.at[q], sib_ss.at[zq], sib_rs.at[zq], sibling))
            swaps[-1].start()
            copies.append(pltpu.make_async_copy(part_ref.at[2 * zq + core], mine_ref.at[q], loc_sem.at[zq]))
            copies[-1].start()
        for c in copies:
            c.wait()
        for zq in range(NZ):
            q = ring_index(1 - core, zq)
            remote(part_ref.at[zq], mine_ref.at[q], sib_ss.at[zq], sib_rs.at[zq], sibling).wait_recv()
        for c in swaps:
            c.wait_send()

    def copy(direction, step, k, src):
        rows = pl.ds(k * piece, piece)
        return remote(
            src,
            buf.at[direction, step, rows],
            ss.at[direction, step, k],
            rs.at[direction, step, k],
            ring_device(right if direction == 0 else left, core, x),
        )

    pending = []
    for step in range(4):
        for k in range(SUB):
            rows = pl.ds(k * piece, piece)
            for direction in (0, 1):
                if k not in ring_parts(direction, step, 0):
                    continue
                far = 4 - step
                q = (p + (far if direction == 0 else RING - far)) % RING
                src = mine_ref.at[q, rows]
                if step > 0 and k in ring_parts(direction, step - 1, 0):
                    src = buf.at[direction, step - 1, rows]
                    copy(direction, step - 1, k, src).wait_recv()
                    total = src[...].astype(F32) + mine_ref[q, rows].astype(F32)
                    src[...] = total.astype(BF)
                c = copy(direction, step, k, src)
                c.start()
                pending.append(c)
    for k in range(SUB):
        rows = pl.ds(k * piece, piece)
        total = mine_ref[p, rows].astype(F32)
        for direction in (0, 1):
            src = buf.at[direction, 3, rows]
            copy(direction, 3, k, src).wait_recv()
            total = total + src[...].astype(F32)
        o_ref[rows] = total
    for c in pending:
        c.wait_send()


def ring_scatter(part, collective_id, paired):
    rows, width = part.shape[0] // RING, part.shape[1]
    blocks = (RING, rows, width)
    sems = [DMA((2, 4, SUB)), DMA((2, 4, SUB))]
    return pl.pallas_call(
        functools.partial(scatter_kernel, paired),
        out_shape=jax.ShapeDtypeStruct((rows, width), F32),
        in_specs=[VMEM],
        out_specs=VMEM,
        scratch_shapes=([pltpu.VMEM(blocks, BF)] if paired else [])
        + [pltpu.VMEM((2, 4, rows, width), BF)]
        + sems
        + ([DMA((NZ,)), DMA((NZ,)), DMA((NZ,))] if paired else []),
        compiler_params=params(collective_id),
    )(part.astype(BF).reshape(blocks))


TOK = 128
UNITS = FF // RING
TILE = 128
GELU_K = 0.7978845608028654
GELU_A = 0.044715


class SlotGather:
    def __init__(self, buf, ss, rs):
        z, core, y, x = my_place()
        p = ring_index(y, z)
        self.buf, self.ss, self.rs = buf, ss, rs
        self.near = (ring_device((p + 1) % RING, core, x), ring_device((p + RING - 1) % RING, core, x))
        self.pending = []

    def copy(self, direction, step, k):
        piece = TOK // SUB
        src = 0 if step == 0 else 2 * step - 1 + direction
        dst = 7 if step == 3 else 2 * step + 1 + direction
        return remote(
            self.buf.at[pl.ds(src * TOK + k * piece, piece)],
            self.buf.at[pl.ds(dst * TOK + k * piece, piece)],
            self.ss.at[direction, step, k],
            self.rs.at[direction, step, k],
            self.near[direction],
        )

    def step(self, step):
        for k in range(SUB):
            for direction in (0, 1):
                if step > 0:
                    self.copy(direction, step - 1, k).wait_recv()
                if k in ring_parts(direction, step, 3):
                    c = self.copy(direction, step, k)
                    c.start()
                    self.pending.append(c)

    def finish(self):
        for direction in (0, 1):
            for k in ring_parts(direction, 3, 3):
                self.copy(direction, 3, k).wait_recv()

    def drain(self):
        for c in self.pending:
            c.wait_send()


class SlotScatter:
    def __init__(self, part, buf, ss, rs):
        z, core, y, x = my_place()
        p = ring_index(y, z)
        self.part, self.buf, self.ss, self.rs = part, buf, ss, rs
        self.near = (ring_device((p + 1) % RING, core, x), ring_device((p + RING - 1) % RING, core, x))
        self.pending = []

    def copy(self, direction, step, k, src):
        rows = pl.ds(k * (TOK // SUB), TOK // SUB)
        return remote(
            src,
            self.buf.at[direction, step, rows],
            self.ss.at[direction, step, k],
            self.rs.at[direction, step, k],
            self.near[direction],
        )

    def step(self, step):
        piece = TOK // SUB
        for k in range(SUB):
            rows = pl.ds(k * piece, piece)
            for direction in (0, 1):
                if k not in ring_parts(direction, step, 0):
                    continue
                slot = 7 if step == 0 else 2 * (4 - step) - direction
                mine = pl.ds(slot * TOK + k * piece, piece)
                src = self.part.at[mine]
                if step > 0 and k in ring_parts(direction, step - 1, 0):
                    src = self.buf.at[direction, step - 1, rows]
                    self.copy(direction, step - 1, k, src).wait_recv()
                    src[...] = (src[...].astype(F32) + self.part[mine].astype(F32)).astype(BF)
                c = self.copy(direction, step, k, src)
                c.start()
                self.pending.append(c)

    def finish(self, total):
        for k in range(SUB):
            rows = pl.ds(k * (TOK // SUB), TOK // SUB)
            for direction in (0, 1):
                src = self.buf.at[direction, 3, rows]
                self.copy(direction, 3, k, src).wait_recv()
                total[rows] = total[rows] + src[...].astype(F32)

    def drain(self):
        for c in self.pending:
            c.wait_send()


def tiles(count, width, body):
    def step(i, carry):
        body(pl.ds(pl.multiple_of(i * width, width), width))
        return carry

    lax.fori_loop(0, count, step, 0)


def gelu_parts(v):
    bent = jnp.tanh(GELU_K * (v + GELU_A * (v * v * v)))
    value = 0.5 * v * (1.0 + bent)
    slope = 0.5 * (1.0 + bent) + 0.5 * v * (1.0 - bent * bent) * (GELU_K * (1.0 + 3.0 * GELU_A * (v * v)))
    return value, slope


PAIRS = ((128, 256), (384, 256), (640, 256))
LAST = (896, 128)
OWN = (0, 128)


def feed_forward_kernel(hid, middle, factor, cot, w_hbm, wd_hbm,
                        out_o, d_hid_o, gain_o, wd_grad, gu_grad,
                        wgu, wd, ha, gu, act, part, buf, df, dgu, total, stage,
                        w_sem, ags, agr, rss, rsr, out_sem):
    gather = [SlotGather(b, ags.at[i], agr.at[i]) for i, b in enumerate((ha, df))]
    scatter = [SlotScatter(part, buf, rss.at[i], rsr.at[i]) for i in range(2)]
    greet(gather[0].near)
    loads = [
        pltpu.make_async_copy(w_hbm.at[:, pl.ds(0, 2 * UNITS)], wgu, w_sem.at[0]),
        pltpu.make_async_copy(wd_hbm, wd, w_sem.at[1]),
    ]
    ha[0:TOK] = hid[...]
    gather[0].step(0)
    for c in loads:
        c.start()
    loads[0].wait()

    def gate_up(first, count):
        rows = pl.ds(first, count)

        def column(cols):
            gu[rows, cols] = fold_rows(ha[rows], wgu[:, cols])

        tiles(3, 768, column)

        def finish(i, carry):
            r = pl.ds(pl.multiple_of(first + i * 32, 32), 32)
            act[r] = (gelu_parts(gu[r, 0:UNITS])[0] * gu[r, UNITS : 2 * UNITS]).astype(BF)
            return carry

        lax.fori_loop(0, count // 32, finish, 0)

    def down_part(first, count, dst):
        def column(cols):
            value = fold_rows(act[pl.ds(first, count)], wd[:, cols])
            dst[pl.ds(first, count), cols] = value.astype(dst.dtype)

        tiles(3, 768, column)

    def active_back(first, count):
        rows = pl.ds(first, count)
        for n in range(3):
            cols, up_cols = pl.ds(n * 384, 384), pl.ds(UNITS + n * 384, 384)
            d_active = contract_cols(df[rows], wd[cols])
            value, slope = gelu_parts(gu[rows, cols])
            dgu[rows, cols] = (d_active * gu[rows, up_cols] * slope).astype(BF)
            dgu[rows, up_cols] = (d_active * value).astype(BF)

    def hidden_part(first, count, dst):
        def column(cols):
            value = contract_cols(dgu[pl.ds(first, count)], wgu[cols])
            dst[pl.ds(first, count), cols] = value.astype(dst.dtype)

        tiles(9, 256, column)

    n_down = UNITS // TILE

    def grad_out(i):
        slot = i % 2
        if i < n_down:
            return pltpu.make_async_copy(stage.at[slot], wd_grad.at[pl.ds(i * TILE, TILE)], out_sem.at[slot])
        return pltpu.make_async_copy(stage.at[slot], gu_grad.at[pl.ds((i - n_down) * TILE, TILE)], out_sem.at[slot])

    def grad_tiles(first, last):
        for i in range(first, last):
            if i >= 2:
                grad_out(i - 2).wait()
            if i < n_down:
                value = contract_rows(act[:, pl.ds(i * TILE, TILE)], df[...])
            else:
                value = contract_rows(ha[:, pl.ds((i - n_down) * TILE, TILE)], dgu[...])
            stage[i % 2] = value.astype(BF)
            grad_out(i).start()

    gate_up(*OWN)
    for step, pair in enumerate(PAIRS):
        gather[0].step(step + 1)
        if step == 0:
            loads[1].wait()
        gate_up(*pair)
    gather[0].finish()
    gate_up(*LAST)
    down_part(*LAST, part)
    scatter[0].step(0)
    for step, pair in enumerate(PAIRS[::-1]):
        down_part(*pair, part)
        scatter[0].step(step + 1)
    down_part(*OWN, total)
    scatter[0].finish(total)
    gather[0].drain()
    scatter[0].drain()

    branch = total[...]
    inverse, normed = rms_parts(branch)
    out_cot = cot[...].astype(F32)
    scale = factor[...]
    df[0:TOK] = norm_back(out_cot * scale, normed, inverse).astype(BF)
    gather[1].step(0)
    out_o[...] = (middle[...] + normed * scale).astype(BF)
    gain_o[...] = jnp.sum(out_cot * normed, axis=0, keepdims=True)
    active_back(*OWN)
    for step, pair in enumerate(PAIRS):
        gather[1].step(step + 1)
        active_back(*pair)
    gather[1].finish()
    active_back(*LAST)
    hidden_part(*LAST, part)
    scatter[1].step(0)
    done = 0
    for step, pair in enumerate(PAIRS[::-1]):
        hidden_part(*pair, part)
        scatter[1].step(step + 1)
        grad_tiles(done, done + 6)
        done += 6
    hidden_part(*OWN, d_hid_o)
    scatter[1].finish(d_hid_o)
    n_tiles = n_down + ha.shape[1] // TILE
    grad_tiles(done, n_tiles)
    for i in (n_tiles - 2, n_tiles - 1):
        grad_out(i).wait()
    gather[1].drain()
    scatter[1].drain()


def feed_forward(hidden_ffn, middle, factor, out_grad, w_in, w_down, collective_id):
    rows, width = hidden_ffn.shape
    total = RING * rows

    def full(*shape, dtype=F32):
        return jax.ShapeDtypeStruct(shape, dtype)

    return pl.pallas_call(
        feed_forward_kernel,
        out_shape=[
            full(rows, width, dtype=BF), full(rows, width), full(1, width),
            full(UNITS, width, dtype=BF), full(width, 2 * UNITS, dtype=BF),
        ],
        in_specs=[VMEM] * 4 + [HBM] * 2,
        out_specs=[VMEM] * 3 + [HBM] * 2,
        scratch_shapes=[
            pltpu.VMEM((width, 2 * UNITS), BF), pltpu.VMEM((UNITS, width), BF),
            pltpu.VMEM((total, width), BF), pltpu.VMEM((total, 2 * UNITS), F32), pltpu.VMEM((total, UNITS), BF),
            pltpu.VMEM((total, width), BF), pltpu.VMEM((2, 4, rows, width), BF),
            pltpu.VMEM((total, width), BF), pltpu.VMEM((total, 2 * UNITS), BF),
            pltpu.VMEM((rows, width), F32), pltpu.VMEM((2, TILE, width), BF),
            DMA((2,)),
            DMA((2, 2, 4, SUB)), DMA((2, 2, 4, SUB)), DMA((2, 2, 4, SUB)), DMA((2, 2, 4, SUB)),
            DMA((2,)),
        ],
        compiler_params=params(collective_id, 60),
    )(hidden_ffn, middle, factor, out_grad, w_in, w_down)


WIDTHS = (UNITS, UNITS, HD, HD, HD)
STARTS = (0, UNITS, 2 * UNITS, 2 * UNITS + HD, 2 * UNITS + 2 * HD)
WIDE = 2 * UNITS + 3 * HD


def member_place(t, core, x):
    return device(t // 2, core, t % 2, x)


def partner(t, j):
    out = 0
    for bit in (1, 2, 4):
        on = (t // bit) % 2
        out = out + bit * (1 - on if j & bit else on)
    return out


def column_start(which, t):
    if which < 2:
        return pl.multiple_of(t * UNITS, 128)
    return pl.multiple_of((t if which == 2 else t // 2) * HD, 128)


def weights_in_kernel(gate, up, query, key, value, down, out, gains, x_ref, w_ref, d_ref, o_ref, g_ref, seq_ref,
                      ring_ref, loc, s1, r1, s2, r2, s3, r3, s4, r4, s5, r5, ring_loc, ss, rs, sib_ss, sib_rs):
    z, core, y, x = my_place()
    t = 2 * z + y
    sibling, across = device(z, 1 - core, y, x), device(z, core, y, 1 - x)

    def slot(tq, corq, xq):
        return (2 * (tq // 2) + corq) * 4 + 2 * (tq % 2) + xq

    me = slot(t, core, x)
    member = [partner(t, j) for j in range(RING)]
    plane = []
    for dc in (0, 1):
        for dy in (0, 1):
            for dx in (0, 1):
                if (dc, dx) != (0, 0):
                    plane.append(device(z, (core + dc) % 2, (y + dy) % 2, (x + dx) % 2))
    greet([member_place(member[j], core, x) for j in range(1, RING)] + plane)
    sources = (gate, up, query, key, value)
    ring = RingGather(x_ref, ring_ref, seq_ref, ring_loc, ss, rs, sib_ss, sib_rs)

    def first(j, a, wait=False):
        tq = member[j]
        if a == 5:
            src, dst = gains, g_ref.at[slot(tq, core, x) if wait else me]
        else:
            src = sources[a].at[:, pl.ds(column_start(a, tq), WIDTHS[a])]
            dst = w_ref.at[slot(tq, core, x) if wait else me, :, pl.ds(STARTS[a], WIDTHS[a])]
        return remote(src, dst, s1.at[j, a], r1.at[j, a], member_place(tq, core, x))

    pending = []

    def go(copies):
        for c in copies:
            c.start()
            pending.append(c)

    def second(j, wait=False):
        i = slot(member[j], core, 1 - x if wait else x)
        return [
            remote(w_ref.at[i], w_ref.at[i], s2.at[j, 0], r2.at[j, 0], across),
            remote(g_ref.at[i], g_ref.at[i], s2.at[j, 1], r2.at[j, 1], across),
        ]

    def third(j, flip, wait=False):
        i = slot(member[j], 1 - core if wait else core, 1 - x if flip else x)
        return [
            remote(w_ref.at[i], w_ref.at[i], s3.at[j, flip, 0], r3.at[j, flip, 0], sibling),
            remote(g_ref.at[i], g_ref.at[i], s3.at[j, flip, 1], r3.at[j, flip, 1], sibling),
        ]

    def start_round(j):
        go([first(j, a) for a in (5, 2, 3, 4, 0, 1)])

    def end_round(j):
        for a in range(6):
            first(j, a, True).wait_recv()
        go(second(j) + third(j, 0))

    def end_across(j):
        for c in second(j, True):
            c.wait_recv()
        go(third(j, 1))

    ring.step(0)
    start_round(4)
    start_round(1)
    locals_ = [pltpu.make_async_copy(gains, g_ref.at[me], loc.at[5])]
    for a in range(5):
        locals_.append(
            pltpu.make_async_copy(
                sources[a].at[:, pl.ds(column_start(a, t), WIDTHS[a])],
                w_ref.at[me, :, pl.ds(STARTS[a], WIDTHS[a])],
                loc.at[a],
            )
        )
    for c in locals_:
        c.start()
    pair = ((down, d_ref), (out, o_ref))
    mine = 2 * y + x
    for xq in (0, 1):
        to_self = (x == core) & (y == core) & (xq == x)
        for a, (src, dst) in enumerate(pair):
            @pl.when(to_self)
            def _():
                pltpu.make_async_copy(src, dst.at[mine], s4.at[xq, a]).start()

            @pl.when(jnp.logical_not(to_self))
            def _():
                remote(src, dst.at[mine], s4.at[xq, a], r4.at[y, a], device(z, x, core, xq)).start()
    for c in locals_:
        c.wait()
    go(second(0) + third(0, 0))
    ring.step(1)
    end_round(1)
    start_round(2)
    end_round(4)
    start_round(5)
    ring.step(2)
    end_round(2)
    start_round(3)
    end_across(0)
    end_across(1)
    end_round(5)
    start_round(6)
    ring.step(3)
    end_round(3)
    start_round(7)
    end_across(4)
    for yq in (0, 1):
        from_self = (core == y) & (yq == y) & (core == x)
        for a, (src, dst) in enumerate(pair):
            @pl.when(from_self)
            def _():
                pltpu.make_async_copy(src, dst.at[mine], s4.at[x, a]).wait()

            @pl.when(jnp.logical_not(from_self))
            def _():
                remote(src, dst.at[2 * yq + core], s4.at[0, a], r4.at[yq, a], sibling).wait_recv()

            go([remote(dst.at[2 * yq + core], dst.at[2 * yq + core], s5.at[yq, a], r5.at[yq, a], sibling)])
    end_across(2)
    end_across(5)
    ring.finish()
    end_round(6)
    end_across(3)
    end_round(7)
    end_across(6)
    end_across(7)
    for j in range(RING):
        for flip in (0, 1):
            for c in third(j, flip, True):
                c.wait_recv()
    for yq in (0, 1):
        for a, (src, dst) in enumerate(pair):
            remote(src, dst.at[2 * yq + 1 - core], s5.at[yq, a], r5.at[yq, a], sibling).wait_recv()
    for c in pending:
        c.wait_send()
    for xq in (0, 1):
        to_self = (x == core) & (y == core) & (xq == x)
        for a, (src, dst) in enumerate(pair):
            @pl.when(jnp.logical_not(to_self))
            def _():
                remote(src, dst.at[mine], s4.at[xq, a], r4.at[y, a], device(z, x, core, xq)).wait_send()


def weights_in(gate, up, query, key, value, down, out, gains, block, collective_id):
    n = 4 * RING
    whole = (RING,) + block.shape
    shapes = [
        jax.ShapeDtypeStruct((n, gate.shape[0], WIDE), BF),
        jax.ShapeDtypeStruct((4,) + down.shape, BF),
        jax.ShapeDtypeStruct((4,) + out.shape, BF),
        jax.ShapeDtypeStruct((n,) + gains.shape, gains.dtype),
        jax.ShapeDtypeStruct(whole, BF),
    ]
    results = pl.pallas_call(
        weights_in_kernel,
        out_shape=shapes,
        in_specs=[VMEM] * 9,
        out_specs=[HBM] * 4 + [VMEM],
        scratch_shapes=[
            pltpu.VMEM(whole, BF),
            DMA((6,)),
            DMA((RING, 6)), DMA((RING, 6)),
            DMA((RING, 2)), DMA((RING, 2)),
            DMA((RING, 2, 2)), DMA((RING, 2, 2)),
            DMA((2, 2)), DMA((2, 2)),
            DMA((2, 2)), DMA((2, 2)),
            DMA((RING + 1,)), DMA((2, 4, SUB)), DMA((2, 4, SUB)), DMA((NZ,)), DMA((NZ,)),
        ],
        compiler_params=params(collective_id, 32),
    )(gate, up, query, key, value, down, out, gains, block)
    return list(results[:4]) + [results[4].reshape(RING * block.shape[0], block.shape[1])]


ROUNDS = (4, 5, 6, 7, 2, 3, 1, 0)
AHEAD = 2


def slot_of(q, p):
    d = (q - p + RING) % RING
    return jnp.where(d == 0, 0, jnp.where(d < 4, 2 * d, jnp.where(d == 4, 7, 15 - 2 * d)))


def backward_kernel(d_branch, gu_in, down_in, hidden, w_hbm, wo, q_in, k_in, v_in, att, inv, cos, sine, normed, gain_in,
                    d_hid_o, gain_o, c_gu, c_q, down_o, out_o,
                    ring, seq, part, buf, wq, d_att, d_qkv, dk, dv, grad_q, aq, bq,
                    own, a_gu, b_gu, down_own, da, db, og, oa, ob, ga, gsum,
                    load, ags, agr, pls, plr, rss, rsr, sws, swr, s1, r1, s2, r2, s3, r3,
                    q1, t1, q2, t2, q3, t3, sx, rx, sg, rg):
    z, core, y, x = my_place()
    t, p = 2 * z + y, ring_index(y, z)
    sibling, across = device(z, 1 - core, y, x), device(z, core, y, 1 - x)
    diagonal = device(z, 1 - core, 1 - y, x)
    members = [member_place(partner(t, j), core, x) for j in range(RING)]
    order = [partner(t, j) for j in ROUNDS]
    greet(members[1:] + [sibling, across, diagonal])
    pending = []

    def go(*copies):
        for c in copies:
            c.start()
            pending.append(c)

    def owner(tq, corq, xq):
        return (2 * (tq // 2) + corq) * 4 + 2 * (tq % 2) + xq

    side_x = (1 - x, x)

    def gu_a(side, j):
        src = gu_in.at[owner(order[j], 1 - core, side_x[side])]
        return remote(src, a_gu.at[side, j], s1.at[side, j], r1.at[side, j], sibling)

    def gu_own(side, j):
        return pltpu.make_async_copy(gu_in.at[owner(order[j], core, side_x[side])], own.at[j % 2], load.at[j % 2])

    def gu_b(j):
        return remote(a_gu.at[0, j], b_gu.at[j], s2.at[j], r2.at[j], across)

    def gu_c(j, wait=False):
        dst = c_gu.at[order[j] if wait else t]
        if ROUNDS[j] == 0:
            return pltpu.make_async_copy(a_gu.at[1, j], dst, load.at[2])
        return remote(a_gu.at[1, j], dst, s3.at[j], r3.at[j], members[ROUNDS[j]])

    def sum_own(side, j, more=None):
        gu_own(side, j).wait()
        gu_a(side, j).wait_recv()
        total = a_gu[side, j].astype(F32) + own[j % 2].astype(F32)
        if more is not None:
            total = total + more[j].astype(F32)
        a_gu[side, j] = total.astype(BF)

    def pump(first, last):
        for j in range(first, last):
            gu_own(1, j).start()
        for j in range(first, last):
            gu_b(j).wait_recv()
            if j + AHEAD < RING:
                go(gu_b(j + AHEAD))
            sum_own(1, j, b_gu)

    small = ((down_in, down_own, da, db, down_o), (og, None, oa, ob, out_o))

    def small_a(a, xo):
        return remote(small[a][0].at[2 * (1 - core) + xo], small[a][2].at[xo], sx.at[a, xo], rx.at[a, xo], sibling)

    def small_b(a):
        return remote(small[a][2].at[1 - x], small[a][3], sx.at[a, 2], rx.at[a, 2], across)

    def small_c(a, act):
        src, dst = small[a][2].at[x], small[a][4]

        @pl.when(core == y)
        def _():
            c = pltpu.make_async_copy(src, dst, load.at[3 + a])
            c.start() if act == 0 else c.wait()

        @pl.when(core != y)
        def _():
            c = remote(src, dst, sx.at[a, 3], rx.at[a, 3], diagonal)
            c.start() if act == 0 else c.wait()

    def q_a(side, j):
        src = grad_q.at[owner(order[j], 1 - core, side_x[side])]
        return remote(src, aq.at[side, j], q1.at[side, j], t1.at[side, j], sibling)

    def q_b(j):
        return remote(grad_q.at[owner(order[j], core, 1 - x)], bq.at[j], q2.at[j], t2.at[j], across)

    def q_c(j, wait=False):
        src, dst = grad_q.at[owner(order[j], core, x)], c_q.at[order[j] if wait else t]
        if ROUNDS[j] == 0:
            return pltpu.make_async_copy(src, dst, load.at[5])
        return remote(src, dst, q3.at[j], t3.at[j], members[ROUNDS[j]])

    def gain_a():
        return remote(gain_in, ga.at[RING], sg.at[RING], rg.at[RING], sibling)

    def gain_b():
        return remote(gsum.at[0], ga.at[RING + 1], sg.at[RING + 1], rg.at[RING + 1], across)

    def gain_c(j):
        return remote(gsum.at[1], ga.at[j], sg.at[j], rg.at[j], members[j])

    gather = SlotGather(ring, ags, agr)

    def block(slot):
        if slot == 0:
            return p
        if slot == 7:
            return (p + 4) % RING
        s = (slot + 1) // 2
        return (p + (RING - s if slot % 2 else s)) % RING

    def place(slot, act):
        yq, zq = ring_yz(block(slot))
        src, dst = ring.at[pl.ds(slot * TOK, TOK)], seq.at[2 * zq + core]

        @pl.when(yq == core)
        def _():
            c = pltpu.make_async_copy(src, dst, load.at[6 + slot])
            c.start() if act == 0 else c.wait()

        @pl.when(yq != core)
        def _():
            c = remote(src, dst, pls.at[zq], plr.at[zq], sibling)
            c.start() if act == 0 else c.wait_send()

    first = pltpu.make_async_copy(d_branch, ring.at[pl.ds(0, TOK)], load.at[14])
    first.start()
    wq_load = pltpu.make_async_copy(w_hbm.at[:, pl.ds(2 * UNITS, 3 * HD)], wq, load.at[15])
    first.wait()
    gather.step(0)
    place(0, 0)
    for side in (0, 1):
        go(*[gu_a(side, j) for j in range(RING)])
        if side == 0:
            go(small_a(0, 0), small_a(0, 1))
    wq_load.start()
    for j in range(RING):
        if j < 2:
            gu_own(0, j).start()
        sum_own(0, j)
        if j + 2 < RING:
            gu_own(0, j + 2).start()
        if j < AHEAD:
            go(gu_b(j))

    def down_sum(xo):
        c = pltpu.make_async_copy(down_in.at[2 * core + xo], down_own, load.at[16])
        c.start()
        small_a(0, xo).wait_recv()
        c.wait()
        da[xo] = (da[xo].astype(F32) + down_own[...].astype(F32)).astype(BF)

    down_sum(0)
    gather.step(1)
    place(1, 0)
    place(2, 0)
    pump(0, 1)
    down_sum(1)
    pump(1, 2)
    gather.step(2)
    place(3, 0)
    place(4, 0)
    pump(2, 4)
    gather.step(3)
    place(5, 0)
    place(6, 0)
    pump(4, 5)
    gather.finish()
    place(7, 0)
    for j in range(5):
        go(gu_c(j))
    for zq in range(NZ):
        dst = seq.at[2 * zq + 1 - core]
        remote(dst, dst, pls.at[zq], plr.at[zq], sibling).wait_recv()
    for slot in range(RING):
        place(slot, 1)
    gather.drain()
    hidden_load = pltpu.make_async_copy(hidden, ring, load.at[14])
    hidden_load.start()

    for c in range(0, RING, 2):
        rows = pl.ds(c * TOK, 2 * TOK)
        d_att[rows] = contract_cols(seq[c : c + 2].reshape(2 * TOK, -1), wo[...]).astype(BF)

    def out_columns(cols):
        value = contract_rows(att[...].astype(BF), seq[:, :, cols].reshape(RING * TOK, 768))
        for f in range(4):
            og[f, :, cols] = value[64 * f : 64 * (f + 1)].astype(BF)

    tiles(3, 768, out_columns)
    go(small_a(1, 0), small_a(1, 1))
    pump(5, 6)
    go(gu_c(5))
    dk[...] = jnp.zeros_like(dk)
    dv[...] = jnp.zeros_like(dv)
    for i in range(4):
        r, upto = pl.ds(i * 256, 256), (i + 1) * 256
        keys, vals, query = k_in[0:upto], v_in[0:upto], q_in[r]
        bent = jnp.tanh(contract_cols(query, keys) / CAP)
        seen = lax.broadcasted_iota(jnp.int32, bent.shape, 1) <= i * 256 + lax.broadcasted_iota(jnp.int32, bent.shape, 0)
        weights = jnp.where(seen, jnp.exp(CAP * bent), 0.0)
        grad = d_att[r].astype(F32)
        delta = jnp.sum(grad * att[r], axis=-1, keepdims=True)
        d_probs = contract_cols(d_att[r], vals)
        d_raw = (weights * inv[r] * (d_probs - delta) * (1.0 - bent * bent)).astype(BF)
        dq = fold_rows(d_raw, keys) * (HD ** (-0.5))
        d_qkv[r, 0:HD] = unrotate(dq, cos[r], sine[r]).astype(BF)
        dk[0:upto] = dk[0:upto] + contract_rows(d_raw, query)
        scaled = grad * inv[r]
        high = scaled.astype(BF)
        rest = (scaled - high.astype(F32)).astype(BF)
        weights_b = weights.astype(BF)
        dv[0:upto] = dv[0:upto] + contract_rows(weights_b, high) + contract_rows(weights_b, rest)
        if i == 1:
            pump(6, 7)
            go(gu_c(6))
            go(small_b(0))
        if i == 3:
            pump(7, 8)
            go_self = gu_c(7)
            go_self.start()
    d_qkv[:, HD : 2 * HD] = unrotate(dk[...], cos[...], sine[...]).astype(BF)
    d_qkv[:, 2 * HD : 3 * HD] = dv[...].astype(BF)

    wq_load.wait()
    scatter = SlotScatter(part, buf, rss, rsr)

    def swap(zq):
        where = pl.ds(pl.multiple_of(slot_of(ring_index(core, zq), p) * TOK, TOK), TOK)
        keep = pltpu.make_async_copy(seq.at[2 * zq + core], part.at[where], load.at[17 + zq])
        return keep, remote(seq.at[2 * zq + 1 - core], part.at[where], sws.at[zq], swr.at[zq], sibling)

    def swapped(zq):
        where = pl.ds(pl.multiple_of(slot_of(ring_index(1 - core, zq), p) * TOK, TOK), TOK)
        return remote(seq.at[0], part.at[where], sws.at[zq], swr.at[zq], sibling)

    for zq in range(NZ):
        rows = d_qkv[2 * zq * TOK : (2 * zq + 2) * TOK]

        def columns(cols):
            value = contract_cols(rows, wq[cols])
            seq[2 * zq, :, cols] = value[0:TOK].astype(BF)
            seq[2 * zq + 1, :, cols] = value[TOK:].astype(BF)

        tiles(3, 768, columns)
        for c in swap(zq):
            c.start()
    for zq in range(NZ):
        swap(zq)[0].wait()
        swapped(zq).wait_recv()
    scatter.step(0)

    hidden_load.wait()

    def grad_half(half):
        def columns(cols):
            value = contract_rows(ring[:, pl.ds(half * 1152, 1152)], d_qkv[:, cols])
            for i in range(16):
                grad_q[half * 16 + i, :, cols] = value[72 * i : 72 * (i + 1)].astype(BF)

        tiles(3, 256, columns)

    grad_half(0)
    scatter.step(1)
    grad_half(1)
    for side in (0, 1):
        go(*[q_a(side, j) for j in range(RING)])
    for xo in (0, 1):
        small_a(1, xo).wait_recv()
        oa[xo] = (oa[xo].astype(F32) + og[2 * core + xo].astype(F32)).astype(BF)
    go(small_b(1))
    scatter.step(2)

    def q_sum(side, j):
        i = owner(order[j], core, side_x[side])
        q_a(side, j).wait_recv()
        total = grad_q[i].astype(F32) + aq[side, j].astype(F32)
        if side == 1:
            q_b(j).wait_recv()
            total = total + bq[j].astype(F32)
        grad_q[i] = total.astype(BF)

    for j in range(RING):
        q_sum(0, j)
        if j < AHEAD:
            go(q_b(j))
    small_b(0).wait_recv()
    da[x] = (da[x].astype(F32) + db[...].astype(F32)).astype(BF)
    small_c(0, 0)
    scatter.step(3)

    def q_round(j):
        q_sum(1, j)
        if j + AHEAD < RING:
            go(q_b(j + AHEAD))
        if ROUNDS[j] == 0:
            q_c(j).start()
        else:
            go(q_c(j))

    for j in range(4):
        q_round(j)
    small_b(1).wait_recv()
    oa[x] = (oa[x].astype(F32) + ob[...].astype(F32)).astype(BF)
    small_c(1, 0)

    def own_part(cols):
        slot = part[0:TOK, cols]
        d_hid_o[:, cols] = slot.astype(F32)

    tiles(3, 768, own_part)
    for j in range(4, RING):
        q_round(j)
    scatter.finish(d_hid_o)
    gain_in[0:1] = jnp.sum(d_hid_o[...] * normed[...], axis=0, keepdims=True)
    go(gain_a())
    gain_a().wait_recv()
    gsum[0] = gain_in[...] + ga[RING]
    go(gain_b())
    gain_b().wait_recv()
    gsum[1] = gsum[0] + ga[RING + 1]
    go(*[gain_c(j) for j in range(1, RING)])
    total = gsum[1]
    for j in range(1, RING):
        gain_c(j).wait_recv()
        total = total + ga[j]
    gain_o[...] = total

    for j in range(RING):
        if ROUNDS[j] == 0:
            gu_c(j).wait()
            q_c(j).wait()
        else:
            gu_c(j, True).wait_recv()
            q_c(j, True).wait_recv()
    small_c(0, 1)
    small_c(1, 1)
    for zq in range(NZ):
        swap(zq)[1].wait_send()
    scatter.drain()
    for c in pending:
        c.wait_send()


def backward(d_branch, gu, down, hidden, w_in, w_out, queries, keys, values, attended, inv_total, cos_tab, sine_tab,
             normed_pre, gain_parts, collective_id):
    n = 4 * RING
    rows, width = d_branch.shape
    shard = gu.shape[0] // n
    gu = gu.reshape(n, shard, 2 * UNITS)
    down = down.reshape(4, -1, width)
    total, down_rows, out_rows = RING * rows, down.shape[1], w_out.shape[0] // 4
    gain_shape = (8, width)

    def out(*shape, dtype=BF):
        return jax.ShapeDtypeStruct(shape, dtype)

    def body(*refs):
        ins, rest = refs[:14], refs[14:]
        gains_ref, rest = rest[0], rest[1:]
        outs, scr = rest[:6], rest[6:]
        gain_scr = scr[0]
        gain_scr[...] = gains_ref[...]
        backward_kernel(*ins, gain_scr, *outs, *scr[1:])

    return pl.pallas_call(
        body,
        out_shape=[
            out(rows, width, dtype=F32), out(*gain_shape, dtype=F32),
            out(RING, shard, 2 * UNITS), out(RING, shard, 3 * HD),
            out(down_rows, width), out(out_rows, width),
        ],
        in_specs=[HBM] * 5 + [VMEM] * 10,
        out_specs=[VMEM] * 2 + [HBM] * 4,
        scratch_shapes=[
            pltpu.VMEM(gain_shape, F32),
            pltpu.VMEM((total, width), BF), pltpu.VMEM((RING, rows, width), BF), pltpu.VMEM((total, width), BF),
            pltpu.VMEM((2, 4, rows, width), BF), pltpu.VMEM((width, 3 * HD), BF),
            pltpu.VMEM((total, HD), BF), pltpu.VMEM((total, 3 * HD), BF),
            pltpu.VMEM((total, HD), F32), pltpu.VMEM((total, HD), F32),
            pltpu.VMEM((n, shard, 3 * HD), BF), pltpu.VMEM((2, RING, shard, 3 * HD), BF), pltpu.VMEM((RING, shard, 3 * HD), BF),
            pltpu.VMEM((2, shard, 2 * UNITS), BF), pltpu.VMEM((2, RING, shard, 2 * UNITS), BF), pltpu.VMEM((RING, shard, 2 * UNITS), BF),
            pltpu.VMEM((down_rows, width), BF), pltpu.VMEM((2, down_rows, width), BF), pltpu.VMEM((down_rows, width), BF),
            pltpu.VMEM((4, out_rows, width), BF), pltpu.VMEM((2, out_rows, width), BF), pltpu.VMEM((out_rows, width), BF),
            pltpu.VMEM((RING + 2,) + gain_shape, F32), pltpu.VMEM((2,) + gain_shape, F32),
            DMA((21,)),
            DMA((2, 4, SUB)), DMA((2, 4, SUB)), DMA((NZ,)), DMA((NZ,)), DMA((2, 4, SUB)), DMA((2, 4, SUB)), DMA((NZ,)), DMA((NZ,)),
            DMA((2, RING)), DMA((2, RING)), DMA((RING,)), DMA((RING,)), DMA((RING,)), DMA((RING,)),
            DMA((2, RING)), DMA((2, RING)), DMA((RING,)), DMA((RING,)), DMA((RING,)), DMA((RING,)),
            DMA((2, 4)), DMA((2, 4)), DMA((RING + 2,)), DMA((RING + 2,)),
        ],
        compiler_params=params(collective_id, 60),
    )(d_branch, gu, down, hidden, w_in, w_out, queries, keys, values, attended, inv_total, cos_tab, sine_tab, normed_pre, gain_parts)


def attend(queries, keys, values, positions):
    raw = contract_cols(queries, keys)
    capped = CAP * jnp.tanh(raw / CAP)
    allowed = positions[None, :] <= positions[:, None]
    weights = jnp.where(allowed, jnp.exp(capped), 0.0)
    inv_total = 1.0 / jnp.sum(weights, axis=-1, keepdims=True)
    attended = fold_rows(weights.astype(BF), values) * inv_total
    return attended, inv_total


def on_ring(
    tokens, w_query, w_key, w_value, w_out, w_gate, w_up, w_down,
    pre_gain, post_gain, pre_ffn_gain, post_ffn_gain, out_grad,
):
    ids = iter(range(32))
    n_shards = 4 * RING
    length = RING * tokens.shape[1]
    shard_gain = pre_gain.shape[0]
    gains = jnp.stack([pre_gain, post_gain, pre_ffn_gain, post_ffn_gain]).astype(F32)
    gains = jnp.pad(gains, ((0, 4), (0, 128 - shard_gain)))
    w_in, down_in, out_in, gains_in, sequence = weights_in(
        w_gate, w_up, w_query, w_key, w_value, w_down, w_out, gains, tokens[0], next(ids)
    )
    w_in = w_in.reshape(-1, WIDE)
    w_qkv = w_in[:, 2 * UNITS :]
    w_dn = down_in.reshape(UNITS, D)
    w_ot = out_in.reshape(HD, D)
    factors = 1.0 + jnp.transpose(gains_in[:, :4, :shard_gain], (1, 0, 2)).reshape(4, D)
    pre_factor, post_factor, pre_ffn_factor, post_ffn_factor = (factors[i] for i in range(4))
    positions = jnp.arange(length, dtype=jnp.int32)
    cos_tab, sine_tab = rope_tables(positions, HD)
    q_scale = HD ** (-0.5)

    resid_in = tokens[0].astype(F32)
    inv_pre, normed_pre = rms_parts(resid_in)
    hidden = (rms_parts(sequence.astype(F32))[1] * pre_factor).astype(BF)
    projected = fold_rows(hidden, w_qkv)
    queries = (rotate(projected[:, :HD], cos_tab, sine_tab) * q_scale).astype(BF)
    keys = rotate(projected[:, HD : 2 * HD], cos_tab, sine_tab).astype(BF)
    values = projected[:, 2 * HD :].astype(BF)
    attended, inv_total = attend(queries, keys, values, positions)
    attended_b = attended.astype(BF)
    branch = ring_scatter(fold_rows(attended_b, w_ot), next(ids), True)
    inv_post, normed_post = rms_parts(branch)
    middle = resid_in + normed_post * post_factor
    inv_mid, normed_mid = rms_parts(middle)
    hidden_ffn = (normed_mid * pre_ffn_factor).astype(BF)
    output, d_hidden_ffn, post_ffn_part, down_part, gu_part = feed_forward(
        hidden_ffn, middle, post_ffn_factor[None], out_grad[0], w_in, w_dn, next(ids)
    )
    post_ffn_part = post_ffn_part[0]
    out_cot = out_grad[0].astype(F32)
    pre_ffn_part = jnp.sum(d_hidden_ffn * normed_mid, axis=0)
    d_middle = out_cot + norm_back(d_hidden_ffn * pre_ffn_factor, normed_mid, inv_mid)
    post_part = jnp.sum(d_middle * normed_post, axis=0)
    d_branch = norm_back(d_middle * post_factor, normed_post, inv_post).astype(BF)
    gain_parts = jnp.stack([jnp.zeros_like(post_part), post_part, pre_ffn_part, post_ffn_part])
    d_hidden, gain_g, gu_g, qkv_g, down_g, out_g = backward(
        d_branch, gu_part, down_part, hidden, w_in, w_ot, queries, keys, values, attended, inv_total,
        cos_tab, sine_tab, normed_pre, jnp.pad(gain_parts, ((0, 4), (0, 0))), next(ids),
    )
    token_grad = d_middle + norm_back(d_hidden * pre_factor, normed_pre, inv_pre)

    def spread(columns):
        return jnp.transpose(columns, (1, 0, 2)).reshape(shard_gain, -1).astype(F32)

    gate_g, up_g, query_g = spread(gu_g[..., :UNITS]), spread(gu_g[..., UNITS:]), spread(qkv_g[..., :HD])
    heads = qkv_g[..., HD:].astype(F32).reshape(KVH, H // KVH, shard_gain, 2 * HD).sum(1)
    key_g, value_g = (
        jnp.transpose(part, (1, 0, 2)).reshape(shard_gain, -1) for part in (heads[..., :HD], heads[..., HD:])
    )
    down_g, out_g = down_g.astype(F32), out_g.astype(F32)
    mine = lax.axis_index("ctx") * 4 + lax.axis_index("fsdp")
    gain_g = lax.dynamic_slice(gain_g, (0, mine * shard_gain), (4, shard_gain))
    return (
        output[None], token_grad.astype(BF)[None],
        query_g, key_g, value_g, out_g, gate_g, up_g, down_g,
        gain_g[0], gain_g[1], gain_g[2], gain_g[3],
    )


ROW_FOLD = 4


def head_tables(positions, width):
    half_width = width // 2
    inv_freqs = ROPE_BASE ** (-jnp.arange(half_width, dtype=jnp.float32) * 2.0 / width)
    angles = positions.astype(jnp.float32)[:, None] * inv_freqs[None, :]
    return (jnp.cos(angles)[:, None, :], jnp.sin(angles)[:, None, :])


def rotate_heads(heads_in, cos_tab, sine_tab):
    half_width = heads_in.shape[-1] // 2
    front_half = heads_in[..., :half_width]
    back_half = heads_in[..., half_width:]
    return jnp.concatenate(
        [front_half * cos_tab - back_half * sine_tab, back_half * cos_tab + front_half * sine_tab],
        axis=-1,
    )


def unrotate_heads(grad_in, cos_tab, sine_tab):
    half_width = grad_in.shape[-1] // 2
    front_half = grad_in[..., :half_width]
    back_half = grad_in[..., half_width:]
    return jnp.concatenate(
        [front_half * cos_tab + back_half * sine_tab, back_half * cos_tab - front_half * sine_tab],
        axis=-1,
    )


def to_groups(flat_heads, tok_rows, q_group):
    shaped = flat_heads.reshape(tok_rows, KVH, q_group, HD)
    return jnp.transpose(shaped, (1, 2, 0, 3)).reshape(KVH, q_group * tok_rows, HD)


def from_groups(grouped, tok_rows, q_group):
    shaped = grouped.reshape(KVH, q_group, tok_rows, HD)
    return jnp.transpose(shaped, (2, 0, 1, 3)).reshape(tok_rows, KVH * q_group * HD)


def grad_rows(left, right, folding, count):
    block = contract_rows(left, right)
    return block.reshape(count, right.shape[1] // folding)


def blockwise(step_fn, carry, piece, width):
    key_count = piece[0].shape[0]
    n_steps = key_count // width
    stacked = tuple((member.reshape(n_steps, width, member.shape[1]) for member in piece))

    def one_step(partial_value, block_item):
        block_index, members = block_item
        return (step_fn(partial_value, members, block_index * width), None)

    carry, unused = lax.scan(one_step, carry, (jnp.arange(n_steps, dtype=jnp.int32), stacked))
    return carry


def block_grads(query_g, query_pos, d_att_g, delta, inv_tot, key_block, value_block, key_first):
    key_count = key_block.shape[0]
    key_grp = key_block.reshape(key_count, KVH, HD)
    value_grp = value_block.reshape(key_count, KVH, HD)
    raw_scores = jnp.einsum("grd,ngd->grn", query_g, key_grp, preferred_element_type=jnp.float32)
    capped = CAP * jnp.tanh(raw_scores / CAP)
    key_pos = key_first + jnp.arange(key_count, dtype=jnp.int32)
    allowed = key_pos[None, None, :] <= query_pos[None, :, None]
    weights = jnp.where(allowed, jnp.exp(capped), 0.0)
    prob_rows = weights * inv_tot[..., None]
    d_probs = jnp.einsum("grd,ngd->grn", d_att_g, value_grp, preferred_element_type=jnp.float32)
    slope = 1.0 - capped / CAP * (capped / CAP)
    d_raw = (prob_rows * (d_probs - delta[..., None]) * slope).astype(jnp.bfloat16)
    d_query = jnp.einsum("grn,ngd->grd", d_raw, key_grp, preferred_element_type=jnp.float32)
    d_key = jnp.einsum("grn,grd->ngd", d_raw, query_g, preferred_element_type=jnp.float32)
    weights_b = weights.astype(jnp.bfloat16)
    d_scaled = d_att_g.astype(jnp.float32) * inv_tot[..., None]
    scaled_high = d_scaled.astype(jnp.bfloat16)
    scaled_rest = (d_scaled - scaled_high.astype(jnp.float32)).astype(jnp.bfloat16)
    d_value = jnp.einsum("grn,grd->ngd", weights_b, scaled_high, preferred_element_type=jnp.float32)
    d_value = d_value + jnp.einsum(
        "grn,grd->ngd", weights_b, scaled_rest, preferred_element_type=jnp.float32
    )
    return (d_query, d_key.reshape(key_count, KVH * HD), d_value.reshape(key_count, KVH * HD))


def on_any_mesh(
    tokens,
    w_query,
    w_key,
    w_value,
    w_out,
    w_gate,
    w_up,
    w_down,
    pre_gain,
    post_gain,
    pre_ffn_gain,
    post_ffn_gain,
    out_grad,
):
    tok_rows = tokens.shape[1]
    q_group = H // KVH
    q_scale = HD ** (-0.5)
    width_q = H * HD
    width_kv = KVH * HD
    width_qkv = width_q + 2 * width_kv
    n_ctx = lax.axis_size("ctx")
    my_block = lax.axis_index("ctx")
    my_start = my_block * tok_rows
    positions = my_start + jnp.arange(tok_rows, dtype=jnp.int32)
    cos_tab, sine_tab = head_tables(positions, HD)
    row_pos = jnp.tile(positions, q_group)
    last_pos = my_start + tok_rows - 1
    resid_in = tokens[0].astype(jnp.float32)
    qkv_shard = jnp.concatenate([w_query, w_key, w_value], axis=1)
    gateup_shard = jnp.concatenate([w_gate, w_up], axis=1)
    shard_rows = qkv_shard.shape[0]
    gains_shard = jnp.stack([pre_gain, post_gain, pre_ffn_gain, post_ffn_gain])
    full_gains, full_qkv, full_out = (
        lax.all_gather(gains_shard, ("ctx", "fsdp"), axis=1, tiled=True),
        lax.all_gather(qkv_shard, ("ctx", "fsdp"), axis=0, tiled=True),
        lax.all_gather(w_out, ("ctx", "fsdp"), axis=0, tiled=True),
    )
    factors = 1.0 + full_gains.astype(jnp.float32)
    pre_factor, post_factor, pre_ffn_factor, post_ffn_factor = (
        factors[0],
        factors[1],
        factors[2],
        factors[3],
    )
    inv_pre, normed_pre = rms_parts(resid_in)
    hidden = (normed_pre * pre_factor).astype(jnp.bfloat16)
    projected = jnp.dot(hidden, full_qkv, preferred_element_type=jnp.float32)
    query_lin = projected[:, :width_q].reshape(tok_rows, H, HD)
    queries = (
        (rotate_heads(query_lin, cos_tab, sine_tab) * q_scale)
        .astype(jnp.bfloat16)
        .reshape(tok_rows, width_q)
    )
    query_grp = to_groups(queries, tok_rows, q_group)
    key_lin = projected[:, width_q : width_q + width_kv].reshape(tok_rows, KVH, HD)
    key_rows = rotate_heads(key_lin, cos_tab, sine_tab).astype(jnp.bfloat16).reshape(tok_rows, width_kv)
    value_rows = projected[:, width_q + width_kv :].astype(jnp.bfloat16)

    def add_block(partial_value, piece, first_row):
        key_block, value_block = piece

        def add_compute_block(state):
            row_total, weighted = state
            key_count = key_block.shape[0]
            key_grp = key_block.reshape(key_count, KVH, HD)
            raw_scores = jnp.einsum(
                "grd,ngd->grn", query_grp, key_grp, preferred_element_type=jnp.float32
            )
            capped = CAP * jnp.tanh(raw_scores / CAP)
            key_pos = first_row + jnp.arange(key_count, dtype=jnp.int32)
            allowed = key_pos[None, None, :] <= row_pos[None, :, None]
            weights = jnp.where(allowed, jnp.exp(capped), 0.0)
            value_grp = value_block.reshape(key_count, KVH, HD)
            weighted = weighted + jnp.einsum(
                "grn,ngd->grd",
                weights.astype(jnp.bfloat16),
                value_grp,
                preferred_element_type=jnp.float32,
            )
            return (row_total + jnp.sum(weights, axis=-1), weighted)

        def add_skip_block(state):
            return state

        return lax.cond(first_row <= last_pos, add_compute_block, add_skip_block, partial_value)

    start_state = (
        jnp.zeros((KVH, q_group * tok_rows), jnp.float32),
        jnp.zeros((KVH, q_group * tok_rows, HD), jnp.float32),
    )
    row_total, weighted = blockwise(
        add_block,
        start_state,
        (
            lax.all_gather(key_rows, "ctx", axis=0, tiled=True),
            lax.all_gather(value_rows, "ctx", axis=0, tiled=True),
        ),
        512,
    )
    inv_total = 1.0 / row_total
    attended_grp = weighted * inv_total[..., None]
    attended_b = from_groups(attended_grp, tok_rows, q_group).astype(jnp.bfloat16)
    branch = jnp.dot(attended_b, full_out, preferred_element_type=jnp.float32)
    inv_post, normed_post = rms_parts(branch)
    middle = resid_in + normed_post * post_factor
    inv_mid, normed_mid = rms_parts(middle)
    hidden_ffn = (normed_mid * pre_ffn_factor).astype(jnp.bfloat16)
    gate_up = fold_rows(
        hidden_ffn, lax.all_gather(gateup_shard, ("ctx", "fsdp"), axis=0, tiled=True)
    )
    gate_lin = gate_up[:, :FF]
    up_lin = gate_up[:, FF:]
    active = gated(gate_lin, up_lin).astype(jnp.bfloat16)
    ffn_branch = fold_rows(active, lax.all_gather(w_down, ("ctx", "fsdp"), axis=0, tiled=True))
    inv_ffn, normed_ffn = rms_parts(ffn_branch)
    output = (middle + normed_ffn * post_ffn_factor).astype(jnp.bfloat16)
    out_cot = out_grad[0].astype(jnp.float32)
    post_ffn_part = jnp.sum(out_cot * normed_ffn, axis=0)
    d_ffn_b = norm_back(out_cot * post_ffn_factor, normed_ffn, inv_ffn).astype(jnp.bfloat16)
    down_total = lax.psum_scatter(
        grad_rows(active, d_ffn_b, 1, lax.axis_size(("ctx", "fsdp")) * w_down.shape[0]),
        ("ctx", "fsdp"),
        scatter_dimension=0,
        tiled=True,
    )
    d_active = contract_cols(d_ffn_b, lax.all_gather(w_down, ("ctx", "fsdp"), axis=0, tiled=True))
    unused_value, gate_pull = jax.vjp(gated, gate_lin, up_lin)
    d_gate, d_up = gate_pull(d_active)
    d_gateup_b = jnp.concatenate([d_gate.astype(jnp.bfloat16), d_up.astype(jnp.bfloat16)], axis=1)
    gateup_folded = lax.psum_scatter(
        grad_rows(
            hidden_ffn,
            d_gateup_b,
            ROW_FOLD,
            lax.axis_size(("ctx", "fsdp")) * (ROW_FOLD * shard_rows),
        ),
        ("ctx", "fsdp"),
        scatter_dimension=0,
        tiled=True,
    )
    gateup_total = gateup_folded.reshape(shard_rows, 2 * FF)
    d_hidden_ffn = contract_cols(
        d_gateup_b, lax.all_gather(gateup_shard, ("ctx", "fsdp"), axis=0, tiled=True)
    )
    pre_ffn_part = jnp.sum(d_hidden_ffn * normed_mid, axis=0)
    d_middle = out_cot + norm_back(d_hidden_ffn * pre_ffn_factor, normed_mid, inv_mid)
    back_qkv, back_out = (
        lax.all_gather(qkv_shard, ("ctx", "fsdp"), axis=0, tiled=True),
        lax.all_gather(w_out, ("ctx", "fsdp"), axis=0, tiled=True),
    )
    post_gain_part = jnp.sum(d_middle * normed_post, axis=0)
    d_branch_b = norm_back(d_middle * post_factor, normed_post, inv_post).astype(jnp.bfloat16)
    w_out_part = contract_rows(attended_b, d_branch_b)
    d_attended = contract_cols(d_branch_b, back_out).astype(jnp.bfloat16)
    d_att_grp = to_groups(d_attended, tok_rows, q_group)
    row_delta = jnp.sum(d_att_grp.astype(jnp.float32) * attended_grp, axis=-1)
    zero_rows = jnp.zeros((tok_rows, width_kv), jnp.float32)
    zero_query = jnp.zeros((KVH, q_group * tok_rows, HD), jnp.float32)
    block_ids = jnp.arange(n_ctx, dtype=jnp.int32)
    all_keys, all_values = (
        lax.all_gather(key_rows, "ctx", axis=0, tiled=True),
        lax.all_gather(value_rows, "ctx", axis=0, tiled=True),
    )

    def returned_step(acc_query, block_item):
        block_index, key_block, value_block = block_item
        first_row = block_index * tok_rows

        def returned_compute_block(acc_in):
            d_query, d_key, d_value = block_grads(
                query_grp,
                row_pos,
                d_att_grp,
                row_delta,
                inv_total,
                key_block,
                value_block,
                first_row,
            )
            return (acc_in + d_query, (d_key, d_value))

        def returned_skip_block(acc_in):
            return (acc_in, (zero_rows, zero_rows))

        return lax.cond(
            first_row <= last_pos, returned_compute_block, returned_skip_block, acc_query
        )

    key_blocks = all_keys.reshape(n_ctx, tok_rows, width_kv)
    value_blocks = all_values.reshape(n_ctx, tok_rows, width_kv)
    d_query_grp, key_terms = lax.scan(
        returned_step, zero_query, (block_ids, key_blocks, value_blocks)
    )
    key_term_rows = key_terms[0].reshape(n_ctx * tok_rows, width_kv)
    value_term_rows = key_terms[1].reshape(n_ctx * tok_rows, width_kv)
    d_keys, d_values = (
        lax.psum_scatter(
            key_term_rows.astype(jnp.bfloat16), "ctx", scatter_dimension=0, tiled=True
        ).astype(jnp.float32),
        lax.psum_scatter(
            value_term_rows.astype(jnp.bfloat16), "ctx", scatter_dimension=0, tiled=True
        ).astype(jnp.float32),
    )
    d_query_flat = from_groups(d_query_grp, tok_rows, q_group).reshape(tok_rows, H, HD) * q_scale
    dq_lin = (
        unrotate_heads(d_query_flat, cos_tab, sine_tab).astype(jnp.bfloat16).reshape(tok_rows, width_q)
    )
    dk_lin = (
        unrotate_heads(d_keys.reshape(tok_rows, KVH, HD), cos_tab, sine_tab)
        .astype(jnp.bfloat16)
        .reshape(tok_rows, width_kv)
    )
    dv_lin = d_values.astype(jnp.bfloat16)
    dqkv_b = jnp.concatenate([dq_lin, dk_lin, dv_lin], axis=1)
    d_hidden = contract_cols(dqkv_b, back_qkv)
    qkv_part = contract_rows(hidden, dqkv_b).reshape(ROW_FOLD * D, width_qkv // ROW_FOLD)
    pre_gain_part = jnp.sum(d_hidden * normed_pre, axis=0)
    token_grad = d_middle + norm_back(d_hidden * pre_factor, normed_pre, inv_pre)
    gain_parts = jnp.stack([pre_gain_part, post_gain_part, pre_ffn_part, post_ffn_part])
    qkv_folded, out_total, gain_totals = (
        lax.psum_scatter(qkv_part, ("ctx", "fsdp"), scatter_dimension=0, tiled=True),
        lax.psum_scatter(w_out_part, ("ctx", "fsdp"), scatter_dimension=0, tiled=True),
        lax.psum_scatter(gain_parts, ("ctx", "fsdp"), scatter_dimension=1, tiled=True),
    )
    qkv_total = qkv_folded.reshape(shard_rows, width_qkv)
    return (
        output[None],
        token_grad.astype(jnp.bfloat16)[None],
        qkv_total[:, :width_q],
        qkv_total[:, width_q : width_q + width_kv],
        qkv_total[:, width_q + width_kv :],
        out_total,
        gateup_total[:, :FF],
        gateup_total[:, FF:],
        down_total,
        gain_totals[0],
        gain_totals[1],
        gain_totals[2],
        gain_totals[3],
    )


def solution(mesh):
    ring = mesh.shape["ctx"] == RING and mesh.shape["fsdp"] == 4
    tokens, rows, gains = P("fsdp", "ctx", None), P(("ctx", "fsdp"), None), P(("ctx", "fsdp"))
    return jax.shard_map(
        on_ring if ring else on_any_mesh,
        mesh=mesh,
        in_specs=(tokens,) + (rows,) * 7 + (gains,) * 4 + (tokens,),
        out_specs=(tokens, tokens) + (rows,) * 7 + (gains,) * 4,
        check_vma=False,
    )
```

```python
import functools

import jax
import jax.numpy as jnp
from jax import lax
from jax.experimental import pallas as pl
from jax.experimental.pallas import tpu as pltpu
from jax.sharding import PartitionSpec as P

D = 2304
H = 8
KVH = 4
HD = 256
CAP = 50
FF = 9216

EPSILON = 1e-06
ROPE_BASE = 10000.0

MESH = pl.DeviceIdType.MESH
HBM = pl.BlockSpec(memory_space=pl.ANY)
VMEM = pl.BlockSpec(memory_space=pltpu.VMEM)
DMA = pltpu.SemaphoreType.DMA
BF = jnp.bfloat16
F32 = jnp.float32


def rope_tables(positions, width):
    half_width = width // 2
    inv_freqs = ROPE_BASE ** (-jnp.arange(half_width, dtype=F32) * 2.0 / width)
    angles = positions.astype(F32)[:, None] * inv_freqs[None, :]
    return (jnp.cos(angles), jnp.sin(angles))


def rotate(rows, cos_tab, sine_tab):
    half_width = rows.shape[-1] // 2
    front, back = rows[..., :half_width], rows[..., half_width:]
    return jnp.concatenate(
        [front * cos_tab - back * sine_tab, back * cos_tab + front * sine_tab], axis=-1
    )


def unrotate(rows, cos_tab, sine_tab):
    half_width = rows.shape[-1] // 2
    front, back = rows[..., :half_width], rows[..., half_width:]
    return jnp.concatenate(
        [front * cos_tab + back * sine_tab, back * cos_tab - front * sine_tab], axis=-1
    )


def rms_parts(values_in):
    inverse = lax.rsqrt(jnp.mean(values_in * values_in, axis=-1, keepdims=True) + EPSILON)
    return (inverse, values_in * inverse)


def norm_back(grad_normed, normed, inverse):
    return inverse * (grad_normed - normed * jnp.mean(grad_normed * normed, axis=-1, keepdims=True))


def contract_rows(left, right):
    return lax.dot_general(left, right, (((0,), (0,)), ((), ())), preferred_element_type=F32)


def contract_cols(left, right):
    return lax.dot_general(left, right, (((1,), (1,)), ((), ())), preferred_element_type=F32)


def fold_rows(left, right):
    return jnp.dot(left, right, preferred_element_type=F32)


def gated(gate_in, up_in):
    return jax.nn.gelu(gate_in, approximate=True) * up_in


NZ = 4
RING = 2 * NZ


def my_place():
    c, f = lax.axis_index("ctx"), lax.axis_index("fsdp")
    return c // 2, c % 2, f // 2, f % 2


def ring_index(y, z):
    return z + y * (RING - 1 - 2 * z)


def ring_yz(q):
    y = q // NZ
    return y, q + y * (RING - 1 - 2 * q)


def device(z, core, y, x):
    return (2 * z + core, 2 * y + x)


def ring_device(q, core, x):
    y, z = ring_yz(q)
    return device(z, core, y, x)


def remote(src, dst, send_sem, recv_sem, where):
    return pltpu.make_async_remote_copy(
        src_ref=src,
        dst_ref=dst,
        send_sem=send_sem,
        recv_sem=recv_sem,
        device_id=where,
        device_id_type=MESH,
    )


def greet(places):
    barrier = pltpu.get_barrier_semaphore()
    for place in places:
        pl.semaphore_signal(barrier, inc=1, device_id=place, device_id_type=MESH)
    pl.semaphore_wait(barrier, len(places))


def params(collective_id, vmem_mib=56):
    return pltpu.CompilerParams(
        collective_id=collective_id,
        has_side_effects=True,
        vmem_limit_bytes=vmem_mib * 2**20,
    )


SUB = 4


def ring_parts(direction, step, half_step):
    if step != half_step:
        return list(range(SUB))
    half = SUB // 2
    return list(range(half)) if direction == 0 else list(range(half, SUB))


TOK = 128
UNITS = FF // RING
TILE = 128
GELU_K = 0.7978845608028654
GELU_A = 0.044715


class SlotGather:
    def __init__(self, buf, ss, rs):
        z, core, y, x = my_place()
        p = ring_index(y, z)
        self.buf, self.ss, self.rs = buf, ss, rs
        self.near = (ring_device((p + 1) % RING, core, x), ring_device((p + RING - 1) % RING, core, x))
        self.pending = []

    def copy(self, direction, step, k):
        piece = TOK // SUB
        src = 0 if step == 0 else 2 * step - 1 + direction
        dst = 7 if step == 3 else 2 * step + 1 + direction
        return remote(
            self.buf.at[pl.ds(src * TOK + k * piece, piece)],
            self.buf.at[pl.ds(dst * TOK + k * piece, piece)],
            self.ss.at[direction, step, k],
            self.rs.at[direction, step, k],
            self.near[direction],
        )

    def step(self, step):
        for k in range(SUB):
            for direction in (0, 1):
                if step > 0:
                    self.copy(direction, step - 1, k).wait_recv()
                if k in ring_parts(direction, step, 3):
                    c = self.copy(direction, step, k)
                    c.start()
                    self.pending.append(c)

    def finish(self):
        for direction in (0, 1):
            for k in ring_parts(direction, 3, 3):
                self.copy(direction, 3, k).wait_recv()

    def drain(self):
        for c in self.pending:
            c.wait_send()


class SlotScatter:
    def __init__(self, part, buf, ss, rs):
        z, core, y, x = my_place()
        p = ring_index(y, z)
        self.part, self.buf, self.ss, self.rs = part, buf, ss, rs
        self.near = (ring_device((p + 1) % RING, core, x), ring_device((p + RING - 1) % RING, core, x))
        self.pending = []

    def copy(self, direction, step, k, src):
        rows = pl.ds(k * (TOK // SUB), TOK // SUB)
        return remote(
            src,
            self.buf.at[direction, step, rows],
            self.ss.at[direction, step, k],
            self.rs.at[direction, step, k],
            self.near[direction],
        )

    def step(self, step):
        piece = TOK // SUB
        for k in range(SUB):
            rows = pl.ds(k * piece, piece)
            for direction in (0, 1):
                if k not in ring_parts(direction, step, 0):
                    continue
                slot = 7 if step == 0 else 2 * (4 - step) - direction
                mine = pl.ds(slot * TOK + k * piece, piece)
                src = self.part.at[mine]
                if step > 0 and k in ring_parts(direction, step - 1, 0):
                    src = self.buf.at[direction, step - 1, rows]
                    self.copy(direction, step - 1, k, src).wait_recv()
                    src[...] = (src[...].astype(F32) + self.part[mine].astype(F32)).astype(BF)
                c = self.copy(direction, step, k, src)
                c.start()
                self.pending.append(c)

    def finish(self, total):
        for k in range(SUB):
            rows = pl.ds(k * (TOK // SUB), TOK // SUB)
            for direction in (0, 1):
                src = self.buf.at[direction, 3, rows]
                self.copy(direction, 3, k, src).wait_recv()
                total[rows] = total[rows] + src[...].astype(F32)

    def drain(self):
        for c in self.pending:
            c.wait_send()


def tiles(count, width, body):
    def step(i, carry):
        body(pl.ds(pl.multiple_of(i * width, width), width))
        return carry

    lax.fori_loop(0, count, step, 0)


def gelu_parts(v):
    bent = jnp.tanh(GELU_K * (v + GELU_A * (v * v * v)))
    value = 0.5 * v * (1.0 + bent)
    slope = 0.5 * (1.0 + bent) + 0.5 * v * (1.0 - bent * bent) * (GELU_K * (1.0 + 3.0 * GELU_A * (v * v)))
    return value, slope


PAIRS = ((128, 256), (384, 256), (640, 256))
LAST = (896, 128)
OWN = (0, 128)


def feed_forward_kernel(hid, middle, factor, cot, w_hbm, wd_hbm,
                        out_o, d_hid_o, gain_o, wd_grad, gu_grad,
                        wgu, wd, ha, gu, act, part, buf, df, dgu, total, stage,
                        w_sem, ags, agr, rss, rsr, out_sem):
    gather = [SlotGather(b, ags.at[i], agr.at[i]) for i, b in enumerate((ha, df))]
    scatter = [SlotScatter(part, buf, rss.at[i], rsr.at[i]) for i in range(2)]
    greet(gather[0].near)
    loads = [
        pltpu.make_async_copy(w_hbm, wgu, w_sem.at[0]),
        pltpu.make_async_copy(wd_hbm, wd, w_sem.at[1]),
    ]
    ha[0:TOK] = hid[...]
    gather[0].step(0)
    for c in loads:
        c.start()
    loads[0].wait()

    def gate_up(first, count):
        rows = pl.ds(first, count)

        def column(cols):
            gu[rows, cols] = fold_rows(ha[rows], wgu[:, cols])

        tiles(3, 768, column)

        def finish(i, carry):
            r = pl.ds(pl.multiple_of(first + i * 32, 32), 32)
            act[r] = (gelu_parts(gu[r, 0:UNITS])[0] * gu[r, UNITS : 2 * UNITS]).astype(BF)
            return carry

        lax.fori_loop(0, count // 32, finish, 0)

    def down_part(first, count, dst):
        def column(cols):
            value = fold_rows(act[pl.ds(first, count)], wd[:, cols])
            dst[pl.ds(first, count), cols] = value.astype(dst.dtype)

        tiles(3, 768, column)

    def active_back(first, count):
        rows = pl.ds(first, count)
        for n in range(3):
            cols, up_cols = pl.ds(n * 384, 384), pl.ds(UNITS + n * 384, 384)
            d_active = contract_cols(df[rows], wd[cols])
            value, slope = gelu_parts(gu[rows, cols])
            dgu[rows, cols] = (d_active * gu[rows, up_cols] * slope).astype(BF)
            dgu[rows, up_cols] = (d_active * value).astype(BF)

    def hidden_part(first, count, dst):
        def column(cols):
            value = contract_cols(dgu[pl.ds(first, count)], wgu[cols])
            dst[pl.ds(first, count), cols] = value.astype(dst.dtype)

        tiles(9, 256, column)

    n_down = UNITS // TILE

    def grad_out(i):
        slot = i % 2
        if i < n_down:
            return pltpu.make_async_copy(stage.at[slot], wd_grad.at[pl.ds(i * TILE, TILE)], out_sem.at[slot])
        return pltpu.make_async_copy(stage.at[slot], gu_grad.at[pl.ds((i - n_down) * TILE, TILE)], out_sem.at[slot])

    def grad_tiles(first, last):
        for i in range(first, last):
            if i >= 2:
                grad_out(i - 2).wait()
            if i < n_down:
                value = contract_rows(act[:, pl.ds(i * TILE, TILE)], df[...])
            else:
                value = contract_rows(ha[:, pl.ds((i - n_down) * TILE, TILE)], dgu[...])
            stage[i % 2] = value.astype(BF)
            grad_out(i).start()

    gate_up(*OWN)
    for step, pair in enumerate(PAIRS):
        gather[0].step(step + 1)
        if step == 0:
            loads[1].wait()
        gate_up(*pair)
    gather[0].finish()
    gate_up(*LAST)
    down_part(*LAST, part)
    scatter[0].step(0)
    for step, pair in enumerate(PAIRS[::-1]):
        down_part(*pair, part)
        scatter[0].step(step + 1)
    down_part(*OWN, total)
    scatter[0].finish(total)
    gather[0].drain()
    scatter[0].drain()

    branch = total[...]
    inverse, normed = rms_parts(branch)
    out_cot = cot[...].astype(F32)
    scale = factor[...]
    df[0:TOK] = norm_back(out_cot * scale, normed, inverse).astype(BF)
    gather[1].step(0)
    out_o[...] = (middle[...] + normed * scale).astype(BF)
    gain_o[...] = jnp.sum(out_cot * normed, axis=0, keepdims=True)
    active_back(*OWN)
    for step, pair in enumerate(PAIRS):
        gather[1].step(step + 1)
        active_back(*pair)
    gather[1].finish()
    active_back(*LAST)
    hidden_part(*LAST, part)
    scatter[1].step(0)
    done = 0
    for step, pair in enumerate(PAIRS[::-1]):
        hidden_part(*pair, part)
        scatter[1].step(step + 1)
        grad_tiles(done, done + 6)
        done += 6
    hidden_part(*OWN, d_hid_o)
    scatter[1].finish(d_hid_o)
    n_tiles = n_down + ha.shape[1] // TILE
    grad_tiles(done, n_tiles)
    for i in (n_tiles - 2, n_tiles - 1):
        grad_out(i).wait()
    gather[1].drain()
    scatter[1].drain()


def feed_forward(hidden_ffn, middle, factor, out_grad, w_in, w_down, collective_id):
    rows, width = hidden_ffn.shape
    total = RING * rows

    def full(*shape, dtype=F32):
        return jax.ShapeDtypeStruct(shape, dtype)

    return pl.pallas_call(
        feed_forward_kernel,
        out_shape=[
            full(rows, width, dtype=BF), full(rows, width), full(1, width),
            full(UNITS, width, dtype=BF), full(width, 2 * UNITS, dtype=BF),
        ],
        in_specs=[VMEM] * 4 + [HBM] * 2,
        out_specs=[VMEM] * 3 + [HBM] * 2,
        scratch_shapes=[
            pltpu.VMEM((width, 2 * UNITS), BF), pltpu.VMEM((UNITS, width), BF),
            pltpu.VMEM((total, width), BF), pltpu.VMEM((total, 2 * UNITS), F32), pltpu.VMEM((total, UNITS), BF),
            pltpu.VMEM((total, width), BF), pltpu.VMEM((2, 4, rows, width), BF),
            pltpu.VMEM((total, width), BF), pltpu.VMEM((total, 2 * UNITS), BF),
            pltpu.VMEM((rows, width), F32), pltpu.VMEM((2, TILE, width), BF),
            DMA((2,)),
            DMA((2, 2, 4, SUB)), DMA((2, 2, 4, SUB)), DMA((2, 2, 4, SUB)), DMA((2, 2, 4, SUB)),
            DMA((2,)),
        ],
        compiler_params=params(collective_id, 60),
    )(hidden_ffn, middle, factor, out_grad, w_in, w_down)


WIDTHS = (UNITS, UNITS, HD, HD, HD)


def member_place(t, core, x):
    return device(t // 2, core, t % 2, x)


def slot_of(q, p):
    d = (q - p + RING) % RING
    return jnp.where(d == 0, 0, jnp.where(d < 4, 2 * d, jnp.where(d == 4, 7, 15 - 2 * d)))


def partner(t, j):
    out = 0
    for bit in (1, 2, 4):
        on = (t // bit) % 2
        out = out + bit * (1 - on if j & bit else on)
    return out


def column_start(which, t):
    if which < 2:
        return pl.multiple_of(t * UNITS, 128)
    return pl.multiple_of((t if which == 2 else t // 2) * HD, 128)


def forward_kernel(gate, up, query, key, value, down, out, block, gain_in, cos, sine,
                   w_gu, d_ref, hidden_o, wq, wo, gain_o, q_o, k_o, v_o, att_o, inv_o, branch_o,
                   ring, seq, seq_part, part, buf, wq_in, own, relay, ga, gsum,
                   load, ags, agr, pls, plr, rss, rsr, sws, swr, s1, r1, s2, r2, s3, r3,
                   q1, t1, q2, t2, q3, t3, s4, r4, s5, r5, sg, rg):
    z, core, y, x = my_place()
    t, p = 2 * z + y, ring_index(y, z)
    sibling, across = device(z, 1 - core, y, x), device(z, core, y, 1 - x)
    member = [partner(t, j) for j in range(RING)]
    members = [member_place(tq, core, x) for tq in member]
    plane = []
    for dc in (0, 1):
        for dy in (0, 1):
            for dx in (0, 1):
                if (dc, dx) != (0, 0):
                    plane.append(device(z, (core + dc) % 2, (y + dy) % 2, (x + dx) % 2))
    greet(members[1:] + plane)
    sources = (gate, up, query, key, value)
    pending = []

    def go(*copies):
        for c in copies:
            c.start()
            pending.append(c)

    def owner(tq, corq, xq):
        return (2 * (tq // 2) + corq) * 4 + 2 * (tq % 2) + xq

    me = owner(t, core, x)

    def columns_of(a, tq):
        return sources[a].at[:, pl.ds(column_start(a, tq), WIDTHS[a])]

    def gain_a(j):
        return remote(gain_in, ga.at[j], sg.at[j], rg.at[j], members[j])

    def gain_b(i):
        return remote(gsum.at[i], ga.at[RING + i], sg.at[RING + i], rg.at[RING + i], (across, sibling)[i])

    def q_first(j, a, wait=False):
        tq = member[j]
        dst = wq_in.at[owner(tq, core, x) if wait else me, :, pl.ds((a - 2) * HD, HD)]
        return remote(columns_of(a, tq), dst, q1.at[j, a - 2], t1.at[j, a - 2], members[j])

    def q_second(j, wait=False):
        i = owner(member[j], core, 1 - x if wait else x)
        return remote(wq_in.at[i], wq_in.at[i], q2.at[j], t2.at[j], across)

    def q_third(j, flip, wait=False):
        i = owner(member[j], 1 - core if wait else core, 1 - x if flip else x)
        return remote(wq_in.at[i], wq_in.at[i], q3.at[j, flip], t3.at[j, flip], sibling)

    def first(j, a, wait=False):
        tq = member[j]
        dst = w_gu.at[owner(tq, core, x) if wait else me, :, pl.ds(a * UNITS, UNITS)]
        return remote(columns_of(a, tq), dst, s1.at[j, a], r1.at[j, a], members[j])

    def second(j, wait=False):
        i = owner(member[j], core, 1 - x if wait else x)
        return remote(own if j == 0 else w_gu.at[i], w_gu.at[i], s2.at[j], r2.at[j], across)

    def third(j, flip, wait=False):
        i = owner(member[j], 1 - core if wait else core, 1 - x if flip else x)
        return remote(own if (j, flip) == (0, 0) else w_gu.at[i], w_gu.at[i], s3.at[j, flip], r3.at[j, flip], sibling)

    def start_round(j):
        go(first(j, 0), first(j, 1))

    def end_round(j):
        first(j, 0, True).wait_recv()
        first(j, 1, True).wait_recv()
        go(second(j), third(j, 0))

    def end_across(j):
        second(j, True).wait_recv()
        go(third(j, 1))

    gather = SlotGather(ring, ags, agr)

    def block_of(slot):
        if slot == 0:
            return p
        if slot == 7:
            return (p + 4) % RING
        s = (slot + 1) // 2
        return (p + (RING - s if slot % 2 else s)) % RING

    def place(slot, act):
        yq, zq = ring_yz(block_of(slot))
        src, dst = ring.at[pl.ds(slot * TOK, TOK)], seq.at[2 * zq + core]

        @pl.when(yq == core)
        def _():
            c = pltpu.make_async_copy(src, dst, load.at[6 + slot])
            c.start() if act == 0 else c.wait()

        @pl.when(yq != core)
        def _():
            c = remote(src, dst, pls.at[zq], plr.at[zq], sibling)
            c.start() if act == 0 else c.wait_send()

    pair = ((down, d_ref), (out, wo))
    mine = 2 * y + x

    def rows_out(xq, a, act):
        src, dst = pair[a][0], pair[a][1].at[mine]
        to_self = (x == core) & (y == core) & (xq == x)

        @pl.when(to_self)
        def _():
            if a == 0:
                c = pltpu.make_async_copy(relay, dst, load.at[5])
            else:
                c = pltpu.make_async_copy(src, dst, load.at[4])
            c.start() if act == 0 else c.wait()

        @pl.when(jnp.logical_not(to_self))
        def _():
            c = remote(src, dst, s4.at[xq, a], r4.at[y, a], device(z, x, core, xq))
            c.start() if act == 0 else c.wait_send()

    def rows_on(yq, a):
        src, dst = pair[a][0], pair[a][1].at[2 * yq + core]
        from_self = (core == y) & (yq == y) & (core == x)

        @pl.when(from_self)
        def _():
            if a == 0:
                pltpu.make_async_copy(relay, dst, load.at[5]).wait()
            else:
                pltpu.make_async_copy(src, dst, load.at[4]).wait()

        @pl.when(jnp.logical_not(from_self))
        def _():
            remote(src, dst, s4.at[0, a], r4.at[yq, a], sibling).wait_recv()

        go(remote(dst, dst, s5.at[yq, a], r5.at[yq, a], sibling))

    locals_ = [pltpu.make_async_copy(columns_of(a, t), wq_in.at[me, :, pl.ds((a - 2) * HD, HD)], load.at[a]) for a in (2, 3)]
    locals_.append(pltpu.make_async_copy(columns_of(4, t), wq_in.at[me, :, pl.ds(2 * HD, HD)], load.at[14]))
    locals_ += [pltpu.make_async_copy(columns_of(a, t), own.at[:, pl.ds(a * UNITS, UNITS)], load.at[a]) for a in (0, 1)]
    relay_load = pltpu.make_async_copy(down, relay, load.at[15])
    for c in locals_:
        c.start()
    relay_load.start()
    ring[0:TOK] = block[...]
    gather.step(0)
    go(*[gain_a(j) for j in range(1, RING)])
    for j in range(1, RING):
        go(*[q_first(j, a) for a in (2, 3, 4)])
    for c in locals_:
        c.wait()
    go(q_second(0), q_third(0, 0))
    relay_load.wait()
    for a in (1, 0):
        for xq in (0, 1):
            rows_out(xq, a, 0)
    keep_own = pltpu.make_async_copy(own, w_gu.at[me], load.at[16])
    keep_own.start()
    go(second(0), third(0, 0))
    place(0, 0)
    total = gain_in[...]
    for j in range(1, RING):
        gain_a(j).wait_recv()
        total = total + ga[j]
    gsum[0] = total
    go(gain_b(0))
    gather.step(1)
    place(1, 0)
    place(2, 0)
    gain_b(0).wait_recv()
    gsum[1] = gsum[0] + ga[RING]
    go(gain_b(1))
    for j in range(1, RING):
        for a in (2, 3, 4):
            q_first(j, a, True).wait_recv()
        go(q_second(j), q_third(j, 0))
    for yq in (0, 1):
        rows_on(yq, 1)
    gather.step(2)
    place(3, 0)
    place(4, 0)
    gain_b(1).wait_recv()
    gain_o[...] = gsum[1] + ga[RING + 1]
    for j in range(RING):
        q_second(j, True).wait_recv()
        go(q_third(j, 1))
    gather.step(3)
    place(5, 0)
    place(6, 0)
    start_round(4)
    start_round(5)
    start_round(1)
    for yq in (0, 1):
        rows_on(yq, 0)
    end_across(0)
    for j in range(RING):
        for flip in (0, 1):
            q_third(j, flip, True).wait_recv()

    def join(g, carry):
        pieces = [wq_in[4 * g + i].astype(F32) for i in range(4)]
        wq[pl.ds(pl.multiple_of(288 * g, 16), 288)] = jnp.concatenate(pieces, axis=0).astype(BF)
        return carry

    lax.fori_loop(0, 8, join, 0)
    gather.finish()
    place(7, 0)
    for zq in range(NZ):
        dst = seq.at[2 * zq + 1 - core]
        remote(dst, dst, pls.at[zq], plr.at[zq], sibling).wait_recv()
    for slot in range(RING):
        place(slot, 1)
    end_round(1)
    start_round(2)

    factor = 1.0 + gain_o[0:1]

    def norm(c, carry):
        for half in range(2):
            rows = pl.ds(half * 64, 64)
            seq[c, rows] = (rms_parts(seq[c, rows].astype(F32))[1] * factor).astype(BF)
        return carry

    lax.fori_loop(0, RING, norm, 0)
    keep_hidden = pltpu.make_async_copy(seq, hidden_o, load.at[17])
    keep_hidden.start()
    for i in range(4):
        r = pl.ds(i * 256, 256)
        rows = seq[2 * i : 2 * i + 2].reshape(256, -1)
        tabs = (cos[r], sine[r])
        q_o[r] = (rotate(fold_rows(rows, wq[:, 0:HD]), *tabs) * (HD ** (-0.5))).astype(BF)
        k_o[r] = rotate(fold_rows(rows, wq[:, HD : 2 * HD]), *tabs).astype(BF)
        v_o[r] = fold_rows(rows, wq[:, 2 * HD : 3 * HD]).astype(BF)
    end_round(4)
    start_round(6)
    end_across(1)

    def swap(zq, kept):
        where = pl.ds(pl.multiple_of(slot_of(ring_index(core, zq), p) * TOK, TOK), TOK)
        if kept:
            return pltpu.make_async_copy(seq_part.at[2 * zq + core], part.at[where], load.at[18 + zq])
        return remote(seq_part.at[2 * zq + 1 - core], part.at[where], sws.at[zq], swr.at[zq], sibling)

    def swapped(zq):
        where = pl.ds(pl.multiple_of(slot_of(ring_index(1 - core, zq), p) * TOK, TOK), TOK)
        return remote(seq_part.at[0], part.at[where], sws.at[zq], swr.at[zq], sibling)

    for yq in (0, 1):
        remote(out, wo.at[2 * yq + 1 - core], s5.at[yq, 1], r5.at[yq, 1], sibling).wait_recv()
    for i in range(4):
        r, upto = pl.ds(i * 256, 256), (i + 1) * 256
        bent = jnp.tanh(contract_cols(q_o[r], k_o[0:upto]) / CAP)
        seen = lax.broadcasted_iota(jnp.int32, bent.shape, 1) <= i * 256 + lax.broadcasted_iota(jnp.int32, bent.shape, 0)
        weights = jnp.where(seen, jnp.exp(CAP * bent), 0.0)
        inverse = 1.0 / jnp.sum(weights, axis=-1, keepdims=True)
        attended = fold_rows(weights.astype(BF), v_o[0:upto]) * inverse
        inv_o[r] = inverse
        att_o[r] = attended
        attended_b = attended.astype(BF)

        def columns(cols):
            sums = fold_rows(attended_b, wo[:, :, cols].reshape(HD, 768))
            seq_part[2 * i, :, cols] = sums[0:TOK].astype(BF)
            seq_part[2 * i + 1, :, cols] = sums[TOK:].astype(BF)

        tiles(3, 768, columns)
        swap(i, True).start()
        swap(i, False).start()
        if i == 0:
            end_round(2)
            start_round(3)
        if i == 2:
            end_round(5)
            start_round(7)
            end_across(2)
    for zq in range(NZ):
        swap(zq, True).wait()
        swapped(zq).wait_recv()
    scatter = SlotScatter(part, buf, rss, rsr)
    scatter.step(0)
    end_round(3)
    end_across(4)
    scatter.step(1)
    end_round(6)
    end_across(5)
    end_across(3)
    scatter.step(2)
    end_round(7)
    end_across(6)
    scatter.step(3)
    branch_o[...] = part[0:TOK].astype(F32)
    end_across(7)
    scatter.finish(branch_o)

    for j in range(RING):
        for flip in (0, 1):
            third(j, flip, True).wait_recv()
    for yq in (0, 1):
        remote(down, d_ref.at[2 * yq + 1 - core], s5.at[yq, 0], r5.at[yq, 0], sibling).wait_recv()
    for xq in (0, 1):
        for a in (0, 1):
            to_self = (x == core) & (y == core) & (xq == x)

            @pl.when(jnp.logical_not(to_self))
            def _():
                remote(pair[a][0], pair[a][1].at[mine], s4.at[xq, a], r4.at[y, a], device(z, x, core, xq)).wait_send()
    keep_own.wait()
    keep_hidden.wait()
    for zq in range(NZ):
        swap(zq, False).wait_send()
    gather.drain()
    scatter.drain()
    for c in pending:
        c.wait_send()


def forward(gate, up, query, key, value, down, out, block, gains, cos_tab, sine_tab, collective_id):
    n = 4 * RING
    rows, width = block.shape
    shard, total = gate.shape[0], RING * block.shape[0]

    def full(*shape, dtype=BF):
        return jax.ShapeDtypeStruct(shape, dtype)

    blocks = (RING, rows, width)
    return pl.pallas_call(
        forward_kernel,
        out_shape=[
            full(n, shard, 2 * UNITS), full(4, *down.shape), full(*blocks), full(width, 3 * HD), full(4, *out.shape),
            full(*gains.shape, dtype=F32), full(total, HD), full(total, HD), full(total, HD),
            full(total, HD, dtype=F32), full(total, 1, dtype=F32), full(rows, width, dtype=F32),
        ],
        in_specs=[HBM] * 7 + [VMEM] * 4,
        out_specs=[HBM] * 3 + [VMEM] * 9,
        scratch_shapes=[
            pltpu.VMEM((total, width), BF), pltpu.VMEM(blocks, BF), pltpu.VMEM(blocks, BF), pltpu.VMEM((total, width), BF),
            pltpu.VMEM((2, 4, rows, width), BF), pltpu.VMEM((n, shard, 3 * HD), BF),
            pltpu.VMEM((shard, 2 * UNITS), BF), pltpu.VMEM(down.shape, BF),
            pltpu.VMEM((RING + 2,) + gains.shape, F32), pltpu.VMEM((2,) + gains.shape, F32),
            DMA((22,)),
            DMA((2, 4, SUB)), DMA((2, 4, SUB)), DMA((NZ,)), DMA((NZ,)), DMA((2, 4, SUB)), DMA((2, 4, SUB)), DMA((NZ,)), DMA((NZ,)),
            DMA((RING, 2)), DMA((RING, 2)), DMA((RING,)), DMA((RING,)), DMA((RING, 2)), DMA((RING, 2)),
            DMA((RING, 3)), DMA((RING, 3)), DMA((RING,)), DMA((RING,)), DMA((RING, 2)), DMA((RING, 2)),
            DMA((2, 2)), DMA((2, 2)), DMA((2, 2)), DMA((2, 2)), DMA((RING + 2,)), DMA((RING + 2,)),
        ],
        compiler_params=params(collective_id, 60),
    )(gate, up, query, key, value, down, out, block, gains, cos_tab, sine_tab)


ROUNDS = (4, 5, 6, 7, 2, 3, 1, 0)
AHEAD = 2


def backward_kernel(d_branch, gu_in, down_in, hidden, wq, wo, q_in, k_in, v_in, att, inv, cos, sine, normed, gain_in,
                    d_hid_o, gain_o, c_gu, c_q, down_o, out_o,
                    ring, seq, part, buf, d_att, d_qkv, dk, dv, grad_q, aq, bq,
                    own, a_gu, b_gu, down_own, da, db, og, oa, ob, ga, gsum,
                    load, ags, agr, pls, plr, rss, rsr, sws, swr, s1, r1, s2, r2, s3, r3,
                    q1, t1, q2, t2, q3, t3, sx, rx, sg, rg):
    z, core, y, x = my_place()
    t, p = 2 * z + y, ring_index(y, z)
    sibling, across = device(z, 1 - core, y, x), device(z, core, y, 1 - x)
    diagonal = device(z, 1 - core, 1 - y, x)
    members = [member_place(partner(t, j), core, x) for j in range(RING)]
    order = [partner(t, j) for j in ROUNDS]
    greet(members[1:] + [sibling, across, diagonal])
    pending = []

    def go(*copies):
        for c in copies:
            c.start()
            pending.append(c)

    def owner(tq, corq, xq):
        return (2 * (tq // 2) + corq) * 4 + 2 * (tq % 2) + xq

    side_x = (1 - x, x)

    def gu_a(side, j):
        src = gu_in.at[owner(order[j], 1 - core, side_x[side])]
        return remote(src, a_gu.at[side, j], s1.at[side, j], r1.at[side, j], sibling)

    def gu_own(side, j):
        return pltpu.make_async_copy(gu_in.at[owner(order[j], core, side_x[side])], own.at[j % 2], load.at[j % 2])

    def gu_b(j):
        return remote(a_gu.at[0, j], b_gu.at[j], s2.at[j], r2.at[j], across)

    def gu_c(j, wait=False):
        dst = c_gu.at[order[j] if wait else t]
        if ROUNDS[j] == 0:
            return pltpu.make_async_copy(a_gu.at[1, j], dst, load.at[2])
        return remote(a_gu.at[1, j], dst, s3.at[j], r3.at[j], members[ROUNDS[j]])

    def sum_own(side, j, more=None):
        gu_own(side, j).wait()
        gu_a(side, j).wait_recv()
        total = a_gu[side, j].astype(F32) + own[j % 2].astype(F32)
        if more is not None:
            total = total + more[j].astype(F32)
        a_gu[side, j] = total.astype(BF)

    def pump(first, last):
        for j in range(first, last):
            gu_own(1, j).start()
        for j in range(first, last):
            gu_b(j).wait_recv()
            if j + AHEAD < RING:
                go(gu_b(j + AHEAD))
            sum_own(1, j, b_gu)

    small = ((down_in, down_own, da, db, down_o), (og, None, oa, ob, out_o))

    def small_a(a, xo):
        return remote(small[a][0].at[2 * (1 - core) + xo], small[a][2].at[xo], sx.at[a, xo], rx.at[a, xo], sibling)

    def small_b(a):
        return remote(small[a][2].at[1 - x], small[a][3], sx.at[a, 2], rx.at[a, 2], across)

    def small_c(a, act):
        src, dst = small[a][2].at[x], small[a][4]

        @pl.when(core == y)
        def _():
            c = pltpu.make_async_copy(src, dst, load.at[3 + a])
            c.start() if act == 0 else c.wait()

        @pl.when(core != y)
        def _():
            c = remote(src, dst, sx.at[a, 3], rx.at[a, 3], diagonal)
            c.start() if act == 0 else c.wait()

    def q_a(side, j):
        src = grad_q.at[owner(order[j], 1 - core, side_x[side])]
        return remote(src, aq.at[side, j], q1.at[side, j], t1.at[side, j], sibling)

    def q_b(j):
        return remote(grad_q.at[owner(order[j], core, 1 - x)], bq.at[j], q2.at[j], t2.at[j], across)

    def q_c(j, wait=False):
        src, dst = grad_q.at[owner(order[j], core, x)], c_q.at[order[j] if wait else t]
        if ROUNDS[j] == 0:
            return pltpu.make_async_copy(src, dst, load.at[5])
        return remote(src, dst, q3.at[j], t3.at[j], members[ROUNDS[j]])

    def gain_a():
        return remote(gain_in, ga.at[RING], sg.at[RING], rg.at[RING], sibling)

    def gain_b():
        return remote(gsum.at[0], ga.at[RING + 1], sg.at[RING + 1], rg.at[RING + 1], across)

    def gain_c(j):
        return remote(gsum.at[1], ga.at[j], sg.at[j], rg.at[j], members[j])

    gather = SlotGather(ring, ags, agr)

    def block(slot):
        if slot == 0:
            return p
        if slot == 7:
            return (p + 4) % RING
        s = (slot + 1) // 2
        return (p + (RING - s if slot % 2 else s)) % RING

    def place(slot, act):
        yq, zq = ring_yz(block(slot))
        src, dst = ring.at[pl.ds(slot * TOK, TOK)], seq.at[2 * zq + core]

        @pl.when(yq == core)
        def _():
            c = pltpu.make_async_copy(src, dst, load.at[6 + slot])
            c.start() if act == 0 else c.wait()

        @pl.when(yq != core)
        def _():
            c = remote(src, dst, pls.at[zq], plr.at[zq], sibling)
            c.start() if act == 0 else c.wait_send()

    first = pltpu.make_async_copy(d_branch, ring.at[pl.ds(0, TOK)], load.at[14])
    first.start()
    first.wait()
    gather.step(0)
    place(0, 0)
    for side in (0, 1):
        go(*[gu_a(side, j) for j in range(RING)])
        if side == 0:
            go(small_a(0, 0), small_a(0, 1))
    for j in range(RING):
        if j < 2:
            gu_own(0, j).start()
        sum_own(0, j)
        if j + 2 < RING:
            gu_own(0, j + 2).start()
        if j < AHEAD:
            go(gu_b(j))

    def down_sum(xo):
        c = pltpu.make_async_copy(down_in.at[2 * core + xo], down_own, load.at[16])
        c.start()
        small_a(0, xo).wait_recv()
        c.wait()
        da[xo] = (da[xo].astype(F32) + down_own[...].astype(F32)).astype(BF)

    down_sum(0)
    gather.step(1)
    place(1, 0)
    place(2, 0)
    pump(0, 1)
    down_sum(1)
    pump(1, 2)
    gather.step(2)
    place(3, 0)
    place(4, 0)
    pump(2, 4)
    gather.step(3)
    place(5, 0)
    place(6, 0)
    pump(4, 5)
    gather.finish()
    place(7, 0)
    for j in range(5):
        go(gu_c(j))
    for zq in range(NZ):
        dst = seq.at[2 * zq + 1 - core]
        remote(dst, dst, pls.at[zq], plr.at[zq], sibling).wait_recv()
    for slot in range(RING):
        place(slot, 1)
    gather.drain()
    hidden_load = pltpu.make_async_copy(hidden, ring, load.at[14])
    hidden_load.start()

    for c in range(0, RING, 2):
        rows = pl.ds(c * TOK, 2 * TOK)
        d_att[rows] = contract_cols(seq[c : c + 2].reshape(2 * TOK, -1), wo[...]).astype(BF)

    def out_columns(cols):
        value = contract_rows(att[...].astype(BF), seq[:, :, cols].reshape(RING * TOK, 768))
        for f in range(4):
            og[f, :, cols] = value[64 * f : 64 * (f + 1)].astype(BF)

    tiles(3, 768, out_columns)
    go(small_a(1, 0), small_a(1, 1))
    pump(5, 6)
    go(gu_c(5))
    dk[...] = jnp.zeros_like(dk)
    dv[...] = jnp.zeros_like(dv)
    for i in range(4):
        r, upto = pl.ds(i * 256, 256), (i + 1) * 256
        keys, vals, query = k_in[0:upto], v_in[0:upto], q_in[r]
        bent = jnp.tanh(contract_cols(query, keys) / CAP)
        seen = lax.broadcasted_iota(jnp.int32, bent.shape, 1) <= i * 256 + lax.broadcasted_iota(jnp.int32, bent.shape, 0)
        weights = jnp.where(seen, jnp.exp(CAP * bent), 0.0)
        grad = d_att[r].astype(F32)
        delta = jnp.sum(grad * att[r], axis=-1, keepdims=True)
        d_probs = contract_cols(d_att[r], vals)
        d_raw = (weights * inv[r] * (d_probs - delta) * (1.0 - bent * bent)).astype(BF)
        dq = fold_rows(d_raw, keys) * (HD ** (-0.5))
        d_qkv[r, 0:HD] = unrotate(dq, cos[r], sine[r]).astype(BF)
        dk[0:upto] = dk[0:upto] + contract_rows(d_raw, query)
        scaled = grad * inv[r]
        high = scaled.astype(BF)
        rest = (scaled - high.astype(F32)).astype(BF)
        weights_b = weights.astype(BF)
        dv[0:upto] = dv[0:upto] + contract_rows(weights_b, high) + contract_rows(weights_b, rest)
        if i == 1:
            pump(6, 7)
            go(gu_c(6))
            go(small_b(0))
        if i == 3:
            pump(7, 8)
            go_self = gu_c(7)
            go_self.start()
    d_qkv[:, HD : 2 * HD] = unrotate(dk[...], cos[...], sine[...]).astype(BF)
    d_qkv[:, 2 * HD : 3 * HD] = dv[...].astype(BF)

    scatter = SlotScatter(part, buf, rss, rsr)

    def swap(zq, kept):
        where = pl.ds(pl.multiple_of(slot_of(ring_index(core, zq), p) * TOK, TOK), TOK)
        if kept:
            return pltpu.make_async_copy(seq.at[2 * zq + core], part.at[where], load.at[17 + zq])
        return remote(seq.at[2 * zq + 1 - core], part.at[where], sws.at[zq], swr.at[zq], sibling)

    def swapped(zq):
        where = pl.ds(pl.multiple_of(slot_of(ring_index(1 - core, zq), p) * TOK, TOK), TOK)
        return remote(seq.at[0], part.at[where], sws.at[zq], swr.at[zq], sibling)

    for zq in range(NZ):
        rows = d_qkv[2 * zq * TOK : (2 * zq + 2) * TOK]

        def columns(cols):
            value = contract_cols(rows, wq[cols])
            seq[2 * zq, :, cols] = value[0:TOK].astype(BF)
            seq[2 * zq + 1, :, cols] = value[TOK:].astype(BF)

        tiles(3, 768, columns)
        swap(zq, True).start()
        swap(zq, False).start()
    for zq in range(NZ):
        swap(zq, True).wait()
        swapped(zq).wait_recv()
    scatter.step(0)

    hidden_load.wait()

    def grad_half(half):
        def columns(cols):
            value = contract_rows(ring[:, pl.ds(half * 1152, 1152)], d_qkv[:, cols])
            for i in range(16):
                grad_q[half * 16 + i, :, cols] = value[72 * i : 72 * (i + 1)].astype(BF)

        tiles(3, 256, columns)

    grad_half(0)
    scatter.step(1)
    grad_half(1)
    for side in (0, 1):
        go(*[q_a(side, j) for j in range(RING)])
    for xo in (0, 1):
        small_a(1, xo).wait_recv()
        oa[xo] = (oa[xo].astype(F32) + og[2 * core + xo].astype(F32)).astype(BF)
    go(small_b(1))
    scatter.step(2)

    def q_sum(side, j):
        i = owner(order[j], core, side_x[side])
        q_a(side, j).wait_recv()
        total = grad_q[i].astype(F32) + aq[side, j].astype(F32)
        if side == 1:
            q_b(j).wait_recv()
            total = total + bq[j].astype(F32)
        grad_q[i] = total.astype(BF)

    for j in range(RING):
        q_sum(0, j)
        if j < AHEAD:
            go(q_b(j))
    small_b(0).wait_recv()
    da[x] = (da[x].astype(F32) + db[...].astype(F32)).astype(BF)
    small_c(0, 0)
    scatter.step(3)

    def q_round(j):
        q_sum(1, j)
        if j + AHEAD < RING:
            go(q_b(j + AHEAD))
        if ROUNDS[j] == 0:
            q_c(j).start()
        else:
            go(q_c(j))

    for j in range(4):
        q_round(j)
    small_b(1).wait_recv()
    oa[x] = (oa[x].astype(F32) + ob[...].astype(F32)).astype(BF)
    small_c(1, 0)

    def own_part(cols):
        slot = part[0:TOK, cols]
        d_hid_o[:, cols] = slot.astype(F32)

    tiles(3, 768, own_part)
    for j in range(4, RING):
        q_round(j)
    scatter.finish(d_hid_o)
    gain_in[0:1] = jnp.sum(d_hid_o[...] * normed[...], axis=0, keepdims=True)
    go(gain_a())
    gain_a().wait_recv()
    gsum[0] = gain_in[...] + ga[RING]
    go(gain_b())
    gain_b().wait_recv()
    gsum[1] = gsum[0] + ga[RING + 1]
    go(*[gain_c(j) for j in range(1, RING)])
    total = gsum[1]
    for j in range(1, RING):
        gain_c(j).wait_recv()
        total = total + ga[j]
    gain_o[...] = total

    for j in range(RING):
        if ROUNDS[j] == 0:
            gu_c(j).wait()
            q_c(j).wait()
        else:
            gu_c(j, True).wait_recv()
            q_c(j, True).wait_recv()
    small_c(0, 1)
    small_c(1, 1)
    for zq in range(NZ):
        swap(zq, False).wait_send()
    scatter.drain()
    for c in pending:
        c.wait_send()


def backward(d_branch, gu, down, hidden, w_qkv, w_out, queries, keys, values, attended, inv_total, cos_tab, sine_tab,
             normed_pre, gain_parts, collective_id):
    n = 4 * RING
    rows, width = d_branch.shape
    shard = gu.shape[0] // n
    gu = gu.reshape(n, shard, 2 * UNITS)
    down = down.reshape(4, -1, width)
    total, down_rows, out_rows = RING * rows, down.shape[1], w_out.shape[0] // 4
    gain_shape = (8, width)

    def out(*shape, dtype=BF):
        return jax.ShapeDtypeStruct(shape, dtype)

    def body(*refs):
        ins, rest = refs[:14], refs[14:]
        gains_ref, rest = rest[0], rest[1:]
        outs, scr = rest[:6], rest[6:]
        gain_scr = scr[0]
        gain_scr[...] = gains_ref[...]
        backward_kernel(*ins, gain_scr, *outs, *scr[1:])

    return pl.pallas_call(
        body,
        out_shape=[
            out(rows, width, dtype=F32), out(*gain_shape, dtype=F32),
            out(RING, shard, 2 * UNITS), out(RING, shard, 3 * HD),
            out(down_rows, width), out(out_rows, width),
        ],
        in_specs=[HBM] * 4 + [VMEM] * 11,
        out_specs=[VMEM] * 2 + [HBM] * 4,
        scratch_shapes=[
            pltpu.VMEM(gain_shape, F32),
            pltpu.VMEM((total, width), BF), pltpu.VMEM((RING, rows, width), BF), pltpu.VMEM((total, width), BF),
            pltpu.VMEM((2, 4, rows, width), BF),
            pltpu.VMEM((total, HD), BF), pltpu.VMEM((total, 3 * HD), BF),
            pltpu.VMEM((total, HD), F32), pltpu.VMEM((total, HD), F32),
            pltpu.VMEM((n, shard, 3 * HD), BF), pltpu.VMEM((2, RING, shard, 3 * HD), BF), pltpu.VMEM((RING, shard, 3 * HD), BF),
            pltpu.VMEM((2, shard, 2 * UNITS), BF), pltpu.VMEM((2, RING, shard, 2 * UNITS), BF), pltpu.VMEM((RING, shard, 2 * UNITS), BF),
            pltpu.VMEM((down_rows, width), BF), pltpu.VMEM((2, down_rows, width), BF), pltpu.VMEM((down_rows, width), BF),
            pltpu.VMEM((4, out_rows, width), BF), pltpu.VMEM((2, out_rows, width), BF), pltpu.VMEM((out_rows, width), BF),
            pltpu.VMEM((RING + 2,) + gain_shape, F32), pltpu.VMEM((2,) + gain_shape, F32),
            DMA((21,)),
            DMA((2, 4, SUB)), DMA((2, 4, SUB)), DMA((NZ,)), DMA((NZ,)), DMA((2, 4, SUB)), DMA((2, 4, SUB)), DMA((NZ,)), DMA((NZ,)),
            DMA((2, RING)), DMA((2, RING)), DMA((RING,)), DMA((RING,)), DMA((RING,)), DMA((RING,)),
            DMA((2, RING)), DMA((2, RING)), DMA((RING,)), DMA((RING,)), DMA((RING,)), DMA((RING,)),
            DMA((2, 4)), DMA((2, 4)), DMA((RING + 2,)), DMA((RING + 2,)),
        ],
        compiler_params=params(collective_id, 60),
    )(d_branch, gu, down, hidden, w_qkv, w_out, queries, keys, values, attended, inv_total, cos_tab, sine_tab, normed_pre, gain_parts)


def on_ring(
    tokens, w_query, w_key, w_value, w_out, w_gate, w_up, w_down,
    pre_gain, post_gain, pre_ffn_gain, post_ffn_gain, out_grad,
):
    ids = iter(range(32))
    length = RING * tokens.shape[1]
    shard_gain = pre_gain.shape[0]
    mine = lax.axis_index("ctx") * 4 + lax.axis_index("fsdp")
    gains = jnp.stack([pre_gain, post_gain, pre_ffn_gain, post_ffn_gain]).astype(F32)
    gains = lax.dynamic_update_slice(jnp.zeros((8, D), F32), gains, (0, mine * shard_gain))
    cos_tab, sine_tab = rope_tables(jnp.arange(length, dtype=jnp.int32), HD)
    w_gu, down_in, hidden, w_qkv, out_in, gains, queries, keys, values, attended, inv_total, branch = forward(
        w_gate, w_up, w_query, w_key, w_value, w_down, w_out, tokens[0], gains, cos_tab, sine_tab, next(ids)
    )
    w_gu, hidden = w_gu.reshape(D, 2 * UNITS), hidden.reshape(length, D)
    w_dn = down_in.reshape(UNITS, D)
    w_ot = out_in.reshape(HD, D)
    pre_factor, post_factor, pre_ffn_factor, post_ffn_factor = (1.0 + gains[i] for i in range(4))
    resid_in = tokens[0].astype(F32)
    inv_pre, normed_pre = rms_parts(resid_in)
    inv_post, normed_post = rms_parts(branch)
    middle = resid_in + normed_post * post_factor
    inv_mid, normed_mid = rms_parts(middle)
    hidden_ffn = (normed_mid * pre_ffn_factor).astype(BF)
    output, d_hidden_ffn, post_ffn_part, down_part, gu_part = feed_forward(
        hidden_ffn, middle, post_ffn_factor[None], out_grad[0], w_gu, w_dn, next(ids)
    )
    post_ffn_part = post_ffn_part[0]
    out_cot = out_grad[0].astype(F32)
    pre_ffn_part = jnp.sum(d_hidden_ffn * normed_mid, axis=0)
    d_middle = out_cot + norm_back(d_hidden_ffn * pre_ffn_factor, normed_mid, inv_mid)
    post_part = jnp.sum(d_middle * normed_post, axis=0)
    d_branch = norm_back(d_middle * post_factor, normed_post, inv_post).astype(BF)
    gain_parts = jnp.stack([jnp.zeros_like(post_part), post_part, pre_ffn_part, post_ffn_part])
    d_hidden, gain_g, gu_g, qkv_g, down_g, out_g = backward(
        d_branch, gu_part, down_part, hidden, w_qkv, w_ot, queries, keys, values, attended, inv_total,
        cos_tab, sine_tab, normed_pre, jnp.pad(gain_parts, ((0, 4), (0, 0))), next(ids),
    )
    token_grad = d_middle + norm_back(d_hidden * pre_factor, normed_pre, inv_pre)

    def spread(columns):
        return jnp.transpose(columns, (1, 0, 2)).reshape(shard_gain, -1).astype(F32)

    gate_g, up_g, query_g = spread(gu_g[..., :UNITS]), spread(gu_g[..., UNITS:]), spread(qkv_g[..., :HD])
    heads = qkv_g[..., HD:].astype(F32).reshape(KVH, H // KVH, shard_gain, 2 * HD).sum(1)
    key_g, value_g = (
        jnp.transpose(part, (1, 0, 2)).reshape(shard_gain, -1) for part in (heads[..., :HD], heads[..., HD:])
    )
    down_g, out_g = down_g.astype(F32), out_g.astype(F32)
    gain_g = lax.dynamic_slice(gain_g, (0, mine * shard_gain), (4, shard_gain))
    return (
        output[None], token_grad.astype(BF)[None],
        query_g, key_g, value_g, out_g, gate_g, up_g, down_g,
        gain_g[0], gain_g[1], gain_g[2], gain_g[3],
    )


ROW_FOLD = 4


def head_tables(positions, width):
    half_width = width // 2
    inv_freqs = ROPE_BASE ** (-jnp.arange(half_width, dtype=jnp.float32) * 2.0 / width)
    angles = positions.astype(jnp.float32)[:, None] * inv_freqs[None, :]
    return (jnp.cos(angles)[:, None, :], jnp.sin(angles)[:, None, :])


def rotate_heads(heads_in, cos_tab, sine_tab):
    half_width = heads_in.shape[-1] // 2
    front_half = heads_in[..., :half_width]
    back_half = heads_in[..., half_width:]
    return jnp.concatenate(
        [front_half * cos_tab - back_half * sine_tab, back_half * cos_tab + front_half * sine_tab],
        axis=-1,
    )


def unrotate_heads(grad_in, cos_tab, sine_tab):
    half_width = grad_in.shape[-1] // 2
    front_half = grad_in[..., :half_width]
    back_half = grad_in[..., half_width:]
    return jnp.concatenate(
        [front_half * cos_tab + back_half * sine_tab, back_half * cos_tab - front_half * sine_tab],
        axis=-1,
    )


def to_groups(flat_heads, tok_rows, q_group):
    shaped = flat_heads.reshape(tok_rows, KVH, q_group, HD)
    return jnp.transpose(shaped, (1, 2, 0, 3)).reshape(KVH, q_group * tok_rows, HD)


def from_groups(grouped, tok_rows, q_group):
    shaped = grouped.reshape(KVH, q_group, tok_rows, HD)
    return jnp.transpose(shaped, (2, 0, 1, 3)).reshape(tok_rows, KVH * q_group * HD)


def grad_rows(left, right, folding, count):
    block = contract_rows(left, right)
    return block.reshape(count, right.shape[1] // folding)


def blockwise(step_fn, carry, piece, width):
    key_count = piece[0].shape[0]
    n_steps = key_count // width
    stacked = tuple((member.reshape(n_steps, width, member.shape[1]) for member in piece))

    def one_step(partial_value, block_item):
        block_index, members = block_item
        return (step_fn(partial_value, members, block_index * width), None)

    carry, unused = lax.scan(one_step, carry, (jnp.arange(n_steps, dtype=jnp.int32), stacked))
    return carry


def block_grads(query_g, query_pos, d_att_g, delta, inv_tot, key_block, value_block, key_first):
    key_count = key_block.shape[0]
    key_grp = key_block.reshape(key_count, KVH, HD)
    value_grp = value_block.reshape(key_count, KVH, HD)
    raw_scores = jnp.einsum("grd,ngd->grn", query_g, key_grp, preferred_element_type=jnp.float32)
    capped = CAP * jnp.tanh(raw_scores / CAP)
    key_pos = key_first + jnp.arange(key_count, dtype=jnp.int32)
    allowed = key_pos[None, None, :] <= query_pos[None, :, None]
    weights = jnp.where(allowed, jnp.exp(capped), 0.0)
    prob_rows = weights * inv_tot[..., None]
    d_probs = jnp.einsum("grd,ngd->grn", d_att_g, value_grp, preferred_element_type=jnp.float32)
    slope = 1.0 - capped / CAP * (capped / CAP)
    d_raw = (prob_rows * (d_probs - delta[..., None]) * slope).astype(jnp.bfloat16)
    d_query = jnp.einsum("grn,ngd->grd", d_raw, key_grp, preferred_element_type=jnp.float32)
    d_key = jnp.einsum("grn,grd->ngd", d_raw, query_g, preferred_element_type=jnp.float32)
    weights_b = weights.astype(jnp.bfloat16)
    d_scaled = d_att_g.astype(jnp.float32) * inv_tot[..., None]
    scaled_high = d_scaled.astype(jnp.bfloat16)
    scaled_rest = (d_scaled - scaled_high.astype(jnp.float32)).astype(jnp.bfloat16)
    d_value = jnp.einsum("grn,grd->ngd", weights_b, scaled_high, preferred_element_type=jnp.float32)
    d_value = d_value + jnp.einsum(
        "grn,grd->ngd", weights_b, scaled_rest, preferred_element_type=jnp.float32
    )
    return (d_query, d_key.reshape(key_count, KVH * HD), d_value.reshape(key_count, KVH * HD))


def on_any_mesh(
    tokens,
    w_query,
    w_key,
    w_value,
    w_out,
    w_gate,
    w_up,
    w_down,
    pre_gain,
    post_gain,
    pre_ffn_gain,
    post_ffn_gain,
    out_grad,
):
    tok_rows = tokens.shape[1]
    q_group = H // KVH
    q_scale = HD ** (-0.5)
    width_q = H * HD
    width_kv = KVH * HD
    width_qkv = width_q + 2 * width_kv
    n_ctx = lax.axis_size("ctx")
    my_block = lax.axis_index("ctx")
    my_start = my_block * tok_rows
    positions = my_start + jnp.arange(tok_rows, dtype=jnp.int32)
    cos_tab, sine_tab = head_tables(positions, HD)
    row_pos = jnp.tile(positions, q_group)
    last_pos = my_start + tok_rows - 1
    resid_in = tokens[0].astype(jnp.float32)
    qkv_shard = jnp.concatenate([w_query, w_key, w_value], axis=1)
    gateup_shard = jnp.concatenate([w_gate, w_up], axis=1)
    shard_rows = qkv_shard.shape[0]
    gains_shard = jnp.stack([pre_gain, post_gain, pre_ffn_gain, post_ffn_gain])
    full_gains, full_qkv, full_out = (
        lax.all_gather(gains_shard, ("ctx", "fsdp"), axis=1, tiled=True),
        lax.all_gather(qkv_shard, ("ctx", "fsdp"), axis=0, tiled=True),
        lax.all_gather(w_out, ("ctx", "fsdp"), axis=0, tiled=True),
    )
    factors = 1.0 + full_gains.astype(jnp.float32)
    pre_factor, post_factor, pre_ffn_factor, post_ffn_factor = (
        factors[0],
        factors[1],
        factors[2],
        factors[3],
    )
    inv_pre, normed_pre = rms_parts(resid_in)
    hidden = (normed_pre * pre_factor).astype(jnp.bfloat16)
    projected = jnp.dot(hidden, full_qkv, preferred_element_type=jnp.float32)
    query_lin = projected[:, :width_q].reshape(tok_rows, H, HD)
    queries = (
        (rotate_heads(query_lin, cos_tab, sine_tab) * q_scale)
        .astype(jnp.bfloat16)
        .reshape(tok_rows, width_q)
    )
    query_grp = to_groups(queries, tok_rows, q_group)
    key_lin = projected[:, width_q : width_q + width_kv].reshape(tok_rows, KVH, HD)
    key_rows = rotate_heads(key_lin, cos_tab, sine_tab).astype(jnp.bfloat16).reshape(tok_rows, width_kv)
    value_rows = projected[:, width_q + width_kv :].astype(jnp.bfloat16)

    def add_block(partial_value, piece, first_row):
        key_block, value_block = piece

        def add_compute_block(state):
            row_total, weighted = state
            key_count = key_block.shape[0]
            key_grp = key_block.reshape(key_count, KVH, HD)
            raw_scores = jnp.einsum(
                "grd,ngd->grn", query_grp, key_grp, preferred_element_type=jnp.float32
            )
            capped = CAP * jnp.tanh(raw_scores / CAP)
            key_pos = first_row + jnp.arange(key_count, dtype=jnp.int32)
            allowed = key_pos[None, None, :] <= row_pos[None, :, None]
            weights = jnp.where(allowed, jnp.exp(capped), 0.0)
            value_grp = value_block.reshape(key_count, KVH, HD)
            weighted = weighted + jnp.einsum(
                "grn,ngd->grd",
                weights.astype(jnp.bfloat16),
                value_grp,
                preferred_element_type=jnp.float32,
            )
            return (row_total + jnp.sum(weights, axis=-1), weighted)

        def add_skip_block(state):
            return state

        return lax.cond(first_row <= last_pos, add_compute_block, add_skip_block, partial_value)

    start_state = (
        jnp.zeros((KVH, q_group * tok_rows), jnp.float32),
        jnp.zeros((KVH, q_group * tok_rows, HD), jnp.float32),
    )
    row_total, weighted = blockwise(
        add_block,
        start_state,
        (
            lax.all_gather(key_rows, "ctx", axis=0, tiled=True),
            lax.all_gather(value_rows, "ctx", axis=0, tiled=True),
        ),
        512,
    )
    inv_total = 1.0 / row_total
    attended_grp = weighted * inv_total[..., None]
    attended_b = from_groups(attended_grp, tok_rows, q_group).astype(jnp.bfloat16)
    branch = jnp.dot(attended_b, full_out, preferred_element_type=jnp.float32)
    inv_post, normed_post = rms_parts(branch)
    middle = resid_in + normed_post * post_factor
    inv_mid, normed_mid = rms_parts(middle)
    hidden_ffn = (normed_mid * pre_ffn_factor).astype(jnp.bfloat16)
    gate_up = fold_rows(
        hidden_ffn, lax.all_gather(gateup_shard, ("ctx", "fsdp"), axis=0, tiled=True)
    )
    gate_lin = gate_up[:, :FF]
    up_lin = gate_up[:, FF:]
    active = gated(gate_lin, up_lin).astype(jnp.bfloat16)
    ffn_branch = fold_rows(active, lax.all_gather(w_down, ("ctx", "fsdp"), axis=0, tiled=True))
    inv_ffn, normed_ffn = rms_parts(ffn_branch)
    output = (middle + normed_ffn * post_ffn_factor).astype(jnp.bfloat16)
    out_cot = out_grad[0].astype(jnp.float32)
    post_ffn_part = jnp.sum(out_cot * normed_ffn, axis=0)
    d_ffn_b = norm_back(out_cot * post_ffn_factor, normed_ffn, inv_ffn).astype(jnp.bfloat16)
    down_total = lax.psum_scatter(
        grad_rows(active, d_ffn_b, 1, lax.axis_size(("ctx", "fsdp")) * w_down.shape[0]),
        ("ctx", "fsdp"),
        scatter_dimension=0,
        tiled=True,
    )
    d_active = contract_cols(d_ffn_b, lax.all_gather(w_down, ("ctx", "fsdp"), axis=0, tiled=True))
    unused_value, gate_pull = jax.vjp(gated, gate_lin, up_lin)
    d_gate, d_up = gate_pull(d_active)
    d_gateup_b = jnp.concatenate([d_gate.astype(jnp.bfloat16), d_up.astype(jnp.bfloat16)], axis=1)
    gateup_folded = lax.psum_scatter(
        grad_rows(
            hidden_ffn,
            d_gateup_b,
            ROW_FOLD,
            lax.axis_size(("ctx", "fsdp")) * (ROW_FOLD * shard_rows),
        ),
        ("ctx", "fsdp"),
        scatter_dimension=0,
        tiled=True,
    )
    gateup_total = gateup_folded.reshape(shard_rows, 2 * FF)
    d_hidden_ffn = contract_cols(
        d_gateup_b, lax.all_gather(gateup_shard, ("ctx", "fsdp"), axis=0, tiled=True)
    )
    pre_ffn_part = jnp.sum(d_hidden_ffn * normed_mid, axis=0)
    d_middle = out_cot + norm_back(d_hidden_ffn * pre_ffn_factor, normed_mid, inv_mid)
    back_qkv, back_out = (
        lax.all_gather(qkv_shard, ("ctx", "fsdp"), axis=0, tiled=True),
        lax.all_gather(w_out, ("ctx", "fsdp"), axis=0, tiled=True),
    )
    post_gain_part = jnp.sum(d_middle * normed_post, axis=0)
    d_branch_b = norm_back(d_middle * post_factor, normed_post, inv_post).astype(jnp.bfloat16)
    w_out_part = contract_rows(attended_b, d_branch_b)
    d_attended = contract_cols(d_branch_b, back_out).astype(jnp.bfloat16)
    d_att_grp = to_groups(d_attended, tok_rows, q_group)
    row_delta = jnp.sum(d_att_grp.astype(jnp.float32) * attended_grp, axis=-1)
    zero_rows = jnp.zeros((tok_rows, width_kv), jnp.float32)
    zero_query = jnp.zeros((KVH, q_group * tok_rows, HD), jnp.float32)
    block_ids = jnp.arange(n_ctx, dtype=jnp.int32)
    all_keys, all_values = (
        lax.all_gather(key_rows, "ctx", axis=0, tiled=True),
        lax.all_gather(value_rows, "ctx", axis=0, tiled=True),
    )

    def returned_step(acc_query, block_item):
        block_index, key_block, value_block = block_item
        first_row = block_index * tok_rows

        def returned_compute_block(acc_in):
            d_query, d_key, d_value = block_grads(
                query_grp,
                row_pos,
                d_att_grp,
                row_delta,
                inv_total,
                key_block,
                value_block,
                first_row,
            )
            return (acc_in + d_query, (d_key, d_value))

        def returned_skip_block(acc_in):
            return (acc_in, (zero_rows, zero_rows))

        return lax.cond(
            first_row <= last_pos, returned_compute_block, returned_skip_block, acc_query
        )

    key_blocks = all_keys.reshape(n_ctx, tok_rows, width_kv)
    value_blocks = all_values.reshape(n_ctx, tok_rows, width_kv)
    d_query_grp, key_terms = lax.scan(
        returned_step, zero_query, (block_ids, key_blocks, value_blocks)
    )
    key_term_rows = key_terms[0].reshape(n_ctx * tok_rows, width_kv)
    value_term_rows = key_terms[1].reshape(n_ctx * tok_rows, width_kv)
    d_keys, d_values = (
        lax.psum_scatter(
            key_term_rows.astype(jnp.bfloat16), "ctx", scatter_dimension=0, tiled=True
        ).astype(jnp.float32),
        lax.psum_scatter(
            value_term_rows.astype(jnp.bfloat16), "ctx", scatter_dimension=0, tiled=True
        ).astype(jnp.float32),
    )
    d_query_flat = from_groups(d_query_grp, tok_rows, q_group).reshape(tok_rows, H, HD) * q_scale
    dq_lin = (
        unrotate_heads(d_query_flat, cos_tab, sine_tab).astype(jnp.bfloat16).reshape(tok_rows, width_q)
    )
    dk_lin = (
        unrotate_heads(d_keys.reshape(tok_rows, KVH, HD), cos_tab, sine_tab)
        .astype(jnp.bfloat16)
        .reshape(tok_rows, width_kv)
    )
    dv_lin = d_values.astype(jnp.bfloat16)
    dqkv_b = jnp.concatenate([dq_lin, dk_lin, dv_lin], axis=1)
    d_hidden = contract_cols(dqkv_b, back_qkv)
    qkv_part = contract_rows(hidden, dqkv_b).reshape(ROW_FOLD * D, width_qkv // ROW_FOLD)
    pre_gain_part = jnp.sum(d_hidden * normed_pre, axis=0)
    token_grad = d_middle + norm_back(d_hidden * pre_factor, normed_pre, inv_pre)
    gain_parts = jnp.stack([pre_gain_part, post_gain_part, pre_ffn_part, post_ffn_part])
    qkv_folded, out_total, gain_totals = (
        lax.psum_scatter(qkv_part, ("ctx", "fsdp"), scatter_dimension=0, tiled=True),
        lax.psum_scatter(w_out_part, ("ctx", "fsdp"), scatter_dimension=0, tiled=True),
        lax.psum_scatter(gain_parts, ("ctx", "fsdp"), scatter_dimension=1, tiled=True),
    )
    qkv_total = qkv_folded.reshape(shard_rows, width_qkv)
    return (
        output[None],
        token_grad.astype(jnp.bfloat16)[None],
        qkv_total[:, :width_q],
        qkv_total[:, width_q : width_q + width_kv],
        qkv_total[:, width_q + width_kv :],
        out_total,
        gateup_total[:, :FF],
        gateup_total[:, FF:],
        down_total,
        gain_totals[0],
        gain_totals[1],
        gain_totals[2],
        gain_totals[3],
    )


def solution(mesh):
    ring = mesh.shape["ctx"] == RING and mesh.shape["fsdp"] == 4
    tokens, rows, gains = P("fsdp", "ctx", None), P(("ctx", "fsdp"), None), P(("ctx", "fsdp"))
    return jax.shard_map(
        on_ring if ring else on_any_mesh,
        mesh=mesh,
        in_specs=(tokens,) + (rows,) * 7 + (gains,) * 4 + (tokens,),
        out_specs=(tokens, tokens) + (rows,) * 7 + (gains,) * 4,
        check_vma=False,
    )
```

```python
import functools

import jax
import jax.numpy as jnp
from jax import lax
from jax.experimental import pallas as pl
from jax.experimental.pallas import tpu as pltpu
from jax.sharding import PartitionSpec as P

D = 2304
H = 8
KVH = 4
HD = 256
CAP = 50
FF = 9216

EPSILON = 1e-06
ROPE_BASE = 10000.0

MESH = pl.DeviceIdType.MESH
HBM = pl.BlockSpec(memory_space=pl.ANY)
VMEM = pl.BlockSpec(memory_space=pltpu.VMEM)
DMA = pltpu.SemaphoreType.DMA
BF = jnp.bfloat16
F32 = jnp.float32


def rope_tables(positions, width):
    half_width = width // 2
    inv_freqs = ROPE_BASE ** (-jnp.arange(half_width, dtype=F32) * 2.0 / width)
    angles = positions.astype(F32)[:, None] * inv_freqs[None, :]
    return (jnp.cos(angles), jnp.sin(angles))


def rotate(rows, cos_tab, sine_tab):
    half_width = rows.shape[-1] // 2
    front, back = rows[..., :half_width], rows[..., half_width:]
    return jnp.concatenate(
        [front * cos_tab - back * sine_tab, back * cos_tab + front * sine_tab], axis=-1
    )


def unrotate(rows, cos_tab, sine_tab):
    half_width = rows.shape[-1] // 2
    front, back = rows[..., :half_width], rows[..., half_width:]
    return jnp.concatenate(
        [front * cos_tab + back * sine_tab, back * cos_tab - front * sine_tab], axis=-1
    )


def rms_parts(values_in):
    inverse = lax.rsqrt(jnp.mean(values_in * values_in, axis=-1, keepdims=True) + EPSILON)
    return (inverse, values_in * inverse)


def norm_back(grad_normed, normed, inverse):
    return inverse * (grad_normed - normed * jnp.mean(grad_normed * normed, axis=-1, keepdims=True))


def contract_rows(left, right):
    return lax.dot_general(left, right, (((0,), (0,)), ((), ())), preferred_element_type=F32)


def contract_cols(left, right):
    return lax.dot_general(left, right, (((1,), (1,)), ((), ())), preferred_element_type=F32)


def fold_rows(left, right):
    return jnp.dot(left, right, preferred_element_type=F32)


def gated(gate_in, up_in):
    return jax.nn.gelu(gate_in, approximate=True) * up_in


NZ = 4
RING = 2 * NZ


def my_place():
    c, f = lax.axis_index("ctx"), lax.axis_index("fsdp")
    return c // 2, c % 2, f // 2, f % 2


def ring_index(y, z):
    return z + y * (RING - 1 - 2 * z)


def ring_yz(q):
    y = q // NZ
    return y, q + y * (RING - 1 - 2 * q)


def device(z, core, y, x):
    return (2 * z + core, 2 * y + x)


def ring_device(q, core, x):
    y, z = ring_yz(q)
    return device(z, core, y, x)


def remote(src, dst, send_sem, recv_sem, where):
    return pltpu.make_async_remote_copy(
        src_ref=src,
        dst_ref=dst,
        send_sem=send_sem,
        recv_sem=recv_sem,
        device_id=where,
        device_id_type=MESH,
    )


def greet(places):
    barrier = pltpu.get_barrier_semaphore()
    for place in places:
        pl.semaphore_signal(barrier, inc=1, device_id=place, device_id_type=MESH)
    pl.semaphore_wait(barrier, len(places))


def params(collective_id, vmem_mib=56):
    return pltpu.CompilerParams(
        collective_id=collective_id,
        has_side_effects=True,
        vmem_limit_bytes=vmem_mib * 2**20,
    )


SUB = 4


def ring_parts(direction, step, half_step):
    if step != half_step:
        return list(range(SUB))
    half = SUB // 2
    return list(range(half)) if direction == 0 else list(range(half, SUB))


TOK = 128
UNITS = FF // RING
TILE = 128
GELU_K = 0.7978845608028654
GELU_A = 0.044715


class SlotGather:
    def __init__(self, buf, ss, rs):
        z, core, y, x = my_place()
        p = ring_index(y, z)
        self.buf, self.ss, self.rs = buf, ss, rs
        self.near = (ring_device((p + 1) % RING, core, x), ring_device((p + RING - 1) % RING, core, x))
        self.pending = []

    def copy(self, direction, step, k):
        piece = TOK // SUB
        src = 0 if step == 0 else 2 * step - 1 + direction
        dst = 7 if step == 3 else 2 * step + 1 + direction
        return remote(
            self.buf.at[pl.ds(src * TOK + k * piece, piece)],
            self.buf.at[pl.ds(dst * TOK + k * piece, piece)],
            self.ss.at[direction, step, k],
            self.rs.at[direction, step, k],
            self.near[direction],
        )

    def step(self, step):
        for k in range(SUB):
            for direction in (0, 1):
                if step > 0:
                    self.copy(direction, step - 1, k).wait_recv()
                if k in ring_parts(direction, step, 3):
                    c = self.copy(direction, step, k)
                    c.start()
                    self.pending.append(c)

    def finish(self):
        for direction in (0, 1):
            for k in ring_parts(direction, 3, 3):
                self.copy(direction, 3, k).wait_recv()

    def drain(self):
        for c in self.pending:
            c.wait_send()


class SlotScatter:
    def __init__(self, part, buf, ss, rs):
        z, core, y, x = my_place()
        p = ring_index(y, z)
        self.part, self.buf, self.ss, self.rs = part, buf, ss, rs
        self.near = (ring_device((p + 1) % RING, core, x), ring_device((p + RING - 1) % RING, core, x))
        self.pending = []

    def copy(self, direction, step, k, src):
        rows = pl.ds(k * (TOK // SUB), TOK // SUB)
        return remote(
            src,
            self.buf.at[direction, step, rows],
            self.ss.at[direction, step, k],
            self.rs.at[direction, step, k],
            self.near[direction],
        )

    def step(self, step):
        piece = TOK // SUB
        for k in range(SUB):
            rows = pl.ds(k * piece, piece)
            for direction in (0, 1):
                if k not in ring_parts(direction, step, 0):
                    continue
                slot = 7 if step == 0 else 2 * (4 - step) - direction
                mine = pl.ds(slot * TOK + k * piece, piece)
                src = self.part.at[mine]
                if step > 0 and k in ring_parts(direction, step - 1, 0):
                    src = self.buf.at[direction, step - 1, rows]
                    self.copy(direction, step - 1, k, src).wait_recv()
                    src[...] = (src[...].astype(F32) + self.part[mine].astype(F32)).astype(BF)
                c = self.copy(direction, step, k, src)
                c.start()
                self.pending.append(c)

    def finish(self, total):
        for k in range(SUB):
            rows = pl.ds(k * (TOK // SUB), TOK // SUB)
            for direction in (0, 1):
                src = self.buf.at[direction, 3, rows]
                self.copy(direction, 3, k, src).wait_recv()
                total[rows] = total[rows] + src[...].astype(F32)

    def drain(self):
        for c in self.pending:
            c.wait_send()


def tiles(count, width, body):
    def step(i, carry):
        body(pl.ds(pl.multiple_of(i * width, width), width))
        return carry

    lax.fori_loop(0, count, step, 0)


def gelu_parts(v):
    bent = jnp.tanh(GELU_K * (v + GELU_A * (v * v * v)))
    value = 0.5 * v * (1.0 + bent)
    slope = 0.5 * (1.0 + bent) + 0.5 * v * (1.0 - bent * bent) * (GELU_K * (1.0 + 3.0 * GELU_A * (v * v)))
    return value, slope


PAIRS = ((128, 256), (384, 256), (640, 256))
LAST = (896, 128)
OWN = (0, 128)


def feed_forward_kernel(hid, middle, factor, cot, w_hbm, wd_hbm,
                        out_o, d_hid_o, gain_o, wd_grad, gu_grad,
                        wgu, wd, ha, gu, act, part, buf, df, dgu, total, stage,
                        w_sem, ags, agr, rss, rsr, out_sem):
    gather = [SlotGather(b, ags.at[i], agr.at[i]) for i, b in enumerate((ha, df))]
    scatter = [SlotScatter(part, buf, rss.at[i], rsr.at[i]) for i in range(2)]
    greet(gather[0].near)
    loads = [
        pltpu.make_async_copy(w_hbm, wgu, w_sem.at[0]),
        pltpu.make_async_copy(wd_hbm, wd, w_sem.at[1]),
    ]
    ha[0:TOK] = hid[...]
    gather[0].step(0)
    for c in loads:
        c.start()
    loads[0].wait()

    def gate_up(first, count):
        rows = pl.ds(first, count)

        def column(cols):
            gu[rows, cols] = fold_rows(ha[rows], wgu[:, cols])

        tiles(3, 768, column)

        def finish(i, carry):
            r = pl.ds(pl.multiple_of(first + i * 32, 32), 32)
            act[r] = (gelu_parts(gu[r, 0:UNITS])[0] * gu[r, UNITS : 2 * UNITS]).astype(BF)
            return carry

        lax.fori_loop(0, count // 32, finish, 0)

    def down_part(first, count, dst):
        def column(cols):
            value = fold_rows(act[pl.ds(first, count)], wd[:, cols])
            dst[pl.ds(first, count), cols] = value.astype(dst.dtype)

        tiles(3, 768, column)

    def active_back(first, count):
        rows = pl.ds(first, count)
        for n in range(3):
            cols, up_cols = pl.ds(n * 384, 384), pl.ds(UNITS + n * 384, 384)
            d_active = contract_cols(df[rows], wd[cols])
            value, slope = gelu_parts(gu[rows, cols])
            dgu[rows, cols] = (d_active * gu[rows, up_cols] * slope).astype(BF)
            dgu[rows, up_cols] = (d_active * value).astype(BF)

    def hidden_part(first, count, dst):
        def column(cols):
            value = contract_cols(dgu[pl.ds(first, count)], wgu[cols])
            dst[pl.ds(first, count), cols] = value.astype(dst.dtype)

        tiles(3, 768, column)

    n_down = UNITS // TILE

    def grad_out(i):
        slot = i % 2
        if i < n_down:
            return pltpu.make_async_copy(stage.at[slot], wd_grad.at[pl.ds(i * TILE, TILE)], out_sem.at[slot])
        return pltpu.make_async_copy(stage.at[slot], gu_grad.at[pl.ds((i - n_down) * TILE, TILE)], out_sem.at[slot])

    def grad_tiles(first, last):
        for i in range(first, last):
            if i >= 2:
                grad_out(i - 2).wait()
            if i < n_down:
                value = contract_rows(act[:, pl.ds(i * TILE, TILE)], df[...])
            else:
                value = contract_rows(ha[:, pl.ds((i - n_down) * TILE, TILE)], dgu[...])
            stage[i % 2] = value.astype(BF)
            grad_out(i).start()

    gate_up(*OWN)
    for step, pair in enumerate(PAIRS):
        gather[0].step(step + 1)
        if step == 0:
            loads[1].wait()
        gate_up(*pair)
    gather[0].finish()
    gate_up(*LAST)
    down_part(*LAST, part)
    scatter[0].step(0)
    for step, pair in enumerate(PAIRS[::-1]):
        down_part(*pair, part)
        scatter[0].step(step + 1)
    down_part(*OWN, total)
    scatter[0].finish(total)
    gather[0].drain()
    scatter[0].drain()

    branch = total[...]
    inverse, normed = rms_parts(branch)
    out_cot = cot[...].astype(F32)
    scale = factor[...]
    df[0:TOK] = norm_back(out_cot * scale, normed, inverse).astype(BF)
    gather[1].step(0)
    out_o[...] = (middle[...] + normed * scale).astype(BF)
    gain_o[...] = jnp.sum(out_cot * normed, axis=0, keepdims=True)
    active_back(*OWN)
    for step, pair in enumerate(PAIRS):
        gather[1].step(step + 1)
        active_back(*pair)
    gather[1].finish()
    active_back(*LAST)
    hidden_part(*LAST, part)
    scatter[1].step(0)
    done = 0
    for step, pair in enumerate(PAIRS[::-1]):
        hidden_part(*pair, part)
        scatter[1].step(step + 1)
        grad_tiles(done, done + 6)
        done += 6
    hidden_part(*OWN, d_hid_o)
    scatter[1].finish(d_hid_o)
    n_tiles = n_down + ha.shape[1] // TILE
    grad_tiles(done, n_tiles)
    for i in (n_tiles - 2, n_tiles - 1):
        grad_out(i).wait()
    gather[1].drain()
    scatter[1].drain()


def feed_forward(hidden_ffn, middle, factor, out_grad, w_in, w_down, collective_id):
    rows, width = hidden_ffn.shape
    total = RING * rows

    def full(*shape, dtype=F32):
        return jax.ShapeDtypeStruct(shape, dtype)

    return pl.pallas_call(
        feed_forward_kernel,
        out_shape=[
            full(rows, width, dtype=BF), full(rows, width), full(1, width),
            full(UNITS, width, dtype=BF), full(width, 2 * UNITS, dtype=BF),
        ],
        in_specs=[VMEM] * 4 + [HBM] * 2,
        out_specs=[VMEM] * 3 + [HBM] * 2,
        scratch_shapes=[
            pltpu.VMEM((width, 2 * UNITS), BF), pltpu.VMEM((UNITS, width), BF),
            pltpu.VMEM((total, width), BF), pltpu.VMEM((total, 2 * UNITS), F32), pltpu.VMEM((total, UNITS), BF),
            pltpu.VMEM((total, width), BF), pltpu.VMEM((2, 4, rows, width), BF),
            pltpu.VMEM((total, width), BF), pltpu.VMEM((total, 2 * UNITS), BF),
            pltpu.VMEM((rows, width), F32), pltpu.VMEM((2, TILE, width), BF),
            DMA((2,)),
            DMA((2, 2, 4, SUB)), DMA((2, 2, 4, SUB)), DMA((2, 2, 4, SUB)), DMA((2, 2, 4, SUB)),
            DMA((2,)),
        ],
        compiler_params=params(collective_id, 60),
    )(hidden_ffn, middle, factor, out_grad, w_in, w_down)


WIDTHS = (UNITS, UNITS, HD, HD, HD)


SHARD = D // (4 * RING)
PADDED = D + 128
WINDOW = 256


def window(i):
    return pl.ds(pl.multiple_of((SHARD * i) // 128 * 128, 128), WINDOW)


def member_place(t, core, x):
    return device(t // 2, core, t % 2, x)


def slot_of(q, p):
    d = (q - p + RING) % RING
    return jnp.where(d == 0, 0, jnp.where(d < 4, 2 * d, jnp.where(d == 4, 7, 15 - 2 * d)))


def partner(t, j):
    out = 0
    for bit in (1, 2, 4):
        on = (t // bit) % 2
        out = out + bit * (1 - on if j & bit else on)
    return out


def column_start(which, t):
    if which < 2:
        return pl.multiple_of(t * UNITS, 128)
    return pl.multiple_of((t if which == 2 else t // 2) * HD, 128)


def forward_kernel(gate, up, query, key, value, down, out, block, gain_in, cos, sine,
                   w_gu, d_ref, hidden_o, wq, wo, gain_o, q_o, k_o, v_o, att_o, inv_o, branch_o,
                   ring, seq, seq_part, part, buf, wq_in, own, relay, ga, gsum,
                   load, ags, agr, pls, plr, rss, rsr, sws, swr, s1, r1, s2, r2, s3, r3,
                   q1, t1, q2, t2, q3, t3, s4, r4, s5, r5, sg, rg):
    z, core, y, x = my_place()
    t, p = 2 * z + y, ring_index(y, z)
    sibling, across = device(z, 1 - core, y, x), device(z, core, y, 1 - x)
    member = [partner(t, j) for j in range(RING)]
    members = [member_place(tq, core, x) for tq in member]
    plane = []
    for dc in (0, 1):
        for dy in (0, 1):
            for dx in (0, 1):
                if (dc, dx) != (0, 0):
                    plane.append(device(z, (core + dc) % 2, (y + dy) % 2, (x + dx) % 2))
    greet(members[1:] + plane)
    sources = (gate, up, query, key, value)
    pending = []

    def go(*copies):
        for c in copies:
            c.start()
            pending.append(c)

    def owner(tq, corq, xq):
        return (2 * (tq // 2) + corq) * 4 + 2 * (tq % 2) + xq

    me = owner(t, core, x)

    def columns_of(a, tq):
        return sources[a].at[:, pl.ds(column_start(a, tq), WIDTHS[a])]

    def gain_a(j):
        return remote(gain_in, ga.at[j], sg.at[j], rg.at[j], members[j])

    def gain_b(i):
        return remote(gsum.at[i], gsum.at[2 + i], sg.at[RING + i], rg.at[RING + i], (across, sibling)[i])

    def q_first(j, a, wait=False):
        tq = member[j]
        dst = wq_in.at[owner(tq, core, x) if wait else me, :, pl.ds((a - 2) * HD, HD)]
        return remote(columns_of(a, tq), dst, q1.at[j, a - 2], t1.at[j, a - 2], members[j])

    def q_second(j, wait=False):
        i = owner(member[j], core, 1 - x if wait else x)
        return remote(wq_in.at[i], wq_in.at[i], q2.at[j], t2.at[j], across)

    def q_third(j, flip, wait=False):
        i = owner(member[j], 1 - core if wait else core, 1 - x if flip else x)
        return remote(wq_in.at[i], wq_in.at[i], q3.at[j, flip], t3.at[j, flip], sibling)

    def first(j, a, wait=False):
        tq = member[j]
        dst = w_gu.at[owner(tq, core, x) if wait else me, :, pl.ds(a * UNITS, UNITS)]
        return remote(columns_of(a, tq), dst, s1.at[j, a], r1.at[j, a], members[j])

    def second(j, wait=False):
        i = owner(member[j], core, 1 - x if wait else x)
        return remote(own if j == 0 else w_gu.at[i], w_gu.at[i], s2.at[j], r2.at[j], across)

    def third(j, flip, wait=False):
        i = owner(member[j], 1 - core if wait else core, 1 - x if flip else x)
        return remote(own if (j, flip) == (0, 0) else w_gu.at[i], w_gu.at[i], s3.at[j, flip], r3.at[j, flip], sibling)

    def start_round(j):
        go(first(j, 0), first(j, 1))

    def end_round(j):
        first(j, 0, True).wait_recv()
        first(j, 1, True).wait_recv()
        go(second(j), third(j, 0))

    def end_across(j):
        second(j, True).wait_recv()
        go(third(j, 1))

    gather = SlotGather(ring, ags, agr)

    def block_of(slot):
        if slot == 0:
            return p
        if slot == 7:
            return (p + 4) % RING
        s = (slot + 1) // 2
        return (p + (RING - s if slot % 2 else s)) % RING

    def place(slot, act):
        yq, zq = ring_yz(block_of(slot))
        src, dst = ring.at[pl.ds(slot * TOK, TOK)], seq.at[2 * zq + core]

        @pl.when(yq == core)
        def _():
            c = pltpu.make_async_copy(src, dst, load.at[6 + slot])
            c.start() if act == 0 else c.wait()

        @pl.when(yq != core)
        def _():
            c = remote(src, dst, pls.at[zq], plr.at[zq], sibling)
            c.start() if act == 0 else c.wait_send()

    pair = ((down, d_ref), (out, wo))
    mine = 2 * y + x

    def rows_out(xq, a, act):
        src, dst = pair[a][0], pair[a][1].at[mine]
        to_self = (x == core) & (y == core) & (xq == x)

        @pl.when(to_self)
        def _():
            if a == 0:
                c = pltpu.make_async_copy(relay, dst, load.at[5])
            else:
                c = pltpu.make_async_copy(src, dst, load.at[4])
            c.start() if act == 0 else c.wait()

        @pl.when(jnp.logical_not(to_self))
        def _():
            c = remote(src, dst, s4.at[xq, a], r4.at[y, a], device(z, x, core, xq))
            c.start() if act == 0 else c.wait_send()

    def rows_on(yq, a):
        src, dst = pair[a][0], pair[a][1].at[2 * yq + core]
        from_self = (core == y) & (yq == y) & (core == x)

        @pl.when(from_self)
        def _():
            if a == 0:
                pltpu.make_async_copy(relay, dst, load.at[5]).wait()
            else:
                pltpu.make_async_copy(src, dst, load.at[4]).wait()

        @pl.when(jnp.logical_not(from_self))
        def _():
            remote(src, dst, s4.at[0, a], r4.at[yq, a], sibling).wait_recv()

        go(remote(dst, dst, s5.at[yq, a], r5.at[yq, a], sibling))

    locals_ = [pltpu.make_async_copy(columns_of(a, t), wq_in.at[me, :, pl.ds((a - 2) * HD, HD)], load.at[a]) for a in (2, 3)]
    locals_.append(pltpu.make_async_copy(columns_of(4, t), wq_in.at[me, :, pl.ds(2 * HD, HD)], load.at[14]))
    locals_ += [pltpu.make_async_copy(columns_of(a, t), own.at[:, pl.ds(a * UNITS, UNITS)], load.at[a]) for a in (0, 1)]
    relay_load = pltpu.make_async_copy(down, relay, load.at[15])
    for c in locals_:
        c.start()
    relay_load.start()
    ring[0:TOK] = block[...]
    gather.step(0)
    go(*[gain_a(j) for j in range(1, RING)])
    for j in range(1, RING):
        go(*[q_first(j, a) for a in (2, 3, 4)])
    for c in locals_:
        c.wait()
    go(q_second(0), q_third(0, 0))
    for xq in (0, 1):
        rows_out(xq, 1, 0)
    keep_own = pltpu.make_async_copy(own, w_gu.at[me], load.at[16])
    keep_own.start()
    go(second(0), third(0, 0))
    place(0, 0)
    gsum[0] = jnp.zeros(gsum.shape[1:], F32)
    gsum[0, :, window(me)] = gain_in[...]
    for j in range(1, RING):
        gain_a(j).wait_recv()
        lanes = window(owner(member[j], core, x))
        gsum[0, :, lanes] = gsum[0, :, lanes] + ga[j]
    go(gain_b(0))
    gather.step(1)
    place(1, 0)
    place(2, 0)
    gain_b(0).wait_recv()
    gsum[1] = gsum[0] + gsum[2]
    go(gain_b(1))
    for j in range(1, RING):
        for a in (2, 3, 4):
            q_first(j, a, True).wait_recv()
        go(q_second(j), q_third(j, 0))
    for yq in (0, 1):
        rows_on(yq, 1)
    gather.step(2)
    place(3, 0)
    place(4, 0)
    gain_b(1).wait_recv()
    gain_o[...] = (gsum[1] + gsum[3])[:, 0:D]
    for j in range(RING):
        q_second(j, True).wait_recv()
        go(q_third(j, 1))
    gather.step(3)
    place(5, 0)
    place(6, 0)
    start_round(4)
    start_round(5)
    start_round(1)
    relay_load.wait()
    for xq in (0, 1):
        rows_out(xq, 0, 0)
    end_across(0)
    for j in range(RING):
        for flip in (0, 1):
            q_third(j, flip, True).wait_recv()

    def join(g, carry):
        pieces = [wq_in[4 * g + i].astype(F32) for i in range(4)]
        wq[pl.ds(pl.multiple_of(288 * g, 16), 288)] = jnp.concatenate(pieces, axis=0).astype(BF)
        return carry

    lax.fori_loop(0, 8, join, 0)
    gather.finish()
    place(7, 0)
    for zq in range(NZ):
        dst = seq.at[2 * zq + 1 - core]
        remote(dst, dst, pls.at[zq], plr.at[zq], sibling).wait_recv()
    for slot in range(RING):
        place(slot, 1)
    end_round(1)
    start_round(2)

    factor = 1.0 + gain_o[0:1]

    def norm(c, carry):
        for half in range(2):
            rows = pl.ds(half * 64, 64)
            seq[c, rows] = (rms_parts(seq[c, rows].astype(F32))[1] * factor).astype(BF)
        return carry

    lax.fori_loop(0, RING, norm, 0)
    keep_hidden = pltpu.make_async_copy(seq, hidden_o, load.at[17])
    keep_hidden.start()
    for i in range(4):
        r = pl.ds(i * 256, 256)
        rows = seq[2 * i : 2 * i + 2].reshape(256, -1)
        tabs = (cos[r], sine[r])
        q_o[r] = (rotate(fold_rows(rows, wq[:, 0:HD]), *tabs) * (HD ** (-0.5))).astype(BF)
        k_o[r] = rotate(fold_rows(rows, wq[:, HD : 2 * HD]), *tabs).astype(BF)
        v_o[r] = fold_rows(rows, wq[:, 2 * HD : 3 * HD]).astype(BF)
    end_round(4)
    start_round(6)
    end_across(1)

    def swap(zq, kept):
        where = pl.ds(pl.multiple_of(slot_of(ring_index(core, zq), p) * TOK, TOK), TOK)
        if kept:
            return pltpu.make_async_copy(seq_part.at[2 * zq + core], part.at[where], load.at[18 + zq])
        return remote(seq_part.at[2 * zq + 1 - core], part.at[where], sws.at[zq], swr.at[zq], sibling)

    def swapped(zq):
        where = pl.ds(pl.multiple_of(slot_of(ring_index(1 - core, zq), p) * TOK, TOK), TOK)
        return remote(seq_part.at[0], part.at[where], sws.at[zq], swr.at[zq], sibling)

    for yq in (0, 1):
        remote(out, wo.at[2 * yq + 1 - core], s5.at[yq, 1], r5.at[yq, 1], sibling).wait_recv()
    for i in range(4):
        r, upto = pl.ds(i * 256, 256), (i + 1) * 256
        bent = jnp.tanh(contract_cols(q_o[r], k_o[0:upto]) / CAP)
        seen = lax.broadcasted_iota(jnp.int32, bent.shape, 1) <= i * 256 + lax.broadcasted_iota(jnp.int32, bent.shape, 0)
        weights = jnp.where(seen, jnp.exp(CAP * bent), 0.0)
        inverse = 1.0 / jnp.sum(weights, axis=-1, keepdims=True)
        attended = fold_rows(weights.astype(BF), v_o[0:upto]) * inverse
        inv_o[r] = inverse
        att_o[r] = attended
        attended_b = attended.astype(BF)

        def columns(cols):
            sums = fold_rows(attended_b, wo[:, :, cols].reshape(HD, 768))
            seq_part[2 * i, :, cols] = sums[0:TOK].astype(BF)
            seq_part[2 * i + 1, :, cols] = sums[TOK:].astype(BF)

        tiles(3, 768, columns)
        swap(i, True).start()
        swap(i, False).start()
        if i == 0:
            end_round(2)
            start_round(3)
        if i == 2:
            end_round(5)
            start_round(7)
            end_across(2)
            for yq in (0, 1):
                rows_on(yq, 0)
    for zq in range(NZ):
        swap(zq, True).wait()
        swapped(zq).wait_recv()
    scatter = SlotScatter(part, buf, rss, rsr)
    scatter.step(0)
    end_round(3)
    end_across(4)
    scatter.step(1)
    end_round(6)
    end_across(5)
    end_across(3)
    scatter.step(2)
    end_round(7)
    end_across(6)
    scatter.step(3)
    branch_o[...] = part[0:TOK].astype(F32)
    end_across(7)
    scatter.finish(branch_o)

    for j in range(RING):
        for flip in (0, 1):
            third(j, flip, True).wait_recv()
    for yq in (0, 1):
        remote(down, d_ref.at[2 * yq + 1 - core], s5.at[yq, 0], r5.at[yq, 0], sibling).wait_recv()
    for xq in (0, 1):
        for a in (0, 1):
            to_self = (x == core) & (y == core) & (xq == x)

            @pl.when(jnp.logical_not(to_self))
            def _():
                remote(pair[a][0], pair[a][1].at[mine], s4.at[xq, a], r4.at[y, a], device(z, x, core, xq)).wait_send()
    keep_own.wait()
    keep_hidden.wait()
    for zq in range(NZ):
        swap(zq, False).wait_send()
    gather.drain()
    scatter.drain()
    for c in pending:
        c.wait_send()


def forward(gate, up, query, key, value, down, out, block, gains, cos_tab, sine_tab, collective_id):
    n = 4 * RING
    rows, width = block.shape
    shard, total = gate.shape[0], RING * block.shape[0]

    def full(*shape, dtype=BF):
        return jax.ShapeDtypeStruct(shape, dtype)

    blocks = (RING, rows, width)
    return pl.pallas_call(
        forward_kernel,
        out_shape=[
            full(n, shard, 2 * UNITS), full(4, *down.shape), full(*blocks), full(width, 3 * HD), full(4, *out.shape),
            full(8, D, dtype=F32), full(total, HD), full(total, HD), full(total, HD),
            full(total, HD, dtype=F32), full(total, 1, dtype=F32), full(rows, width, dtype=F32),
        ],
        in_specs=[HBM] * 7 + [VMEM] * 4,
        out_specs=[HBM] * 3 + [VMEM] * 9,
        scratch_shapes=[
            pltpu.VMEM((total, width), BF), pltpu.VMEM(blocks, BF), pltpu.VMEM(blocks, BF), pltpu.VMEM((total, width), BF),
            pltpu.VMEM((2, 4, rows, width), BF), pltpu.VMEM((n, shard, 3 * HD), BF),
            pltpu.VMEM((shard, 2 * UNITS), BF), pltpu.VMEM(down.shape, BF),
            pltpu.VMEM((RING,) + gains.shape, F32), pltpu.VMEM((4, 8, PADDED), F32),
            DMA((22,)),
            DMA((2, 4, SUB)), DMA((2, 4, SUB)), DMA((NZ,)), DMA((NZ,)), DMA((2, 4, SUB)), DMA((2, 4, SUB)), DMA((NZ,)), DMA((NZ,)),
            DMA((RING, 2)), DMA((RING, 2)), DMA((RING,)), DMA((RING,)), DMA((RING, 2)), DMA((RING, 2)),
            DMA((RING, 3)), DMA((RING, 3)), DMA((RING,)), DMA((RING,)), DMA((RING, 2)), DMA((RING, 2)),
            DMA((2, 2)), DMA((2, 2)), DMA((2, 2)), DMA((2, 2)), DMA((RING + 2,)), DMA((RING + 2,)),
        ],
        compiler_params=params(collective_id, 60),
    )(gate, up, query, key, value, down, out, block, gains, cos_tab, sine_tab)


ROUNDS = (4, 5, 6, 7, 2, 3, 1, 0)
AHEAD = 2


def backward_kernel(d_branch, gu_in, down_in, hidden, wq, wo, q_in, k_in, v_in, att, inv, cos, sine, normed, gain_in,
                    d_hid_o, gain_o, c_gu, c_q, down_o, out_o,
                    ring, seq, part, buf, d_att, d_qkv, dk, dv, grad_q, aq, bq,
                    own, a_gu, b_gu, down_own, da, db, og, oa, ob, ga, gsum,
                    load, ags, agr, pls, plr, rss, rsr, sws, swr, s1, r1, s2, r2, s3, r3,
                    q1, t1, q2, t2, q3, t3, sx, rx, sg, rg):
    z, core, y, x = my_place()
    t, p = 2 * z + y, ring_index(y, z)
    sibling, across = device(z, 1 - core, y, x), device(z, core, y, 1 - x)
    diagonal = device(z, 1 - core, 1 - y, x)
    members = [member_place(partner(t, j), core, x) for j in range(RING)]
    order = [partner(t, j) for j in ROUNDS]
    greet(members[1:] + [sibling, across, diagonal])
    pending = []

    def go(*copies):
        for c in copies:
            c.start()
            pending.append(c)

    def owner(tq, corq, xq):
        return (2 * (tq // 2) + corq) * 4 + 2 * (tq % 2) + xq

    side_x = (1 - x, x)

    def gu_a(side, j):
        src = gu_in.at[owner(order[j], 1 - core, side_x[side])]
        return remote(src, a_gu.at[side, j], s1.at[side, j], r1.at[side, j], sibling)

    def gu_own(side, j):
        return pltpu.make_async_copy(gu_in.at[owner(order[j], core, side_x[side])], own.at[j % 2], load.at[j % 2])

    def gu_b(j):
        return remote(a_gu.at[0, j], b_gu.at[j], s2.at[j], r2.at[j], across)

    def gu_c(j, wait=False):
        dst = c_gu.at[order[j] if wait else t]
        if ROUNDS[j] == 0:
            return pltpu.make_async_copy(a_gu.at[1, j], dst, load.at[2])
        return remote(a_gu.at[1, j], dst, s3.at[j], r3.at[j], members[ROUNDS[j]])

    def sum_own(side, j, more=None):
        gu_own(side, j).wait()
        gu_a(side, j).wait_recv()
        total = a_gu[side, j].astype(F32) + own[j % 2].astype(F32)
        if more is not None:
            total = total + more[j].astype(F32)
        a_gu[side, j] = total.astype(BF)

    def pump(first, last):
        for j in range(first, last):
            gu_own(1, j).start()
        for j in range(first, last):
            gu_b(j).wait_recv()
            if j + AHEAD < RING:
                go(gu_b(j + AHEAD))
            sum_own(1, j, b_gu)

    small = ((down_in, down_own, da, db, down_o), (og, None, oa, ob, out_o))

    def small_a(a, xo):
        return remote(small[a][0].at[2 * (1 - core) + xo], small[a][2].at[xo], sx.at[a, xo], rx.at[a, xo], sibling)

    def small_b(a):
        return remote(small[a][2].at[1 - x], small[a][3], sx.at[a, 2], rx.at[a, 2], across)

    def small_c(a, act):
        src, dst = small[a][2].at[x], small[a][4]

        @pl.when(core == y)
        def _():
            c = pltpu.make_async_copy(src, dst, load.at[3 + a])
            c.start() if act == 0 else c.wait()

        @pl.when(core != y)
        def _():
            c = remote(src, dst, sx.at[a, 3], rx.at[a, 3], diagonal)
            c.start() if act == 0 else c.wait()

    def q_a(side, j):
        src = grad_q.at[owner(order[j], 1 - core, side_x[side])]
        return remote(src, aq.at[side, j], q1.at[side, j], t1.at[side, j], sibling)

    def q_b(j):
        return remote(grad_q.at[owner(order[j], core, 1 - x)], bq.at[j], q2.at[j], t2.at[j], across)

    def q_c(j, wait=False):
        src, dst = grad_q.at[owner(order[j], core, x)], c_q.at[order[j] if wait else t]
        if ROUNDS[j] == 0:
            return pltpu.make_async_copy(src, dst, load.at[5])
        return remote(src, dst, q3.at[j], t3.at[j], members[ROUNDS[j]])

    def gain_a():
        return remote(gain_in, gsum.at[2], sg.at[RING], rg.at[RING], sibling)

    def gain_b():
        return remote(gsum.at[0], gsum.at[3], sg.at[RING + 1], rg.at[RING + 1], across)

    def gain_c(j):
        lanes = window(owner(partner(t, j), core, x))
        return remote(gsum.at[1, :, lanes], ga.at[j], sg.at[j], rg.at[j], members[j])

    gather = SlotGather(ring, ags, agr)

    def block(slot):
        if slot == 0:
            return p
        if slot == 7:
            return (p + 4) % RING
        s = (slot + 1) // 2
        return (p + (RING - s if slot % 2 else s)) % RING

    def place(slot, act):
        yq, zq = ring_yz(block(slot))
        src, dst = ring.at[pl.ds(slot * TOK, TOK)], seq.at[2 * zq + core]

        @pl.when(yq == core)
        def _():
            c = pltpu.make_async_copy(src, dst, load.at[6 + slot])
            c.start() if act == 0 else c.wait()

        @pl.when(yq != core)
        def _():
            c = remote(src, dst, pls.at[zq], plr.at[zq], sibling)
            c.start() if act == 0 else c.wait_send()

    first = pltpu.make_async_copy(d_branch, ring.at[pl.ds(0, TOK)], load.at[14])
    first.start()
    first.wait()
    gather.step(0)
    place(0, 0)
    for side in (0, 1):
        go(*[gu_a(side, j) for j in range(RING)])
        if side == 0:
            go(small_a(0, 0), small_a(0, 1))
    for j in range(RING):
        if j < 2:
            gu_own(0, j).start()
        sum_own(0, j)
        if j + 2 < RING:
            gu_own(0, j + 2).start()
        if j < AHEAD:
            go(gu_b(j))

    def down_sum(xo):
        c = pltpu.make_async_copy(down_in.at[2 * core + xo], down_own, load.at[16])
        c.start()
        small_a(0, xo).wait_recv()
        c.wait()
        da[xo] = (da[xo].astype(F32) + down_own[...].astype(F32)).astype(BF)

    down_sum(0)
    gather.step(1)
    place(1, 0)
    place(2, 0)
    pump(0, 1)
    down_sum(1)
    pump(1, 2)
    gather.step(2)
    place(3, 0)
    place(4, 0)
    pump(2, 4)
    gather.step(3)
    place(5, 0)
    place(6, 0)
    pump(4, 5)
    gather.finish()
    place(7, 0)
    for j in range(5):
        go(gu_c(j))
    for zq in range(NZ):
        dst = seq.at[2 * zq + 1 - core]
        remote(dst, dst, pls.at[zq], plr.at[zq], sibling).wait_recv()
    for slot in range(RING):
        place(slot, 1)
    gather.drain()
    hidden_load = pltpu.make_async_copy(hidden, ring, load.at[14])
    hidden_load.start()

    for c in range(0, RING, 2):
        rows = pl.ds(c * TOK, 2 * TOK)
        d_att[rows] = contract_cols(seq[c : c + 2].reshape(2 * TOK, -1), wo[...]).astype(BF)

    def out_columns(cols):
        value = contract_rows(att[...].astype(BF), seq[:, :, cols].reshape(RING * TOK, 768))
        for f in range(4):
            og[f, :, cols] = value[64 * f : 64 * (f + 1)].astype(BF)

    tiles(3, 768, out_columns)
    go(small_a(1, 0), small_a(1, 1))
    pump(5, 6)
    go(gu_c(5))
    dk[...] = jnp.zeros_like(dk)
    dv[...] = jnp.zeros_like(dv)
    for i in range(4):
        r, upto = pl.ds(i * 256, 256), (i + 1) * 256
        keys, vals, query = k_in[0:upto], v_in[0:upto], q_in[r]
        bent = jnp.tanh(contract_cols(query, keys) / CAP)
        seen = lax.broadcasted_iota(jnp.int32, bent.shape, 1) <= i * 256 + lax.broadcasted_iota(jnp.int32, bent.shape, 0)
        weights = jnp.where(seen, jnp.exp(CAP * bent), 0.0)
        grad = d_att[r].astype(F32)
        delta = jnp.sum(grad * att[r], axis=-1, keepdims=True)
        d_probs = contract_cols(d_att[r], vals)
        d_raw = (weights * inv[r] * (d_probs - delta) * (1.0 - bent * bent)).astype(BF)
        dq = fold_rows(d_raw, keys) * (HD ** (-0.5))
        d_qkv[r, 0:HD] = unrotate(dq, cos[r], sine[r]).astype(BF)
        dk[0:upto] = dk[0:upto] + contract_rows(d_raw, query)
        scaled = grad * inv[r]
        high = scaled.astype(BF)
        rest = (scaled - high.astype(F32)).astype(BF)
        weights_b = weights.astype(BF)
        dv[0:upto] = dv[0:upto] + contract_rows(weights_b, high) + contract_rows(weights_b, rest)
        if i == 1:
            pump(6, 7)
            go(gu_c(6))
            go(small_b(0))
        if i == 3:
            pump(7, 8)
            go_self = gu_c(7)
            go_self.start()
    d_qkv[:, HD : 2 * HD] = unrotate(dk[...], cos[...], sine[...]).astype(BF)
    d_qkv[:, 2 * HD : 3 * HD] = dv[...].astype(BF)

    scatter = SlotScatter(part, buf, rss, rsr)

    def swap(zq, kept):
        where = pl.ds(pl.multiple_of(slot_of(ring_index(core, zq), p) * TOK, TOK), TOK)
        if kept:
            return pltpu.make_async_copy(seq.at[2 * zq + core], part.at[where], load.at[17 + zq])
        return remote(seq.at[2 * zq + 1 - core], part.at[where], sws.at[zq], swr.at[zq], sibling)

    def swapped(zq):
        where = pl.ds(pl.multiple_of(slot_of(ring_index(1 - core, zq), p) * TOK, TOK), TOK)
        return remote(seq.at[0], part.at[where], sws.at[zq], swr.at[zq], sibling)

    for zq in range(NZ):
        rows = d_qkv[2 * zq * TOK : (2 * zq + 2) * TOK]

        def columns(cols):
            value = contract_cols(rows, wq[cols])
            seq[2 * zq, :, cols] = value[0:TOK].astype(BF)
            seq[2 * zq + 1, :, cols] = value[TOK:].astype(BF)

        tiles(3, 768, columns)
        swap(zq, True).start()
        swap(zq, False).start()
    for zq in range(NZ):
        swap(zq, True).wait()
        swapped(zq).wait_recv()
    scatter.step(0)

    hidden_load.wait()

    def grad_half(half):
        def columns(cols):
            value = contract_rows(ring[:, pl.ds(half * 1152, 1152)], d_qkv[:, cols])
            for i in range(16):
                grad_q[half * 16 + i, :, cols] = value[72 * i : 72 * (i + 1)].astype(BF)

        tiles(3, 256, columns)

    grad_half(0)
    scatter.step(1)
    grad_half(1)
    for side in (0, 1):
        go(*[q_a(side, j) for j in range(RING)])
    for xo in (0, 1):
        small_a(1, xo).wait_recv()
        oa[xo] = (oa[xo].astype(F32) + og[2 * core + xo].astype(F32)).astype(BF)
    go(small_b(1))
    scatter.step(2)

    def q_sum(side, j):
        i = owner(order[j], core, side_x[side])
        q_a(side, j).wait_recv()
        total = grad_q[i].astype(F32) + aq[side, j].astype(F32)
        if side == 1:
            q_b(j).wait_recv()
            total = total + bq[j].astype(F32)
        grad_q[i] = total.astype(BF)

    for j in range(RING):
        q_sum(0, j)
        if j < AHEAD:
            go(q_b(j))
    small_b(0).wait_recv()
    da[x] = (da[x].astype(F32) + db[...].astype(F32)).astype(BF)
    small_c(0, 0)
    scatter.step(3)

    def q_round(j):
        q_sum(1, j)
        if j + AHEAD < RING:
            go(q_b(j + AHEAD))
        if ROUNDS[j] == 0:
            q_c(j).start()
        else:
            go(q_c(j))

    for j in range(4):
        q_round(j)
    small_b(1).wait_recv()
    oa[x] = (oa[x].astype(F32) + ob[...].astype(F32)).astype(BF)
    small_c(1, 0)

    def own_part(cols):
        slot = part[0:TOK, cols]
        d_hid_o[:, cols] = slot.astype(F32)

    tiles(3, 768, own_part)
    for j in range(4, RING):
        q_round(j)
    scatter.finish(d_hid_o)
    gain_in[0:1, 0:D] = jnp.sum(d_hid_o[...] * normed[...], axis=0, keepdims=True)
    go(gain_a())
    gain_a().wait_recv()
    gsum[0] = gain_in[...] + gsum[2]
    go(gain_b())
    gain_b().wait_recv()
    gsum[1] = gsum[0] + gsum[3]
    go(*[gain_c(j) for j in range(1, RING)])
    total = gsum[1, :, window(owner(t, core, x))]
    for j in range(1, RING):
        gain_c(j).wait_recv()
        total = total + ga[j]
    gain_o[...] = total

    for j in range(RING):
        if ROUNDS[j] == 0:
            gu_c(j).wait()
            q_c(j).wait()
        else:
            gu_c(j, True).wait_recv()
            q_c(j, True).wait_recv()
    small_c(0, 1)
    small_c(1, 1)
    for zq in range(NZ):
        swap(zq, False).wait_send()
    scatter.drain()
    for c in pending:
        c.wait_send()


def backward(d_branch, gu, down, hidden, w_qkv, w_out, queries, keys, values, attended, inv_total, cos_tab, sine_tab,
             normed_pre, gain_parts, collective_id):
    n = 4 * RING
    rows, width = d_branch.shape
    shard = gu.shape[0] // n
    gu = gu.reshape(n, shard, 2 * UNITS)
    down = down.reshape(4, -1, width)
    total, down_rows, out_rows = RING * rows, down.shape[1], w_out.shape[0] // 4
    gain_shape = (8, PADDED)

    def out(*shape, dtype=BF):
        return jax.ShapeDtypeStruct(shape, dtype)

    def body(*refs):
        ins, rest = refs[:14], refs[14:]
        gains_ref, rest = rest[0], rest[1:]
        outs, scr = rest[:6], rest[6:]
        gain_scr = scr[0]
        gain_scr[...] = gains_ref[...]
        backward_kernel(*ins, gain_scr, *outs, *scr[1:])

    return pl.pallas_call(
        body,
        out_shape=[
            out(rows, width, dtype=F32), out(8, WINDOW, dtype=F32),
            out(RING, shard, 2 * UNITS), out(RING, shard, 3 * HD),
            out(down_rows, width), out(out_rows, width),
        ],
        in_specs=[HBM] * 4 + [VMEM] * 11,
        out_specs=[VMEM] * 2 + [HBM] * 4,
        scratch_shapes=[
            pltpu.VMEM(gain_shape, F32),
            pltpu.VMEM((total, width), BF), pltpu.VMEM((RING, rows, width), BF), pltpu.VMEM((total, width), BF),
            pltpu.VMEM((2, 4, rows, width), BF),
            pltpu.VMEM((total, HD), BF), pltpu.VMEM((total, 3 * HD), BF),
            pltpu.VMEM((total, HD), F32), pltpu.VMEM((total, HD), F32),
            pltpu.VMEM((n, shard, 3 * HD), BF), pltpu.VMEM((2, RING, shard, 3 * HD), BF), pltpu.VMEM((RING, shard, 3 * HD), BF),
            pltpu.VMEM((2, shard, 2 * UNITS), BF), pltpu.VMEM((2, RING, shard, 2 * UNITS), BF), pltpu.VMEM((RING, shard, 2 * UNITS), BF),
            pltpu.VMEM((down_rows, width), BF), pltpu.VMEM((2, down_rows, width), BF), pltpu.VMEM((down_rows, width), BF),
            pltpu.VMEM((4, out_rows, width), BF), pltpu.VMEM((2, out_rows, width), BF), pltpu.VMEM((out_rows, width), BF),
            pltpu.VMEM((RING, 8, WINDOW), F32), pltpu.VMEM((4,) + gain_shape, F32),
            DMA((21,)),
            DMA((2, 4, SUB)), DMA((2, 4, SUB)), DMA((NZ,)), DMA((NZ,)), DMA((2, 4, SUB)), DMA((2, 4, SUB)), DMA((NZ,)), DMA((NZ,)),
            DMA((2, RING)), DMA((2, RING)), DMA((RING,)), DMA((RING,)), DMA((RING,)), DMA((RING,)),
            DMA((2, RING)), DMA((2, RING)), DMA((RING,)), DMA((RING,)), DMA((RING,)), DMA((RING,)),
            DMA((2, 4)), DMA((2, 4)), DMA((RING + 2,)), DMA((RING + 2,)),
        ],
        compiler_params=params(collective_id, 60),
    )(d_branch, gu, down, hidden, w_qkv, w_out, queries, keys, values, attended, inv_total, cos_tab, sine_tab, normed_pre, gain_parts)


def results_kernel(gu, qkv, down, out, d_hidden, d_middle, normed, inverse, factor,
                   gate_o, up_o, query_o, key_o, value_o, down_o, out_o, token_o):
    for i in range(2):
        units, heads = pl.ds(i * UNITS, UNITS), pl.ds(i * HD, HD)
        gate_o[:, units] = gu[i, :, 0:UNITS].astype(F32)
        up_o[:, units] = gu[i, :, UNITS : 2 * UNITS].astype(F32)
        query_o[:, heads] = qkv[i, :, 0:HD].astype(F32)
    key_o[...] = qkv[0, :, HD : 2 * HD].astype(F32) + qkv[1, :, HD : 2 * HD].astype(F32)
    value_o[...] = qkv[0, :, 2 * HD :].astype(F32) + qkv[1, :, 2 * HD :].astype(F32)
    down_o[...] = down[...].astype(F32)
    out_o[...] = out[...].astype(F32)
    back = norm_back(d_hidden[...] * factor[...], normed[...], inverse[...])
    token_o[...] = (d_middle[...] + back).astype(BF)


def results(gu, qkv, down, out, d_hidden, d_middle, normed, inverse, factor):
    steps = RING // 2
    shard, width = gu.shape[1], down.shape[1]
    tok, down_rows, out_rows = d_hidden.shape[0] // steps, down.shape[0] // steps, out.shape[0] // steps

    def rows(n, wide):
        return pl.BlockSpec((n, wide), lambda i: (i, 0))

    def columns(wide):
        return pl.BlockSpec((shard, wide), lambda i: (0, i))

    def full(*shape):
        return jax.ShapeDtypeStruct(shape, F32)

    return pl.pallas_call(
        results_kernel,
        grid=(steps,),
        out_shape=[
            full(shard, FF), full(shard, FF), full(shard, H * HD), full(shard, KVH * HD), full(shard, KVH * HD),
            full(*down.shape), full(*out.shape), jax.ShapeDtypeStruct(d_hidden.shape, BF),
        ],
        in_specs=[
            pl.BlockSpec((2, shard, 2 * UNITS), lambda i: (i, 0, 0)), pl.BlockSpec((2, shard, 3 * HD), lambda i: (i, 0, 0)),
            rows(down_rows, width), rows(out_rows, width), rows(tok, width), rows(tok, width), rows(tok, width),
            rows(tok, 1), pl.BlockSpec((1, width), lambda i: (0, 0)),
        ],
        out_specs=[
            columns(2 * UNITS), columns(2 * UNITS), columns(2 * HD), columns(HD), columns(HD),
            rows(down_rows, width), rows(out_rows, width), rows(tok, width),
        ],
        compiler_params=pltpu.CompilerParams(vmem_limit_bytes=60 * 2**20),
    )(gu, qkv, down, out, d_hidden, d_middle, normed, inverse, factor)


def on_ring(
    tokens, w_query, w_key, w_value, w_out, w_gate, w_up, w_down,
    pre_gain, post_gain, pre_ffn_gain, post_ffn_gain, out_grad,
):
    ids = iter(range(32))
    length = RING * tokens.shape[1]
    shard_gain = pre_gain.shape[0]
    mine = lax.axis_index("ctx") * 4 + lax.axis_index("fsdp")
    gains = jnp.stack([pre_gain, post_gain, pre_ffn_gain, post_ffn_gain]).astype(F32)
    gains = lax.dynamic_update_slice(jnp.zeros((8, WINDOW), F32), gains, (0, (mine * shard_gain) % 128))
    cos_tab, sine_tab = rope_tables(jnp.arange(length, dtype=jnp.int32), HD)
    w_gu, down_in, hidden, w_qkv, out_in, gains, queries, keys, values, attended, inv_total, branch = forward(
        w_gate, w_up, w_query, w_key, w_value, w_down, w_out, tokens[0], gains, cos_tab, sine_tab, next(ids)
    )
    w_gu, hidden = w_gu.reshape(D, 2 * UNITS), hidden.reshape(length, D)
    w_dn = down_in.reshape(UNITS, D)
    w_ot = out_in.reshape(HD, D)
    pre_factor, post_factor, pre_ffn_factor, post_ffn_factor = (1.0 + gains[i] for i in range(4))
    resid_in = tokens[0].astype(F32)
    inv_pre, normed_pre = rms_parts(resid_in)
    inv_post, normed_post = rms_parts(branch)
    middle = resid_in + normed_post * post_factor
    inv_mid, normed_mid = rms_parts(middle)
    hidden_ffn = (normed_mid * pre_ffn_factor).astype(BF)
    output, d_hidden_ffn, post_ffn_part, down_part, gu_part = feed_forward(
        hidden_ffn, middle, post_ffn_factor[None], out_grad[0], w_gu, w_dn, next(ids)
    )
    post_ffn_part = post_ffn_part[0]
    out_cot = out_grad[0].astype(F32)
    pre_ffn_part = jnp.sum(d_hidden_ffn * normed_mid, axis=0)
    d_middle = out_cot + norm_back(d_hidden_ffn * pre_ffn_factor, normed_mid, inv_mid)
    post_part = jnp.sum(d_middle * normed_post, axis=0)
    d_branch = norm_back(d_middle * post_factor, normed_post, inv_post).astype(BF)
    gain_parts = jnp.stack([jnp.zeros_like(post_part), post_part, pre_ffn_part, post_ffn_part])
    d_hidden, gain_g, gu_g, qkv_g, down_g, out_g = backward(
        d_branch, gu_part, down_part, hidden, w_qkv, w_ot, queries, keys, values, attended, inv_total,
        cos_tab, sine_tab, normed_pre, jnp.pad(gain_parts, ((0, 4), (0, PADDED - D))), next(ids),
    )
    gate_g, up_g, query_g, key_g, value_g, down_g, out_g, token_grad = results(
        gu_g, qkv_g, down_g, out_g, d_hidden, d_middle, normed_pre, inv_pre, pre_factor[None]
    )
    gain_g = lax.dynamic_slice(gain_g, (0, (mine * shard_gain) % 128), (4, shard_gain))
    return (
        output[None], token_grad[None],
        query_g, key_g, value_g, out_g, gate_g, up_g, down_g,
        gain_g[0], gain_g[1], gain_g[2], gain_g[3],
    )


ROW_FOLD = 4


def head_tables(positions, width):
    half_width = width // 2
    inv_freqs = ROPE_BASE ** (-jnp.arange(half_width, dtype=jnp.float32) * 2.0 / width)
    angles = positions.astype(jnp.float32)[:, None] * inv_freqs[None, :]
    return (jnp.cos(angles)[:, None, :], jnp.sin(angles)[:, None, :])


def rotate_heads(heads_in, cos_tab, sine_tab):
    half_width = heads_in.shape[-1] // 2
    front_half = heads_in[..., :half_width]
    back_half = heads_in[..., half_width:]
    return jnp.concatenate(
        [front_half * cos_tab - back_half * sine_tab, back_half * cos_tab + front_half * sine_tab],
        axis=-1,
    )


def unrotate_heads(grad_in, cos_tab, sine_tab):
    half_width = grad_in.shape[-1] // 2
    front_half = grad_in[..., :half_width]
    back_half = grad_in[..., half_width:]
    return jnp.concatenate(
        [front_half * cos_tab + back_half * sine_tab, back_half * cos_tab - front_half * sine_tab],
        axis=-1,
    )


def to_groups(flat_heads, tok_rows, q_group):
    shaped = flat_heads.reshape(tok_rows, KVH, q_group, HD)
    return jnp.transpose(shaped, (1, 2, 0, 3)).reshape(KVH, q_group * tok_rows, HD)


def from_groups(grouped, tok_rows, q_group):
    shaped = grouped.reshape(KVH, q_group, tok_rows, HD)
    return jnp.transpose(shaped, (2, 0, 1, 3)).reshape(tok_rows, KVH * q_group * HD)


def grad_rows(left, right, folding, count):
    block = contract_rows(left, right)
    return block.reshape(count, right.shape[1] // folding)


def blockwise(step_fn, carry, piece, width):
    key_count = piece[0].shape[0]
    n_steps = key_count // width
    stacked = tuple((member.reshape(n_steps, width, member.shape[1]) for member in piece))

    def one_step(partial_value, block_item):
        block_index, members = block_item
        return (step_fn(partial_value, members, block_index * width), None)

    carry, unused = lax.scan(one_step, carry, (jnp.arange(n_steps, dtype=jnp.int32), stacked))
    return carry


def block_grads(query_g, query_pos, d_att_g, delta, inv_tot, key_block, value_block, key_first):
    key_count = key_block.shape[0]
    key_grp = key_block.reshape(key_count, KVH, HD)
    value_grp = value_block.reshape(key_count, KVH, HD)
    raw_scores = jnp.einsum("grd,ngd->grn", query_g, key_grp, preferred_element_type=jnp.float32)
    capped = CAP * jnp.tanh(raw_scores / CAP)
    key_pos = key_first + jnp.arange(key_count, dtype=jnp.int32)
    allowed = key_pos[None, None, :] <= query_pos[None, :, None]
    weights = jnp.where(allowed, jnp.exp(capped), 0.0)
    prob_rows = weights * inv_tot[..., None]
    d_probs = jnp.einsum("grd,ngd->grn", d_att_g, value_grp, preferred_element_type=jnp.float32)
    slope = 1.0 - capped / CAP * (capped / CAP)
    d_raw = (prob_rows * (d_probs - delta[..., None]) * slope).astype(jnp.bfloat16)
    d_query = jnp.einsum("grn,ngd->grd", d_raw, key_grp, preferred_element_type=jnp.float32)
    d_key = jnp.einsum("grn,grd->ngd", d_raw, query_g, preferred_element_type=jnp.float32)
    weights_b = weights.astype(jnp.bfloat16)
    d_scaled = d_att_g.astype(jnp.float32) * inv_tot[..., None]
    scaled_high = d_scaled.astype(jnp.bfloat16)
    scaled_rest = (d_scaled - scaled_high.astype(jnp.float32)).astype(jnp.bfloat16)
    d_value = jnp.einsum("grn,grd->ngd", weights_b, scaled_high, preferred_element_type=jnp.float32)
    d_value = d_value + jnp.einsum(
        "grn,grd->ngd", weights_b, scaled_rest, preferred_element_type=jnp.float32
    )
    return (d_query, d_key.reshape(key_count, KVH * HD), d_value.reshape(key_count, KVH * HD))


def on_any_mesh(
    tokens,
    w_query,
    w_key,
    w_value,
    w_out,
    w_gate,
    w_up,
    w_down,
    pre_gain,
    post_gain,
    pre_ffn_gain,
    post_ffn_gain,
    out_grad,
):
    tok_rows = tokens.shape[1]
    q_group = H // KVH
    q_scale = HD ** (-0.5)
    width_q = H * HD
    width_kv = KVH * HD
    width_qkv = width_q + 2 * width_kv
    n_ctx = lax.axis_size("ctx")
    my_block = lax.axis_index("ctx")
    my_start = my_block * tok_rows
    positions = my_start + jnp.arange(tok_rows, dtype=jnp.int32)
    cos_tab, sine_tab = head_tables(positions, HD)
    row_pos = jnp.tile(positions, q_group)
    last_pos = my_start + tok_rows - 1
    resid_in = tokens[0].astype(jnp.float32)
    qkv_shard = jnp.concatenate([w_query, w_key, w_value], axis=1)
    gateup_shard = jnp.concatenate([w_gate, w_up], axis=1)
    shard_rows = qkv_shard.shape[0]
    gains_shard = jnp.stack([pre_gain, post_gain, pre_ffn_gain, post_ffn_gain])
    full_gains, full_qkv, full_out = (
        lax.all_gather(gains_shard, ("ctx", "fsdp"), axis=1, tiled=True),
        lax.all_gather(qkv_shard, ("ctx", "fsdp"), axis=0, tiled=True),
        lax.all_gather(w_out, ("ctx", "fsdp"), axis=0, tiled=True),
    )
    factors = 1.0 + full_gains.astype(jnp.float32)
    pre_factor, post_factor, pre_ffn_factor, post_ffn_factor = (
        factors[0],
        factors[1],
        factors[2],
        factors[3],
    )
    inv_pre, normed_pre = rms_parts(resid_in)
    hidden = (normed_pre * pre_factor).astype(jnp.bfloat16)
    projected = jnp.dot(hidden, full_qkv, preferred_element_type=jnp.float32)
    query_lin = projected[:, :width_q].reshape(tok_rows, H, HD)
    queries = (
        (rotate_heads(query_lin, cos_tab, sine_tab) * q_scale)
        .astype(jnp.bfloat16)
        .reshape(tok_rows, width_q)
    )
    query_grp = to_groups(queries, tok_rows, q_group)
    key_lin = projected[:, width_q : width_q + width_kv].reshape(tok_rows, KVH, HD)
    key_rows = rotate_heads(key_lin, cos_tab, sine_tab).astype(jnp.bfloat16).reshape(tok_rows, width_kv)
    value_rows = projected[:, width_q + width_kv :].astype(jnp.bfloat16)

    def add_block(partial_value, piece, first_row):
        key_block, value_block = piece

        def add_compute_block(state):
            row_total, weighted = state
            key_count = key_block.shape[0]
            key_grp = key_block.reshape(key_count, KVH, HD)
            raw_scores = jnp.einsum(
                "grd,ngd->grn", query_grp, key_grp, preferred_element_type=jnp.float32
            )
            capped = CAP * jnp.tanh(raw_scores / CAP)
            key_pos = first_row + jnp.arange(key_count, dtype=jnp.int32)
            allowed = key_pos[None, None, :] <= row_pos[None, :, None]
            weights = jnp.where(allowed, jnp.exp(capped), 0.0)
            value_grp = value_block.reshape(key_count, KVH, HD)
            weighted = weighted + jnp.einsum(
                "grn,ngd->grd",
                weights.astype(jnp.bfloat16),
                value_grp,
                preferred_element_type=jnp.float32,
            )
            return (row_total + jnp.sum(weights, axis=-1), weighted)

        def add_skip_block(state):
            return state

        return lax.cond(first_row <= last_pos, add_compute_block, add_skip_block, partial_value)

    start_state = (
        jnp.zeros((KVH, q_group * tok_rows), jnp.float32),
        jnp.zeros((KVH, q_group * tok_rows, HD), jnp.float32),
    )
    row_total, weighted = blockwise(
        add_block,
        start_state,
        (
            lax.all_gather(key_rows, "ctx", axis=0, tiled=True),
            lax.all_gather(value_rows, "ctx", axis=0, tiled=True),
        ),
        512,
    )
    inv_total = 1.0 / row_total
    attended_grp = weighted * inv_total[..., None]
    attended_b = from_groups(attended_grp, tok_rows, q_group).astype(jnp.bfloat16)
    branch = jnp.dot(attended_b, full_out, preferred_element_type=jnp.float32)
    inv_post, normed_post = rms_parts(branch)
    middle = resid_in + normed_post * post_factor
    inv_mid, normed_mid = rms_parts(middle)
    hidden_ffn = (normed_mid * pre_ffn_factor).astype(jnp.bfloat16)
    gate_up = fold_rows(
        hidden_ffn, lax.all_gather(gateup_shard, ("ctx", "fsdp"), axis=0, tiled=True)
    )
    gate_lin = gate_up[:, :FF]
    up_lin = gate_up[:, FF:]
    active = gated(gate_lin, up_lin).astype(jnp.bfloat16)
    ffn_branch = fold_rows(active, lax.all_gather(w_down, ("ctx", "fsdp"), axis=0, tiled=True))
    inv_ffn, normed_ffn = rms_parts(ffn_branch)
    output = (middle + normed_ffn * post_ffn_factor).astype(jnp.bfloat16)
    out_cot = out_grad[0].astype(jnp.float32)
    post_ffn_part = jnp.sum(out_cot * normed_ffn, axis=0)
    d_ffn_b = norm_back(out_cot * post_ffn_factor, normed_ffn, inv_ffn).astype(jnp.bfloat16)
    down_total = lax.psum_scatter(
        grad_rows(active, d_ffn_b, 1, lax.axis_size(("ctx", "fsdp")) * w_down.shape[0]),
        ("ctx", "fsdp"),
        scatter_dimension=0,
        tiled=True,
    )
    d_active = contract_cols(d_ffn_b, lax.all_gather(w_down, ("ctx", "fsdp"), axis=0, tiled=True))
    unused_value, gate_pull = jax.vjp(gated, gate_lin, up_lin)
    d_gate, d_up = gate_pull(d_active)
    d_gateup_b = jnp.concatenate([d_gate.astype(jnp.bfloat16), d_up.astype(jnp.bfloat16)], axis=1)
    gateup_folded = lax.psum_scatter(
        grad_rows(
            hidden_ffn,
            d_gateup_b,
            ROW_FOLD,
            lax.axis_size(("ctx", "fsdp")) * (ROW_FOLD * shard_rows),
        ),
        ("ctx", "fsdp"),
        scatter_dimension=0,
        tiled=True,
    )
    gateup_total = gateup_folded.reshape(shard_rows, 2 * FF)
    d_hidden_ffn = contract_cols(
        d_gateup_b, lax.all_gather(gateup_shard, ("ctx", "fsdp"), axis=0, tiled=True)
    )
    pre_ffn_part = jnp.sum(d_hidden_ffn * normed_mid, axis=0)
    d_middle = out_cot + norm_back(d_hidden_ffn * pre_ffn_factor, normed_mid, inv_mid)
    back_qkv, back_out = (
        lax.all_gather(qkv_shard, ("ctx", "fsdp"), axis=0, tiled=True),
        lax.all_gather(w_out, ("ctx", "fsdp"), axis=0, tiled=True),
    )
    post_gain_part = jnp.sum(d_middle * normed_post, axis=0)
    d_branch_b = norm_back(d_middle * post_factor, normed_post, inv_post).astype(jnp.bfloat16)
    w_out_part = contract_rows(attended_b, d_branch_b)
    d_attended = contract_cols(d_branch_b, back_out).astype(jnp.bfloat16)
    d_att_grp = to_groups(d_attended, tok_rows, q_group)
    row_delta = jnp.sum(d_att_grp.astype(jnp.float32) * attended_grp, axis=-1)
    zero_rows = jnp.zeros((tok_rows, width_kv), jnp.float32)
    zero_query = jnp.zeros((KVH, q_group * tok_rows, HD), jnp.float32)
    block_ids = jnp.arange(n_ctx, dtype=jnp.int32)
    all_keys, all_values = (
        lax.all_gather(key_rows, "ctx", axis=0, tiled=True),
        lax.all_gather(value_rows, "ctx", axis=0, tiled=True),
    )

    def returned_step(acc_query, block_item):
        block_index, key_block, value_block = block_item
        first_row = block_index * tok_rows

        def returned_compute_block(acc_in):
            d_query, d_key, d_value = block_grads(
                query_grp,
                row_pos,
                d_att_grp,
                row_delta,
                inv_total,
                key_block,
                value_block,
                first_row,
            )
            return (acc_in + d_query, (d_key, d_value))

        def returned_skip_block(acc_in):
            return (acc_in, (zero_rows, zero_rows))

        return lax.cond(
            first_row <= last_pos, returned_compute_block, returned_skip_block, acc_query
        )

    key_blocks = all_keys.reshape(n_ctx, tok_rows, width_kv)
    value_blocks = all_values.reshape(n_ctx, tok_rows, width_kv)
    d_query_grp, key_terms = lax.scan(
        returned_step, zero_query, (block_ids, key_blocks, value_blocks)
    )
    key_term_rows = key_terms[0].reshape(n_ctx * tok_rows, width_kv)
    value_term_rows = key_terms[1].reshape(n_ctx * tok_rows, width_kv)
    d_keys, d_values = (
        lax.psum_scatter(
            key_term_rows.astype(jnp.bfloat16), "ctx", scatter_dimension=0, tiled=True
        ).astype(jnp.float32),
        lax.psum_scatter(
            value_term_rows.astype(jnp.bfloat16), "ctx", scatter_dimension=0, tiled=True
        ).astype(jnp.float32),
    )
    d_query_flat = from_groups(d_query_grp, tok_rows, q_group).reshape(tok_rows, H, HD) * q_scale
    dq_lin = (
        unrotate_heads(d_query_flat, cos_tab, sine_tab).astype(jnp.bfloat16).reshape(tok_rows, width_q)
    )
    dk_lin = (
        unrotate_heads(d_keys.reshape(tok_rows, KVH, HD), cos_tab, sine_tab)
        .astype(jnp.bfloat16)
        .reshape(tok_rows, width_kv)
    )
    dv_lin = d_values.astype(jnp.bfloat16)
    dqkv_b = jnp.concatenate([dq_lin, dk_lin, dv_lin], axis=1)
    d_hidden = contract_cols(dqkv_b, back_qkv)
    qkv_part = contract_rows(hidden, dqkv_b).reshape(ROW_FOLD * D, width_qkv // ROW_FOLD)
    pre_gain_part = jnp.sum(d_hidden * normed_pre, axis=0)
    token_grad = d_middle + norm_back(d_hidden * pre_factor, normed_pre, inv_pre)
    gain_parts = jnp.stack([pre_gain_part, post_gain_part, pre_ffn_part, post_ffn_part])
    qkv_folded, out_total, gain_totals = (
        lax.psum_scatter(qkv_part, ("ctx", "fsdp"), scatter_dimension=0, tiled=True),
        lax.psum_scatter(w_out_part, ("ctx", "fsdp"), scatter_dimension=0, tiled=True),
        lax.psum_scatter(gain_parts, ("ctx", "fsdp"), scatter_dimension=1, tiled=True),
    )
    qkv_total = qkv_folded.reshape(shard_rows, width_qkv)
    return (
        output[None],
        token_grad.astype(jnp.bfloat16)[None],
        qkv_total[:, :width_q],
        qkv_total[:, width_q : width_q + width_kv],
        qkv_total[:, width_q + width_kv :],
        out_total,
        gateup_total[:, :FF],
        gateup_total[:, FF:],
        down_total,
        gain_totals[0],
        gain_totals[1],
        gain_totals[2],
        gain_totals[3],
    )


def solution(mesh):
    ring = mesh.shape["ctx"] == RING and mesh.shape["fsdp"] == 4
    tokens, rows, gains = P("fsdp", "ctx", None), P(("ctx", "fsdp"), None), P(("ctx", "fsdp"))
    return jax.shard_map(
        on_ring if ring else on_any_mesh,
        mesh=mesh,
        in_specs=(tokens,) + (rows,) * 7 + (gains,) * 4 + (tokens,),
        out_specs=(tokens, tokens) + (rows,) * 7 + (gains,) * 4,
        check_vma=False,
    )
```

```python
import functools

import jax
import jax.numpy as jnp
import numpy as np
from jax import lax
from jax.experimental import pallas as pl
from jax.experimental.pallas import tpu as pltpu
from jax.sharding import PartitionSpec as P

D = 2304
H = 8
KVH = 4
HD = 256
CAP = 50
FF = 9216

EPSILON = 1e-06
ROPE_BASE = 10000.0

MESH = pl.DeviceIdType.MESH
HBM = pl.BlockSpec(memory_space=pl.ANY)
VMEM = pl.BlockSpec(memory_space=pltpu.VMEM)
DMA = pltpu.SemaphoreType.DMA
BF = jnp.bfloat16
F32 = jnp.float32


def rope_tables(positions, width):
    half_width = width // 2
    inv_freqs = ROPE_BASE ** (-jnp.arange(half_width, dtype=F32) * 2.0 / width)
    angles = positions.astype(F32)[:, None] * inv_freqs[None, :]
    return (jnp.cos(angles), jnp.sin(angles))


def constant_tables(length, width):
    exponents = -np.arange(width // 2, dtype=np.float32) * np.float32(2.0) / np.float32(width)
    inv_freqs = np.power(np.float32(ROPE_BASE), exponents, dtype=np.float32)
    angles = np.arange(length, dtype=np.float32)[:, None] * inv_freqs[None, :]
    return np.cos(angles), np.sin(angles)


def rotate(rows, cos_tab, sine_tab):
    half_width = rows.shape[-1] // 2
    front, back = rows[..., :half_width], rows[..., half_width:]
    return jnp.concatenate(
        [front * cos_tab - back * sine_tab, back * cos_tab + front * sine_tab], axis=-1
    )


def unrotate(rows, cos_tab, sine_tab):
    half_width = rows.shape[-1] // 2
    front, back = rows[..., :half_width], rows[..., half_width:]
    return jnp.concatenate(
        [front * cos_tab + back * sine_tab, back * cos_tab - front * sine_tab], axis=-1
    )


def rms_parts(values_in):
    inverse = lax.rsqrt(jnp.mean(values_in * values_in, axis=-1, keepdims=True) + EPSILON)
    return (inverse, values_in * inverse)


def norm_back(grad_normed, normed, inverse):
    return inverse * (grad_normed - normed * jnp.mean(grad_normed * normed, axis=-1, keepdims=True))


def contract_rows(left, right):
    return lax.dot_general(left, right, (((0,), (0,)), ((), ())), preferred_element_type=F32)


def contract_cols(left, right):
    return lax.dot_general(left, right, (((1,), (1,)), ((), ())), preferred_element_type=F32)


def fold_rows(left, right):
    return jnp.dot(left, right, preferred_element_type=F32)


def gated(gate_in, up_in):
    return jax.nn.gelu(gate_in, approximate=True) * up_in


NZ = 4
RING = 2 * NZ


def my_place():
    c, f = lax.axis_index("ctx"), lax.axis_index("fsdp")
    return c // 2, c % 2, f // 2, f % 2


def ring_index(y, z):
    return z + y * (RING - 1 - 2 * z)


def ring_yz(q):
    y = q // NZ
    return y, q + y * (RING - 1 - 2 * q)


def device(z, core, y, x):
    return (2 * z + core, 2 * y + x)


def ring_device(q, core, x):
    y, z = ring_yz(q)
    return device(z, core, y, x)


def remote(src, dst, send_sem, recv_sem, where):
    return pltpu.make_async_remote_copy(
        src_ref=src,
        dst_ref=dst,
        send_sem=send_sem,
        recv_sem=recv_sem,
        device_id=where,
        device_id_type=MESH,
    )


def greet(places, meanwhile=None):
    barrier = pltpu.get_barrier_semaphore()
    for place in places:
        pl.semaphore_signal(barrier, inc=1, device_id=place, device_id_type=MESH)
    if meanwhile is not None:
        meanwhile()
    pl.semaphore_wait(barrier, len(places))


def params(collective_id, vmem_mib=56):
    return pltpu.CompilerParams(
        collective_id=collective_id,
        has_side_effects=True,
        vmem_limit_bytes=vmem_mib * 2**20,
    )


SUB = 4


def ring_parts(direction, step, half_step):
    if step != half_step:
        return list(range(SUB))
    half = SUB // 2
    return list(range(half)) if direction == 0 else list(range(half, SUB))


TOK = 128
UNITS = FF // RING
TILE = 128
GELU_K = 0.7978845608028654
GELU_A = 0.044715


class SlotGather:
    def __init__(self, buf, ss, rs):
        z, core, y, x = my_place()
        p = ring_index(y, z)
        self.buf, self.ss, self.rs = buf, ss, rs
        self.near = (ring_device((p + 1) % RING, core, x), ring_device((p + RING - 1) % RING, core, x))
        self.pending = []

    def copy(self, direction, step, k):
        piece = TOK // SUB
        src = 0 if step == 0 else 2 * step - 1 + direction
        dst = 7 if step == 3 else 2 * step + 1 + direction
        return remote(
            self.buf.at[pl.ds(src * TOK + k * piece, piece)],
            self.buf.at[pl.ds(dst * TOK + k * piece, piece)],
            self.ss.at[direction, step, k],
            self.rs.at[direction, step, k],
            self.near[direction],
        )

    def step(self, step):
        for k in range(SUB):
            for direction in (0, 1):
                if step > 0:
                    self.copy(direction, step - 1, k).wait_recv()
                if k in ring_parts(direction, step, 3):
                    c = self.copy(direction, step, k)
                    c.start()
                    self.pending.append(c)

    def finish(self):
        for direction in (0, 1):
            for k in ring_parts(direction, 3, 3):
                self.copy(direction, 3, k).wait_recv()

    def drain(self):
        for c in self.pending:
            c.wait_send()


class SlotScatter:
    def __init__(self, part, buf, ss, rs):
        z, core, y, x = my_place()
        p = ring_index(y, z)
        self.part, self.buf, self.ss, self.rs = part, buf, ss, rs
        self.near = (ring_device((p + 1) % RING, core, x), ring_device((p + RING - 1) % RING, core, x))
        self.pending = []

    def copy(self, direction, step, k, src):
        rows = pl.ds(k * (TOK // SUB), TOK // SUB)
        return remote(
            src,
            self.buf.at[direction, step, rows],
            self.ss.at[direction, step, k],
            self.rs.at[direction, step, k],
            self.near[direction],
        )

    def step(self, step):
        piece = TOK // SUB
        for k in range(SUB):
            rows = pl.ds(k * piece, piece)
            for direction in (0, 1):
                if k not in ring_parts(direction, step, 0):
                    continue
                slot = 7 if step == 0 else 2 * (4 - step) - direction
                mine = pl.ds(slot * TOK + k * piece, piece)
                src = self.part.at[mine]
                if step > 0 and k in ring_parts(direction, step - 1, 0):
                    src = self.buf.at[direction, step - 1, rows]
                    self.copy(direction, step - 1, k, src).wait_recv()
                    src[...] = (src[...].astype(F32) + self.part[mine].astype(F32)).astype(BF)
                c = self.copy(direction, step, k, src)
                c.start()
                self.pending.append(c)

    def finish(self, total):
        for k in range(SUB):
            rows = pl.ds(k * (TOK // SUB), TOK // SUB)
            for direction in (0, 1):
                src = self.buf.at[direction, 3, rows]
                self.copy(direction, 3, k, src).wait_recv()
                total[rows] = total[rows] + src[...].astype(F32)

    def drain(self):
        for c in self.pending:
            c.wait_send()


def tiles(count, width, body):
    def step(i, carry):
        body(pl.ds(pl.multiple_of(i * width, width), width))
        return carry

    lax.fori_loop(0, count, step, 0)


def gelu_parts(v):
    bent = jnp.tanh(GELU_K * (v + GELU_A * (v * v * v)))
    value = 0.5 * v * (1.0 + bent)
    slope = 0.5 * (1.0 + bent) + 0.5 * v * (1.0 - bent * bent) * (GELU_K * (1.0 + 3.0 * GELU_A * (v * v)))
    return value, slope


PAIRS = ((128, 256), (384, 256), (640, 256))
LAST = (896, 128)
OWN = (0, 128)


def by_rows(body):
    def step(i, carry):
        body(pl.ds(pl.multiple_of(i * 16, 16), 16))
        return carry

    lax.fori_loop(0, TOK // 16, step, 0)


def feed_forward_kernel(branch, block, gains, cot, w_hbm, wd_hbm,
                        out_o, d_mid_o, d_branch_o, gain_o, wd_grad, gu_grad,
                        wgu, wd, ha, gu, act, part, buf, df, dgu, middle, total, stage,
                        w_sem, ags, agr, rss, rsr, out_sem):
    gather = [SlotGather(b, ags.at[i], agr.at[i]) for i, b in enumerate((ha, df))]
    scatter = [SlotScatter(part, buf, rss.at[i], rsr.at[i]) for i in range(2)]
    loads = [
        pltpu.make_async_copy(w_hbm, wgu, w_sem.at[0]),
        pltpu.make_async_copy(wd_hbm, wd, w_sem.at[1]),
    ]
    for c in loads:
        c.start()

    def head():
        def rows(r):
            mid = block[r].astype(F32) + rms_parts(branch[r])[1] * (1.0 + gains[1:2])
            middle[r] = mid
            ha[r] = (rms_parts(mid)[1] * (1.0 + gains[2:3])).astype(BF)

        by_rows(rows)

    greet(gather[0].near, head)
    gather[0].step(0)
    gain_o[...] = jnp.zeros(gain_o.shape, F32)
    loads[0].wait()

    def gate_up(first, count):
        rows = pl.ds(first, count)

        def column(cols):
            gu[rows, cols] = fold_rows(ha[rows], wgu[:, cols])

        tiles(3, 768, column)

        def finish(i, carry):
            r = pl.ds(pl.multiple_of(first + i * 32, 32), 32)
            act[r] = (gelu_parts(gu[r, 0:UNITS])[0] * gu[r, UNITS : 2 * UNITS]).astype(BF)
            return carry

        lax.fori_loop(0, count // 32, finish, 0)

    def down_part(first, count, dst):
        def column(cols):
            value = fold_rows(act[pl.ds(first, count)], wd[:, cols])
            dst[pl.ds(first, count), cols] = value.astype(dst.dtype)

        tiles(3, 768, column)

    def active_back(first, count):
        rows = pl.ds(first, count)
        for n in range(3):
            cols, up_cols = pl.ds(n * 384, 384), pl.ds(UNITS + n * 384, 384)
            d_active = contract_cols(df[rows], wd[cols])
            value, slope = gelu_parts(gu[rows, cols])
            dgu[rows, cols] = (d_active * gu[rows, up_cols] * slope).astype(BF)
            dgu[rows, up_cols] = (d_active * value).astype(BF)

    def hidden_part(first, count, dst):
        def column(cols):
            value = contract_cols(dgu[pl.ds(first, count)], wgu[cols])
            dst[pl.ds(first, count), cols] = value.astype(dst.dtype)

        tiles(3, 768, column)

    n_down = UNITS // TILE

    def grad_out(i):
        slot = i % 2
        if i < n_down:
            return pltpu.make_async_copy(stage.at[slot], wd_grad.at[pl.ds(i * TILE, TILE)], out_sem.at[slot])
        return pltpu.make_async_copy(stage.at[slot], gu_grad.at[pl.ds((i - n_down) * TILE, TILE)], out_sem.at[slot])

    def grad_tiles(first, last):
        for i in range(first, last):
            if i >= 2:
                grad_out(i - 2).wait()
            if i < n_down:
                value = contract_rows(act[:, pl.ds(i * TILE, TILE)], df[...])
            else:
                value = contract_rows(ha[:, pl.ds((i - n_down) * TILE, TILE)], dgu[...])
            stage[i % 2] = value.astype(BF)
            grad_out(i).start()

    gate_up(*OWN)
    for step, pair in enumerate(PAIRS):
        gather[0].step(step + 1)
        if step == 0:
            loads[1].wait()
        gate_up(*pair)
    gather[0].finish()
    gate_up(*LAST)
    down_part(*LAST, part)
    scatter[0].step(0)
    for step, pair in enumerate(PAIRS[::-1]):
        down_part(*pair, part)
        scatter[0].step(step + 1)
    down_part(*OWN, total)
    scatter[0].finish(total)
    gather[0].drain()
    scatter[0].drain()

    def turn(r):
        inverse, normed = rms_parts(total[r])
        df[r] = norm_back(cot[r].astype(F32) * (1.0 + gains[3:4]), normed, inverse).astype(BF)

    def add_gain(i, value):
        gain_o[i : i + 1, 0:D] = gain_o[i : i + 1, 0:D] + jnp.sum(value, axis=0, keepdims=True)

    def outputs(r):
        normed = rms_parts(total[r])[1]
        out_o[r] = (middle[r] + normed * (1.0 + gains[3:4])).astype(BF)
        add_gain(3, cot[r].astype(F32) * normed)

    by_rows(turn)
    gather[1].step(0)
    by_rows(outputs)
    active_back(*OWN)
    for step, pair in enumerate(PAIRS):
        gather[1].step(step + 1)
        active_back(*pair)
    gather[1].finish()
    active_back(*LAST)
    hidden_part(*LAST, part)
    scatter[1].step(0)
    done = 0
    for step, pair in enumerate(PAIRS[::-1]):
        hidden_part(*pair, part)
        scatter[1].step(step + 1)
        grad_tiles(done, done + 8 + step // 2)
        done += 8 + step // 2
    hidden_part(*OWN, total)
    n_tiles = n_down + ha.shape[1] // TILE
    grad_tiles(done, n_tiles)
    scatter[1].finish(total)

    def tail(r):
        inv_mid, normed_mid = rms_parts(middle[r])
        d_hidden = total[r]
        add_gain(2, d_hidden * normed_mid)
        d_mid = cot[r].astype(F32) + norm_back(d_hidden * (1.0 + gains[2:3]), normed_mid, inv_mid)
        d_mid_o[r] = d_mid
        inv_post, normed_post = rms_parts(branch[r])
        add_gain(1, d_mid * normed_post)
        d_branch_o[r] = norm_back(d_mid * (1.0 + gains[1:2]), normed_post, inv_post).astype(BF)

    by_rows(tail)
    for i in (n_tiles - 2, n_tiles - 1):
        grad_out(i).wait()
    gather[1].drain()
    scatter[1].drain()


def feed_forward(branch, block, gains, out_grad, w_in, w_down, collective_id):
    rows, width = branch.shape
    total = RING * rows

    def full(*shape, dtype=F32):
        return jax.ShapeDtypeStruct(shape, dtype)

    return pl.pallas_call(
        feed_forward_kernel,
        out_shape=[
            full(rows, width, dtype=BF), full(rows, width), full(rows, width, dtype=BF), full(8, PADDED),
            full(UNITS, width, dtype=BF), full(width, 2 * UNITS, dtype=BF),
        ],
        in_specs=[VMEM] * 4 + [HBM] * 2,
        out_specs=[VMEM] * 4 + [HBM] * 2,
        scratch_shapes=[
            pltpu.VMEM((width, 2 * UNITS), BF), pltpu.VMEM((UNITS, width), BF),
            pltpu.VMEM((total, width), BF), pltpu.VMEM((total, 2 * UNITS), F32), pltpu.VMEM((total, UNITS), BF),
            pltpu.VMEM((total, width), BF), pltpu.VMEM((2, 4, rows, width), BF),
            pltpu.VMEM((total, width), BF), pltpu.VMEM((total, 2 * UNITS), BF),
            pltpu.VMEM((rows, width), F32), pltpu.VMEM((rows, width), F32), pltpu.VMEM((2, TILE, width), BF),
            DMA((2,)),
            DMA((2, 2, 4, SUB)), DMA((2, 2, 4, SUB)), DMA((2, 2, 4, SUB)), DMA((2, 2, 4, SUB)),
            DMA((2,)),
        ],
        compiler_params=params(collective_id, 60),
    )(branch, block, gains, out_grad, w_in, w_down)


WIDTHS = (UNITS, UNITS, HD, HD, HD)


SHARD = D // (4 * RING)
PADDED = D + 128
WINDOW = 256


def window(i):
    return pl.ds(pl.multiple_of((SHARD * i) // 128 * 128, 128), WINDOW)


def member_place(t, core, x):
    return device(t // 2, core, t % 2, x)


def slot_of(q, p):
    d = (q - p + RING) % RING
    return jnp.where(d == 0, 0, jnp.where(d < 4, 2 * d, jnp.where(d == 4, 7, 15 - 2 * d)))


def partner(t, j):
    out = 0
    for bit in (1, 2, 4):
        on = (t // bit) % 2
        out = out + bit * (1 - on if j & bit else on)
    return out


def column_start(which, t):
    if which < 2:
        return pl.multiple_of(t * UNITS, 128)
    return pl.multiple_of((t if which == 2 else t // 2) * HD, 128)


def forward_kernel(gate, up, query, key, value, down, out, block, gain_in, cos, sine,
                   w_gu, d_ref, hidden_o, wq, wo, gain_o, q_o, k_o, v_o, att_o, inv_o, branch_o,
                   ring, seq, seq_part, part, buf, wq_in, own, relay, ga, gsum,
                   load, ags, agr, pls, plr, rss, rsr, sws, swr, s1, r1, s2, r2, s3, r3,
                   q1, t1, q2, t2, q3, t3, s4, r4, s5, r5, sg, rg):
    z, core, y, x = my_place()
    t, p = 2 * z + y, ring_index(y, z)
    sibling, across = device(z, 1 - core, y, x), device(z, core, y, 1 - x)
    member = [partner(t, j) for j in range(RING)]
    members = [member_place(tq, core, x) for tq in member]
    plane = []
    for dc in (0, 1):
        for dy in (0, 1):
            for dx in (0, 1):
                if (dc, dx) != (0, 0):
                    plane.append(device(z, (core + dc) % 2, (y + dy) % 2, (x + dx) % 2))
    greet(members[1:] + plane)
    sources = (gate, up, query, key, value)
    pending = []

    def go(*copies):
        for c in copies:
            c.start()
            pending.append(c)

    def owner(tq, corq, xq):
        return (2 * (tq // 2) + corq) * 4 + 2 * (tq % 2) + xq

    me = owner(t, core, x)

    def columns_of(a, tq):
        return sources[a].at[:, pl.ds(column_start(a, tq), WIDTHS[a])]

    def gain_a(j):
        return remote(gain_in, ga.at[j], sg.at[j], rg.at[j], members[j])

    def gain_b(i):
        return remote(gsum.at[i], gsum.at[2 + i], sg.at[RING + i], rg.at[RING + i], (across, sibling)[i])

    def q_first(j, a, wait=False):
        tq = member[j]
        dst = wq_in.at[owner(tq, core, x) if wait else me, :, pl.ds((a - 2) * HD, HD)]
        return remote(columns_of(a, tq), dst, q1.at[j, a - 2], t1.at[j, a - 2], members[j])

    def q_second(j, wait=False):
        i = owner(member[j], core, 1 - x if wait else x)
        return remote(wq_in.at[i], wq_in.at[i], q2.at[j], t2.at[j], across)

    def q_third(j, flip, wait=False):
        i = owner(member[j], 1 - core if wait else core, 1 - x if flip else x)
        return remote(wq_in.at[i], wq_in.at[i], q3.at[j, flip], t3.at[j, flip], sibling)

    def first(j, a, wait=False):
        tq = member[j]
        dst = w_gu.at[owner(tq, core, x) if wait else me, :, pl.ds(a * UNITS, UNITS)]
        return remote(columns_of(a, tq), dst, s1.at[j, a], r1.at[j, a], members[j])

    def second(j, wait=False):
        i = owner(member[j], core, 1 - x if wait else x)
        return remote(own if j == 0 else w_gu.at[i], w_gu.at[i], s2.at[j], r2.at[j], across)

    def third(j, flip, wait=False):
        i = owner(member[j], 1 - core if wait else core, 1 - x if flip else x)
        return remote(own if (j, flip) == (0, 0) else w_gu.at[i], w_gu.at[i], s3.at[j, flip], r3.at[j, flip], sibling)

    def start_round(j):
        go(first(j, 0), first(j, 1))

    def end_round(j):
        first(j, 0, True).wait_recv()
        first(j, 1, True).wait_recv()
        go(second(j), third(j, 0))

    def end_across(j):
        second(j, True).wait_recv()
        go(third(j, 1))

    gather = SlotGather(ring, ags, agr)

    def block_of(slot):
        if slot == 0:
            return p
        if slot == 7:
            return (p + 4) % RING
        s = (slot + 1) // 2
        return (p + (RING - s if slot % 2 else s)) % RING

    def place(slot, act):
        yq, zq = ring_yz(block_of(slot))
        src, dst = ring.at[pl.ds(slot * TOK, TOK)], seq.at[2 * zq + core]

        @pl.when(yq == core)
        def _():
            c = pltpu.make_async_copy(src, dst, load.at[6 + slot])
            c.start() if act == 0 else c.wait()

        @pl.when(yq != core)
        def _():
            c = remote(src, dst, pls.at[zq], plr.at[zq], sibling)
            c.start() if act == 0 else c.wait_send()

    pair = ((down, d_ref), (out, wo))
    mine = 2 * y + x

    def rows_out(xq, a, act):
        src, dst = pair[a][0], pair[a][1].at[mine]
        to_self = (x == core) & (y == core) & (xq == x)

        @pl.when(to_self)
        def _():
            if a == 0:
                c = pltpu.make_async_copy(relay, dst, load.at[5])
            else:
                c = pltpu.make_async_copy(src, dst, load.at[4])
            c.start() if act == 0 else c.wait()

        @pl.when(jnp.logical_not(to_self))
        def _():
            c = remote(src, dst, s4.at[xq, a], r4.at[y, a], device(z, x, core, xq))
            c.start() if act == 0 else c.wait_send()

    def rows_on(yq, a):
        src, dst = pair[a][0], pair[a][1].at[2 * yq + core]
        from_self = (core == y) & (yq == y) & (core == x)

        @pl.when(from_self)
        def _():
            if a == 0:
                pltpu.make_async_copy(relay, dst, load.at[5]).wait()
            else:
                pltpu.make_async_copy(src, dst, load.at[4]).wait()

        @pl.when(jnp.logical_not(from_self))
        def _():
            remote(src, dst, s4.at[0, a], r4.at[yq, a], sibling).wait_recv()

        go(remote(dst, dst, s5.at[yq, a], r5.at[yq, a], sibling))

    locals_ = [pltpu.make_async_copy(columns_of(a, t), wq_in.at[me, :, pl.ds((a - 2) * HD, HD)], load.at[a]) for a in (2, 3)]
    locals_.append(pltpu.make_async_copy(columns_of(4, t), wq_in.at[me, :, pl.ds(2 * HD, HD)], load.at[14]))
    locals_ += [pltpu.make_async_copy(columns_of(a, t), own.at[:, pl.ds(a * UNITS, UNITS)], load.at[a]) for a in (0, 1)]
    relay_load = pltpu.make_async_copy(down, relay, load.at[15])
    for c in locals_:
        c.start()
    relay_load.start()
    ring[0:TOK] = block[...]
    gather.step(0)
    go(*[gain_a(j) for j in range(1, RING)])
    for j in range(1, RING):
        go(*[q_first(j, a) for a in (2, 3, 4)])
    for c in locals_:
        c.wait()
    go(q_second(0), q_third(0, 0))
    for xq in (0, 1):
        rows_out(xq, 1, 0)
    keep_own = pltpu.make_async_copy(own, w_gu.at[me], load.at[16])
    keep_own.start()
    go(second(0), third(0, 0))
    place(0, 0)
    gsum[0] = jnp.zeros(gsum.shape[1:], F32)
    gsum[0, :, window(me)] = gain_in[...]
    for j in range(1, RING):
        gain_a(j).wait_recv()
        lanes = window(owner(member[j], core, x))
        gsum[0, :, lanes] = gsum[0, :, lanes] + ga[j]
    go(gain_b(0))
    gather.step(1)
    place(1, 0)
    place(2, 0)
    gain_b(0).wait_recv()
    gsum[1] = gsum[0] + gsum[2]
    go(gain_b(1))
    for j in range(1, RING):
        for a in (2, 3, 4):
            q_first(j, a, True).wait_recv()
        go(q_second(j), q_third(j, 0))
    for yq in (0, 1):
        rows_on(yq, 1)
    gather.step(2)
    place(3, 0)
    place(4, 0)
    gain_b(1).wait_recv()
    gain_o[...] = (gsum[1] + gsum[3])[:, 0:D]
    for j in range(RING):
        q_second(j, True).wait_recv()
        go(q_third(j, 1))
    gather.step(3)
    place(5, 0)
    place(6, 0)
    start_round(4)
    start_round(5)
    start_round(1)
    relay_load.wait()
    for xq in (0, 1):
        rows_out(xq, 0, 0)
    end_across(0)
    for j in range(RING):
        for flip in (0, 1):
            q_third(j, flip, True).wait_recv()

    def join(g, carry):
        pieces = [wq_in[4 * g + i].astype(F32) for i in range(4)]
        wq[pl.ds(pl.multiple_of(288 * g, 16), 288)] = jnp.concatenate(pieces, axis=0).astype(BF)
        return carry

    lax.fori_loop(0, 8, join, 0)
    gather.finish()
    place(7, 0)
    for zq in range(NZ):
        dst = seq.at[2 * zq + 1 - core]
        remote(dst, dst, pls.at[zq], plr.at[zq], sibling).wait_recv()
    for slot in range(RING):
        place(slot, 1)
    start_round(6)
    start_round(2)
    end_round(1)

    factor = 1.0 + gain_o[0:1]

    def norm(c, carry):
        for half in range(2):
            rows = pl.ds(half * 64, 64)
            seq[c, rows] = (rms_parts(seq[c, rows].astype(F32))[1] * factor).astype(BF)
        return carry

    lax.fori_loop(0, RING, norm, 0)
    keep_hidden = pltpu.make_async_copy(seq, hidden_o, load.at[17])
    keep_hidden.start()
    for i in range(4):
        r = pl.ds(i * 256, 256)
        rows = seq[2 * i : 2 * i + 2].reshape(256, -1)
        tabs = (cos[r], sine[r])
        q_o[r] = (rotate(fold_rows(rows, wq[:, 0:HD]), *tabs) * (HD ** (-0.5))).astype(BF)
        k_o[r] = rotate(fold_rows(rows, wq[:, HD : 2 * HD]), *tabs).astype(BF)
        v_o[r] = fold_rows(rows, wq[:, 2 * HD : 3 * HD]).astype(BF)
    end_round(4)
    start_round(7)
    start_round(3)
    end_across(1)

    def swap(zq, kept):
        where = pl.ds(pl.multiple_of(slot_of(ring_index(core, zq), p) * TOK, TOK), TOK)
        if kept:
            return pltpu.make_async_copy(seq_part.at[2 * zq + core], part.at[where], load.at[18 + zq])
        return remote(seq_part.at[2 * zq + 1 - core], part.at[where], sws.at[zq], swr.at[zq], sibling)

    def swapped(zq):
        where = pl.ds(pl.multiple_of(slot_of(ring_index(1 - core, zq), p) * TOK, TOK), TOK)
        return remote(seq_part.at[0], part.at[where], sws.at[zq], swr.at[zq], sibling)

    for yq in (0, 1):
        remote(out, wo.at[2 * yq + 1 - core], s5.at[yq, 1], r5.at[yq, 1], sibling).wait_recv()
    for i in range(4):
        r, upto = pl.ds(i * 256, 256), (i + 1) * 256
        bent = jnp.tanh(contract_cols(q_o[r], k_o[0:upto]) / CAP)
        seen = lax.broadcasted_iota(jnp.int32, bent.shape, 1) <= i * 256 + lax.broadcasted_iota(jnp.int32, bent.shape, 0)
        weights = jnp.where(seen, jnp.exp(CAP * bent), 0.0)
        inverse = 1.0 / jnp.sum(weights, axis=-1, keepdims=True)
        attended = fold_rows(weights.astype(BF), v_o[0:upto]) * inverse
        inv_o[r] = inverse
        att_o[r] = attended
        attended_b = attended.astype(BF)

        def columns(cols):
            sums = fold_rows(attended_b, wo[:, :, cols].reshape(HD, 768))
            seq_part[2 * i, :, cols] = sums[0:TOK].astype(BF)
            seq_part[2 * i + 1, :, cols] = sums[TOK:].astype(BF)

        tiles(3, 768, columns)
        swap(i, True).start()
        swap(i, False).start()
        if i == 0:
            end_round(2)
        if i == 2:
            end_round(5)
            end_across(2)
            for yq in (0, 1):
                rows_on(yq, 0)
    for zq in range(NZ):
        swap(zq, True).wait()
        swapped(zq).wait_recv()
    scatter = SlotScatter(part, buf, rss, rsr)
    scatter.step(0)
    end_round(3)
    end_across(4)
    scatter.step(1)
    end_round(6)
    end_across(5)
    end_across(3)
    scatter.step(2)
    end_round(7)
    end_across(6)
    scatter.step(3)
    branch_o[...] = part[0:TOK].astype(F32)
    end_across(7)
    scatter.finish(branch_o)

    for j in range(RING):
        for flip in (0, 1):
            third(j, flip, True).wait_recv()
    for yq in (0, 1):
        remote(down, d_ref.at[2 * yq + 1 - core], s5.at[yq, 0], r5.at[yq, 0], sibling).wait_recv()
    for xq in (0, 1):
        for a in (0, 1):
            to_self = (x == core) & (y == core) & (xq == x)

            @pl.when(jnp.logical_not(to_self))
            def _():
                remote(pair[a][0], pair[a][1].at[mine], s4.at[xq, a], r4.at[y, a], device(z, x, core, xq)).wait_send()
    keep_own.wait()
    keep_hidden.wait()
    for zq in range(NZ):
        swap(zq, False).wait_send()
    gather.drain()
    scatter.drain()
    for c in pending:
        c.wait_send()


def forward(gate, up, query, key, value, down, out, block, gains, cos_tab, sine_tab, collective_id):
    n = 4 * RING
    rows, width = block.shape
    shard, total = gate.shape[0], RING * block.shape[0]

    def full(*shape, dtype=BF):
        return jax.ShapeDtypeStruct(shape, dtype)

    blocks = (RING, rows, width)
    return pl.pallas_call(
        forward_kernel,
        out_shape=[
            full(n, shard, 2 * UNITS), full(4, *down.shape), full(*blocks), full(width, 3 * HD), full(4, *out.shape),
            full(8, D, dtype=F32), full(total, HD), full(total, HD), full(total, HD),
            full(total, HD, dtype=F32), full(total, 1, dtype=F32), full(rows, width, dtype=F32),
        ],
        in_specs=[HBM] * 7 + [VMEM] * 4,
        out_specs=[HBM] * 3 + [VMEM] * 9,
        scratch_shapes=[
            pltpu.VMEM((total, width), BF), pltpu.VMEM(blocks, BF), pltpu.VMEM(blocks, BF), pltpu.VMEM((total, width), BF),
            pltpu.VMEM((2, 4, rows, width), BF), pltpu.VMEM((n, shard, 3 * HD), BF),
            pltpu.VMEM((shard, 2 * UNITS), BF), pltpu.VMEM(down.shape, BF),
            pltpu.VMEM((RING,) + gains.shape, F32), pltpu.VMEM((4, 8, PADDED), F32),
            DMA((22,)),
            DMA((2, 4, SUB)), DMA((2, 4, SUB)), DMA((NZ,)), DMA((NZ,)), DMA((2, 4, SUB)), DMA((2, 4, SUB)), DMA((NZ,)), DMA((NZ,)),
            DMA((RING, 2)), DMA((RING, 2)), DMA((RING,)), DMA((RING,)), DMA((RING, 2)), DMA((RING, 2)),
            DMA((RING, 3)), DMA((RING, 3)), DMA((RING,)), DMA((RING,)), DMA((RING, 2)), DMA((RING, 2)),
            DMA((2, 2)), DMA((2, 2)), DMA((2, 2)), DMA((2, 2)), DMA((RING + 2,)), DMA((RING + 2,)),
        ],
        compiler_params=params(collective_id, 60),
    )(gate, up, query, key, value, down, out, block, gains, cos_tab, sine_tab)


ROUNDS = (4, 5, 6, 7, 2, 3, 1, 0)
AHEAD = 2


def backward_kernel(d_branch, gu_in, down_in, hidden, wq, wo, q_in, k_in, v_in, att, inv, cos, sine, block_in, gain_in,
                    d_hid_o, gain_o, c_gu, c_q, down_o, out_o,
                    ring, seq, part, buf, d_att, d_qkv, dk, dv, grad_q, aq, bq,
                    own, a_gu, b_gu, down_own, da, db, og, oa, ob, ga, gsum,
                    load, ags, agr, pls, plr, rss, rsr, sws, swr, s1, r1, s2, r2, s3, r3,
                    q1, t1, q2, t2, q3, t3, sx, rx, sg, rg):
    z, core, y, x = my_place()
    t, p = 2 * z + y, ring_index(y, z)
    sibling, across = device(z, 1 - core, y, x), device(z, core, y, 1 - x)
    diagonal = device(z, 1 - core, 1 - y, x)
    members = [member_place(partner(t, j), core, x) for j in range(RING)]
    order = [partner(t, j) for j in ROUNDS]
    greet(members[1:] + [sibling, across, diagonal])
    pending = []

    def go(*copies):
        for c in copies:
            c.start()
            pending.append(c)

    def owner(tq, corq, xq):
        return (2 * (tq // 2) + corq) * 4 + 2 * (tq % 2) + xq

    side_x = (1 - x, x)

    def gu_a(side, j):
        src = gu_in.at[owner(order[j], 1 - core, side_x[side])]
        return remote(src, a_gu.at[side, j], s1.at[side, j], r1.at[side, j], sibling)

    def gu_own(side, j):
        return pltpu.make_async_copy(gu_in.at[owner(order[j], core, side_x[side])], own.at[j % 2], load.at[j % 2])

    def gu_b(j):
        return remote(a_gu.at[0, j], b_gu.at[j], s2.at[j], r2.at[j], across)

    def gu_c(j, wait=False):
        dst = c_gu.at[order[j] if wait else t]
        if ROUNDS[j] == 0:
            return pltpu.make_async_copy(a_gu.at[1, j], dst, load.at[2])
        return remote(a_gu.at[1, j], dst, s3.at[j], r3.at[j], members[ROUNDS[j]])

    def sum_own(side, j, more=None):
        gu_own(side, j).wait()
        gu_a(side, j).wait_recv()
        total = a_gu[side, j].astype(F32) + own[j % 2].astype(F32)
        if more is not None:
            total = total + more[j].astype(F32)
        a_gu[side, j] = total.astype(BF)

    def pump(first, last):
        for j in range(first, last):
            gu_own(1, j).start()
        for j in range(first, last):
            gu_b(j).wait_recv()
            if j + AHEAD < RING:
                go(gu_b(j + AHEAD))
            sum_own(1, j, b_gu)

    small = ((down_in, down_own, da, db, down_o), (og, None, oa, ob, out_o))

    def small_a(a, xo):
        return remote(small[a][0].at[2 * (1 - core) + xo], small[a][2].at[xo], sx.at[a, xo], rx.at[a, xo], sibling)

    def small_b(a):
        return remote(small[a][2].at[1 - x], small[a][3], sx.at[a, 2], rx.at[a, 2], across)

    def small_c(a, act):
        src, dst = small[a][2].at[x], small[a][4]

        @pl.when(core == y)
        def _():
            c = pltpu.make_async_copy(src, dst, load.at[3 + a])
            c.start() if act == 0 else c.wait()

        @pl.when(core != y)
        def _():
            c = remote(src, dst, sx.at[a, 3], rx.at[a, 3], diagonal)
            c.start() if act == 0 else c.wait()

    def q_a(side, j):
        src = grad_q.at[owner(order[j], 1 - core, side_x[side])]
        return remote(src, aq.at[side, j], q1.at[side, j], t1.at[side, j], sibling)

    def q_b(j):
        return remote(grad_q.at[owner(order[j], core, 1 - x)], bq.at[j], q2.at[j], t2.at[j], across)

    def q_c(j, wait=False):
        src, dst = grad_q.at[owner(order[j], core, x)], c_q.at[order[j] if wait else t]
        if ROUNDS[j] == 0:
            return pltpu.make_async_copy(src, dst, load.at[5])
        return remote(src, dst, q3.at[j], t3.at[j], members[ROUNDS[j]])

    def gain_a():
        return remote(gain_in, gsum.at[2], sg.at[RING], rg.at[RING], sibling)

    def gain_b():
        return remote(gsum.at[0], gsum.at[3], sg.at[RING + 1], rg.at[RING + 1], across)

    def gain_c(j):
        lanes = window(owner(partner(t, j), core, x))
        return remote(gsum.at[1, :, lanes], ga.at[j], sg.at[j], rg.at[j], members[j])

    gather = SlotGather(ring, ags, agr)

    def block(slot):
        if slot == 0:
            return p
        if slot == 7:
            return (p + 4) % RING
        s = (slot + 1) // 2
        return (p + (RING - s if slot % 2 else s)) % RING

    def place(slot, act):
        yq, zq = ring_yz(block(slot))
        src, dst = ring.at[pl.ds(slot * TOK, TOK)], seq.at[2 * zq + core]

        @pl.when(yq == core)
        def _():
            c = pltpu.make_async_copy(src, dst, load.at[6 + slot])
            c.start() if act == 0 else c.wait()

        @pl.when(yq != core)
        def _():
            c = remote(src, dst, pls.at[zq], plr.at[zq], sibling)
            c.start() if act == 0 else c.wait_send()

    first = pltpu.make_async_copy(d_branch, ring.at[pl.ds(0, TOK)], load.at[14])
    first.start()
    first.wait()
    gather.step(0)
    place(0, 0)
    for side in (0, 1):
        go(*[gu_a(side, j) for j in range(RING)])
        if side == 0:
            go(small_a(0, 0), small_a(0, 1))
    for j in range(RING):
        if j < 2:
            gu_own(0, j).start()
        sum_own(0, j)
        if j + 2 < RING:
            gu_own(0, j + 2).start()
        if j < AHEAD:
            go(gu_b(j))

    def down_sum(xo):
        c = pltpu.make_async_copy(down_in.at[2 * core + xo], down_own, load.at[16])
        c.start()
        small_a(0, xo).wait_recv()
        c.wait()
        da[xo] = (da[xo].astype(F32) + down_own[...].astype(F32)).astype(BF)

    down_sum(0)
    gather.step(1)
    place(1, 0)
    place(2, 0)
    pump(0, 1)
    down_sum(1)
    pump(1, 2)
    gather.step(2)
    place(3, 0)
    place(4, 0)
    pump(2, 4)
    gather.step(3)
    place(5, 0)
    place(6, 0)
    pump(4, 5)
    gather.finish()
    place(7, 0)
    for j in range(5):
        go(gu_c(j))
    for zq in range(NZ):
        dst = seq.at[2 * zq + 1 - core]
        remote(dst, dst, pls.at[zq], plr.at[zq], sibling).wait_recv()
    for slot in range(RING):
        place(slot, 1)
    gather.drain()
    hidden_load = pltpu.make_async_copy(hidden, ring, load.at[14])
    hidden_load.start()

    for c in range(0, RING, 2):
        rows = pl.ds(c * TOK, 2 * TOK)
        d_att[rows] = contract_cols(seq[c : c + 2].reshape(2 * TOK, -1), wo[...]).astype(BF)

    def out_columns(cols):
        value = contract_rows(att[...].astype(BF), seq[:, :, cols].reshape(RING * TOK, 768))
        for f in range(4):
            og[f, :, cols] = value[64 * f : 64 * (f + 1)].astype(BF)

    tiles(3, 768, out_columns)
    go(small_a(1, 0), small_a(1, 1))
    pump(5, 6)
    go(gu_c(5))
    dk[...] = jnp.zeros_like(dk)
    dv[...] = jnp.zeros_like(dv)
    for i in range(4):
        r, upto = pl.ds(i * 256, 256), (i + 1) * 256
        keys, vals, query = k_in[0:upto], v_in[0:upto], q_in[r]
        bent = jnp.tanh(contract_cols(query, keys) / CAP)
        seen = lax.broadcasted_iota(jnp.int32, bent.shape, 1) <= i * 256 + lax.broadcasted_iota(jnp.int32, bent.shape, 0)
        weights = jnp.where(seen, jnp.exp(CAP * bent), 0.0)
        grad = d_att[r].astype(F32)
        delta = jnp.sum(grad * att[r], axis=-1, keepdims=True)
        d_probs = contract_cols(d_att[r], vals)
        d_raw = (weights * inv[r] * (d_probs - delta) * (1.0 - bent * bent)).astype(BF)
        dq = fold_rows(d_raw, keys) * (HD ** (-0.5))
        d_qkv[r, 0:HD] = unrotate(dq, cos[r], sine[r]).astype(BF)
        dk[0:upto] = dk[0:upto] + contract_rows(d_raw, query)
        scaled = grad * inv[r]
        high = scaled.astype(BF)
        rest = (scaled - high.astype(F32)).astype(BF)
        weights_b = weights.astype(BF)
        dv[0:upto] = dv[0:upto] + contract_rows(weights_b, high) + contract_rows(weights_b, rest)
        if i == 1:
            pump(6, 7)
            go(gu_c(6))
            go(small_b(0))
        if i == 3:
            pump(7, 8)
            go_self = gu_c(7)
            go_self.start()
    d_qkv[:, HD : 2 * HD] = unrotate(dk[...], cos[...], sine[...]).astype(BF)
    d_qkv[:, 2 * HD : 3 * HD] = dv[...].astype(BF)

    scatter = SlotScatter(part, buf, rss, rsr)

    def swap(zq, kept):
        where = pl.ds(pl.multiple_of(slot_of(ring_index(core, zq), p) * TOK, TOK), TOK)
        if kept:
            return pltpu.make_async_copy(seq.at[2 * zq + core], part.at[where], load.at[17 + zq])
        return remote(seq.at[2 * zq + 1 - core], part.at[where], sws.at[zq], swr.at[zq], sibling)

    def swapped(zq):
        where = pl.ds(pl.multiple_of(slot_of(ring_index(1 - core, zq), p) * TOK, TOK), TOK)
        return remote(seq.at[0], part.at[where], sws.at[zq], swr.at[zq], sibling)

    for zq in range(NZ):
        rows = d_qkv[2 * zq * TOK : (2 * zq + 2) * TOK]

        def columns(cols):
            value = contract_cols(rows, wq[cols])
            seq[2 * zq, :, cols] = value[0:TOK].astype(BF)
            seq[2 * zq + 1, :, cols] = value[TOK:].astype(BF)

        tiles(3, 768, columns)
        swap(zq, True).start()
        swap(zq, False).start()
    for zq in range(NZ):
        swap(zq, True).wait()
        swapped(zq).wait_recv()
    scatter.step(0)

    hidden_load.wait()

    def grad_half(half):
        def columns(cols):
            value = contract_rows(ring[:, pl.ds(half * 1152, 1152)], d_qkv[:, cols])
            for i in range(16):
                grad_q[half * 16 + i, :, cols] = value[72 * i : 72 * (i + 1)].astype(BF)

        tiles(3, 256, columns)

    grad_half(0)
    scatter.step(1)
    grad_half(1)
    for side in (0, 1):
        go(*[q_a(side, j) for j in range(RING)])
    for xo in (0, 1):
        small_a(1, xo).wait_recv()
        oa[xo] = (oa[xo].astype(F32) + og[2 * core + xo].astype(F32)).astype(BF)
    go(small_b(1))
    scatter.step(2)

    def q_sum(side, j):
        i = owner(order[j], core, side_x[side])
        q_a(side, j).wait_recv()
        total = grad_q[i].astype(F32) + aq[side, j].astype(F32)
        if side == 1:
            q_b(j).wait_recv()
            total = total + bq[j].astype(F32)
        grad_q[i] = total.astype(BF)

    for j in range(RING):
        q_sum(0, j)
        if j < AHEAD:
            go(q_b(j))
    small_b(0).wait_recv()
    da[x] = (da[x].astype(F32) + db[...].astype(F32)).astype(BF)
    small_c(0, 0)
    scatter.step(3)

    def q_round(j):
        q_sum(1, j)
        if j + AHEAD < RING:
            go(q_b(j + AHEAD))
        if ROUNDS[j] == 0:
            q_c(j).start()
        else:
            go(q_c(j))

    for j in range(4):
        q_round(j)
    small_b(1).wait_recv()
    oa[x] = (oa[x].astype(F32) + ob[...].astype(F32)).astype(BF)
    small_c(1, 0)

    def own_part(cols):
        slot = part[0:TOK, cols]
        d_hid_o[:, cols] = slot.astype(F32)

    tiles(3, 768, own_part)
    for j in range(4, RING):
        q_round(j)
    scatter.finish(d_hid_o)
    def pre_gain(r):
        value = d_hid_o[r] * rms_parts(block_in[r].astype(F32))[1]
        gain_in[0:1, 0:D] = gain_in[0:1, 0:D] + jnp.sum(value, axis=0, keepdims=True)

    by_rows(pre_gain)
    go(gain_a())
    gain_a().wait_recv()
    gsum[0] = gain_in[...] + gsum[2]
    go(gain_b())
    gain_b().wait_recv()
    gsum[1] = gsum[0] + gsum[3]
    go(*[gain_c(j) for j in range(1, RING)])
    total = gsum[1, :, window(owner(t, core, x))]
    for j in range(1, RING):
        gain_c(j).wait_recv()
        total = total + ga[j]
    gain_o[...] = total

    for j in range(RING):
        if ROUNDS[j] == 0:
            gu_c(j).wait()
            q_c(j).wait()
        else:
            gu_c(j, True).wait_recv()
            q_c(j, True).wait_recv()
    small_c(0, 1)
    small_c(1, 1)
    for zq in range(NZ):
        swap(zq, False).wait_send()
    scatter.drain()
    for c in pending:
        c.wait_send()


def backward(d_branch, gu, down, hidden, w_qkv, w_out, queries, keys, values, attended, inv_total, cos_tab, sine_tab,
             block, gain_parts, collective_id):
    n = 4 * RING
    rows, width = d_branch.shape
    shard = gu.shape[0] // n
    gu = gu.reshape(n, shard, 2 * UNITS)
    down = down.reshape(4, -1, width)
    total, down_rows, out_rows = RING * rows, down.shape[1], w_out.shape[0] // 4
    gain_shape = (8, PADDED)

    def out(*shape, dtype=BF):
        return jax.ShapeDtypeStruct(shape, dtype)

    def body(*refs):
        ins, rest = refs[:14], refs[14:]
        gains_ref, rest = rest[0], rest[1:]
        outs, scr = rest[:6], rest[6:]
        gain_scr = scr[0]
        gain_scr[...] = gains_ref[...]
        backward_kernel(*ins, gain_scr, *outs, *scr[1:])

    return pl.pallas_call(
        body,
        out_shape=[
            out(rows, width, dtype=F32), out(8, WINDOW, dtype=F32),
            out(RING, shard, 2 * UNITS), out(RING, shard, 3 * HD),
            out(down_rows, width), out(out_rows, width),
        ],
        in_specs=[HBM] * 4 + [VMEM] * 11,
        out_specs=[VMEM] * 2 + [HBM] * 4,
        scratch_shapes=[
            pltpu.VMEM(gain_shape, F32),
            pltpu.VMEM((total, width), BF), pltpu.VMEM((RING, rows, width), BF), pltpu.VMEM((total, width), BF),
            pltpu.VMEM((2, 4, rows, width), BF),
            pltpu.VMEM((total, HD), BF), pltpu.VMEM((total, 3 * HD), BF),
            pltpu.VMEM((total, HD), F32), pltpu.VMEM((total, HD), F32),
            pltpu.VMEM((n, shard, 3 * HD), BF), pltpu.VMEM((2, RING, shard, 3 * HD), BF), pltpu.VMEM((RING, shard, 3 * HD), BF),
            pltpu.VMEM((2, shard, 2 * UNITS), BF), pltpu.VMEM((2, RING, shard, 2 * UNITS), BF), pltpu.VMEM((RING, shard, 2 * UNITS), BF),
            pltpu.VMEM((down_rows, width), BF), pltpu.VMEM((2, down_rows, width), BF), pltpu.VMEM((down_rows, width), BF),
            pltpu.VMEM((4, out_rows, width), BF), pltpu.VMEM((2, out_rows, width), BF), pltpu.VMEM((out_rows, width), BF),
            pltpu.VMEM((RING, 8, WINDOW), F32), pltpu.VMEM((4,) + gain_shape, F32),
            DMA((21,)),
            DMA((2, 4, SUB)), DMA((2, 4, SUB)), DMA((NZ,)), DMA((NZ,)), DMA((2, 4, SUB)), DMA((2, 4, SUB)), DMA((NZ,)), DMA((NZ,)),
            DMA((2, RING)), DMA((2, RING)), DMA((RING,)), DMA((RING,)), DMA((RING,)), DMA((RING,)),
            DMA((2, RING)), DMA((2, RING)), DMA((RING,)), DMA((RING,)), DMA((RING,)), DMA((RING,)),
            DMA((2, 4)), DMA((2, 4)), DMA((RING + 2,)), DMA((RING + 2,)),
        ],
        compiler_params=params(collective_id, 60),
    )(d_branch, gu, down, hidden, w_qkv, w_out, queries, keys, values, attended, inv_total, cos_tab, sine_tab, block, gain_parts)


def results_kernel(gu, qkv, down, out, d_hidden, d_middle, block, gains,
                   gate_o, up_o, query_o, key_o, value_o, down_o, out_o, token_o):
    for i in range(2):
        units, heads = pl.ds(i * UNITS, UNITS), pl.ds(i * HD, HD)
        gate_o[:, units] = gu[i, :, 0:UNITS].astype(F32)
        up_o[:, units] = gu[i, :, UNITS : 2 * UNITS].astype(F32)
        query_o[:, heads] = qkv[i, :, 0:HD].astype(F32)
    key_o[...] = qkv[0, :, HD : 2 * HD].astype(F32) + qkv[1, :, HD : 2 * HD].astype(F32)
    value_o[...] = qkv[0, :, 2 * HD :].astype(F32) + qkv[1, :, 2 * HD :].astype(F32)
    down_o[...] = down[...].astype(F32)
    out_o[...] = out[...].astype(F32)
    inverse, normed = rms_parts(block[...].astype(F32))
    back = norm_back(d_hidden[...] * (1.0 + gains[0:1]), normed, inverse)
    token_o[...] = (d_middle[...] + back).astype(BF)


def results(gu, qkv, down, out, d_hidden, d_middle, block, gains):
    steps = RING // 2
    shard, width = gu.shape[1], down.shape[1]
    tok, down_rows, out_rows = d_hidden.shape[0] // steps, down.shape[0] // steps, out.shape[0] // steps

    def rows(n, wide):
        return pl.BlockSpec((n, wide), lambda i: (i, 0))

    def columns(wide):
        return pl.BlockSpec((shard, wide), lambda i: (0, i))

    def full(*shape):
        return jax.ShapeDtypeStruct(shape, F32)

    return pl.pallas_call(
        results_kernel,
        grid=(steps,),
        out_shape=[
            full(shard, FF), full(shard, FF), full(shard, H * HD), full(shard, KVH * HD), full(shard, KVH * HD),
            full(*down.shape), full(*out.shape), jax.ShapeDtypeStruct(d_hidden.shape, BF),
        ],
        in_specs=[
            pl.BlockSpec((2, shard, 2 * UNITS), lambda i: (i, 0, 0)), pl.BlockSpec((2, shard, 3 * HD), lambda i: (i, 0, 0)),
            rows(down_rows, width), rows(out_rows, width), rows(tok, width), rows(tok, width), rows(tok, width),
            pl.BlockSpec(gains.shape, lambda i: (0, 0)),
        ],
        out_specs=[
            columns(2 * UNITS), columns(2 * UNITS), columns(2 * HD), columns(HD), columns(HD),
            rows(down_rows, width), rows(out_rows, width), rows(tok, width),
        ],
        compiler_params=pltpu.CompilerParams(vmem_limit_bytes=60 * 2**20),
    )(gu, qkv, down, out, d_hidden, d_middle, block, gains)


def on_ring(
    tokens, w_query, w_key, w_value, w_out, w_gate, w_up, w_down,
    pre_gain, post_gain, pre_ffn_gain, post_ffn_gain, out_grad,
):
    ids = iter(range(32))
    length = RING * tokens.shape[1]
    shard_gain = pre_gain.shape[0]
    mine = lax.axis_index("ctx") * 4 + lax.axis_index("fsdp")
    gains = jnp.stack([pre_gain, post_gain, pre_ffn_gain, post_ffn_gain]).astype(F32)
    gains = lax.dynamic_update_slice(jnp.zeros((8, WINDOW), F32), gains, (0, (mine * shard_gain) % 128))
    cos_tab, sine_tab = (jnp.asarray(table) for table in constant_tables(length, HD))
    w_gu, down_in, hidden, w_qkv, out_in, gains, queries, keys, values, attended, inv_total, branch = forward(
        w_gate, w_up, w_query, w_key, w_value, w_down, w_out, tokens[0], gains, cos_tab, sine_tab, next(ids)
    )
    w_gu, hidden = w_gu.reshape(D, 2 * UNITS), hidden.reshape(length, D)
    w_dn = down_in.reshape(UNITS, D)
    w_ot = out_in.reshape(HD, D)
    output, d_middle, d_branch, gain_parts, down_part, gu_part = feed_forward(
        branch, tokens[0], gains, out_grad[0], w_gu, w_dn, next(ids)
    )
    d_hidden, gain_g, gu_g, qkv_g, down_g, out_g = backward(
        d_branch, gu_part, down_part, hidden, w_qkv, w_ot, queries, keys, values, attended, inv_total,
        cos_tab, sine_tab, tokens[0], gain_parts, next(ids),
    )
    gate_g, up_g, query_g, key_g, value_g, down_g, out_g, token_grad = results(
        gu_g, qkv_g, down_g, out_g, d_hidden, d_middle, tokens[0], gains
    )
    gain_g = lax.dynamic_slice(gain_g, (0, (mine * shard_gain) % 128), (4, shard_gain))
    return (
        output[None], token_grad[None],
        query_g, key_g, value_g, out_g, gate_g, up_g, down_g,
        gain_g[0], gain_g[1], gain_g[2], gain_g[3],
    )


ROW_FOLD = 4


def head_tables(positions, width):
    half_width = width // 2
    inv_freqs = ROPE_BASE ** (-jnp.arange(half_width, dtype=jnp.float32) * 2.0 / width)
    angles = positions.astype(jnp.float32)[:, None] * inv_freqs[None, :]
    return (jnp.cos(angles)[:, None, :], jnp.sin(angles)[:, None, :])


def rotate_heads(heads_in, cos_tab, sine_tab):
    half_width = heads_in.shape[-1] // 2
    front_half = heads_in[..., :half_width]
    back_half = heads_in[..., half_width:]
    return jnp.concatenate(
        [front_half * cos_tab - back_half * sine_tab, back_half * cos_tab + front_half * sine_tab],
        axis=-1,
    )


def unrotate_heads(grad_in, cos_tab, sine_tab):
    half_width = grad_in.shape[-1] // 2
    front_half = grad_in[..., :half_width]
    back_half = grad_in[..., half_width:]
    return jnp.concatenate(
        [front_half * cos_tab + back_half * sine_tab, back_half * cos_tab - front_half * sine_tab],
        axis=-1,
    )


def to_groups(flat_heads, tok_rows, q_group):
    shaped = flat_heads.reshape(tok_rows, KVH, q_group, HD)
    return jnp.transpose(shaped, (1, 2, 0, 3)).reshape(KVH, q_group * tok_rows, HD)


def from_groups(grouped, tok_rows, q_group):
    shaped = grouped.reshape(KVH, q_group, tok_rows, HD)
    return jnp.transpose(shaped, (2, 0, 1, 3)).reshape(tok_rows, KVH * q_group * HD)


def grad_rows(left, right, folding, count):
    block = contract_rows(left, right)
    return block.reshape(count, right.shape[1] // folding)


def blockwise(step_fn, carry, piece, width):
    key_count = piece[0].shape[0]
    n_steps = key_count // width
    stacked = tuple((member.reshape(n_steps, width, member.shape[1]) for member in piece))

    def one_step(partial_value, block_item):
        block_index, members = block_item
        return (step_fn(partial_value, members, block_index * width), None)

    carry, unused = lax.scan(one_step, carry, (jnp.arange(n_steps, dtype=jnp.int32), stacked))
    return carry


def block_grads(query_g, query_pos, d_att_g, delta, inv_tot, key_block, value_block, key_first):
    key_count = key_block.shape[0]
    key_grp = key_block.reshape(key_count, KVH, HD)
    value_grp = value_block.reshape(key_count, KVH, HD)
    raw_scores = jnp.einsum("grd,ngd->grn", query_g, key_grp, preferred_element_type=jnp.float32)
    capped = CAP * jnp.tanh(raw_scores / CAP)
    key_pos = key_first + jnp.arange(key_count, dtype=jnp.int32)
    allowed = key_pos[None, None, :] <= query_pos[None, :, None]
    weights = jnp.where(allowed, jnp.exp(capped), 0.0)
    prob_rows = weights * inv_tot[..., None]
    d_probs = jnp.einsum("grd,ngd->grn", d_att_g, value_grp, preferred_element_type=jnp.float32)
    slope = 1.0 - capped / CAP * (capped / CAP)
    d_raw = (prob_rows * (d_probs - delta[..., None]) * slope).astype(jnp.bfloat16)
    d_query = jnp.einsum("grn,ngd->grd", d_raw, key_grp, preferred_element_type=jnp.float32)
    d_key = jnp.einsum("grn,grd->ngd", d_raw, query_g, preferred_element_type=jnp.float32)
    weights_b = weights.astype(jnp.bfloat16)
    d_scaled = d_att_g.astype(jnp.float32) * inv_tot[..., None]
    scaled_high = d_scaled.astype(jnp.bfloat16)
    scaled_rest = (d_scaled - scaled_high.astype(jnp.float32)).astype(jnp.bfloat16)
    d_value = jnp.einsum("grn,grd->ngd", weights_b, scaled_high, preferred_element_type=jnp.float32)
    d_value = d_value + jnp.einsum(
        "grn,grd->ngd", weights_b, scaled_rest, preferred_element_type=jnp.float32
    )
    return (d_query, d_key.reshape(key_count, KVH * HD), d_value.reshape(key_count, KVH * HD))


def on_any_mesh(
    tokens,
    w_query,
    w_key,
    w_value,
    w_out,
    w_gate,
    w_up,
    w_down,
    pre_gain,
    post_gain,
    pre_ffn_gain,
    post_ffn_gain,
    out_grad,
):
    tok_rows = tokens.shape[1]
    q_group = H // KVH
    q_scale = HD ** (-0.5)
    width_q = H * HD
    width_kv = KVH * HD
    width_qkv = width_q + 2 * width_kv
    n_ctx = lax.axis_size("ctx")
    my_block = lax.axis_index("ctx")
    my_start = my_block * tok_rows
    positions = my_start + jnp.arange(tok_rows, dtype=jnp.int32)
    cos_tab, sine_tab = head_tables(positions, HD)
    row_pos = jnp.tile(positions, q_group)
    last_pos = my_start + tok_rows - 1
    resid_in = tokens[0].astype(jnp.float32)
    qkv_shard = jnp.concatenate([w_query, w_key, w_value], axis=1)
    gateup_shard = jnp.concatenate([w_gate, w_up], axis=1)
    shard_rows = qkv_shard.shape[0]
    gains_shard = jnp.stack([pre_gain, post_gain, pre_ffn_gain, post_ffn_gain])
    full_gains, full_qkv, full_out = (
        lax.all_gather(gains_shard, ("ctx", "fsdp"), axis=1, tiled=True),
        lax.all_gather(qkv_shard, ("ctx", "fsdp"), axis=0, tiled=True),
        lax.all_gather(w_out, ("ctx", "fsdp"), axis=0, tiled=True),
    )
    factors = 1.0 + full_gains.astype(jnp.float32)
    pre_factor, post_factor, pre_ffn_factor, post_ffn_factor = (
        factors[0],
        factors[1],
        factors[2],
        factors[3],
    )
    inv_pre, normed_pre = rms_parts(resid_in)
    hidden = (normed_pre * pre_factor).astype(jnp.bfloat16)
    projected = jnp.dot(hidden, full_qkv, preferred_element_type=jnp.float32)
    query_lin = projected[:, :width_q].reshape(tok_rows, H, HD)
    queries = (
        (rotate_heads(query_lin, cos_tab, sine_tab) * q_scale)
        .astype(jnp.bfloat16)
        .reshape(tok_rows, width_q)
    )
    query_grp = to_groups(queries, tok_rows, q_group)
    key_lin = projected[:, width_q : width_q + width_kv].reshape(tok_rows, KVH, HD)
    key_rows = rotate_heads(key_lin, cos_tab, sine_tab).astype(jnp.bfloat16).reshape(tok_rows, width_kv)
    value_rows = projected[:, width_q + width_kv :].astype(jnp.bfloat16)

    def add_block(partial_value, piece, first_row):
        key_block, value_block = piece

        def add_compute_block(state):
            row_total, weighted = state
            key_count = key_block.shape[0]
            key_grp = key_block.reshape(key_count, KVH, HD)
            raw_scores = jnp.einsum(
                "grd,ngd->grn", query_grp, key_grp, preferred_element_type=jnp.float32
            )
            capped = CAP * jnp.tanh(raw_scores / CAP)
            key_pos = first_row + jnp.arange(key_count, dtype=jnp.int32)
            allowed = key_pos[None, None, :] <= row_pos[None, :, None]
            weights = jnp.where(allowed, jnp.exp(capped), 0.0)
            value_grp = value_block.reshape(key_count, KVH, HD)
            weighted = weighted + jnp.einsum(
                "grn,ngd->grd",
                weights.astype(jnp.bfloat16),
                value_grp,
                preferred_element_type=jnp.float32,
            )
            return (row_total + jnp.sum(weights, axis=-1), weighted)

        def add_skip_block(state):
            return state

        return lax.cond(first_row <= last_pos, add_compute_block, add_skip_block, partial_value)

    start_state = (
        jnp.zeros((KVH, q_group * tok_rows), jnp.float32),
        jnp.zeros((KVH, q_group * tok_rows, HD), jnp.float32),
    )
    row_total, weighted = blockwise(
        add_block,
        start_state,
        (
            lax.all_gather(key_rows, "ctx", axis=0, tiled=True),
            lax.all_gather(value_rows, "ctx", axis=0, tiled=True),
        ),
        512,
    )
    inv_total = 1.0 / row_total
    attended_grp = weighted * inv_total[..., None]
    attended_b = from_groups(attended_grp, tok_rows, q_group).astype(jnp.bfloat16)
    branch = jnp.dot(attended_b, full_out, preferred_element_type=jnp.float32)
    inv_post, normed_post = rms_parts(branch)
    middle = resid_in + normed_post * post_factor
    inv_mid, normed_mid = rms_parts(middle)
    hidden_ffn = (normed_mid * pre_ffn_factor).astype(jnp.bfloat16)
    gate_up = fold_rows(
        hidden_ffn, lax.all_gather(gateup_shard, ("ctx", "fsdp"), axis=0, tiled=True)
    )
    gate_lin = gate_up[:, :FF]
    up_lin = gate_up[:, FF:]
    active = gated(gate_lin, up_lin).astype(jnp.bfloat16)
    ffn_branch = fold_rows(active, lax.all_gather(w_down, ("ctx", "fsdp"), axis=0, tiled=True))
    inv_ffn, normed_ffn = rms_parts(ffn_branch)
    output = (middle + normed_ffn * post_ffn_factor).astype(jnp.bfloat16)
    out_cot = out_grad[0].astype(jnp.float32)
    post_ffn_part = jnp.sum(out_cot * normed_ffn, axis=0)
    d_ffn_b = norm_back(out_cot * post_ffn_factor, normed_ffn, inv_ffn).astype(jnp.bfloat16)
    down_total = lax.psum_scatter(
        grad_rows(active, d_ffn_b, 1, lax.axis_size(("ctx", "fsdp")) * w_down.shape[0]),
        ("ctx", "fsdp"),
        scatter_dimension=0,
        tiled=True,
    )
    d_active = contract_cols(d_ffn_b, lax.all_gather(w_down, ("ctx", "fsdp"), axis=0, tiled=True))
    unused_value, gate_pull = jax.vjp(gated, gate_lin, up_lin)
    d_gate, d_up = gate_pull(d_active)
    d_gateup_b = jnp.concatenate([d_gate.astype(jnp.bfloat16), d_up.astype(jnp.bfloat16)], axis=1)
    gateup_folded = lax.psum_scatter(
        grad_rows(
            hidden_ffn,
            d_gateup_b,
            ROW_FOLD,
            lax.axis_size(("ctx", "fsdp")) * (ROW_FOLD * shard_rows),
        ),
        ("ctx", "fsdp"),
        scatter_dimension=0,
        tiled=True,
    )
    gateup_total = gateup_folded.reshape(shard_rows, 2 * FF)
    d_hidden_ffn = contract_cols(
        d_gateup_b, lax.all_gather(gateup_shard, ("ctx", "fsdp"), axis=0, tiled=True)
    )
    pre_ffn_part = jnp.sum(d_hidden_ffn * normed_mid, axis=0)
    d_middle = out_cot + norm_back(d_hidden_ffn * pre_ffn_factor, normed_mid, inv_mid)
    back_qkv, back_out = (
        lax.all_gather(qkv_shard, ("ctx", "fsdp"), axis=0, tiled=True),
        lax.all_gather(w_out, ("ctx", "fsdp"), axis=0, tiled=True),
    )
    post_gain_part = jnp.sum(d_middle * normed_post, axis=0)
    d_branch_b = norm_back(d_middle * post_factor, normed_post, inv_post).astype(jnp.bfloat16)
    w_out_part = contract_rows(attended_b, d_branch_b)
    d_attended = contract_cols(d_branch_b, back_out).astype(jnp.bfloat16)
    d_att_grp = to_groups(d_attended, tok_rows, q_group)
    row_delta = jnp.sum(d_att_grp.astype(jnp.float32) * attended_grp, axis=-1)
    zero_rows = jnp.zeros((tok_rows, width_kv), jnp.float32)
    zero_query = jnp.zeros((KVH, q_group * tok_rows, HD), jnp.float32)
    block_ids = jnp.arange(n_ctx, dtype=jnp.int32)
    all_keys, all_values = (
        lax.all_gather(key_rows, "ctx", axis=0, tiled=True),
        lax.all_gather(value_rows, "ctx", axis=0, tiled=True),
    )

    def returned_step(acc_query, block_item):
        block_index, key_block, value_block = block_item
        first_row = block_index * tok_rows

        def returned_compute_block(acc_in):
            d_query, d_key, d_value = block_grads(
                query_grp,
                row_pos,
                d_att_grp,
                row_delta,
                inv_total,
                key_block,
                value_block,
                first_row,
            )
            return (acc_in + d_query, (d_key, d_value))

        def returned_skip_block(acc_in):
            return (acc_in, (zero_rows, zero_rows))

        return lax.cond(
            first_row <= last_pos, returned_compute_block, returned_skip_block, acc_query
        )

    key_blocks = all_keys.reshape(n_ctx, tok_rows, width_kv)
    value_blocks = all_values.reshape(n_ctx, tok_rows, width_kv)
    d_query_grp, key_terms = lax.scan(
        returned_step, zero_query, (block_ids, key_blocks, value_blocks)
    )
    key_term_rows = key_terms[0].reshape(n_ctx * tok_rows, width_kv)
    value_term_rows = key_terms[1].reshape(n_ctx * tok_rows, width_kv)
    d_keys, d_values = (
        lax.psum_scatter(
            key_term_rows.astype(jnp.bfloat16), "ctx", scatter_dimension=0, tiled=True
        ).astype(jnp.float32),
        lax.psum_scatter(
            value_term_rows.astype(jnp.bfloat16), "ctx", scatter_dimension=0, tiled=True
        ).astype(jnp.float32),
    )
    d_query_flat = from_groups(d_query_grp, tok_rows, q_group).reshape(tok_rows, H, HD) * q_scale
    dq_lin = (
        unrotate_heads(d_query_flat, cos_tab, sine_tab).astype(jnp.bfloat16).reshape(tok_rows, width_q)
    )
    dk_lin = (
        unrotate_heads(d_keys.reshape(tok_rows, KVH, HD), cos_tab, sine_tab)
        .astype(jnp.bfloat16)
        .reshape(tok_rows, width_kv)
    )
    dv_lin = d_values.astype(jnp.bfloat16)
    dqkv_b = jnp.concatenate([dq_lin, dk_lin, dv_lin], axis=1)
    d_hidden = contract_cols(dqkv_b, back_qkv)
    qkv_part = contract_rows(hidden, dqkv_b).reshape(ROW_FOLD * D, width_qkv // ROW_FOLD)
    pre_gain_part = jnp.sum(d_hidden * normed_pre, axis=0)
    token_grad = d_middle + norm_back(d_hidden * pre_factor, normed_pre, inv_pre)
    gain_parts = jnp.stack([pre_gain_part, post_gain_part, pre_ffn_part, post_ffn_part])
    qkv_folded, out_total, gain_totals = (
        lax.psum_scatter(qkv_part, ("ctx", "fsdp"), scatter_dimension=0, tiled=True),
        lax.psum_scatter(w_out_part, ("ctx", "fsdp"), scatter_dimension=0, tiled=True),
        lax.psum_scatter(gain_parts, ("ctx", "fsdp"), scatter_dimension=1, tiled=True),
    )
    qkv_total = qkv_folded.reshape(shard_rows, width_qkv)
    return (
        output[None],
        token_grad.astype(jnp.bfloat16)[None],
        qkv_total[:, :width_q],
        qkv_total[:, width_q : width_q + width_kv],
        qkv_total[:, width_q + width_kv :],
        out_total,
        gateup_total[:, :FF],
        gateup_total[:, FF:],
        down_total,
        gain_totals[0],
        gain_totals[1],
        gain_totals[2],
        gain_totals[3],
    )


def solution(mesh):
    ring = mesh.shape["ctx"] == RING and mesh.shape["fsdp"] == 4
    tokens, rows, gains = P("fsdp", "ctx", None), P(("ctx", "fsdp"), None), P(("ctx", "fsdp"))
    return jax.shard_map(
        on_ring if ring else on_any_mesh,
        mesh=mesh,
        in_specs=(tokens,) + (rows,) * 7 + (gains,) * 4 + (tokens,),
        out_specs=(tokens, tokens) + (rows,) * 7 + (gains,) * 4,
        check_vma=False,
    )
```

```python
import jax
import jax.numpy as jnp
import numpy as np
from jax import lax
from jax.experimental import pallas as pl
from jax.experimental.pallas import tpu as pltpu
from jax.sharding import PartitionSpec as P

D = 2304
H = 8
KVH = 4
HD = 256
CAP = 50
FF = 9216

EPSILON = 1e-06
ROPE_BASE = 10000.0

MESH = pl.DeviceIdType.MESH
HBM = pl.BlockSpec(memory_space=pl.ANY)
VMEM = pl.BlockSpec(memory_space=pltpu.VMEM)
DMA = pltpu.SemaphoreType.DMA
BF = jnp.bfloat16
F32 = jnp.float32


def constant_tables(length, width):
    exponents = -np.arange(width // 2, dtype=np.float32) * np.float32(2.0) / np.float32(width)
    inv_freqs = np.power(np.float32(ROPE_BASE), exponents, dtype=np.float32)
    angles = np.arange(length, dtype=np.float32)[:, None] * inv_freqs[None, :]
    return np.cos(angles), np.sin(angles)


def rotate(rows, cos_tab, sine_tab):
    half_width = rows.shape[-1] // 2
    front, back = rows[..., :half_width], rows[..., half_width:]
    return jnp.concatenate(
        [front * cos_tab - back * sine_tab, back * cos_tab + front * sine_tab], axis=-1
    )


def unrotate(rows, cos_tab, sine_tab):
    half_width = rows.shape[-1] // 2
    front, back = rows[..., :half_width], rows[..., half_width:]
    return jnp.concatenate(
        [front * cos_tab + back * sine_tab, back * cos_tab - front * sine_tab], axis=-1
    )


def rms_parts(values_in):
    inverse = lax.rsqrt(jnp.mean(values_in * values_in, axis=-1, keepdims=True) + EPSILON)
    return (inverse, values_in * inverse)


def norm_back(grad_normed, normed, inverse):
    return inverse * (grad_normed - normed * jnp.mean(grad_normed * normed, axis=-1, keepdims=True))


def contract_rows(left, right):
    return lax.dot_general(left, right, (((0,), (0,)), ((), ())), preferred_element_type=F32)


def contract_cols(left, right):
    return lax.dot_general(left, right, (((1,), (1,)), ((), ())), preferred_element_type=F32)


def fold_rows(left, right):
    return jnp.dot(left, right, preferred_element_type=F32)


def gated(gate_in, up_in):
    return jax.nn.gelu(gate_in, approximate=True) * up_in


NZ = 4
RING = 2 * NZ


def my_place():
    c, f = lax.axis_index("ctx"), lax.axis_index("fsdp")
    return c // 2, c % 2, f // 2, f % 2


def ring_index(y, z):
    return z + y * (RING - 1 - 2 * z)


def ring_yz(q):
    y = q // NZ
    return y, q + y * (RING - 1 - 2 * q)


def device(z, core, y, x):
    return (2 * z + core, 2 * y + x)


def ring_device(q, core, x):
    y, z = ring_yz(q)
    return device(z, core, y, x)


def remote(src, dst, send_sem, recv_sem, where):
    return pltpu.make_async_remote_copy(
        src_ref=src,
        dst_ref=dst,
        send_sem=send_sem,
        recv_sem=recv_sem,
        device_id=where,
        device_id_type=MESH,
    )


def greet(places, meanwhile=None):
    barrier = pltpu.get_barrier_semaphore()
    for place in places:
        pl.semaphore_signal(barrier, inc=1, device_id=place, device_id_type=MESH)
    if meanwhile is not None:
        meanwhile()
    pl.semaphore_wait(barrier, len(places))


def params(collective_id, vmem_mib=56):
    return pltpu.CompilerParams(
        collective_id=collective_id,
        has_side_effects=True,
        vmem_limit_bytes=vmem_mib * 2**20,
    )


SUB = 4


def ring_parts(direction, step, half_step):
    if step != half_step:
        return list(range(SUB))
    half = SUB // 2
    return list(range(half)) if direction == 0 else list(range(half, SUB))


TOK = 128
UNITS = FF // RING
TILE = 128
GELU_K = 0.7978845608028654
GELU_A = 0.044715


class SlotGather:
    def __init__(self, buf, ss, rs):
        z, core, y, x = my_place()
        p = ring_index(y, z)
        self.buf, self.ss, self.rs = buf, ss, rs
        self.near = (ring_device((p + 1) % RING, core, x), ring_device((p + RING - 1) % RING, core, x))
        self.pending = []

    def copy(self, direction, step, k):
        piece = TOK // SUB
        src = 0 if step == 0 else 2 * step - 1 + direction
        dst = 7 if step == 3 else 2 * step + 1 + direction
        return remote(
            self.buf.at[pl.ds(src * TOK + k * piece, piece)],
            self.buf.at[pl.ds(dst * TOK + k * piece, piece)],
            self.ss.at[direction, step, k],
            self.rs.at[direction, step, k],
            self.near[direction],
        )

    def step(self, step):
        for k in range(SUB):
            for direction in (0, 1):
                if step > 0:
                    self.copy(direction, step - 1, k).wait_recv()
                if k in ring_parts(direction, step, 3):
                    c = self.copy(direction, step, k)
                    c.start()
                    self.pending.append(c)

    def finish(self):
        for direction in (0, 1):
            for k in ring_parts(direction, 3, 3):
                self.copy(direction, 3, k).wait_recv()

    def drain(self):
        for c in self.pending:
            c.wait_send()


class SlotScatter:
    def __init__(self, part, buf, ss, rs):
        z, core, y, x = my_place()
        p = ring_index(y, z)
        self.part, self.buf, self.ss, self.rs = part, buf, ss, rs
        self.near = (ring_device((p + 1) % RING, core, x), ring_device((p + RING - 1) % RING, core, x))
        self.pending = []

    def copy(self, direction, step, k, src):
        rows = pl.ds(k * (TOK // SUB), TOK // SUB)
        return remote(
            src,
            self.buf.at[direction, step, rows],
            self.ss.at[direction, step, k],
            self.rs.at[direction, step, k],
            self.near[direction],
        )

    def step(self, step):
        piece = TOK // SUB
        for k in range(SUB):
            rows = pl.ds(k * piece, piece)
            for direction in (0, 1):
                if k not in ring_parts(direction, step, 0):
                    continue
                slot = 7 if step == 0 else 2 * (4 - step) - direction
                mine = pl.ds(slot * TOK + k * piece, piece)
                src = self.part.at[mine]
                if step > 0 and k in ring_parts(direction, step - 1, 0):
                    src = self.buf.at[direction, step - 1, rows]
                    self.copy(direction, step - 1, k, src).wait_recv()
                    src[...] = (src[...].astype(F32) + self.part[mine].astype(F32)).astype(BF)
                c = self.copy(direction, step, k, src)
                c.start()
                self.pending.append(c)

    def finish(self, total):
        for k in range(SUB):
            rows = pl.ds(k * (TOK // SUB), TOK // SUB)
            for direction in (0, 1):
                src = self.buf.at[direction, 3, rows]
                self.copy(direction, 3, k, src).wait_recv()
                total[rows] = total[rows] + src[...].astype(F32)

    def drain(self):
        for c in self.pending:
            c.wait_send()


def tiles(count, width, body):
    def step(i, carry):
        body(pl.ds(pl.multiple_of(i * width, width), width))
        return carry

    lax.fori_loop(0, count, step, 0)


def gelu_parts(v):
    bent = jnp.tanh(GELU_K * (v + GELU_A * (v * v * v)))
    value = 0.5 * v * (1.0 + bent)
    slope = 0.5 * (1.0 + bent) + 0.5 * v * (1.0 - bent * bent) * (GELU_K * (1.0 + 3.0 * GELU_A * (v * v)))
    return value, slope


PAIRS = ((128, 256), (384, 256), (640, 256))
LAST = (896, 128)
OWN = (0, 128)


def by_rows(body):
    def step(i, carry):
        body(pl.ds(pl.multiple_of(i * 32, 32), 32))
        return carry

    lax.fori_loop(0, TOK // 32, step, 0)


def feed_forward_kernel(branch, block, gains, cot, w_hbm, wd_hbm,
                        out_o, d_mid_o, d_branch_o, gain_o, wd_grad, gu_grad,
                        wgu, wd, ha, gu, act, part, buf, df, dgu, middle, total, stage,
                        w_sem, ags, agr, rss, rsr, out_sem):
    gather = [SlotGather(b, ags.at[i], agr.at[i]) for i, b in enumerate((ha, df))]
    scatter = [SlotScatter(part, buf, rss.at[i], rsr.at[i]) for i in range(2)]
    loads = [
        pltpu.make_async_copy(w_hbm, wgu, w_sem.at[0]),
        pltpu.make_async_copy(wd_hbm, wd, w_sem.at[1]),
    ]
    for c in loads:
        c.start()

    def head():
        def rows(r):
            mid = block[r].astype(F32) + rms_parts(branch[r])[1] * (1.0 + gains[1:2])
            middle[r] = mid
            ha[r] = (rms_parts(mid)[1] * (1.0 + gains[2:3])).astype(BF)

        by_rows(rows)

    greet(gather[0].near, head)
    gather[0].step(0)
    gain_o[...] = jnp.zeros(gain_o.shape, F32)
    loads[0].wait()

    def gate_up(first, count):
        rows = pl.ds(first, count)

        def column(cols):
            gu[rows, cols] = fold_rows(ha[rows], wgu[:, cols])

        tiles(3, 768, column)

        def finish(i, carry):
            r = pl.ds(pl.multiple_of(first + i * 32, 32), 32)
            act[r] = (gelu_parts(gu[r, 0:UNITS])[0] * gu[r, UNITS : 2 * UNITS]).astype(BF)
            return carry

        lax.fori_loop(0, count // 32, finish, 0)

    def down_part(first, count, dst):
        def column(cols):
            value = fold_rows(act[pl.ds(first, count)], wd[:, cols])
            dst[pl.ds(first, count), cols] = value.astype(dst.dtype)

        tiles(3, 768, column)

    def active_back(first, count):
        rows = pl.ds(first, count)
        for n in range(3):
            cols, up_cols = pl.ds(n * 384, 384), pl.ds(UNITS + n * 384, 384)
            d_active = contract_cols(df[rows], wd[cols])
            value, slope = gelu_parts(gu[rows, cols])
            dgu[rows, cols] = (d_active * gu[rows, up_cols] * slope).astype(BF)
            dgu[rows, up_cols] = (d_active * value).astype(BF)

    def hidden_part(first, count, dst):
        def column(cols):
            value = contract_cols(dgu[pl.ds(first, count)], wgu[cols])
            dst[pl.ds(first, count), cols] = value.astype(dst.dtype)

        tiles(3, 768, column)

    n_down = UNITS // TILE

    def grad_out(i):
        slot = i % 2
        if i < n_down:
            return pltpu.make_async_copy(stage.at[slot], wd_grad.at[pl.ds(i * TILE, TILE)], out_sem.at[slot])
        return pltpu.make_async_copy(stage.at[slot], gu_grad.at[pl.ds((i - n_down) * TILE, TILE)], out_sem.at[slot])

    def grad_tiles(first, last):
        for i in range(first, last):
            if i >= 2:
                grad_out(i - 2).wait()
            if i < n_down:
                value = contract_rows(act[:, pl.ds(i * TILE, TILE)], df[...])
            else:
                value = contract_rows(ha[:, pl.ds((i - n_down) * TILE, TILE)], dgu[...])
            stage[i % 2] = value.astype(BF)
            grad_out(i).start()

    gate_up(*OWN)
    for step, pair in enumerate(PAIRS):
        gather[0].step(step + 1)
        if step == 0:
            loads[1].wait()
        gate_up(*pair)
    gather[0].finish()
    gate_up(*LAST)
    down_part(*LAST, part)
    scatter[0].step(0)
    for step, pair in enumerate(PAIRS[::-1]):
        down_part(*pair, part)
        scatter[0].step(step + 1)
    down_part(*OWN, total)
    scatter[0].finish(total)
    gather[0].drain()
    scatter[0].drain()

    def turn(r):
        inverse, normed = rms_parts(total[r])
        df[r] = norm_back(cot[r].astype(F32) * (1.0 + gains[3:4]), normed, inverse).astype(BF)

    def add_gain(i, value):
        gain_o[i : i + 1, 0:D] = gain_o[i : i + 1, 0:D] + jnp.sum(value, axis=0, keepdims=True)

    def outputs(r):
        normed = rms_parts(total[r])[1]
        out_o[r] = (middle[r] + normed * (1.0 + gains[3:4])).astype(BF)
        add_gain(3, cot[r].astype(F32) * normed)

    by_rows(turn)
    gather[1].step(0)
    by_rows(outputs)
    active_back(*OWN)
    for step, pair in enumerate(PAIRS):
        gather[1].step(step + 1)
        active_back(*pair)
    gather[1].finish()
    active_back(*LAST)
    hidden_part(*LAST, part)
    scatter[1].step(0)
    done = 0
    for step, pair in enumerate(PAIRS[::-1]):
        hidden_part(*pair, part)
        scatter[1].step(step + 1)
        grad_tiles(done, done + 8 + step // 2)
        done += 8 + step // 2
    hidden_part(*OWN, total)
    n_tiles = n_down + ha.shape[1] // TILE
    grad_tiles(done, n_tiles)
    scatter[1].finish(total)

    def tail(r):
        inv_mid, normed_mid = rms_parts(middle[r])
        d_hidden = total[r]
        add_gain(2, d_hidden * normed_mid)
        d_mid = cot[r].astype(F32) + norm_back(d_hidden * (1.0 + gains[2:3]), normed_mid, inv_mid)
        d_mid_o[r] = d_mid
        inv_post, normed_post = rms_parts(branch[r])
        add_gain(1, d_mid * normed_post)
        d_branch_o[r] = norm_back(d_mid * (1.0 + gains[1:2]), normed_post, inv_post).astype(BF)

    by_rows(tail)
    for i in (n_tiles - 2, n_tiles - 1):
        grad_out(i).wait()
    gather[1].drain()
    scatter[1].drain()


def feed_forward(branch, block, gains, out_grad, w_in, w_down, collective_id):
    rows, width = branch.shape
    total = RING * rows

    def full(*shape, dtype=F32):
        return jax.ShapeDtypeStruct(shape, dtype)

    return pl.pallas_call(
        feed_forward_kernel,
        out_shape=[
            full(rows, width, dtype=BF), full(rows, width), full(rows, width, dtype=BF), full(8, PADDED),
            full(UNITS, width, dtype=BF), full(width, 2 * UNITS, dtype=BF),
        ],
        in_specs=[VMEM] * 4 + [HBM] * 2,
        out_specs=[VMEM] * 4 + [HBM] * 2,
        scratch_shapes=[
            pltpu.VMEM((width, 2 * UNITS), BF), pltpu.VMEM((UNITS, width), BF),
            pltpu.VMEM((total, width), BF), pltpu.VMEM((total, 2 * UNITS), F32), pltpu.VMEM((total, UNITS), BF),
            pltpu.VMEM((total, width), BF), pltpu.VMEM((2, 4, rows, width), BF),
            pltpu.VMEM((total, width), BF), pltpu.VMEM((total, 2 * UNITS), BF),
            pltpu.VMEM((rows, width), F32), pltpu.VMEM((rows, width), F32), pltpu.VMEM((2, TILE, width), BF),
            DMA((2,)),
            DMA((2, 2, 4, SUB)), DMA((2, 2, 4, SUB)), DMA((2, 2, 4, SUB)), DMA((2, 2, 4, SUB)),
            DMA((2,)),
        ],
        compiler_params=params(collective_id, 60),
    )(branch, block, gains, out_grad, w_in, w_down)


WIDTHS = (UNITS, UNITS, HD, HD, HD)


SHARD = D // (4 * RING)
PADDED = D + 128
WINDOW = 256


def window(i):
    return pl.ds(pl.multiple_of((SHARD * i) // 128 * 128, 128), WINDOW)


def member_place(t, core, x):
    return device(t // 2, core, t % 2, x)


def slot_of(q, p):
    d = (q - p + RING) % RING
    return jnp.where(d == 0, 0, jnp.where(d < 4, 2 * d, jnp.where(d == 4, 7, 15 - 2 * d)))


def partner(t, j):
    out = 0
    for bit in (1, 2, 4):
        on = (t // bit) % 2
        out = out + bit * (1 - on if j & bit else on)
    return out


def column_start(which, t):
    if which < 2:
        return pl.multiple_of(t * UNITS, 128)
    return pl.multiple_of((t if which == 2 else t // 2) * HD, 128)


def forward_kernel(gate, up, query, key, value, down, out, block, gain_in, cos, sine,
                   w_gu, d_ref, hidden_o, wq_h, q_h, k_h, v_h, att_h, wo, gain_o, inv_o, branch_o,
                   wq, q_o, k_o, v_o, att_o, ring, seq, seq_part, part, buf, wq_in, own, relay, ga, gsum,
                   load, ags, agr, pls, plr, rss, rsr, sws, swr, s1, r1, s2, r2, s3, r3,
                   q1, t1, q2, t2, q3, t3, s4, r4, s5, r5, sg, rg):
    z, core, y, x = my_place()
    t, p = 2 * z + y, ring_index(y, z)
    sibling, across = device(z, 1 - core, y, x), device(z, core, y, 1 - x)
    member = [partner(t, j) for j in range(RING)]
    members = [member_place(tq, core, x) for tq in member]
    plane = []
    for dc in (0, 1):
        for dy in (0, 1):
            for dx in (0, 1):
                if (dc, dx) != (0, 0):
                    plane.append(device(z, (core + dc) % 2, (y + dy) % 2, (x + dx) % 2))
    greet(members[1:] + plane)
    sources = (gate, up, query, key, value)
    pending = []

    def go(*copies):
        for c in copies:
            c.start()
            pending.append(c)

    def owner(tq, corq, xq):
        return (2 * (tq // 2) + corq) * 4 + 2 * (tq % 2) + xq

    me = owner(t, core, x)

    def columns_of(a, tq):
        return sources[a].at[:, pl.ds(column_start(a, tq), WIDTHS[a])]

    def gain_a(j):
        return remote(gain_in, ga.at[j], sg.at[j], rg.at[j], members[j])

    def gain_b(i):
        return remote(gsum.at[i], gsum.at[2 + i], sg.at[RING + i], rg.at[RING + i], (across, sibling)[i])

    def q_first(j, a, wait=False):
        tq = member[j]
        dst = wq_in.at[owner(tq, core, x) if wait else me, :, pl.ds((a - 2) * HD, HD)]
        return remote(columns_of(a, tq), dst, q1.at[j, a - 2], t1.at[j, a - 2], members[j])

    def q_second(j, wait=False):
        i = owner(member[j], core, 1 - x if wait else x)
        return remote(wq_in.at[i], wq_in.at[i], q2.at[j], t2.at[j], across)

    def q_third(j, flip, wait=False):
        i = owner(member[j], 1 - core if wait else core, 1 - x if flip else x)
        return remote(wq_in.at[i], wq_in.at[i], q3.at[j, flip], t3.at[j, flip], sibling)

    def first(j, a, wait=False):
        tq = member[j]
        dst = w_gu.at[owner(tq, core, x) if wait else me, :, pl.ds(a * UNITS, UNITS)]
        return remote(columns_of(a, tq), dst, s1.at[j, a], r1.at[j, a], members[j])

    def second(j, wait=False):
        i = owner(member[j], core, 1 - x if wait else x)
        return remote(own if j == 0 else w_gu.at[i], w_gu.at[i], s2.at[j], r2.at[j], across)

    def third(j, flip, wait=False):
        i = owner(member[j], 1 - core if wait else core, 1 - x if flip else x)
        return remote(own if (j, flip) == (0, 0) else w_gu.at[i], w_gu.at[i], s3.at[j, flip], r3.at[j, flip], sibling)

    def start_round(j):
        go(first(j, 0), first(j, 1))

    def end_round(j):
        first(j, 0, True).wait_recv()
        first(j, 1, True).wait_recv()
        go(second(j), third(j, 0))

    def end_across(j):
        second(j, True).wait_recv()
        go(third(j, 1))

    gather = SlotGather(ring, ags, agr)

    def block_of(slot):
        if slot == 0:
            return p
        if slot == 7:
            return (p + 4) % RING
        s = (slot + 1) // 2
        return (p + (RING - s if slot % 2 else s)) % RING

    def place(slot, act):
        yq, zq = ring_yz(block_of(slot))
        src, dst = ring.at[pl.ds(slot * TOK, TOK)], seq.at[2 * zq + core]

        @pl.when(yq == core)
        def _():
            c = pltpu.make_async_copy(src, dst, load.at[6 + slot])
            c.start() if act == 0 else c.wait()

        @pl.when(yq != core)
        def _():
            c = remote(src, dst, pls.at[zq], plr.at[zq], sibling)
            c.start() if act == 0 else c.wait_send()

    pair = ((down, d_ref), (out, wo))
    mine = 2 * y + x

    def rows_out(xq, a, act):
        src, dst = pair[a][0], pair[a][1].at[mine]
        to_self = (x == core) & (y == core) & (xq == x)

        @pl.when(to_self)
        def _():
            if a == 0:
                c = pltpu.make_async_copy(relay, dst, load.at[5])
            else:
                c = pltpu.make_async_copy(src, dst, load.at[4])
            c.start() if act == 0 else c.wait()

        @pl.when(jnp.logical_not(to_self))
        def _():
            c = remote(src, dst, s4.at[xq, a], r4.at[y, a], device(z, x, core, xq))
            c.start() if act == 0 else c.wait_send()

    def rows_on(yq, a):
        src, dst = pair[a][0], pair[a][1].at[2 * yq + core]
        from_self = (core == y) & (yq == y) & (core == x)

        @pl.when(from_self)
        def _():
            if a == 0:
                pltpu.make_async_copy(relay, dst, load.at[5]).wait()
            else:
                pltpu.make_async_copy(src, dst, load.at[4]).wait()

        @pl.when(jnp.logical_not(from_self))
        def _():
            remote(src, dst, s4.at[0, a], r4.at[yq, a], sibling).wait_recv()

        go(remote(dst, dst, s5.at[yq, a], r5.at[yq, a], sibling))

    locals_ = [pltpu.make_async_copy(columns_of(a, t), wq_in.at[me, :, pl.ds((a - 2) * HD, HD)], load.at[a]) for a in (2, 3)]
    locals_.append(pltpu.make_async_copy(columns_of(4, t), wq_in.at[me, :, pl.ds(2 * HD, HD)], load.at[14]))
    locals_ += [pltpu.make_async_copy(columns_of(a, t), own.at[:, pl.ds(a * UNITS, UNITS)], load.at[a]) for a in (0, 1)]
    relay_load = pltpu.make_async_copy(down, relay, load.at[15])
    for c in locals_:
        c.start()
    relay_load.start()
    ring[0:TOK] = block[...]
    gather.step(0)
    go(*[gain_a(j) for j in range(1, RING)])
    for j in range(1, RING):
        go(*[q_first(j, a) for a in (2, 3, 4)])
    for c in locals_:
        c.wait()
    go(q_second(0), q_third(0, 0))
    for xq in (0, 1):
        rows_out(xq, 1, 0)
    keep_own = pltpu.make_async_copy(own, w_gu.at[me], load.at[16])
    keep_own.start()
    go(second(0), third(0, 0))
    place(0, 0)
    gsum[0] = jnp.zeros(gsum.shape[1:], F32)
    gsum[0, :, window(me)] = gain_in[...]
    for j in range(1, RING):
        gain_a(j).wait_recv()
        lanes = window(owner(member[j], core, x))
        gsum[0, :, lanes] = gsum[0, :, lanes] + ga[j]
    go(gain_b(0))
    gather.step(1)
    place(1, 0)
    place(2, 0)
    gain_b(0).wait_recv()
    gsum[1] = gsum[0] + gsum[2]
    go(gain_b(1))
    for j in range(1, RING):
        for a in (2, 3, 4):
            q_first(j, a, True).wait_recv()
        go(q_second(j), q_third(j, 0))
    for yq in (0, 1):
        rows_on(yq, 1)
    gather.step(2)
    place(3, 0)
    place(4, 0)
    gain_b(1).wait_recv()
    gain_o[...] = (gsum[1] + gsum[3])[:, 0:D]
    for j in range(RING):
        q_second(j, True).wait_recv()
        go(q_third(j, 1))
    gather.step(3)
    place(5, 0)
    place(6, 0)
    for j in (4, 5, 1, 6, 2, 7, 3):
        start_round(j)
    relay_load.wait()
    for xq in (0, 1):
        rows_out(xq, 0, 0)
    end_across(0)
    for j in range(RING):
        for flip in (0, 1):
            q_third(j, flip, True).wait_recv()

    def join(g, carry):
        pieces = [wq_in[4 * g + i].astype(F32) for i in range(4)]
        wq[pl.ds(pl.multiple_of(288 * g, 16), 288)] = jnp.concatenate(pieces, axis=0).astype(BF)
        return carry

    lax.fori_loop(0, 8, join, 0)
    results_out = [pltpu.make_async_copy(wq, wq_h, load.at[22])]
    results_out[0].start()
    gather.finish()
    place(7, 0)
    for zq in range(NZ):
        dst = seq.at[2 * zq + 1 - core]
        remote(dst, dst, pls.at[zq], plr.at[zq], sibling).wait_recv()
    for slot in range(RING):
        place(slot, 1)
    end_round(1)

    factor = 1.0 + gain_o[0:1]

    def norm(c, carry):
        for half in range(2):
            rows = pl.ds(half * 64, 64)
            seq[c, rows] = (rms_parts(seq[c, rows].astype(F32))[1] * factor).astype(BF)
        return carry

    lax.fori_loop(0, RING, norm, 0)
    keep_hidden = pltpu.make_async_copy(seq, hidden_o, load.at[17])
    keep_hidden.start()
    for i in range(4):
        r = pl.ds(i * 256, 256)
        rows = seq[2 * i : 2 * i + 2].reshape(256, -1)
        tabs = (cos[r], sine[r])
        q_o[r] = (rotate(fold_rows(rows, wq[:, 0:HD]), *tabs) * (HD ** (-0.5))).astype(BF)
        k_o[r] = rotate(fold_rows(rows, wq[:, HD : 2 * HD]), *tabs).astype(BF)
        v_o[r] = fold_rows(rows, wq[:, 2 * HD : 3 * HD]).astype(BF)
    for i, (src, dst) in enumerate(((q_o, q_h), (k_o, k_h), (v_o, v_h))):
        results_out.append(pltpu.make_async_copy(src, dst, load.at[23 + i]))
        results_out[-1].start()
    end_round(4)
    end_across(1)

    def swap(zq, kept):
        where = pl.ds(pl.multiple_of(slot_of(ring_index(core, zq), p) * TOK, TOK), TOK)
        if kept:
            return pltpu.make_async_copy(seq_part.at[2 * zq + core], part.at[where], load.at[18 + zq])
        return remote(seq_part.at[2 * zq + 1 - core], part.at[where], sws.at[zq], swr.at[zq], sibling)

    def swapped(zq):
        where = pl.ds(pl.multiple_of(slot_of(ring_index(1 - core, zq), p) * TOK, TOK), TOK)
        return remote(seq_part.at[0], part.at[where], sws.at[zq], swr.at[zq], sibling)

    for yq in (0, 1):
        remote(out, wo.at[2 * yq + 1 - core], s5.at[yq, 1], r5.at[yq, 1], sibling).wait_recv()
    for i in range(4):
        r, upto = pl.ds(i * 256, 256), (i + 1) * 256
        bent = jnp.tanh(contract_cols(q_o[r], k_o[0:upto]) / CAP)
        seen = lax.broadcasted_iota(jnp.int32, bent.shape, 1) <= i * 256 + lax.broadcasted_iota(jnp.int32, bent.shape, 0)
        weights = jnp.where(seen, jnp.exp(CAP * bent), 0.0)
        inverse = 1.0 / jnp.sum(weights, axis=-1, keepdims=True)
        attended = fold_rows(weights.astype(BF), v_o[0:upto]) * inverse
        inv_o[r] = inverse
        att_o[r] = attended
        attended_b = attended.astype(BF)

        def columns(cols):
            sums = fold_rows(attended_b, wo[:, :, cols].reshape(HD, 768))
            seq_part[2 * i, :, cols] = sums[0:TOK].astype(BF)
            seq_part[2 * i + 1, :, cols] = sums[TOK:].astype(BF)

        tiles(3, 768, columns)
        swap(i, True).start()
        swap(i, False).start()
        if i == 0:
            end_round(2)
        if i == 2:
            end_round(5)
            end_across(2)
            for yq in (0, 1):
                rows_on(yq, 0)
    results_out.append(pltpu.make_async_copy(att_o, att_h, load.at[26]))
    results_out[-1].start()
    for zq in range(NZ):
        swap(zq, True).wait()
        swapped(zq).wait_recv()
    scatter = SlotScatter(part, buf, rss, rsr)
    scatter.step(0)
    end_round(3)
    end_across(4)
    scatter.step(1)
    end_round(6)
    end_across(5)
    end_across(3)
    scatter.step(2)
    end_round(7)
    end_across(6)
    scatter.step(3)
    branch_o[...] = part[0:TOK].astype(F32)
    end_across(7)
    scatter.finish(branch_o)

    for j in range(RING):
        for flip in (0, 1):
            third(j, flip, True).wait_recv()
    for yq in (0, 1):
        remote(down, d_ref.at[2 * yq + 1 - core], s5.at[yq, 0], r5.at[yq, 0], sibling).wait_recv()
    for xq in (0, 1):
        for a in (0, 1):
            to_self = (x == core) & (y == core) & (xq == x)

            @pl.when(jnp.logical_not(to_self))
            def _():
                remote(pair[a][0], pair[a][1].at[mine], s4.at[xq, a], r4.at[y, a], device(z, x, core, xq)).wait_send()
    keep_own.wait()
    keep_hidden.wait()
    for c in results_out:
        c.wait()
    for zq in range(NZ):
        swap(zq, False).wait_send()
    gather.drain()
    scatter.drain()
    for c in pending:
        c.wait_send()


def forward(gate, up, query, key, value, down, out, block, gains, cos_tab, sine_tab, collective_id):
    n = 4 * RING
    rows, width = block.shape
    shard, total = gate.shape[0], RING * block.shape[0]

    def full(*shape, dtype=BF):
        return jax.ShapeDtypeStruct(shape, dtype)

    blocks = (RING, rows, width)
    return pl.pallas_call(
        forward_kernel,
        out_shape=[
            full(n, shard, 2 * UNITS), full(4, *down.shape), full(*blocks), full(width, 3 * HD),
            full(total, HD), full(total, HD), full(total, HD), full(total, HD, dtype=F32),
            full(4, *out.shape), full(8, D, dtype=F32), full(total, 1, dtype=F32), full(rows, width, dtype=F32),
        ],
        in_specs=[HBM] * 7 + [VMEM] * 4,
        out_specs=[HBM] * 8 + [VMEM] * 4,
        scratch_shapes=[
            pltpu.VMEM((width, 3 * HD), BF), pltpu.VMEM((total, HD), BF), pltpu.VMEM((total, HD), BF), pltpu.VMEM((total, HD), BF),
            pltpu.VMEM((total, HD), F32),
            pltpu.VMEM((total, width), BF), pltpu.VMEM(blocks, BF), pltpu.VMEM(blocks, BF), pltpu.VMEM((total, width), BF),
            pltpu.VMEM((2, 4, rows, width), BF), pltpu.VMEM((n, shard, 3 * HD), BF),
            pltpu.VMEM((shard, 2 * UNITS), BF), pltpu.VMEM(down.shape, BF),
            pltpu.VMEM((RING,) + gains.shape, F32), pltpu.VMEM((4, 8, PADDED), F32),
            DMA((27,)),
            DMA((2, 4, SUB)), DMA((2, 4, SUB)), DMA((NZ,)), DMA((NZ,)), DMA((2, 4, SUB)), DMA((2, 4, SUB)), DMA((NZ,)), DMA((NZ,)),
            DMA((RING, 2)), DMA((RING, 2)), DMA((RING,)), DMA((RING,)), DMA((RING, 2)), DMA((RING, 2)),
            DMA((RING, 3)), DMA((RING, 3)), DMA((RING,)), DMA((RING,)), DMA((RING, 2)), DMA((RING, 2)),
            DMA((2, 2)), DMA((2, 2)), DMA((2, 2)), DMA((2, 2)), DMA((RING + 2,)), DMA((RING + 2,)),
        ],
        compiler_params=params(collective_id, 60),
    )(gate, up, query, key, value, down, out, block, gains, cos_tab, sine_tab)


ROUNDS = (4, 5, 6, 7, 2, 3, 1, 0)
AHEAD = 2


def backward_kernel(ready, d_branch, gu_in, down_in, hidden, wq, wo, q_in, k_in, v_in, att, inv, cos, sine, block_in, gain_in,
                    d_hid_o, gain_o, c_gu, c_q, down_o, out_o,
                    ring, seq, part, buf, d_att, d_qkv, dk, dv, grad_q, aq, bq,
                    own, a_gu, b_gu, down_own, da, db, og, oa, ob, ga, gsum,
                    load, ags, agr, pls, plr, rss, rsr, sws, swr, s1, r1, s2, r2, s3, r3,
                    q1, t1, q2, t2, q3, t3, sx, rx, sg, rg):
    z, core, y, x = my_place()
    t, p = 2 * z + y, ring_index(y, z)
    sibling, across = device(z, 1 - core, y, x), device(z, core, y, 1 - x)
    diagonal = device(z, 1 - core, 1 - y, x)
    members = [member_place(partner(t, j), core, x) for j in range(RING)]
    order = [partner(t, j) for j in ROUNDS]
    greet(members[1:] + [sibling, across, diagonal])
    pending = []

    def go(*copies):
        for c in copies:
            c.start()
            pending.append(c)

    def owner(tq, corq, xq):
        return (2 * (tq // 2) + corq) * 4 + 2 * (tq % 2) + xq

    side_x = (1 - x, x)

    def gu_a(side, j):
        src = gu_in.at[owner(order[j], 1 - core, side_x[side])]
        return remote(src, a_gu.at[side, j], s1.at[side, j], r1.at[side, j], sibling)

    def gu_own(side, j):
        return pltpu.make_async_copy(gu_in.at[owner(order[j], core, side_x[side])], own.at[j % 2], load.at[j % 2])

    def gu_b(j):
        return remote(a_gu.at[0, j], b_gu.at[j], s2.at[j], r2.at[j], across)

    def gu_c(j, wait=False):
        dst = c_gu.at[order[j] if wait else t]
        if ROUNDS[j] == 0:
            return pltpu.make_async_copy(a_gu.at[1, j], dst, load.at[2])
        return remote(a_gu.at[1, j], dst, s3.at[j], r3.at[j], members[ROUNDS[j]])

    def sum_own(side, j, more=None):
        gu_own(side, j).wait()
        gu_a(side, j).wait_recv()
        total = a_gu[side, j].astype(F32) + own[j % 2].astype(F32)
        if more is not None:
            total = total + more[j].astype(F32)
        a_gu[side, j] = total.astype(BF)

    def pump(first, last):
        for j in range(first, last):
            gu_own(1, j).start()
        for j in range(first, last):
            gu_b(j).wait_recv()
            if j + AHEAD < RING:
                go(gu_b(j + AHEAD))
            sum_own(1, j, b_gu)

    small = ((down_in, down_own, da, db, down_o), (og, None, oa, ob, out_o))

    def small_a(a, xo):
        return remote(small[a][0].at[2 * (1 - core) + xo], small[a][2].at[xo], sx.at[a, xo], rx.at[a, xo], sibling)

    def small_b(a):
        return remote(small[a][2].at[1 - x], small[a][3], sx.at[a, 2], rx.at[a, 2], across)

    def small_c(a, act):
        src, dst = small[a][2].at[x], small[a][4]

        @pl.when(core == y)
        def _():
            c = pltpu.make_async_copy(src, dst, load.at[3 + a])
            c.start() if act == 0 else c.wait()

        @pl.when(core != y)
        def _():
            c = remote(src, dst, sx.at[a, 3], rx.at[a, 3], diagonal)
            c.start() if act == 0 else c.wait()

    def q_a(side, j):
        src = grad_q.at[owner(order[j], 1 - core, side_x[side])]
        return remote(src, aq.at[side, j], q1.at[side, j], t1.at[side, j], sibling)

    def q_b(j):
        return remote(grad_q.at[owner(order[j], core, 1 - x)], bq.at[j], q2.at[j], t2.at[j], across)

    def q_c(j, wait=False):
        src, dst = grad_q.at[owner(order[j], core, x)], c_q.at[order[j] if wait else t]
        if ROUNDS[j] == 0:
            return pltpu.make_async_copy(src, dst, load.at[5])
        return remote(src, dst, q3.at[j], t3.at[j], members[ROUNDS[j]])

    def gain_a():
        return remote(gain_in, gsum.at[2], sg.at[RING], rg.at[RING], sibling)

    def gain_b():
        return remote(gsum.at[0], gsum.at[3], sg.at[RING + 1], rg.at[RING + 1], across)

    def gain_c(j):
        lanes = window(owner(partner(t, j), core, x))
        return remote(gsum.at[1, :, lanes], ga.at[j], sg.at[j], rg.at[j], members[j])

    gather = SlotGather(ring, ags, agr)

    def block(slot):
        if slot == 0:
            return p
        if slot == 7:
            return (p + 4) % RING
        s = (slot + 1) // 2
        return (p + (RING - s if slot % 2 else s)) % RING

    def place(slot, act):
        yq, zq = ring_yz(block(slot))
        src, dst = ring.at[pl.ds(slot * TOK, TOK)], seq.at[2 * zq + core]

        @pl.when(yq == core)
        def _():
            c = pltpu.make_async_copy(src, dst, load.at[6 + slot])
            c.start() if act == 0 else c.wait()

        @pl.when(yq != core)
        def _():
            c = remote(src, dst, pls.at[zq], plr.at[zq], sibling)
            c.start() if act == 0 else c.wait_send()

    first = pltpu.make_async_copy(d_branch, ring.at[pl.ds(0, TOK)], load.at[14])
    first.start()
    first.wait()
    gather.step(0)
    place(0, 0)
    for side in (0, 1):
        go(*[gu_a(side, j) for j in range(RING)])
        if side == 0:
            go(small_a(0, 0), small_a(0, 1))
    for j in range(RING):
        if j < 2:
            gu_own(0, j).start()
        sum_own(0, j)
        if j + 2 < RING:
            gu_own(0, j + 2).start()
        if j < AHEAD:
            go(gu_b(j))

    def down_sum(xo):
        c = pltpu.make_async_copy(down_in.at[2 * core + xo], down_own, load.at[16])
        c.start()
        small_a(0, xo).wait_recv()
        c.wait()
        da[xo] = (da[xo].astype(F32) + down_own[...].astype(F32)).astype(BF)

    down_sum(0)
    gather.step(1)
    place(1, 0)
    place(2, 0)
    pump(0, 1)
    down_sum(1)
    pump(1, 2)
    gather.step(2)
    place(3, 0)
    place(4, 0)
    pump(2, 4)
    gather.step(3)
    place(5, 0)
    place(6, 0)
    pump(4, 5)
    gather.finish()
    place(7, 0)
    for j in range(5):
        go(gu_c(j))
    for zq in range(NZ):
        dst = seq.at[2 * zq + 1 - core]
        remote(dst, dst, pls.at[zq], plr.at[zq], sibling).wait_recv()
    for slot in range(RING):
        place(slot, 1)
    gather.drain()
    hidden_load = pltpu.make_async_copy(hidden, ring, load.at[14])
    hidden_load.start()
    ready()

    for c in range(0, RING, 2):
        rows = pl.ds(c * TOK, 2 * TOK)
        d_att[rows] = contract_cols(seq[c : c + 2].reshape(2 * TOK, -1), wo[...]).astype(BF)

    def out_columns(cols):
        value = contract_rows(att[...].astype(BF), seq[:, :, cols].reshape(RING * TOK, 768))
        for f in range(4):
            og[f, :, cols] = value[64 * f : 64 * (f + 1)].astype(BF)

    tiles(3, 768, out_columns)
    go(small_a(1, 0), small_a(1, 1))
    pump(5, 6)
    go(gu_c(5))
    dk[...] = jnp.zeros_like(dk)
    dv[...] = jnp.zeros_like(dv)
    for i in range(4):
        r, upto = pl.ds(i * 256, 256), (i + 1) * 256
        keys, vals, query = k_in[0:upto], v_in[0:upto], q_in[r]
        bent = jnp.tanh(contract_cols(query, keys) / CAP)
        seen = lax.broadcasted_iota(jnp.int32, bent.shape, 1) <= i * 256 + lax.broadcasted_iota(jnp.int32, bent.shape, 0)
        weights = jnp.where(seen, jnp.exp(CAP * bent), 0.0)
        grad = d_att[r].astype(F32)
        delta = jnp.sum(grad * att[r], axis=-1, keepdims=True)
        d_probs = contract_cols(d_att[r], vals)
        d_raw = (weights * inv[r] * (d_probs - delta) * (1.0 - bent * bent)).astype(BF)
        dq = fold_rows(d_raw, keys) * (HD ** (-0.5))
        d_qkv[r, 0:HD] = unrotate(dq, cos[r], sine[r]).astype(BF)
        dk[0:upto] = dk[0:upto] + contract_rows(d_raw, query)
        scaled = grad * inv[r]
        high = scaled.astype(BF)
        rest = (scaled - high.astype(F32)).astype(BF)
        weights_b = weights.astype(BF)
        dv[0:upto] = dv[0:upto] + contract_rows(weights_b, high) + contract_rows(weights_b, rest)
        if i == 1:
            pump(6, 7)
            go(gu_c(6))
            go(small_b(0))
        if i == 3:
            pump(7, 8)
            go_self = gu_c(7)
            go_self.start()
    d_qkv[:, HD : 2 * HD] = unrotate(dk[...], cos[...], sine[...]).astype(BF)
    d_qkv[:, 2 * HD : 3 * HD] = dv[...].astype(BF)

    scatter = SlotScatter(part, buf, rss, rsr)

    def swap(zq, kept):
        where = pl.ds(pl.multiple_of(slot_of(ring_index(core, zq), p) * TOK, TOK), TOK)
        if kept:
            return pltpu.make_async_copy(seq.at[2 * zq + core], part.at[where], load.at[17 + zq])
        return remote(seq.at[2 * zq + 1 - core], part.at[where], sws.at[zq], swr.at[zq], sibling)

    def swapped(zq):
        where = pl.ds(pl.multiple_of(slot_of(ring_index(1 - core, zq), p) * TOK, TOK), TOK)
        return remote(seq.at[0], part.at[where], sws.at[zq], swr.at[zq], sibling)

    for zq in range(NZ):
        rows = d_qkv[2 * zq * TOK : (2 * zq + 2) * TOK]

        def columns(cols):
            value = contract_cols(rows, wq[cols])
            seq[2 * zq, :, cols] = value[0:TOK].astype(BF)
            seq[2 * zq + 1, :, cols] = value[TOK:].astype(BF)

        tiles(3, 768, columns)
        swap(zq, True).start()
        swap(zq, False).start()
    for zq in range(NZ):
        swap(zq, True).wait()
        swapped(zq).wait_recv()
    scatter.step(0)

    hidden_load.wait()

    def grad_half(half):
        def columns(cols):
            value = contract_rows(ring[:, pl.ds(half * 1152, 1152)], d_qkv[:, cols])
            for i in range(16):
                grad_q[half * 16 + i, :, cols] = value[72 * i : 72 * (i + 1)].astype(BF)

        tiles(3, 256, columns)

    grad_half(0)
    scatter.step(1)
    grad_half(1)
    for side in (0, 1):
        go(*[q_a(side, j) for j in range(RING)])
    for xo in (0, 1):
        small_a(1, xo).wait_recv()
        oa[xo] = (oa[xo].astype(F32) + og[2 * core + xo].astype(F32)).astype(BF)
    go(small_b(1))
    scatter.step(2)

    def q_sum(side, j):
        i = owner(order[j], core, side_x[side])
        q_a(side, j).wait_recv()
        total = grad_q[i].astype(F32) + aq[side, j].astype(F32)
        if side == 1:
            q_b(j).wait_recv()
            total = total + bq[j].astype(F32)
        grad_q[i] = total.astype(BF)

    for j in range(RING):
        q_sum(0, j)
        if j < AHEAD:
            go(q_b(j))
    small_b(0).wait_recv()
    da[x] = (da[x].astype(F32) + db[...].astype(F32)).astype(BF)
    small_c(0, 0)
    scatter.step(3)

    def q_round(j):
        q_sum(1, j)
        if j + AHEAD < RING:
            go(q_b(j + AHEAD))
        if ROUNDS[j] == 0:
            q_c(j).start()
        else:
            go(q_c(j))

    for j in range(4):
        q_round(j)
    small_b(1).wait_recv()
    oa[x] = (oa[x].astype(F32) + ob[...].astype(F32)).astype(BF)
    small_c(1, 0)

    def own_part(cols):
        slot = part[0:TOK, cols]
        d_hid_o[:, cols] = slot.astype(F32)

    tiles(3, 768, own_part)
    for j in range(4, RING):
        q_round(j)
    scatter.finish(d_hid_o)
    def pre_gain(r):
        value = d_hid_o[r] * rms_parts(block_in[r].astype(F32))[1]
        gain_in[0:1, 0:D] = gain_in[0:1, 0:D] + jnp.sum(value, axis=0, keepdims=True)

    by_rows(pre_gain)
    go(gain_a())
    gain_a().wait_recv()
    gsum[0] = gain_in[...] + gsum[2]
    go(gain_b())
    gain_b().wait_recv()
    gsum[1] = gsum[0] + gsum[3]
    go(*[gain_c(j) for j in range(1, RING)])
    total = gsum[1, :, window(owner(t, core, x))]
    for j in range(1, RING):
        gain_c(j).wait_recv()
        total = total + ga[j]
    gain_o[...] = total

    for j in range(RING):
        if ROUNDS[j] == 0:
            gu_c(j).wait()
            q_c(j).wait()
        else:
            gu_c(j, True).wait_recv()
            q_c(j, True).wait_recv()
    small_c(0, 1)
    small_c(1, 1)
    for zq in range(NZ):
        swap(zq, False).wait_send()
    scatter.drain()
    for c in pending:
        c.wait_send()


def backward(d_branch, gu, down, hidden, w_qkv, w_out, queries, keys, values, attended, inv_total, cos_tab, sine_tab,
             block, gain_parts, collective_id):
    n = 4 * RING
    rows, width = d_branch.shape
    shard = gu.shape[0] // n
    gu = gu.reshape(n, shard, 2 * UNITS)
    down = down.reshape(4, -1, width)
    total, down_rows, out_rows = RING * rows, down.shape[1], w_out.shape[0] // 4
    gain_shape = (8, PADDED)

    def out(*shape, dtype=BF):
        return jax.ShapeDtypeStruct(shape, dtype)

    def body(*refs):
        ins, rest = refs[:14], refs[14:]
        gains_ref, rest = rest[0], rest[1:]
        outs, scr = rest[:6], rest[6:]
        gain_scr, loaded, sems, scr = scr[0], scr[1:8], scr[8], scr[9:]
        gain_scr[...] = gains_ref[...]
        ins = list(ins)
        copies = []
        for i, place in enumerate((4, 6, 7, 8, 9, 11, 12)):
            copies.append(pltpu.make_async_copy(ins[place], loaded[i], sems.at[i]))
            copies[-1].start()
            ins[place] = loaded[i]

        def ready():
            for c in copies:
                c.wait()

        backward_kernel(ready, *ins, gain_scr, *outs, *scr)

    return pl.pallas_call(
        body,
        out_shape=[
            out(rows, width, dtype=F32), out(8, WINDOW, dtype=F32),
            out(RING, shard, 2 * UNITS), out(RING, shard, 3 * HD),
            out(down_rows, width), out(out_rows, width),
        ],
        in_specs=[HBM] * 5 + [VMEM] + [HBM] * 4 + [VMEM] + [HBM] * 2 + [VMEM] * 2,
        out_specs=[VMEM] * 2 + [HBM] * 4,
        scratch_shapes=[
            pltpu.VMEM(gain_shape, F32),
            pltpu.VMEM((width, 3 * HD), BF), pltpu.VMEM((total, HD), BF), pltpu.VMEM((total, HD), BF), pltpu.VMEM((total, HD), BF),
            pltpu.VMEM((total, HD), F32), pltpu.VMEM((total, HD // 2), F32), pltpu.VMEM((total, HD // 2), F32),
            DMA((7,)),
            pltpu.VMEM((total, width), BF), pltpu.VMEM((RING, rows, width), BF), pltpu.VMEM((total, width), BF),
            pltpu.VMEM((2, 4, rows, width), BF),
            pltpu.VMEM((total, HD), BF), pltpu.VMEM((total, 3 * HD), BF),
            pltpu.VMEM((total, HD), F32), pltpu.VMEM((total, HD), F32),
            pltpu.VMEM((n, shard, 3 * HD), BF), pltpu.VMEM((2, RING, shard, 3 * HD), BF), pltpu.VMEM((RING, shard, 3 * HD), BF),
            pltpu.VMEM((2, shard, 2 * UNITS), BF), pltpu.VMEM((2, RING, shard, 2 * UNITS), BF), pltpu.VMEM((RING, shard, 2 * UNITS), BF),
            pltpu.VMEM((down_rows, width), BF), pltpu.VMEM((2, down_rows, width), BF), pltpu.VMEM((down_rows, width), BF),
            pltpu.VMEM((4, out_rows, width), BF), pltpu.VMEM((2, out_rows, width), BF), pltpu.VMEM((out_rows, width), BF),
            pltpu.VMEM((RING, 8, WINDOW), F32), pltpu.VMEM((4,) + gain_shape, F32),
            DMA((21,)),
            DMA((2, 4, SUB)), DMA((2, 4, SUB)), DMA((NZ,)), DMA((NZ,)), DMA((2, 4, SUB)), DMA((2, 4, SUB)), DMA((NZ,)), DMA((NZ,)),
            DMA((2, RING)), DMA((2, RING)), DMA((RING,)), DMA((RING,)), DMA((RING,)), DMA((RING,)),
            DMA((2, RING)), DMA((2, RING)), DMA((RING,)), DMA((RING,)), DMA((RING,)), DMA((RING,)),
            DMA((2, 4)), DMA((2, 4)), DMA((RING + 2,)), DMA((RING + 2,)),
        ],
        compiler_params=params(collective_id, 60),
    )(d_branch, gu, down, hidden, w_qkv, w_out, queries, keys, values, attended, inv_total, cos_tab, sine_tab, block, gain_parts)


def results_kernel(gu, qkv, down, out, d_hidden, d_middle, block, gains,
                   gate_o, up_o, query_o, key_o, value_o, down_o, out_o, token_o):
    for i in range(2):
        units, heads = pl.ds(i * UNITS, UNITS), pl.ds(i * HD, HD)
        gate_o[:, units] = gu[i, :, 0:UNITS].astype(F32)
        up_o[:, units] = gu[i, :, UNITS : 2 * UNITS].astype(F32)
        query_o[:, heads] = qkv[i, :, 0:HD].astype(F32)
    key_o[...] = qkv[0, :, HD : 2 * HD].astype(F32) + qkv[1, :, HD : 2 * HD].astype(F32)
    value_o[...] = qkv[0, :, 2 * HD :].astype(F32) + qkv[1, :, 2 * HD :].astype(F32)
    down_o[...] = down[...].astype(F32)
    out_o[...] = out[...].astype(F32)
    inverse, normed = rms_parts(block[...].astype(F32))
    back = norm_back(d_hidden[...] * (1.0 + gains[0:1]), normed, inverse)
    token_o[...] = (d_middle[...] + back).astype(BF)


def results(gu, qkv, down, out, d_hidden, d_middle, block, gains):
    steps = RING // 2
    shard, width = gu.shape[1], down.shape[1]
    tok, down_rows, out_rows = d_hidden.shape[0] // steps, down.shape[0] // steps, out.shape[0] // steps

    def rows(n, wide):
        return pl.BlockSpec((n, wide), lambda i: (i, 0))

    def columns(wide):
        return pl.BlockSpec((shard, wide), lambda i: (0, i))

    def full(*shape):
        return jax.ShapeDtypeStruct(shape, F32)

    return pl.pallas_call(
        results_kernel,
        grid=(steps,),
        out_shape=[
            full(shard, FF), full(shard, FF), full(shard, H * HD), full(shard, KVH * HD), full(shard, KVH * HD),
            full(*down.shape), full(*out.shape), jax.ShapeDtypeStruct(d_hidden.shape, BF),
        ],
        in_specs=[
            pl.BlockSpec((2, shard, 2 * UNITS), lambda i: (i, 0, 0)), pl.BlockSpec((2, shard, 3 * HD), lambda i: (i, 0, 0)),
            rows(down_rows, width), rows(out_rows, width), rows(tok, width), rows(tok, width), rows(tok, width),
            pl.BlockSpec(gains.shape, lambda i: (0, 0)),
        ],
        out_specs=[
            columns(2 * UNITS), columns(2 * UNITS), columns(2 * HD), columns(HD), columns(HD),
            rows(down_rows, width), rows(out_rows, width), rows(tok, width),
        ],
        compiler_params=pltpu.CompilerParams(vmem_limit_bytes=60 * 2**20),
    )(gu, qkv, down, out, d_hidden, d_middle, block, gains)


def on_ring(
    tokens, w_query, w_key, w_value, w_out, w_gate, w_up, w_down,
    pre_gain, post_gain, pre_ffn_gain, post_ffn_gain, out_grad,
):
    ids = iter(range(32))
    length = RING * tokens.shape[1]
    shard_gain = pre_gain.shape[0]
    mine = lax.axis_index("ctx") * 4 + lax.axis_index("fsdp")
    gains = jnp.stack([pre_gain, post_gain, pre_ffn_gain, post_ffn_gain]).astype(F32)
    gains = lax.dynamic_update_slice(jnp.zeros((8, WINDOW), F32), gains, (0, (mine * shard_gain) % 128))
    cos_tab, sine_tab = (jnp.asarray(table) for table in constant_tables(length, HD))
    w_gu, down_in, hidden, w_qkv, queries, keys, values, attended, out_in, gains, inv_total, branch = forward(
        w_gate, w_up, w_query, w_key, w_value, w_down, w_out, tokens[0], gains, cos_tab, sine_tab, next(ids)
    )
    w_gu, hidden = w_gu.reshape(D, 2 * UNITS), hidden.reshape(length, D)
    w_dn = down_in.reshape(UNITS, D)
    w_ot = out_in.reshape(HD, D)
    output, d_middle, d_branch, gain_parts, down_part, gu_part = feed_forward(
        branch, tokens[0], gains, out_grad[0], w_gu, w_dn, next(ids)
    )
    d_hidden, gain_g, gu_g, qkv_g, down_g, out_g = backward(
        d_branch, gu_part, down_part, hidden, w_qkv, w_ot, queries, keys, values, attended, inv_total,
        cos_tab, sine_tab, tokens[0], gain_parts, next(ids),
    )
    gate_g, up_g, query_g, key_g, value_g, down_g, out_g, token_grad = results(
        gu_g, qkv_g, down_g, out_g, d_hidden, d_middle, tokens[0], gains
    )
    gain_g = lax.dynamic_slice(gain_g, (0, (mine * shard_gain) % 128), (4, shard_gain))
    return (
        output[None], token_grad[None],
        query_g, key_g, value_g, out_g, gate_g, up_g, down_g,
        gain_g[0], gain_g[1], gain_g[2], gain_g[3],
    )


ROW_FOLD = 4


def head_tables(positions, width):
    half_width = width // 2
    inv_freqs = ROPE_BASE ** (-jnp.arange(half_width, dtype=jnp.float32) * 2.0 / width)
    angles = positions.astype(jnp.float32)[:, None] * inv_freqs[None, :]
    return (jnp.cos(angles)[:, None, :], jnp.sin(angles)[:, None, :])


def rotate_heads(heads_in, cos_tab, sine_tab):
    half_width = heads_in.shape[-1] // 2
    front_half = heads_in[..., :half_width]
    back_half = heads_in[..., half_width:]
    return jnp.concatenate(
        [front_half * cos_tab - back_half * sine_tab, back_half * cos_tab + front_half * sine_tab],
        axis=-1,
    )


def unrotate_heads(grad_in, cos_tab, sine_tab):
    half_width = grad_in.shape[-1] // 2
    front_half = grad_in[..., :half_width]
    back_half = grad_in[..., half_width:]
    return jnp.concatenate(
        [front_half * cos_tab + back_half * sine_tab, back_half * cos_tab - front_half * sine_tab],
        axis=-1,
    )


def to_groups(flat_heads, tok_rows, q_group):
    shaped = flat_heads.reshape(tok_rows, KVH, q_group, HD)
    return jnp.transpose(shaped, (1, 2, 0, 3)).reshape(KVH, q_group * tok_rows, HD)


def from_groups(grouped, tok_rows, q_group):
    shaped = grouped.reshape(KVH, q_group, tok_rows, HD)
    return jnp.transpose(shaped, (2, 0, 1, 3)).reshape(tok_rows, KVH * q_group * HD)


def grad_rows(left, right, folding, count):
    block = contract_rows(left, right)
    return block.reshape(count, right.shape[1] // folding)


def blockwise(step_fn, carry, piece, width):
    key_count = piece[0].shape[0]
    n_steps = key_count // width
    stacked = tuple((member.reshape(n_steps, width, member.shape[1]) for member in piece))

    def one_step(partial_value, block_item):
        block_index, members = block_item
        return (step_fn(partial_value, members, block_index * width), None)

    carry, unused = lax.scan(one_step, carry, (jnp.arange(n_steps, dtype=jnp.int32), stacked))
    return carry


def block_grads(query_g, query_pos, d_att_g, delta, inv_tot, key_block, value_block, key_first):
    key_count = key_block.shape[0]
    key_grp = key_block.reshape(key_count, KVH, HD)
    value_grp = value_block.reshape(key_count, KVH, HD)
    raw_scores = jnp.einsum("grd,ngd->grn", query_g, key_grp, preferred_element_type=jnp.float32)
    capped = CAP * jnp.tanh(raw_scores / CAP)
    key_pos = key_first + jnp.arange(key_count, dtype=jnp.int32)
    allowed = key_pos[None, None, :] <= query_pos[None, :, None]
    weights = jnp.where(allowed, jnp.exp(capped), 0.0)
    prob_rows = weights * inv_tot[..., None]
    d_probs = jnp.einsum("grd,ngd->grn", d_att_g, value_grp, preferred_element_type=jnp.float32)
    slope = 1.0 - capped / CAP * (capped / CAP)
    d_raw = (prob_rows * (d_probs - delta[..., None]) * slope).astype(jnp.bfloat16)
    d_query = jnp.einsum("grn,ngd->grd", d_raw, key_grp, preferred_element_type=jnp.float32)
    d_key = jnp.einsum("grn,grd->ngd", d_raw, query_g, preferred_element_type=jnp.float32)
    weights_b = weights.astype(jnp.bfloat16)
    d_scaled = d_att_g.astype(jnp.float32) * inv_tot[..., None]
    scaled_high = d_scaled.astype(jnp.bfloat16)
    scaled_rest = (d_scaled - scaled_high.astype(jnp.float32)).astype(jnp.bfloat16)
    d_value = jnp.einsum("grn,grd->ngd", weights_b, scaled_high, preferred_element_type=jnp.float32)
    d_value = d_value + jnp.einsum(
        "grn,grd->ngd", weights_b, scaled_rest, preferred_element_type=jnp.float32
    )
    return (d_query, d_key.reshape(key_count, KVH * HD), d_value.reshape(key_count, KVH * HD))


def on_any_mesh(
    tokens,
    w_query,
    w_key,
    w_value,
    w_out,
    w_gate,
    w_up,
    w_down,
    pre_gain,
    post_gain,
    pre_ffn_gain,
    post_ffn_gain,
    out_grad,
):
    tok_rows = tokens.shape[1]
    q_group = H // KVH
    q_scale = HD ** (-0.5)
    width_q = H * HD
    width_kv = KVH * HD
    width_qkv = width_q + 2 * width_kv
    n_ctx = lax.axis_size("ctx")
    my_block = lax.axis_index("ctx")
    my_start = my_block * tok_rows
    positions = my_start + jnp.arange(tok_rows, dtype=jnp.int32)
    cos_tab, sine_tab = head_tables(positions, HD)
    row_pos = jnp.tile(positions, q_group)
    last_pos = my_start + tok_rows - 1
    resid_in = tokens[0].astype(jnp.float32)
    qkv_shard = jnp.concatenate([w_query, w_key, w_value], axis=1)
    gateup_shard = jnp.concatenate([w_gate, w_up], axis=1)
    shard_rows = qkv_shard.shape[0]
    gains_shard = jnp.stack([pre_gain, post_gain, pre_ffn_gain, post_ffn_gain])
    full_gains, full_qkv, full_out = (
        lax.all_gather(gains_shard, ("ctx", "fsdp"), axis=1, tiled=True),
        lax.all_gather(qkv_shard, ("ctx", "fsdp"), axis=0, tiled=True),
        lax.all_gather(w_out, ("ctx", "fsdp"), axis=0, tiled=True),
    )
    factors = 1.0 + full_gains.astype(jnp.float32)
    pre_factor, post_factor, pre_ffn_factor, post_ffn_factor = (
        factors[0],
        factors[1],
        factors[2],
        factors[3],
    )
    inv_pre, normed_pre = rms_parts(resid_in)
    hidden = (normed_pre * pre_factor).astype(jnp.bfloat16)
    projected = jnp.dot(hidden, full_qkv, preferred_element_type=jnp.float32)
    query_lin = projected[:, :width_q].reshape(tok_rows, H, HD)
    queries = (
        (rotate_heads(query_lin, cos_tab, sine_tab) * q_scale)
        .astype(jnp.bfloat16)
        .reshape(tok_rows, width_q)
    )
    query_grp = to_groups(queries, tok_rows, q_group)
    key_lin = projected[:, width_q : width_q + width_kv].reshape(tok_rows, KVH, HD)
    key_rows = rotate_heads(key_lin, cos_tab, sine_tab).astype(jnp.bfloat16).reshape(tok_rows, width_kv)
    value_rows = projected[:, width_q + width_kv :].astype(jnp.bfloat16)

    def add_block(partial_value, piece, first_row):
        key_block, value_block = piece

        def add_compute_block(state):
            row_total, weighted = state
            key_count = key_block.shape[0]
            key_grp = key_block.reshape(key_count, KVH, HD)
            raw_scores = jnp.einsum(
                "grd,ngd->grn", query_grp, key_grp, preferred_element_type=jnp.float32
            )
            capped = CAP * jnp.tanh(raw_scores / CAP)
            key_pos = first_row + jnp.arange(key_count, dtype=jnp.int32)
            allowed = key_pos[None, None, :] <= row_pos[None, :, None]
            weights = jnp.where(allowed, jnp.exp(capped), 0.0)
            value_grp = value_block.reshape(key_count, KVH, HD)
            weighted = weighted + jnp.einsum(
                "grn,ngd->grd",
                weights.astype(jnp.bfloat16),
                value_grp,
                preferred_element_type=jnp.float32,
            )
            return (row_total + jnp.sum(weights, axis=-1), weighted)

        def add_skip_block(state):
            return state

        return lax.cond(first_row <= last_pos, add_compute_block, add_skip_block, partial_value)

    start_state = (
        jnp.zeros((KVH, q_group * tok_rows), jnp.float32),
        jnp.zeros((KVH, q_group * tok_rows, HD), jnp.float32),
    )
    row_total, weighted = blockwise(
        add_block,
        start_state,
        (
            lax.all_gather(key_rows, "ctx", axis=0, tiled=True),
            lax.all_gather(value_rows, "ctx", axis=0, tiled=True),
        ),
        512,
    )
    inv_total = 1.0 / row_total
    attended_grp = weighted * inv_total[..., None]
    attended_b = from_groups(attended_grp, tok_rows, q_group).astype(jnp.bfloat16)
    branch = jnp.dot(attended_b, full_out, preferred_element_type=jnp.float32)
    inv_post, normed_post = rms_parts(branch)
    middle = resid_in + normed_post * post_factor
    inv_mid, normed_mid = rms_parts(middle)
    hidden_ffn = (normed_mid * pre_ffn_factor).astype(jnp.bfloat16)
    gate_up = fold_rows(
        hidden_ffn, lax.all_gather(gateup_shard, ("ctx", "fsdp"), axis=0, tiled=True)
    )
    gate_lin = gate_up[:, :FF]
    up_lin = gate_up[:, FF:]
    active = gated(gate_lin, up_lin).astype(jnp.bfloat16)
    ffn_branch = fold_rows(active, lax.all_gather(w_down, ("ctx", "fsdp"), axis=0, tiled=True))
    inv_ffn, normed_ffn = rms_parts(ffn_branch)
    output = (middle + normed_ffn * post_ffn_factor).astype(jnp.bfloat16)
    out_cot = out_grad[0].astype(jnp.float32)
    post_ffn_part = jnp.sum(out_cot * normed_ffn, axis=0)
    d_ffn_b = norm_back(out_cot * post_ffn_factor, normed_ffn, inv_ffn).astype(jnp.bfloat16)
    down_total = lax.psum_scatter(
        grad_rows(active, d_ffn_b, 1, lax.axis_size(("ctx", "fsdp")) * w_down.shape[0]),
        ("ctx", "fsdp"),
        scatter_dimension=0,
        tiled=True,
    )
    d_active = contract_cols(d_ffn_b, lax.all_gather(w_down, ("ctx", "fsdp"), axis=0, tiled=True))
    unused_value, gate_pull = jax.vjp(gated, gate_lin, up_lin)
    d_gate, d_up = gate_pull(d_active)
    d_gateup_b = jnp.concatenate([d_gate.astype(jnp.bfloat16), d_up.astype(jnp.bfloat16)], axis=1)
    gateup_folded = lax.psum_scatter(
        grad_rows(
            hidden_ffn,
            d_gateup_b,
            ROW_FOLD,
            lax.axis_size(("ctx", "fsdp")) * (ROW_FOLD * shard_rows),
        ),
        ("ctx", "fsdp"),
        scatter_dimension=0,
        tiled=True,
    )
    gateup_total = gateup_folded.reshape(shard_rows, 2 * FF)
    d_hidden_ffn = contract_cols(
        d_gateup_b, lax.all_gather(gateup_shard, ("ctx", "fsdp"), axis=0, tiled=True)
    )
    pre_ffn_part = jnp.sum(d_hidden_ffn * normed_mid, axis=0)
    d_middle = out_cot + norm_back(d_hidden_ffn * pre_ffn_factor, normed_mid, inv_mid)
    back_qkv, back_out = (
        lax.all_gather(qkv_shard, ("ctx", "fsdp"), axis=0, tiled=True),
        lax.all_gather(w_out, ("ctx", "fsdp"), axis=0, tiled=True),
    )
    post_gain_part = jnp.sum(d_middle * normed_post, axis=0)
    d_branch_b = norm_back(d_middle * post_factor, normed_post, inv_post).astype(jnp.bfloat16)
    w_out_part = contract_rows(attended_b, d_branch_b)
    d_attended = contract_cols(d_branch_b, back_out).astype(jnp.bfloat16)
    d_att_grp = to_groups(d_attended, tok_rows, q_group)
    row_delta = jnp.sum(d_att_grp.astype(jnp.float32) * attended_grp, axis=-1)
    zero_rows = jnp.zeros((tok_rows, width_kv), jnp.float32)
    zero_query = jnp.zeros((KVH, q_group * tok_rows, HD), jnp.float32)
    block_ids = jnp.arange(n_ctx, dtype=jnp.int32)
    all_keys, all_values = (
        lax.all_gather(key_rows, "ctx", axis=0, tiled=True),
        lax.all_gather(value_rows, "ctx", axis=0, tiled=True),
    )

    def returned_step(acc_query, block_item):
        block_index, key_block, value_block = block_item
        first_row = block_index * tok_rows

        def returned_compute_block(acc_in):
            d_query, d_key, d_value = block_grads(
                query_grp,
                row_pos,
                d_att_grp,
                row_delta,
                inv_total,
                key_block,
                value_block,
                first_row,
            )
            return (acc_in + d_query, (d_key, d_value))

        def returned_skip_block(acc_in):
            return (acc_in, (zero_rows, zero_rows))

        return lax.cond(
            first_row <= last_pos, returned_compute_block, returned_skip_block, acc_query
        )

    key_blocks = all_keys.reshape(n_ctx, tok_rows, width_kv)
    value_blocks = all_values.reshape(n_ctx, tok_rows, width_kv)
    d_query_grp, key_terms = lax.scan(
        returned_step, zero_query, (block_ids, key_blocks, value_blocks)
    )
    key_term_rows = key_terms[0].reshape(n_ctx * tok_rows, width_kv)
    value_term_rows = key_terms[1].reshape(n_ctx * tok_rows, width_kv)
    d_keys, d_values = (
        lax.psum_scatter(
            key_term_rows.astype(jnp.bfloat16), "ctx", scatter_dimension=0, tiled=True
        ).astype(jnp.float32),
        lax.psum_scatter(
            value_term_rows.astype(jnp.bfloat16), "ctx", scatter_dimension=0, tiled=True
        ).astype(jnp.float32),
    )
    d_query_flat = from_groups(d_query_grp, tok_rows, q_group).reshape(tok_rows, H, HD) * q_scale
    dq_lin = (
        unrotate_heads(d_query_flat, cos_tab, sine_tab).astype(jnp.bfloat16).reshape(tok_rows, width_q)
    )
    dk_lin = (
        unrotate_heads(d_keys.reshape(tok_rows, KVH, HD), cos_tab, sine_tab)
        .astype(jnp.bfloat16)
        .reshape(tok_rows, width_kv)
    )
    dv_lin = d_values.astype(jnp.bfloat16)
    dqkv_b = jnp.concatenate([dq_lin, dk_lin, dv_lin], axis=1)
    d_hidden = contract_cols(dqkv_b, back_qkv)
    qkv_part = contract_rows(hidden, dqkv_b).reshape(ROW_FOLD * D, width_qkv // ROW_FOLD)
    pre_gain_part = jnp.sum(d_hidden * normed_pre, axis=0)
    token_grad = d_middle + norm_back(d_hidden * pre_factor, normed_pre, inv_pre)
    gain_parts = jnp.stack([pre_gain_part, post_gain_part, pre_ffn_part, post_ffn_part])
    qkv_folded, out_total, gain_totals = (
        lax.psum_scatter(qkv_part, ("ctx", "fsdp"), scatter_dimension=0, tiled=True),
        lax.psum_scatter(w_out_part, ("ctx", "fsdp"), scatter_dimension=0, tiled=True),
        lax.psum_scatter(gain_parts, ("ctx", "fsdp"), scatter_dimension=1, tiled=True),
    )
    qkv_total = qkv_folded.reshape(shard_rows, width_qkv)
    return (
        output[None],
        token_grad.astype(jnp.bfloat16)[None],
        qkv_total[:, :width_q],
        qkv_total[:, width_q : width_q + width_kv],
        qkv_total[:, width_q + width_kv :],
        out_total,
        gateup_total[:, :FF],
        gateup_total[:, FF:],
        down_total,
        gain_totals[0],
        gain_totals[1],
        gain_totals[2],
        gain_totals[3],
    )


def solution(mesh):
    ring = mesh.shape["ctx"] == RING and mesh.shape["fsdp"] == 4
    tokens, rows, gains = P("fsdp", "ctx", None), P(("ctx", "fsdp"), None), P(("ctx", "fsdp"))
    return jax.shard_map(
        on_ring if ring else on_any_mesh,
        mesh=mesh,
        in_specs=(tokens,) + (rows,) * 7 + (gains,) * 4 + (tokens,),
        out_specs=(tokens, tokens) + (rows,) * 7 + (gains,) * 4,
        check_vma=False,
    )
```

```python
import jax
import jax.numpy as jnp
import numpy as np
from jax import lax
from jax.experimental import pallas as pl
from jax.experimental.pallas import tpu as pltpu
from jax.sharding import PartitionSpec as P

D = 2304
H = 8
KVH = 4
HD = 256
CAP = 50
FF = 9216

EPSILON = 1e-06
ROPE_BASE = 10000.0

MESH = pl.DeviceIdType.MESH
HBM = pl.BlockSpec(memory_space=pl.ANY)
VMEM = pl.BlockSpec(memory_space=pltpu.VMEM)
DMA = pltpu.SemaphoreType.DMA
BF = jnp.bfloat16
F32 = jnp.float32


def constant_tables(length, width):
    exponents = -np.arange(width // 2, dtype=np.float32) * np.float32(2.0) / np.float32(width)
    inv_freqs = np.power(np.float32(ROPE_BASE), exponents, dtype=np.float32)
    angles = np.arange(length, dtype=np.float32)[:, None] * inv_freqs[None, :]
    return np.cos(angles), np.sin(angles)


def rotate(rows, cos_tab, sine_tab):
    half_width = rows.shape[-1] // 2
    front, back = rows[..., :half_width], rows[..., half_width:]
    return jnp.concatenate(
        [front * cos_tab - back * sine_tab, back * cos_tab + front * sine_tab], axis=-1
    )


def unrotate(rows, cos_tab, sine_tab):
    half_width = rows.shape[-1] // 2
    front, back = rows[..., :half_width], rows[..., half_width:]
    return jnp.concatenate(
        [front * cos_tab + back * sine_tab, back * cos_tab - front * sine_tab], axis=-1
    )


def rms_parts(values_in):
    inverse = lax.rsqrt(jnp.mean(values_in * values_in, axis=-1, keepdims=True) + EPSILON)
    return (inverse, values_in * inverse)


def norm_back(grad_normed, normed, inverse):
    return inverse * (grad_normed - normed * jnp.mean(grad_normed * normed, axis=-1, keepdims=True))


def contract_rows(left, right):
    return lax.dot_general(left, right, (((0,), (0,)), ((), ())), preferred_element_type=F32)


def contract_cols(left, right):
    return lax.dot_general(left, right, (((1,), (1,)), ((), ())), preferred_element_type=F32)


def fold_rows(left, right):
    return jnp.dot(left, right, preferred_element_type=F32)


def gated(gate_in, up_in):
    return jax.nn.gelu(gate_in, approximate=True) * up_in


NZ = 4
RING = 2 * NZ


def my_place():
    c, f = lax.axis_index("ctx"), lax.axis_index("fsdp")
    return c // 2, c % 2, f // 2, f % 2


def ring_index(y, z):
    return z + y * (RING - 1 - 2 * z)


def ring_yz(q):
    y = q // NZ
    return y, q + y * (RING - 1 - 2 * q)


def device(z, core, y, x):
    return (2 * z + core, 2 * y + x)


def ring_device(q, core, x):
    y, z = ring_yz(q)
    return device(z, core, y, x)


def remote(src, dst, send_sem, recv_sem, where):
    return pltpu.make_async_remote_copy(
        src_ref=src,
        dst_ref=dst,
        send_sem=send_sem,
        recv_sem=recv_sem,
        device_id=where,
        device_id_type=MESH,
    )


def greet(places, meanwhile=None):
    barrier = pltpu.get_barrier_semaphore()
    for place in places:
        pl.semaphore_signal(barrier, inc=1, device_id=place, device_id_type=MESH)
    if meanwhile is not None:
        meanwhile()
    pl.semaphore_wait(barrier, len(places))


def params(collective_id, vmem_mib=56):
    return pltpu.CompilerParams(
        collective_id=collective_id,
        has_side_effects=True,
        vmem_limit_bytes=vmem_mib * 2**20,
    )


SUB = 4


def ring_parts(direction, step, half_step):
    if step != half_step:
        return list(range(SUB))
    half = SUB // 2
    return list(range(half)) if direction == 0 else list(range(half, SUB))


TOK = 128
UNITS = FF // RING
TILE = 128
GELU_K = 0.7978845608028654
GELU_A = 0.044715


class SlotGather:
    def __init__(self, buf, ss, rs):
        z, core, y, x = my_place()
        p = ring_index(y, z)
        self.buf, self.ss, self.rs = buf, ss, rs
        self.near = (ring_device((p + 1) % RING, core, x), ring_device((p + RING - 1) % RING, core, x))
        self.pending = []

    def copy(self, direction, step, k):
        piece = TOK // SUB
        src = 0 if step == 0 else 2 * step - 1 + direction
        dst = 7 if step == 3 else 2 * step + 1 + direction
        return remote(
            self.buf.at[pl.ds(src * TOK + k * piece, piece)],
            self.buf.at[pl.ds(dst * TOK + k * piece, piece)],
            self.ss.at[direction, step, k],
            self.rs.at[direction, step, k],
            self.near[direction],
        )

    def step(self, step):
        for k in range(SUB):
            for direction in (0, 1):
                if step > 0:
                    self.copy(direction, step - 1, k).wait_recv()
                if k in ring_parts(direction, step, 3):
                    c = self.copy(direction, step, k)
                    c.start()
                    self.pending.append(c)

    def finish(self):
        for direction in (0, 1):
            for k in ring_parts(direction, 3, 3):
                self.copy(direction, 3, k).wait_recv()

    def drain(self):
        for c in self.pending:
            c.wait_send()


class SlotScatter:
    def __init__(self, part, buf, ss, rs):
        z, core, y, x = my_place()
        p = ring_index(y, z)
        self.part, self.buf, self.ss, self.rs = part, buf, ss, rs
        self.near = (ring_device((p + 1) % RING, core, x), ring_device((p + RING - 1) % RING, core, x))
        self.pending = []

    def copy(self, direction, step, k, src):
        rows = pl.ds(k * (TOK // SUB), TOK // SUB)
        return remote(
            src,
            self.buf.at[direction, step, rows],
            self.ss.at[direction, step, k],
            self.rs.at[direction, step, k],
            self.near[direction],
        )

    def step(self, step):
        piece = TOK // SUB
        for k in range(SUB):
            rows = pl.ds(k * piece, piece)
            for direction in (0, 1):
                if k not in ring_parts(direction, step, 0):
                    continue
                slot = 7 if step == 0 else 2 * (4 - step) - direction
                mine = pl.ds(slot * TOK + k * piece, piece)
                src = self.part.at[mine]
                if step > 0 and k in ring_parts(direction, step - 1, 0):
                    src = self.buf.at[direction, step - 1, rows]
                    self.copy(direction, step - 1, k, src).wait_recv()
                    src[...] = (src[...].astype(F32) + self.part[mine].astype(F32)).astype(BF)
                c = self.copy(direction, step, k, src)
                c.start()
                self.pending.append(c)

    def finish(self, total):
        for k in range(SUB):
            rows = pl.ds(k * (TOK // SUB), TOK // SUB)
            for direction in (0, 1):
                src = self.buf.at[direction, 3, rows]
                self.copy(direction, 3, k, src).wait_recv()
                total[rows] = total[rows] + src[...].astype(F32)

    def drain(self):
        for c in self.pending:
            c.wait_send()


def tiles(count, width, body):
    def step(i, carry):
        body(pl.ds(pl.multiple_of(i * width, width), width))
        return carry

    lax.fori_loop(0, count, step, 0)


def gelu_parts(v):
    bent = jnp.tanh(GELU_K * (v + GELU_A * (v * v * v)))
    value = 0.5 * v * (1.0 + bent)
    slope = 0.5 * (1.0 + bent) + 0.5 * v * (1.0 - bent * bent) * (GELU_K * (1.0 + 3.0 * GELU_A * (v * v)))
    return value, slope


PAIRS = ((128, 256), (384, 256), (640, 256))
LAST = (896, 128)
OWN = (0, 128)


def by_rows(body):
    def step(i, carry):
        body(pl.ds(pl.multiple_of(i * 32, 32), 32))
        return carry

    lax.fori_loop(0, TOK // 32, step, 0)


def feed_forward_kernel(branch, block, gains, cot, w_hbm, wd_hbm,
                        out_o, d_mid_o, d_branch_o, gain_o, wd_grad, gu_grad,
                        wgu, wd, ha, gu, act, part, buf, df, dgu, middle, total, stage,
                        w_sem, ags, agr, rss, rsr, out_sem):
    gather = [SlotGather(b, ags.at[i], agr.at[i]) for i, b in enumerate((ha, df))]
    scatter = [SlotScatter(part, buf, rss.at[i], rsr.at[i]) for i in range(2)]
    loads = [
        pltpu.make_async_copy(w_hbm, wgu, w_sem.at[0]),
        pltpu.make_async_copy(wd_hbm, wd, w_sem.at[1]),
    ]
    for c in loads:
        c.start()

    def head():
        def rows(r):
            mid = block[r].astype(F32) + rms_parts(branch[r])[1] * (1.0 + gains[1:2])
            middle[r] = mid
            ha[r] = (rms_parts(mid)[1] * (1.0 + gains[2:3])).astype(BF)

        by_rows(rows)

    greet(gather[0].near, head)
    gather[0].step(0)
    gain_o[...] = jnp.zeros(gain_o.shape, F32)
    loads[0].wait()

    def gate_up(first, count):
        rows = pl.ds(first, count)

        def column(cols):
            gu[rows, cols] = fold_rows(ha[rows], wgu[:, cols])

        tiles(3, 768, column)

        def finish(i, carry):
            r = pl.ds(pl.multiple_of(first + i * 32, 32), 32)
            act[r] = (gelu_parts(gu[r, 0:UNITS])[0] * gu[r, UNITS : 2 * UNITS]).astype(BF)
            return carry

        lax.fori_loop(0, count // 32, finish, 0)

    def down_part(first, count, dst):
        def column(cols):
            value = fold_rows(act[pl.ds(first, count)], wd[:, cols])
            dst[pl.ds(first, count), cols] = value.astype(dst.dtype)

        tiles(3, 768, column)

    def active_back(first, count):
        rows = pl.ds(first, count)
        for n in range(3):
            cols, up_cols = pl.ds(n * 384, 384), pl.ds(UNITS + n * 384, 384)
            d_active = contract_cols(df[rows], wd[cols])
            value, slope = gelu_parts(gu[rows, cols])
            dgu[rows, cols] = (d_active * gu[rows, up_cols] * slope).astype(BF)
            dgu[rows, up_cols] = (d_active * value).astype(BF)

    def hidden_part(first, count, dst):
        def column(cols):
            value = contract_cols(dgu[pl.ds(first, count)], wgu[cols])
            dst[pl.ds(first, count), cols] = value.astype(dst.dtype)

        tiles(3, 768, column)

    def hidden_near():
        def column(cols):
            value = contract_cols(dgu[0 : 3 * TOK], wgu[cols])
            total[:, cols] = value[0:TOK]
            part[TOK : 3 * TOK, cols] = value[TOK:].astype(BF)

        tiles(3, 768, column)

    n_down = UNITS // TILE
    n_tiles = n_down + ha.shape[1] // TILE

    def grad_out(i):
        slot = i % 2
        if i < n_down:
            return pltpu.make_async_copy(stage.at[slot], wd_grad.at[pl.ds(i * TILE, TILE)], out_sem.at[slot])
        return pltpu.make_async_copy(stage.at[slot], gu_grad.at[pl.ds((i - n_down) * TILE, TILE)], out_sem.at[slot])

    def grad_tiles(first, last):
        for i in range(first, last):
            if i >= 2:
                grad_out(i - 2).wait()
            if i < n_down:
                value = contract_rows(act[:, pl.ds(i * TILE, TILE)], df[...])
            else:
                value = contract_rows(ha[:, pl.ds((i - n_down) * TILE, TILE)], dgu[...])
            stage[i % 2] = value.astype(BF)
            grad_out(i).start()

    gate_up(*OWN)
    for step, pair in enumerate(PAIRS):
        gather[0].step(step + 1)
        if step == 0:
            loads[1].wait()
        gate_up(*pair)
    gather[0].finish()
    gate_up(*LAST)
    down_part(*LAST, part)
    scatter[0].step(0)
    for step, pair in enumerate(PAIRS[::-1]):
        down_part(*pair, part)
        scatter[0].step(step + 1)
    down_part(*OWN, total)
    scatter[0].finish(total)
    gather[0].drain()
    scatter[0].drain()

    def turn(r):
        inverse, normed = rms_parts(total[r])
        df[r] = norm_back(cot[r].astype(F32) * (1.0 + gains[3:4]), normed, inverse).astype(BF)

    def add_gain(i, value):
        gain_o[i : i + 1, 0:D] = gain_o[i : i + 1, 0:D] + jnp.sum(value, axis=0, keepdims=True)

    def outputs(r):
        normed = rms_parts(total[r])[1]
        out_o[r] = (middle[r] + normed * (1.0 + gains[3:4])).astype(BF)
        add_gain(3, cot[r].astype(F32) * normed)

    by_rows(turn)
    gather[1].step(0)
    by_rows(outputs)
    active_back(*OWN)
    for step, pair in enumerate(PAIRS):
        gather[1].step(step + 1)
        active_back(*pair)
    gather[1].finish()
    active_back(*LAST)
    hidden_part(*LAST, part)
    scatter[1].step(0)
    done = 0
    for step, pair in enumerate(PAIRS[::-1]):
        if pair[0] == TOK:
            hidden_near()
        else:
            hidden_part(*pair, part)
        scatter[1].step(step + 1)
        count = (8, 6, n_tiles - 14)[step]
        grad_tiles(done, done + count)
        done += count
    scatter[1].finish(total)

    def tail(r):
        inv_mid, normed_mid = rms_parts(middle[r])
        d_hidden = total[r]
        add_gain(2, d_hidden * normed_mid)
        d_mid = cot[r].astype(F32) + norm_back(d_hidden * (1.0 + gains[2:3]), normed_mid, inv_mid)
        d_mid_o[r] = d_mid
        inv_post, normed_post = rms_parts(branch[r])
        add_gain(1, d_mid * normed_post)
        d_branch_o[r] = norm_back(d_mid * (1.0 + gains[1:2]), normed_post, inv_post).astype(BF)

    by_rows(tail)
    for i in (n_tiles - 2, n_tiles - 1):
        grad_out(i).wait()
    gather[1].drain()
    scatter[1].drain()


def feed_forward(branch, block, gains, out_grad, w_in, w_down, collective_id):
    rows, width = branch.shape
    total = RING * rows

    def full(*shape, dtype=F32):
        return jax.ShapeDtypeStruct(shape, dtype)

    return pl.pallas_call(
        feed_forward_kernel,
        out_shape=[
            full(rows, width, dtype=BF), full(rows, width), full(rows, width, dtype=BF), full(8, PADDED),
            full(UNITS, width, dtype=BF), full(width, 2 * UNITS, dtype=BF),
        ],
        in_specs=[VMEM] * 4 + [HBM] * 2,
        out_specs=[VMEM] * 4 + [HBM] * 2,
        scratch_shapes=[
            pltpu.VMEM((width, 2 * UNITS), BF), pltpu.VMEM((UNITS, width), BF),
            pltpu.VMEM((total, width), BF), pltpu.VMEM((total, 2 * UNITS), F32), pltpu.VMEM((total, UNITS), BF),
            pltpu.VMEM((total, width), BF), pltpu.VMEM((2, 4, rows, width), BF),
            pltpu.VMEM((total, width), BF), pltpu.VMEM((total, 2 * UNITS), BF),
            pltpu.VMEM((rows, width), F32), pltpu.VMEM((rows, width), F32), pltpu.VMEM((2, TILE, width), BF),
            DMA((2,)),
            DMA((2, 2, 4, SUB)), DMA((2, 2, 4, SUB)), DMA((2, 2, 4, SUB)), DMA((2, 2, 4, SUB)),
            DMA((2,)),
        ],
        compiler_params=params(collective_id, 60),
    )(branch, block, gains, out_grad, w_in, w_down)


WIDTHS = (UNITS, UNITS, HD, HD, HD)


SHARD = D // (4 * RING)
PADDED = D + 128
WINDOW = 256


def window(i):
    return pl.ds(pl.multiple_of((SHARD * i) // 128 * 128, 128), WINDOW)


def member_place(t, core, x):
    return device(t // 2, core, t % 2, x)


def slot_of(q, p):
    d = (q - p + RING) % RING
    return jnp.where(d == 0, 0, jnp.where(d < 4, 2 * d, jnp.where(d == 4, 7, 15 - 2 * d)))


def partner(t, j):
    out = 0
    for bit in (1, 2, 4):
        on = (t // bit) % 2
        out = out + bit * (1 - on if j & bit else on)
    return out


def column_start(which, t):
    if which < 2:
        return pl.multiple_of(t * UNITS, 128)
    return pl.multiple_of((t if which == 2 else t // 2) * HD, 128)


def forward_kernel(gate, up, query, key, value, down, out, block, gain_in, cos, sine,
                   w_gu, d_ref, hidden_o, wq_h, q_h, k_h, v_h, att_h, wo, gain_o, inv_o, branch_o,
                   wq, q_o, k_o, v_o, att_o, ring, seq, seq_part, part, buf, wq_in, own, relay, ga, gsum,
                   load, ags, agr, pls, plr, rss, rsr, sws, swr, s1, r1, s2, r2, s3, r3,
                   q1, t1, q2, t2, q3, t3, s4, r4, s5, r5, sg, rg):
    z, core, y, x = my_place()
    t, p = 2 * z + y, ring_index(y, z)
    sibling, across = device(z, 1 - core, y, x), device(z, core, y, 1 - x)
    member = [partner(t, j) for j in range(RING)]
    members = [member_place(tq, core, x) for tq in member]
    plane = []
    for dc in (0, 1):
        for dy in (0, 1):
            for dx in (0, 1):
                if (dc, dx) != (0, 0):
                    plane.append(device(z, (core + dc) % 2, (y + dy) % 2, (x + dx) % 2))
    greet(members[1:] + plane)
    sources = (gate, up, query, key, value)
    pending = []

    def go(*copies):
        for c in copies:
            c.start()
            pending.append(c)

    def owner(tq, corq, xq):
        return (2 * (tq // 2) + corq) * 4 + 2 * (tq % 2) + xq

    me = owner(t, core, x)

    def columns_of(a, tq):
        return sources[a].at[:, pl.ds(column_start(a, tq), WIDTHS[a])]

    def gain_a(j):
        return remote(gain_in, ga.at[j], sg.at[j], rg.at[j], members[j])

    def gain_b(i):
        return remote(gsum.at[i], gsum.at[2 + i], sg.at[RING + i], rg.at[RING + i], (across, sibling)[i])

    def q_first(j, a, wait=False):
        tq = member[j]
        dst = wq_in.at[owner(tq, core, x) if wait else me, :, pl.ds((a - 2) * HD, HD)]
        return remote(columns_of(a, tq), dst, q1.at[j, a - 2], t1.at[j, a - 2], members[j])

    def q_second(j, wait=False):
        i = owner(member[j], core, 1 - x if wait else x)
        return remote(wq_in.at[i], wq_in.at[i], q2.at[j], t2.at[j], across)

    def q_third(j, flip, wait=False):
        i = owner(member[j], 1 - core if wait else core, 1 - x if flip else x)
        return remote(wq_in.at[i], wq_in.at[i], q3.at[j, flip], t3.at[j, flip], sibling)

    def first(j, a, wait=False):
        tq = member[j]
        dst = w_gu.at[owner(tq, core, x) if wait else me, :, pl.ds(a * UNITS, UNITS)]
        return remote(columns_of(a, tq), dst, s1.at[j, a], r1.at[j, a], members[j])

    def second(j, wait=False):
        i = owner(member[j], core, 1 - x if wait else x)
        return remote(own if j == 0 else w_gu.at[i], w_gu.at[i], s2.at[j], r2.at[j], across)

    def third(j, flip, wait=False):
        i = owner(member[j], 1 - core if wait else core, 1 - x if flip else x)
        return remote(own if (j, flip) == (0, 0) else w_gu.at[i], w_gu.at[i], s3.at[j, flip], r3.at[j, flip], sibling)

    def start_round(j):
        go(first(j, 0), first(j, 1))

    def end_round(j):
        first(j, 0, True).wait_recv()
        first(j, 1, True).wait_recv()
        go(second(j), third(j, 0))

    def end_across(j):
        second(j, True).wait_recv()
        go(third(j, 1))

    gather = SlotGather(ring, ags, agr)

    def block_of(slot):
        if slot == 0:
            return p
        if slot == 7:
            return (p + 4) % RING
        s = (slot + 1) // 2
        return (p + (RING - s if slot % 2 else s)) % RING

    def place(slot, act):
        yq, zq = ring_yz(block_of(slot))
        src, dst = ring.at[pl.ds(slot * TOK, TOK)], seq.at[2 * zq + core]

        @pl.when(yq == core)
        def _():
            c = pltpu.make_async_copy(src, dst, load.at[6 + slot])
            c.start() if act == 0 else c.wait()

        @pl.when(yq != core)
        def _():
            c = remote(src, dst, pls.at[zq], plr.at[zq], sibling)
            c.start() if act == 0 else c.wait_send()

    pair = ((down, d_ref), (out, wo))
    mine = 2 * y + x

    def rows_out(xq, a, act):
        src, dst = pair[a][0], pair[a][1].at[mine]
        to_self = (x == core) & (y == core) & (xq == x)

        @pl.when(to_self)
        def _():
            if a == 0:
                c = pltpu.make_async_copy(relay, dst, load.at[5])
            else:
                c = pltpu.make_async_copy(src, dst, load.at[4])
            c.start() if act == 0 else c.wait()

        @pl.when(jnp.logical_not(to_self))
        def _():
            c = remote(src, dst, s4.at[xq, a], r4.at[y, a], device(z, x, core, xq))
            c.start() if act == 0 else c.wait_send()

    def rows_on(yq, a):
        src, dst = pair[a][0], pair[a][1].at[2 * yq + core]
        from_self = (core == y) & (yq == y) & (core == x)

        @pl.when(from_self)
        def _():
            if a == 0:
                pltpu.make_async_copy(relay, dst, load.at[5]).wait()
            else:
                pltpu.make_async_copy(src, dst, load.at[4]).wait()

        @pl.when(jnp.logical_not(from_self))
        def _():
            remote(src, dst, s4.at[0, a], r4.at[yq, a], sibling).wait_recv()

        go(remote(dst, dst, s5.at[yq, a], r5.at[yq, a], sibling))

    locals_ = [pltpu.make_async_copy(columns_of(a, t), wq_in.at[me, :, pl.ds((a - 2) * HD, HD)], load.at[a]) for a in (2, 3)]
    locals_.append(pltpu.make_async_copy(columns_of(4, t), wq_in.at[me, :, pl.ds(2 * HD, HD)], load.at[14]))
    locals_ += [pltpu.make_async_copy(columns_of(a, t), own.at[:, pl.ds(a * UNITS, UNITS)], load.at[a]) for a in (0, 1)]
    relay_load = pltpu.make_async_copy(down, relay, load.at[15])
    for c in locals_:
        c.start()
    relay_load.start()
    ring[0:TOK] = block[...]
    gather.step(0)
    go(*[gain_a(j) for j in range(1, RING)])
    for j in range(1, RING):
        go(*[q_first(j, a) for a in (2, 3, 4)])
    for c in locals_:
        c.wait()
    go(q_second(0), q_third(0, 0))
    for xq in (0, 1):
        rows_out(xq, 1, 0)
    keep_own = pltpu.make_async_copy(own, w_gu.at[me], load.at[16])
    keep_own.start()
    go(second(0), third(0, 0))
    place(0, 0)
    gsum[0] = jnp.zeros(gsum.shape[1:], F32)
    gsum[0, :, window(me)] = gain_in[...]
    for j in range(1, RING):
        gain_a(j).wait_recv()
        lanes = window(owner(member[j], core, x))
        gsum[0, :, lanes] = gsum[0, :, lanes] + ga[j]
    go(gain_b(0))
    gather.step(1)
    place(1, 0)
    place(2, 0)
    gain_b(0).wait_recv()
    gsum[1] = gsum[0] + gsum[2]
    go(gain_b(1))
    for j in range(1, RING):
        for a in (2, 3, 4):
            q_first(j, a, True).wait_recv()
        go(q_second(j), q_third(j, 0))
    for yq in (0, 1):
        rows_on(yq, 1)
    gather.step(2)
    place(3, 0)
    place(4, 0)
    gain_b(1).wait_recv()
    gain_o[...] = (gsum[1] + gsum[3])[:, 0:D]
    for j in range(RING):
        q_second(j, True).wait_recv()
        go(q_third(j, 1))
    gather.step(3)
    place(5, 0)
    place(6, 0)
    for j in (4, 5, 1, 6, 2, 7, 3):
        start_round(j)
    relay_load.wait()
    for xq in (0, 1):
        rows_out(xq, 0, 0)
    end_across(0)
    for j in range(RING):
        for flip in (0, 1):
            q_third(j, flip, True).wait_recv()

    def join(g, carry):
        pieces = [wq_in[4 * g + i].astype(F32) for i in range(4)]
        wq[pl.ds(pl.multiple_of(288 * g, 16), 288)] = jnp.concatenate(pieces, axis=0).astype(BF)
        return carry

    lax.fori_loop(0, 8, join, 0)
    results_out = [pltpu.make_async_copy(wq, wq_h, load.at[22])]
    results_out[0].start()
    gather.finish()
    place(7, 0)
    for zq in range(NZ):
        dst = seq.at[2 * zq + 1 - core]
        remote(dst, dst, pls.at[zq], plr.at[zq], sibling).wait_recv()
    for slot in range(RING):
        place(slot, 1)
    end_round(1)

    factor = 1.0 + gain_o[0:1]

    def norm(c, carry):
        for half in range(2):
            rows = pl.ds(half * 64, 64)
            seq[c, rows] = (rms_parts(seq[c, rows].astype(F32))[1] * factor).astype(BF)
        return carry

    lax.fori_loop(0, RING, norm, 0)
    keep_hidden = pltpu.make_async_copy(seq, hidden_o, load.at[17])
    keep_hidden.start()
    for i in range(4):
        r = pl.ds(i * 256, 256)
        rows = seq[2 * i : 2 * i + 2].reshape(256, -1)
        tabs = (cos[r], sine[r])
        q_o[r] = (rotate(fold_rows(rows, wq[:, 0:HD]), *tabs) * (HD ** (-0.5))).astype(BF)
        k_o[r] = rotate(fold_rows(rows, wq[:, HD : 2 * HD]), *tabs).astype(BF)
        v_o[r] = fold_rows(rows, wq[:, 2 * HD : 3 * HD]).astype(BF)
    for i, (src, dst) in enumerate(((q_o, q_h), (k_o, k_h), (v_o, v_h))):
        results_out.append(pltpu.make_async_copy(src, dst, load.at[23 + i]))
        results_out[-1].start()
    end_round(4)
    end_across(1)

    def swap(zq, kept):
        where = pl.ds(pl.multiple_of(slot_of(ring_index(core, zq), p) * TOK, TOK), TOK)
        if kept:
            return pltpu.make_async_copy(seq_part.at[2 * zq + core], part.at[where], load.at[18 + zq])
        return remote(seq_part.at[2 * zq + 1 - core], part.at[where], sws.at[zq], swr.at[zq], sibling)

    def swapped(zq):
        where = pl.ds(pl.multiple_of(slot_of(ring_index(1 - core, zq), p) * TOK, TOK), TOK)
        return remote(seq_part.at[0], part.at[where], sws.at[zq], swr.at[zq], sibling)

    for yq in (0, 1):
        remote(out, wo.at[2 * yq + 1 - core], s5.at[yq, 1], r5.at[yq, 1], sibling).wait_recv()
    for i in range(4):
        r, upto = pl.ds(i * 256, 256), (i + 1) * 256
        bent = jnp.tanh(contract_cols(q_o[r], k_o[0:upto]) / CAP)
        seen = lax.broadcasted_iota(jnp.int32, bent.shape, 1) <= i * 256 + lax.broadcasted_iota(jnp.int32, bent.shape, 0)
        weights = jnp.where(seen, jnp.exp(CAP * bent), 0.0)
        inverse = 1.0 / jnp.sum(weights, axis=-1, keepdims=True)
        attended = fold_rows(weights.astype(BF), v_o[0:upto]) * inverse
        inv_o[r] = inverse
        att_o[r] = attended
        attended_b = attended.astype(BF)

        def columns(cols):
            sums = fold_rows(attended_b, wo[:, :, cols].reshape(HD, 768))
            seq_part[2 * i, :, cols] = sums[0:TOK].astype(BF)
            seq_part[2 * i + 1, :, cols] = sums[TOK:].astype(BF)

        tiles(3, 768, columns)
        swap(i, True).start()
        swap(i, False).start()
        if i == 0:
            end_round(2)
        if i == 2:
            end_round(5)
            end_across(2)
            for yq in (0, 1):
                rows_on(yq, 0)
    results_out.append(pltpu.make_async_copy(att_o, att_h, load.at[26]))
    results_out[-1].start()
    for zq in range(NZ):
        swap(zq, True).wait()
        swapped(zq).wait_recv()
    scatter = SlotScatter(part, buf, rss, rsr)
    scatter.step(0)
    end_round(3)
    end_across(4)
    scatter.step(1)
    end_round(6)
    end_across(5)
    end_across(3)
    scatter.step(2)
    end_round(7)
    end_across(6)
    scatter.step(3)
    branch_o[...] = part[0:TOK].astype(F32)
    end_across(7)
    scatter.finish(branch_o)

    for j in range(RING):
        for flip in (0, 1):
            third(j, flip, True).wait_recv()
    for yq in (0, 1):
        remote(down, d_ref.at[2 * yq + 1 - core], s5.at[yq, 0], r5.at[yq, 0], sibling).wait_recv()
    for xq in (0, 1):
        for a in (0, 1):
            to_self = (x == core) & (y == core) & (xq == x)

            @pl.when(jnp.logical_not(to_self))
            def _():
                remote(pair[a][0], pair[a][1].at[mine], s4.at[xq, a], r4.at[y, a], device(z, x, core, xq)).wait_send()
    keep_own.wait()
    keep_hidden.wait()
    for c in results_out:
        c.wait()
    for zq in range(NZ):
        swap(zq, False).wait_send()
    gather.drain()
    scatter.drain()
    for c in pending:
        c.wait_send()


def forward(gate, up, query, key, value, down, out, block, gains, cos_tab, sine_tab, collective_id):
    n = 4 * RING
    rows, width = block.shape
    shard, total = gate.shape[0], RING * block.shape[0]

    def full(*shape, dtype=BF):
        return jax.ShapeDtypeStruct(shape, dtype)

    blocks = (RING, rows, width)
    return pl.pallas_call(
        forward_kernel,
        out_shape=[
            full(n, shard, 2 * UNITS), full(4, *down.shape), full(*blocks), full(width, 3 * HD),
            full(total, HD), full(total, HD), full(total, HD), full(total, HD, dtype=F32),
            full(4, *out.shape), full(8, D, dtype=F32), full(total, 1, dtype=F32), full(rows, width, dtype=F32),
        ],
        in_specs=[HBM] * 7 + [VMEM] * 4,
        out_specs=[HBM] * 8 + [VMEM] * 4,
        scratch_shapes=[
            pltpu.VMEM((width, 3 * HD), BF), pltpu.VMEM((total, HD), BF), pltpu.VMEM((total, HD), BF), pltpu.VMEM((total, HD), BF),
            pltpu.VMEM((total, HD), F32),
            pltpu.VMEM((total, width), BF), pltpu.VMEM(blocks, BF), pltpu.VMEM(blocks, BF), pltpu.VMEM((total, width), BF),
            pltpu.VMEM((2, 4, rows, width), BF), pltpu.VMEM((n, shard, 3 * HD), BF),
            pltpu.VMEM((shard, 2 * UNITS), BF), pltpu.VMEM(down.shape, BF),
            pltpu.VMEM((RING,) + gains.shape, F32), pltpu.VMEM((4, 8, PADDED), F32),
            DMA((27,)),
            DMA((2, 4, SUB)), DMA((2, 4, SUB)), DMA((NZ,)), DMA((NZ,)), DMA((2, 4, SUB)), DMA((2, 4, SUB)), DMA((NZ,)), DMA((NZ,)),
            DMA((RING, 2)), DMA((RING, 2)), DMA((RING,)), DMA((RING,)), DMA((RING, 2)), DMA((RING, 2)),
            DMA((RING, 3)), DMA((RING, 3)), DMA((RING,)), DMA((RING,)), DMA((RING, 2)), DMA((RING, 2)),
            DMA((2, 2)), DMA((2, 2)), DMA((2, 2)), DMA((2, 2)), DMA((RING + 2,)), DMA((RING + 2,)),
        ],
        compiler_params=params(collective_id, 60),
    )(gate, up, query, key, value, down, out, block, gains, cos_tab, sine_tab)


ROUNDS = (4, 5, 6, 7, 2, 3, 1, 0)
AHEAD = 2


def backward_kernel(ready, d_branch, gu_in, down_in, hidden, wq, wo, q_in, k_in, v_in, att, inv, cos, sine, block_in, gain_in,
                    d_hid_o, gain_o, c_gu, c_q, down_o, out_o,
                    ring, seq, part, buf, d_att, d_qkv, dk, dv, grad_q, aq, bq,
                    own, a_gu, b_gu, down_own, da, db, og, oa, ob, ga, gsum,
                    load, ags, agr, pls, plr, rss, rsr, sws, swr, s1, r1, s2, r2, s3, r3,
                    q1, t1, q2, t2, q3, t3, sx, rx, sg, rg):
    z, core, y, x = my_place()
    t, p = 2 * z + y, ring_index(y, z)
    sibling, across = device(z, 1 - core, y, x), device(z, core, y, 1 - x)
    diagonal = device(z, 1 - core, 1 - y, x)
    members = [member_place(partner(t, j), core, x) for j in range(RING)]
    order = [partner(t, j) for j in ROUNDS]
    greet(members[1:] + [sibling, across, diagonal])
    pending = []

    def go(*copies):
        for c in copies:
            c.start()
            pending.append(c)

    def owner(tq, corq, xq):
        return (2 * (tq // 2) + corq) * 4 + 2 * (tq % 2) + xq

    side_x = (1 - x, x)

    def gu_a(side, j):
        src = gu_in.at[owner(order[j], 1 - core, side_x[side])]
        return remote(src, a_gu.at[side, j], s1.at[side, j], r1.at[side, j], sibling)

    def gu_own(side, j):
        return pltpu.make_async_copy(gu_in.at[owner(order[j], core, side_x[side])], own.at[j % 2], load.at[j % 2])

    def gu_b(j):
        return remote(a_gu.at[0, j], b_gu.at[j], s2.at[j], r2.at[j], across)

    def gu_c(j, wait=False):
        dst = c_gu.at[order[j] if wait else t]
        if ROUNDS[j] == 0:
            return pltpu.make_async_copy(a_gu.at[1, j], dst, load.at[2])
        return remote(a_gu.at[1, j], dst, s3.at[j], r3.at[j], members[ROUNDS[j]])

    def sum_own(side, j, more=None):
        gu_own(side, j).wait()
        gu_a(side, j).wait_recv()
        total = a_gu[side, j].astype(F32) + own[j % 2].astype(F32)
        if more is not None:
            total = total + more[j].astype(F32)
        a_gu[side, j] = total.astype(BF)

    def pump(first, last):
        for j in range(first, last):
            gu_own(1, j).start()
        for j in range(first, last):
            gu_b(j).wait_recv()
            if j + AHEAD < RING:
                go(gu_b(j + AHEAD))
            sum_own(1, j, b_gu)

    small = ((down_in, down_own, da, db, down_o), (og, None, oa, ob, out_o))

    def small_a(a, xo):
        return remote(small[a][0].at[2 * (1 - core) + xo], small[a][2].at[xo], sx.at[a, xo], rx.at[a, xo], sibling)

    def small_b(a):
        return remote(small[a][2].at[1 - x], small[a][3], sx.at[a, 2], rx.at[a, 2], across)

    def small_c(a, act):
        src, dst = small[a][2].at[x], small[a][4]

        @pl.when(core == y)
        def _():
            c = pltpu.make_async_copy(src, dst, load.at[3 + a])
            c.start() if act == 0 else c.wait()

        @pl.when(core != y)
        def _():
            c = remote(src, dst, sx.at[a, 3], rx.at[a, 3], diagonal)
            c.start() if act == 0 else c.wait()

    def q_a(side, j):
        src = grad_q.at[owner(order[j], 1 - core, side_x[side])]
        return remote(src, aq.at[side, j], q1.at[side, j], t1.at[side, j], sibling)

    def q_b(j):
        return remote(grad_q.at[owner(order[j], core, 1 - x)], bq.at[j], q2.at[j], t2.at[j], across)

    def q_c(j, wait=False):
        src, dst = grad_q.at[owner(order[j], core, x)], c_q.at[order[j] if wait else t]
        if ROUNDS[j] == 0:
            return pltpu.make_async_copy(src, dst, load.at[5])
        return remote(src, dst, q3.at[j], t3.at[j], members[ROUNDS[j]])

    def gain_a():
        return remote(gain_in, gsum.at[2], sg.at[RING], rg.at[RING], sibling)

    def gain_b():
        return remote(gsum.at[0], gsum.at[3], sg.at[RING + 1], rg.at[RING + 1], across)

    def gain_c(j):
        lanes = window(owner(partner(t, j), core, x))
        return remote(gsum.at[1, :, lanes], ga.at[j], sg.at[j], rg.at[j], members[j])

    gather = SlotGather(ring, ags, agr)

    def block(slot):
        if slot == 0:
            return p
        if slot == 7:
            return (p + 4) % RING
        s = (slot + 1) // 2
        return (p + (RING - s if slot % 2 else s)) % RING

    def place(slot, act):
        yq, zq = ring_yz(block(slot))
        src, dst = ring.at[pl.ds(slot * TOK, TOK)], seq.at[2 * zq + core]

        @pl.when(yq == core)
        def _():
            c = pltpu.make_async_copy(src, dst, load.at[6 + slot])
            c.start() if act == 0 else c.wait()

        @pl.when(yq != core)
        def _():
            c = remote(src, dst, pls.at[zq], plr.at[zq], sibling)
            c.start() if act == 0 else c.wait_send()

    first = pltpu.make_async_copy(d_branch, ring.at[pl.ds(0, TOK)], load.at[14])
    first.start()
    first.wait()
    gather.step(0)
    place(0, 0)
    for side in (0, 1):
        go(*[gu_a(side, j) for j in range(RING)])
        if side == 0:
            go(small_a(0, 0), small_a(0, 1))
    for j in range(RING):
        if j < 2:
            gu_own(0, j).start()
        sum_own(0, j)
        if j + 2 < RING:
            gu_own(0, j + 2).start()
        if j < AHEAD:
            go(gu_b(j))

    def down_sum(xo):
        c = pltpu.make_async_copy(down_in.at[2 * core + xo], down_own, load.at[16])
        c.start()
        small_a(0, xo).wait_recv()
        c.wait()
        da[xo] = (da[xo].astype(F32) + down_own[...].astype(F32)).astype(BF)

    down_sum(0)
    gather.step(1)
    place(1, 0)
    place(2, 0)
    pump(0, 1)
    down_sum(1)
    pump(1, 2)
    gather.step(2)
    place(3, 0)
    place(4, 0)
    pump(2, 4)
    gather.step(3)
    place(5, 0)
    place(6, 0)
    pump(4, 5)
    gather.finish()
    place(7, 0)
    for j in range(5):
        go(gu_c(j))
    for zq in range(NZ):
        dst = seq.at[2 * zq + 1 - core]
        remote(dst, dst, pls.at[zq], plr.at[zq], sibling).wait_recv()
    for slot in range(RING):
        place(slot, 1)
    gather.drain()
    hidden_load = pltpu.make_async_copy(hidden, ring, load.at[14])
    hidden_load.start()
    ready()

    for c in range(0, RING, 2):
        rows = pl.ds(c * TOK, 2 * TOK)
        d_att[rows] = contract_cols(seq[c : c + 2].reshape(2 * TOK, -1), wo[...]).astype(BF)

    def out_columns(cols):
        value = contract_rows(att[...].astype(BF), seq[:, :, cols].reshape(RING * TOK, 768))
        for f in range(4):
            og[f, :, cols] = value[64 * f : 64 * (f + 1)].astype(BF)

    tiles(3, 768, out_columns)
    go(small_a(1, 0), small_a(1, 1))
    pump(5, 6)
    go(gu_c(5))
    dk[...] = jnp.zeros_like(dk)
    dv[...] = jnp.zeros_like(dv)
    for i in range(4):
        r, upto = pl.ds(i * 256, 256), (i + 1) * 256
        keys, vals, query = k_in[0:upto], v_in[0:upto], q_in[r]
        bent = jnp.tanh(contract_cols(query, keys) / CAP)
        seen = lax.broadcasted_iota(jnp.int32, bent.shape, 1) <= i * 256 + lax.broadcasted_iota(jnp.int32, bent.shape, 0)
        weights = jnp.where(seen, jnp.exp(CAP * bent), 0.0)
        grad = d_att[r].astype(F32)
        delta = jnp.sum(grad * att[r], axis=-1, keepdims=True)
        d_probs = contract_cols(d_att[r], vals)
        d_raw = (weights * inv[r] * (d_probs - delta) * (1.0 - bent * bent)).astype(BF)
        dq = fold_rows(d_raw, keys) * (HD ** (-0.5))
        d_qkv[r, 0:HD] = unrotate(dq, cos[r], sine[r]).astype(BF)
        dk[0:upto] = dk[0:upto] + contract_rows(d_raw, query)
        scaled = grad * inv[r]
        high = scaled.astype(BF)
        rest = (scaled - high.astype(F32)).astype(BF)
        weights_b = weights.astype(BF)
        dv[0:upto] = dv[0:upto] + contract_rows(weights_b, high) + contract_rows(weights_b, rest)
        if i == 1:
            pump(6, 7)
            go(gu_c(6))
            go(small_b(0))
        if i == 3:
            pump(7, 8)
            go_self = gu_c(7)
            go_self.start()
    d_qkv[:, HD : 2 * HD] = unrotate(dk[...], cos[...], sine[...]).astype(BF)
    d_qkv[:, 2 * HD : 3 * HD] = dv[...].astype(BF)

    scatter = SlotScatter(part, buf, rss, rsr)

    def swap(zq, kept):
        where = pl.ds(pl.multiple_of(slot_of(ring_index(core, zq), p) * TOK, TOK), TOK)
        if kept:
            return pltpu.make_async_copy(seq.at[2 * zq + core], part.at[where], load.at[17 + zq])
        return remote(seq.at[2 * zq + 1 - core], part.at[where], sws.at[zq], swr.at[zq], sibling)

    def swapped(zq):
        where = pl.ds(pl.multiple_of(slot_of(ring_index(1 - core, zq), p) * TOK, TOK), TOK)
        return remote(seq.at[0], part.at[where], sws.at[zq], swr.at[zq], sibling)

    for zq in range(NZ):
        rows = d_qkv[2 * zq * TOK : (2 * zq + 2) * TOK]

        def columns(cols):
            value = contract_cols(rows, wq[cols])
            seq[2 * zq, :, cols] = value[0:TOK].astype(BF)
            seq[2 * zq + 1, :, cols] = value[TOK:].astype(BF)

        tiles(3, 768, columns)
        swap(zq, True).start()
        swap(zq, False).start()
    for zq in range(NZ):
        swap(zq, True).wait()
        swapped(zq).wait_recv()
    scatter.step(0)

    hidden_load.wait()

    def grad_half(half):
        def columns(cols):
            value = contract_rows(ring[:, pl.ds(half * 1152, 1152)], d_qkv[:, cols])
            for i in range(16):
                grad_q[half * 16 + i, :, cols] = value[72 * i : 72 * (i + 1)].astype(BF)

        tiles(3, 256, columns)

    grad_half(0)
    scatter.step(1)
    grad_half(1)
    for side in (0, 1):
        go(*[q_a(side, j) for j in range(RING)])
    for xo in (0, 1):
        small_a(1, xo).wait_recv()
        oa[xo] = (oa[xo].astype(F32) + og[2 * core + xo].astype(F32)).astype(BF)
    go(small_b(1))
    scatter.step(2)

    def q_sum(side, j):
        i = owner(order[j], core, side_x[side])
        q_a(side, j).wait_recv()
        total = grad_q[i].astype(F32) + aq[side, j].astype(F32)
        if side == 1:
            q_b(j).wait_recv()
            total = total + bq[j].astype(F32)
        grad_q[i] = total.astype(BF)

    for j in range(RING):
        q_sum(0, j)
        if j < AHEAD:
            go(q_b(j))
    small_b(0).wait_recv()
    da[x] = (da[x].astype(F32) + db[...].astype(F32)).astype(BF)
    small_c(0, 0)
    scatter.step(3)

    def q_round(j):
        q_sum(1, j)
        if j + AHEAD < RING:
            go(q_b(j + AHEAD))
        if ROUNDS[j] == 0:
            q_c(j).start()
        else:
            go(q_c(j))

    for j in range(4):
        q_round(j)
    small_b(1).wait_recv()
    oa[x] = (oa[x].astype(F32) + ob[...].astype(F32)).astype(BF)
    small_c(1, 0)

    def own_part(cols):
        slot = part[0:TOK, cols]
        d_hid_o[:, cols] = slot.astype(F32)

    tiles(3, 768, own_part)
    for j in range(4, RING):
        q_round(j)
    scatter.finish(d_hid_o)
    def pre_gain(r):
        value = d_hid_o[r] * rms_parts(block_in[r].astype(F32))[1]
        gain_in[0:1, 0:D] = gain_in[0:1, 0:D] + jnp.sum(value, axis=0, keepdims=True)

    by_rows(pre_gain)
    go(gain_a())
    gain_a().wait_recv()
    gsum[0] = gain_in[...] + gsum[2]
    go(gain_b())
    gain_b().wait_recv()
    gsum[1] = gsum[0] + gsum[3]
    go(*[gain_c(j) for j in range(1, RING)])
    total = gsum[1, :, window(owner(t, core, x))]
    for j in range(1, RING):
        gain_c(j).wait_recv()
        total = total + ga[j]
    gain_o[...] = total

    for j in range(RING):
        if ROUNDS[j] == 0:
            gu_c(j).wait()
            q_c(j).wait()
        else:
            gu_c(j, True).wait_recv()
            q_c(j, True).wait_recv()
    small_c(0, 1)
    small_c(1, 1)
    for zq in range(NZ):
        swap(zq, False).wait_send()
    scatter.drain()
    for c in pending:
        c.wait_send()


def backward(d_branch, gu, down, hidden, w_qkv, w_out, queries, keys, values, attended, inv_total, cos_tab, sine_tab,
             block, gain_parts, collective_id):
    n = 4 * RING
    rows, width = d_branch.shape
    shard = gu.shape[0] // n
    gu = gu.reshape(n, shard, 2 * UNITS)
    down = down.reshape(4, -1, width)
    total, down_rows, out_rows = RING * rows, down.shape[1], w_out.shape[0] // 4
    gain_shape = (8, PADDED)

    def out(*shape, dtype=BF):
        return jax.ShapeDtypeStruct(shape, dtype)

    def body(*refs):
        ins, rest = refs[:14], refs[14:]
        gains_ref, rest = rest[0], rest[1:]
        outs, scr = rest[:6], rest[6:]
        gain_scr, loaded, sems, scr = scr[0], scr[1:8], scr[8], scr[9:]
        gain_scr[...] = gains_ref[...]
        ins = list(ins)
        copies = []
        for i, place in enumerate((4, 6, 7, 8, 9, 11, 12)):
            copies.append(pltpu.make_async_copy(ins[place], loaded[i], sems.at[i]))
            copies[-1].start()
            ins[place] = loaded[i]

        def ready():
            for c in copies:
                c.wait()

        backward_kernel(ready, *ins, gain_scr, *outs, *scr)

    return pl.pallas_call(
        body,
        out_shape=[
            out(rows, width, dtype=F32), out(8, WINDOW, dtype=F32),
            out(RING, shard, 2 * UNITS), out(RING, shard, 3 * HD),
            out(down_rows, width), out(out_rows, width),
        ],
        in_specs=[HBM] * 5 + [VMEM] + [HBM] * 4 + [VMEM] + [HBM] * 2 + [VMEM] * 2,
        out_specs=[VMEM] * 2 + [HBM] * 4,
        scratch_shapes=[
            pltpu.VMEM(gain_shape, F32),
            pltpu.VMEM((width, 3 * HD), BF), pltpu.VMEM((total, HD), BF), pltpu.VMEM((total, HD), BF), pltpu.VMEM((total, HD), BF),
            pltpu.VMEM((total, HD), F32), pltpu.VMEM((total, HD // 2), F32), pltpu.VMEM((total, HD // 2), F32),
            DMA((7,)),
            pltpu.VMEM((total, width), BF), pltpu.VMEM((RING, rows, width), BF), pltpu.VMEM((total, width), BF),
            pltpu.VMEM((2, 4, rows, width), BF),
            pltpu.VMEM((total, HD), BF), pltpu.VMEM((total, 3 * HD), BF),
            pltpu.VMEM((total, HD), F32), pltpu.VMEM((total, HD), F32),
            pltpu.VMEM((n, shard, 3 * HD), BF), pltpu.VMEM((2, RING, shard, 3 * HD), BF), pltpu.VMEM((RING, shard, 3 * HD), BF),
            pltpu.VMEM((2, shard, 2 * UNITS), BF), pltpu.VMEM((2, RING, shard, 2 * UNITS), BF), pltpu.VMEM((RING, shard, 2 * UNITS), BF),
            pltpu.VMEM((down_rows, width), BF), pltpu.VMEM((2, down_rows, width), BF), pltpu.VMEM((down_rows, width), BF),
            pltpu.VMEM((4, out_rows, width), BF), pltpu.VMEM((2, out_rows, width), BF), pltpu.VMEM((out_rows, width), BF),
            pltpu.VMEM((RING, 8, WINDOW), F32), pltpu.VMEM((4,) + gain_shape, F32),
            DMA((21,)),
            DMA((2, 4, SUB)), DMA((2, 4, SUB)), DMA((NZ,)), DMA((NZ,)), DMA((2, 4, SUB)), DMA((2, 4, SUB)), DMA((NZ,)), DMA((NZ,)),
            DMA((2, RING)), DMA((2, RING)), DMA((RING,)), DMA((RING,)), DMA((RING,)), DMA((RING,)),
            DMA((2, RING)), DMA((2, RING)), DMA((RING,)), DMA((RING,)), DMA((RING,)), DMA((RING,)),
            DMA((2, 4)), DMA((2, 4)), DMA((RING + 2,)), DMA((RING + 2,)),
        ],
        compiler_params=params(collective_id, 60),
    )(d_branch, gu, down, hidden, w_qkv, w_out, queries, keys, values, attended, inv_total, cos_tab, sine_tab, block, gain_parts)


def results_kernel(gu, qkv, down, out, d_hidden, d_middle, block, gains,
                   gate_o, up_o, query_o, key_o, value_o, down_o, out_o, token_o):
    for i in range(2):
        units, heads = pl.ds(i * UNITS, UNITS), pl.ds(i * HD, HD)
        gate_o[:, units] = gu[i, :, 0:UNITS].astype(F32)
        up_o[:, units] = gu[i, :, UNITS : 2 * UNITS].astype(F32)
        query_o[:, heads] = qkv[i, :, 0:HD].astype(F32)
    key_o[...] = qkv[0, :, HD : 2 * HD].astype(F32) + qkv[1, :, HD : 2 * HD].astype(F32)
    value_o[...] = qkv[0, :, 2 * HD :].astype(F32) + qkv[1, :, 2 * HD :].astype(F32)
    down_o[...] = down[...].astype(F32)
    out_o[...] = out[...].astype(F32)
    inverse, normed = rms_parts(block[...].astype(F32))
    back = norm_back(d_hidden[...] * (1.0 + gains[0:1]), normed, inverse)
    token_o[...] = (d_middle[...] + back).astype(BF)


def results(gu, qkv, down, out, d_hidden, d_middle, block, gains):
    steps = RING // 2
    shard, width = gu.shape[1], down.shape[1]
    tok, down_rows, out_rows = d_hidden.shape[0] // steps, down.shape[0] // steps, out.shape[0] // steps

    def rows(n, wide):
        return pl.BlockSpec((n, wide), lambda i: (i, 0))

    def columns(wide):
        return pl.BlockSpec((shard, wide), lambda i: (0, i))

    def full(*shape):
        return jax.ShapeDtypeStruct(shape, F32)

    return pl.pallas_call(
        results_kernel,
        grid=(steps,),
        out_shape=[
            full(shard, FF), full(shard, FF), full(shard, H * HD), full(shard, KVH * HD), full(shard, KVH * HD),
            full(*down.shape), full(*out.shape), jax.ShapeDtypeStruct(d_hidden.shape, BF),
        ],
        in_specs=[
            pl.BlockSpec((2, shard, 2 * UNITS), lambda i: (i, 0, 0)), pl.BlockSpec((2, shard, 3 * HD), lambda i: (i, 0, 0)),
            rows(down_rows, width), rows(out_rows, width), rows(tok, width), rows(tok, width), rows(tok, width),
            pl.BlockSpec(gains.shape, lambda i: (0, 0)),
        ],
        out_specs=[
            columns(2 * UNITS), columns(2 * UNITS), columns(2 * HD), columns(HD), columns(HD),
            rows(down_rows, width), rows(out_rows, width), rows(tok, width),
        ],
        compiler_params=pltpu.CompilerParams(vmem_limit_bytes=60 * 2**20),
    )(gu, qkv, down, out, d_hidden, d_middle, block, gains)


def on_ring(
    tokens, w_query, w_key, w_value, w_out, w_gate, w_up, w_down,
    pre_gain, post_gain, pre_ffn_gain, post_ffn_gain, out_grad,
):
    ids = iter(range(32))
    length = RING * tokens.shape[1]
    shard_gain = pre_gain.shape[0]
    mine = lax.axis_index("ctx") * 4 + lax.axis_index("fsdp")
    gains = jnp.stack([pre_gain, post_gain, pre_ffn_gain, post_ffn_gain]).astype(F32)
    gains = lax.dynamic_update_slice(jnp.zeros((8, WINDOW), F32), gains, (0, (mine * shard_gain) % 128))
    cos_tab, sine_tab = (jnp.asarray(table) for table in constant_tables(length, HD))
    w_gu, down_in, hidden, w_qkv, queries, keys, values, attended, out_in, gains, inv_total, branch = forward(
        w_gate, w_up, w_query, w_key, w_value, w_down, w_out, tokens[0], gains, cos_tab, sine_tab, next(ids)
    )
    w_gu, hidden = w_gu.reshape(D, 2 * UNITS), hidden.reshape(length, D)
    w_dn = down_in.reshape(UNITS, D)
    w_ot = out_in.reshape(HD, D)
    output, d_middle, d_branch, gain_parts, down_part, gu_part = feed_forward(
        branch, tokens[0], gains, out_grad[0], w_gu, w_dn, next(ids)
    )
    d_hidden, gain_g, gu_g, qkv_g, down_g, out_g = backward(
        d_branch, gu_part, down_part, hidden, w_qkv, w_ot, queries, keys, values, attended, inv_total,
        cos_tab, sine_tab, tokens[0], gain_parts, next(ids),
    )
    gate_g, up_g, query_g, key_g, value_g, down_g, out_g, token_grad = results(
        gu_g, qkv_g, down_g, out_g, d_hidden, d_middle, tokens[0], gains
    )
    gain_g = lax.dynamic_slice(gain_g, (0, (mine * shard_gain) % 128), (4, shard_gain))
    return (
        output[None], token_grad[None],
        query_g, key_g, value_g, out_g, gate_g, up_g, down_g,
        gain_g[0], gain_g[1], gain_g[2], gain_g[3],
    )


ROW_FOLD = 4


def head_tables(positions, width):
    half_width = width // 2
    inv_freqs = ROPE_BASE ** (-jnp.arange(half_width, dtype=jnp.float32) * 2.0 / width)
    angles = positions.astype(jnp.float32)[:, None] * inv_freqs[None, :]
    return (jnp.cos(angles)[:, None, :], jnp.sin(angles)[:, None, :])


def rotate_heads(heads_in, cos_tab, sine_tab):
    half_width = heads_in.shape[-1] // 2
    front_half = heads_in[..., :half_width]
    back_half = heads_in[..., half_width:]
    return jnp.concatenate(
        [front_half * cos_tab - back_half * sine_tab, back_half * cos_tab + front_half * sine_tab],
        axis=-1,
    )


def unrotate_heads(grad_in, cos_tab, sine_tab):
    half_width = grad_in.shape[-1] // 2
    front_half = grad_in[..., :half_width]
    back_half = grad_in[..., half_width:]
    return jnp.concatenate(
        [front_half * cos_tab + back_half * sine_tab, back_half * cos_tab - front_half * sine_tab],
        axis=-1,
    )


def to_groups(flat_heads, tok_rows, q_group):
    shaped = flat_heads.reshape(tok_rows, KVH, q_group, HD)
    return jnp.transpose(shaped, (1, 2, 0, 3)).reshape(KVH, q_group * tok_rows, HD)


def from_groups(grouped, tok_rows, q_group):
    shaped = grouped.reshape(KVH, q_group, tok_rows, HD)
    return jnp.transpose(shaped, (2, 0, 1, 3)).reshape(tok_rows, KVH * q_group * HD)


def grad_rows(left, right, folding, count):
    block = contract_rows(left, right)
    return block.reshape(count, right.shape[1] // folding)


def blockwise(step_fn, carry, piece, width):
    key_count = piece[0].shape[0]
    n_steps = key_count // width
    stacked = tuple((member.reshape(n_steps, width, member.shape[1]) for member in piece))

    def one_step(partial_value, block_item):
        block_index, members = block_item
        return (step_fn(partial_value, members, block_index * width), None)

    carry, unused = lax.scan(one_step, carry, (jnp.arange(n_steps, dtype=jnp.int32), stacked))
    return carry


def block_grads(query_g, query_pos, d_att_g, delta, inv_tot, key_block, value_block, key_first):
    key_count = key_block.shape[0]
    key_grp = key_block.reshape(key_count, KVH, HD)
    value_grp = value_block.reshape(key_count, KVH, HD)
    raw_scores = jnp.einsum("grd,ngd->grn", query_g, key_grp, preferred_element_type=jnp.float32)
    capped = CAP * jnp.tanh(raw_scores / CAP)
    key_pos = key_first + jnp.arange(key_count, dtype=jnp.int32)
    allowed = key_pos[None, None, :] <= query_pos[None, :, None]
    weights = jnp.where(allowed, jnp.exp(capped), 0.0)
    prob_rows = weights * inv_tot[..., None]
    d_probs = jnp.einsum("grd,ngd->grn", d_att_g, value_grp, preferred_element_type=jnp.float32)
    slope = 1.0 - capped / CAP * (capped / CAP)
    d_raw = (prob_rows * (d_probs - delta[..., None]) * slope).astype(jnp.bfloat16)
    d_query = jnp.einsum("grn,ngd->grd", d_raw, key_grp, preferred_element_type=jnp.float32)
    d_key = jnp.einsum("grn,grd->ngd", d_raw, query_g, preferred_element_type=jnp.float32)
    weights_b = weights.astype(jnp.bfloat16)
    d_scaled = d_att_g.astype(jnp.float32) * inv_tot[..., None]
    scaled_high = d_scaled.astype(jnp.bfloat16)
    scaled_rest = (d_scaled - scaled_high.astype(jnp.float32)).astype(jnp.bfloat16)
    d_value = jnp.einsum("grn,grd->ngd", weights_b, scaled_high, preferred_element_type=jnp.float32)
    d_value = d_value + jnp.einsum(
        "grn,grd->ngd", weights_b, scaled_rest, preferred_element_type=jnp.float32
    )
    return (d_query, d_key.reshape(key_count, KVH * HD), d_value.reshape(key_count, KVH * HD))


def on_any_mesh(
    tokens,
    w_query,
    w_key,
    w_value,
    w_out,
    w_gate,
    w_up,
    w_down,
    pre_gain,
    post_gain,
    pre_ffn_gain,
    post_ffn_gain,
    out_grad,
):
    tok_rows = tokens.shape[1]
    q_group = H // KVH
    q_scale = HD ** (-0.5)
    width_q = H * HD
    width_kv = KVH * HD
    width_qkv = width_q + 2 * width_kv
    n_ctx = lax.axis_size("ctx")
    my_block = lax.axis_index("ctx")
    my_start = my_block * tok_rows
    positions = my_start + jnp.arange(tok_rows, dtype=jnp.int32)
    cos_tab, sine_tab = head_tables(positions, HD)
    row_pos = jnp.tile(positions, q_group)
    last_pos = my_start + tok_rows - 1
    resid_in = tokens[0].astype(jnp.float32)
    qkv_shard = jnp.concatenate([w_query, w_key, w_value], axis=1)
    gateup_shard = jnp.concatenate([w_gate, w_up], axis=1)
    shard_rows = qkv_shard.shape[0]
    gains_shard = jnp.stack([pre_gain, post_gain, pre_ffn_gain, post_ffn_gain])
    full_gains, full_qkv, full_out = (
        lax.all_gather(gains_shard, ("ctx", "fsdp"), axis=1, tiled=True),
        lax.all_gather(qkv_shard, ("ctx", "fsdp"), axis=0, tiled=True),
        lax.all_gather(w_out, ("ctx", "fsdp"), axis=0, tiled=True),
    )
    factors = 1.0 + full_gains.astype(jnp.float32)
    pre_factor, post_factor, pre_ffn_factor, post_ffn_factor = (
        factors[0],
        factors[1],
        factors[2],
        factors[3],
    )
    inv_pre, normed_pre = rms_parts(resid_in)
    hidden = (normed_pre * pre_factor).astype(jnp.bfloat16)
    projected = jnp.dot(hidden, full_qkv, preferred_element_type=jnp.float32)
    query_lin = projected[:, :width_q].reshape(tok_rows, H, HD)
    queries = (
        (rotate_heads(query_lin, cos_tab, sine_tab) * q_scale)
        .astype(jnp.bfloat16)
        .reshape(tok_rows, width_q)
    )
    query_grp = to_groups(queries, tok_rows, q_group)
    key_lin = projected[:, width_q : width_q + width_kv].reshape(tok_rows, KVH, HD)
    key_rows = rotate_heads(key_lin, cos_tab, sine_tab).astype(jnp.bfloat16).reshape(tok_rows, width_kv)
    value_rows = projected[:, width_q + width_kv :].astype(jnp.bfloat16)

    def add_block(partial_value, piece, first_row):
        key_block, value_block = piece

        def add_compute_block(state):
            row_total, weighted = state
            key_count = key_block.shape[0]
            key_grp = key_block.reshape(key_count, KVH, HD)
            raw_scores = jnp.einsum(
                "grd,ngd->grn", query_grp, key_grp, preferred_element_type=jnp.float32
            )
            capped = CAP * jnp.tanh(raw_scores / CAP)
            key_pos = first_row + jnp.arange(key_count, dtype=jnp.int32)
            allowed = key_pos[None, None, :] <= row_pos[None, :, None]
            weights = jnp.where(allowed, jnp.exp(capped), 0.0)
            value_grp = value_block.reshape(key_count, KVH, HD)
            weighted = weighted + jnp.einsum(
                "grn,ngd->grd",
                weights.astype(jnp.bfloat16),
                value_grp,
                preferred_element_type=jnp.float32,
            )
            return (row_total + jnp.sum(weights, axis=-1), weighted)

        def add_skip_block(state):
            return state

        return lax.cond(first_row <= last_pos, add_compute_block, add_skip_block, partial_value)

    start_state = (
        jnp.zeros((KVH, q_group * tok_rows), jnp.float32),
        jnp.zeros((KVH, q_group * tok_rows, HD), jnp.float32),
    )
    row_total, weighted = blockwise(
        add_block,
        start_state,
        (
            lax.all_gather(key_rows, "ctx", axis=0, tiled=True),
            lax.all_gather(value_rows, "ctx", axis=0, tiled=True),
        ),
        512,
    )
    inv_total = 1.0 / row_total
    attended_grp = weighted * inv_total[..., None]
    attended_b = from_groups(attended_grp, tok_rows, q_group).astype(jnp.bfloat16)
    branch = jnp.dot(attended_b, full_out, preferred_element_type=jnp.float32)
    inv_post, normed_post = rms_parts(branch)
    middle = resid_in + normed_post * post_factor
    inv_mid, normed_mid = rms_parts(middle)
    hidden_ffn = (normed_mid * pre_ffn_factor).astype(jnp.bfloat16)
    gate_up = fold_rows(
        hidden_ffn, lax.all_gather(gateup_shard, ("ctx", "fsdp"), axis=0, tiled=True)
    )
    gate_lin = gate_up[:, :FF]
    up_lin = gate_up[:, FF:]
    active = gated(gate_lin, up_lin).astype(jnp.bfloat16)
    ffn_branch = fold_rows(active, lax.all_gather(w_down, ("ctx", "fsdp"), axis=0, tiled=True))
    inv_ffn, normed_ffn = rms_parts(ffn_branch)
    output = (middle + normed_ffn * post_ffn_factor).astype(jnp.bfloat16)
    out_cot = out_grad[0].astype(jnp.float32)
    post_ffn_part = jnp.sum(out_cot * normed_ffn, axis=0)
    d_ffn_b = norm_back(out_cot * post_ffn_factor, normed_ffn, inv_ffn).astype(jnp.bfloat16)
    down_total = lax.psum_scatter(
        grad_rows(active, d_ffn_b, 1, lax.axis_size(("ctx", "fsdp")) * w_down.shape[0]),
        ("ctx", "fsdp"),
        scatter_dimension=0,
        tiled=True,
    )
    d_active = contract_cols(d_ffn_b, lax.all_gather(w_down, ("ctx", "fsdp"), axis=0, tiled=True))
    unused_value, gate_pull = jax.vjp(gated, gate_lin, up_lin)
    d_gate, d_up = gate_pull(d_active)
    d_gateup_b = jnp.concatenate([d_gate.astype(jnp.bfloat16), d_up.astype(jnp.bfloat16)], axis=1)
    gateup_folded = lax.psum_scatter(
        grad_rows(
            hidden_ffn,
            d_gateup_b,
            ROW_FOLD,
            lax.axis_size(("ctx", "fsdp")) * (ROW_FOLD * shard_rows),
        ),
        ("ctx", "fsdp"),
        scatter_dimension=0,
        tiled=True,
    )
    gateup_total = gateup_folded.reshape(shard_rows, 2 * FF)
    d_hidden_ffn = contract_cols(
        d_gateup_b, lax.all_gather(gateup_shard, ("ctx", "fsdp"), axis=0, tiled=True)
    )
    pre_ffn_part = jnp.sum(d_hidden_ffn * normed_mid, axis=0)
    d_middle = out_cot + norm_back(d_hidden_ffn * pre_ffn_factor, normed_mid, inv_mid)
    back_qkv, back_out = (
        lax.all_gather(qkv_shard, ("ctx", "fsdp"), axis=0, tiled=True),
        lax.all_gather(w_out, ("ctx", "fsdp"), axis=0, tiled=True),
    )
    post_gain_part = jnp.sum(d_middle * normed_post, axis=0)
    d_branch_b = norm_back(d_middle * post_factor, normed_post, inv_post).astype(jnp.bfloat16)
    w_out_part = contract_rows(attended_b, d_branch_b)
    d_attended = contract_cols(d_branch_b, back_out).astype(jnp.bfloat16)
    d_att_grp = to_groups(d_attended, tok_rows, q_group)
    row_delta = jnp.sum(d_att_grp.astype(jnp.float32) * attended_grp, axis=-1)
    zero_rows = jnp.zeros((tok_rows, width_kv), jnp.float32)
    zero_query = jnp.zeros((KVH, q_group * tok_rows, HD), jnp.float32)
    block_ids = jnp.arange(n_ctx, dtype=jnp.int32)
    all_keys, all_values = (
        lax.all_gather(key_rows, "ctx", axis=0, tiled=True),
        lax.all_gather(value_rows, "ctx", axis=0, tiled=True),
    )

    def returned_step(acc_query, block_item):
        block_index, key_block, value_block = block_item
        first_row = block_index * tok_rows

        def returned_compute_block(acc_in):
            d_query, d_key, d_value = block_grads(
                query_grp,
                row_pos,
                d_att_grp,
                row_delta,
                inv_total,
                key_block,
                value_block,
                first_row,
            )
            return (acc_in + d_query, (d_key, d_value))

        def returned_skip_block(acc_in):
            return (acc_in, (zero_rows, zero_rows))

        return lax.cond(
            first_row <= last_pos, returned_compute_block, returned_skip_block, acc_query
        )

    key_blocks = all_keys.reshape(n_ctx, tok_rows, width_kv)
    value_blocks = all_values.reshape(n_ctx, tok_rows, width_kv)
    d_query_grp, key_terms = lax.scan(
        returned_step, zero_query, (block_ids, key_blocks, value_blocks)
    )
    key_term_rows = key_terms[0].reshape(n_ctx * tok_rows, width_kv)
    value_term_rows = key_terms[1].reshape(n_ctx * tok_rows, width_kv)
    d_keys, d_values = (
        lax.psum_scatter(
            key_term_rows.astype(jnp.bfloat16), "ctx", scatter_dimension=0, tiled=True
        ).astype(jnp.float32),
        lax.psum_scatter(
            value_term_rows.astype(jnp.bfloat16), "ctx", scatter_dimension=0, tiled=True
        ).astype(jnp.float32),
    )
    d_query_flat = from_groups(d_query_grp, tok_rows, q_group).reshape(tok_rows, H, HD) * q_scale
    dq_lin = (
        unrotate_heads(d_query_flat, cos_tab, sine_tab).astype(jnp.bfloat16).reshape(tok_rows, width_q)
    )
    dk_lin = (
        unrotate_heads(d_keys.reshape(tok_rows, KVH, HD), cos_tab, sine_tab)
        .astype(jnp.bfloat16)
        .reshape(tok_rows, width_kv)
    )
    dv_lin = d_values.astype(jnp.bfloat16)
    dqkv_b = jnp.concatenate([dq_lin, dk_lin, dv_lin], axis=1)
    d_hidden = contract_cols(dqkv_b, back_qkv)
    qkv_part = contract_rows(hidden, dqkv_b).reshape(ROW_FOLD * D, width_qkv // ROW_FOLD)
    pre_gain_part = jnp.sum(d_hidden * normed_pre, axis=0)
    token_grad = d_middle + norm_back(d_hidden * pre_factor, normed_pre, inv_pre)
    gain_parts = jnp.stack([pre_gain_part, post_gain_part, pre_ffn_part, post_ffn_part])
    qkv_folded, out_total, gain_totals = (
        lax.psum_scatter(qkv_part, ("ctx", "fsdp"), scatter_dimension=0, tiled=True),
        lax.psum_scatter(w_out_part, ("ctx", "fsdp"), scatter_dimension=0, tiled=True),
        lax.psum_scatter(gain_parts, ("ctx", "fsdp"), scatter_dimension=1, tiled=True),
    )
    qkv_total = qkv_folded.reshape(shard_rows, width_qkv)
    return (
        output[None],
        token_grad.astype(jnp.bfloat16)[None],
        qkv_total[:, :width_q],
        qkv_total[:, width_q : width_q + width_kv],
        qkv_total[:, width_q + width_kv :],
        out_total,
        gateup_total[:, :FF],
        gateup_total[:, FF:],
        down_total,
        gain_totals[0],
        gain_totals[1],
        gain_totals[2],
        gain_totals[3],
    )


def solution(mesh):
    ring = mesh.shape["ctx"] == RING and mesh.shape["fsdp"] == 4
    tokens, rows, gains = P("fsdp", "ctx", None), P(("ctx", "fsdp"), None), P(("ctx", "fsdp"))
    return jax.shard_map(
        on_ring if ring else on_any_mesh,
        mesh=mesh,
        in_specs=(tokens,) + (rows,) * 7 + (gains,) * 4 + (tokens,),
        out_specs=(tokens, tokens) + (rows,) * 7 + (gains,) * 4,
        check_vma=False,
    )
```

```python
import jax
import jax.numpy as jnp
import numpy as np
from jax import lax
from jax.experimental import pallas as pl
from jax.experimental.pallas import tpu as pltpu
from jax.sharding import PartitionSpec as P

D = 2304
H = 8
KVH = 4
HD = 256
CAP = 50
FF = 9216

EPSILON = 1e-06
ROPE_BASE = 10000.0

MESH = pl.DeviceIdType.MESH
HBM = pl.BlockSpec(memory_space=pl.ANY)
VMEM = pl.BlockSpec(memory_space=pltpu.VMEM)
DMA = pltpu.SemaphoreType.DMA
BF = jnp.bfloat16
F32 = jnp.float32


def constant_tables(length, width):
    exponents = -np.arange(width // 2, dtype=np.float32) * np.float32(2.0) / np.float32(width)
    inv_freqs = np.power(np.float32(ROPE_BASE), exponents, dtype=np.float32)
    angles = np.arange(length, dtype=np.float32)[:, None] * inv_freqs[None, :]
    return np.cos(angles), np.sin(angles)


def rotate(rows, cos_tab, sine_tab):
    half_width = rows.shape[-1] // 2
    front, back = rows[..., :half_width], rows[..., half_width:]
    return jnp.concatenate(
        [front * cos_tab - back * sine_tab, back * cos_tab + front * sine_tab], axis=-1
    )


def unrotate(rows, cos_tab, sine_tab):
    half_width = rows.shape[-1] // 2
    front, back = rows[..., :half_width], rows[..., half_width:]
    return jnp.concatenate(
        [front * cos_tab + back * sine_tab, back * cos_tab - front * sine_tab], axis=-1
    )


def rms_parts(values_in):
    inverse = lax.rsqrt(jnp.mean(values_in * values_in, axis=-1, keepdims=True) + EPSILON)
    return (inverse, values_in * inverse)


def norm_back(grad_normed, normed, inverse):
    return inverse * (grad_normed - normed * jnp.mean(grad_normed * normed, axis=-1, keepdims=True))


def contract_rows(left, right):
    return lax.dot_general(left, right, (((0,), (0,)), ((), ())), preferred_element_type=F32)


def contract_cols(left, right):
    return lax.dot_general(left, right, (((1,), (1,)), ((), ())), preferred_element_type=F32)


def fold_rows(left, right):
    return jnp.dot(left, right, preferred_element_type=F32)


def gated(gate_in, up_in):
    return jax.nn.gelu(gate_in, approximate=True) * up_in


NZ = 4
RING = 2 * NZ


def my_place():
    c, f = lax.axis_index("ctx"), lax.axis_index("fsdp")
    return c // 2, c % 2, f // 2, f % 2


def ring_index(y, z):
    return z + y * (RING - 1 - 2 * z)


def ring_yz(q):
    y = q // NZ
    return y, q + y * (RING - 1 - 2 * q)


def device(z, core, y, x):
    return (2 * z + core, 2 * y + x)


def ring_device(q, core, x):
    y, z = ring_yz(q)
    return device(z, core, y, x)


def remote(src, dst, send_sem, recv_sem, where):
    return pltpu.make_async_remote_copy(
        src_ref=src,
        dst_ref=dst,
        send_sem=send_sem,
        recv_sem=recv_sem,
        device_id=where,
        device_id_type=MESH,
    )


def greet(places, meanwhile=None):
    barrier = pltpu.get_barrier_semaphore()
    for place in places:
        pl.semaphore_signal(barrier, inc=1, device_id=place, device_id_type=MESH)
    if meanwhile is not None:
        meanwhile()
    pl.semaphore_wait(barrier, len(places))


def params(collective_id, vmem_mib=56):
    return pltpu.CompilerParams(
        collective_id=collective_id,
        has_side_effects=True,
        vmem_limit_bytes=vmem_mib * 2**20,
    )


SUB = 4


def ring_parts(direction, step, half_step):
    if step != half_step:
        return list(range(SUB))
    half = SUB // 2
    return list(range(half)) if direction == 0 else list(range(half, SUB))


TOK = 128
UNITS = FF // RING
TILE = 128
GELU_K = 0.7978845608028654
GELU_A = 0.044715


class SlotGather:
    def __init__(self, buf, ss, rs):
        z, core, y, x = my_place()
        p = ring_index(y, z)
        self.buf, self.ss, self.rs = buf, ss, rs
        self.near = (ring_device((p + 1) % RING, core, x), ring_device((p + RING - 1) % RING, core, x))
        self.pending = []

    def copy(self, direction, step, k):
        piece = TOK // SUB
        src = 0 if step == 0 else 2 * step - 1 + direction
        dst = 7 if step == 3 else 2 * step + 1 + direction
        return remote(
            self.buf.at[pl.ds(src * TOK + k * piece, piece)],
            self.buf.at[pl.ds(dst * TOK + k * piece, piece)],
            self.ss.at[direction, step, k],
            self.rs.at[direction, step, k],
            self.near[direction],
        )

    def step(self, step):
        for k in range(SUB):
            for direction in (0, 1):
                if step > 0:
                    self.copy(direction, step - 1, k).wait_recv()
                if k in ring_parts(direction, step, 3):
                    c = self.copy(direction, step, k)
                    c.start()
                    self.pending.append(c)

    def finish(self):
        for direction in (0, 1):
            for k in ring_parts(direction, 3, 3):
                self.copy(direction, 3, k).wait_recv()

    def drain(self):
        for c in self.pending:
            c.wait_send()


class SlotScatter:
    def __init__(self, part, buf, ss, rs):
        z, core, y, x = my_place()
        p = ring_index(y, z)
        self.part, self.buf, self.ss, self.rs = part, buf, ss, rs
        self.near = (ring_device((p + 1) % RING, core, x), ring_device((p + RING - 1) % RING, core, x))
        self.pending = []

    def copy(self, direction, step, k, src):
        rows = pl.ds(k * (TOK // SUB), TOK // SUB)
        return remote(
            src,
            self.buf.at[direction, step, rows],
            self.ss.at[direction, step, k],
            self.rs.at[direction, step, k],
            self.near[direction],
        )

    def step(self, step):
        piece = TOK // SUB
        for k in range(SUB):
            rows = pl.ds(k * piece, piece)
            for direction in (0, 1):
                if k not in ring_parts(direction, step, 0):
                    continue
                slot = 7 if step == 0 else 2 * (4 - step) - direction
                mine = pl.ds(slot * TOK + k * piece, piece)
                src = self.part.at[mine]
                if step > 0 and k in ring_parts(direction, step - 1, 0):
                    src = self.buf.at[direction, step - 1, rows]
                    self.copy(direction, step - 1, k, src).wait_recv()
                    src[...] = (src[...].astype(F32) + self.part[mine].astype(F32)).astype(BF)
                c = self.copy(direction, step, k, src)
                c.start()
                self.pending.append(c)

    def finish(self, total):
        for k in range(SUB):
            rows = pl.ds(k * (TOK // SUB), TOK // SUB)
            for direction in (0, 1):
                src = self.buf.at[direction, 3, rows]
                self.copy(direction, 3, k, src).wait_recv()
                total[rows] = total[rows] + src[...].astype(F32)

    def drain(self):
        for c in self.pending:
            c.wait_send()


def tiles(count, width, body):
    def step(i, carry):
        body(pl.ds(pl.multiple_of(i * width, width), width))
        return carry

    lax.fori_loop(0, count, step, 0)


def gelu_parts(v):
    bent = jnp.tanh(GELU_K * (v + GELU_A * (v * v * v)))
    value = 0.5 * v * (1.0 + bent)
    slope = 0.5 * (1.0 + bent) + 0.5 * v * (1.0 - bent * bent) * (GELU_K * (1.0 + 3.0 * GELU_A * (v * v)))
    return value, slope


PAIRS = ((128, 256), (384, 256), (640, 256))
LAST = (896, 128)
OWN = (0, 128)


def by_rows(body):
    def step(i, carry):
        body(pl.ds(pl.multiple_of(i * 32, 32), 32))
        return carry

    lax.fori_loop(0, TOK // 32, step, 0)


def feed_forward_kernel(branch, block, gains, cot, w_hbm, wd_hbm,
                        out_o, d_mid_o, d_branch_o, gain_o, wd_grad, gu_grad,
                        wgu, wd, ha, gu, act, part, buf, df, dgu, middle, total, stage,
                        w_sem, ags, agr, rss, rsr, out_sem):
    gather = [SlotGather(b, ags.at[i], agr.at[i]) for i, b in enumerate((ha, df))]
    scatter = [SlotScatter(part, buf, rss.at[i], rsr.at[i]) for i in range(2)]
    loads = [
        pltpu.make_async_copy(w_hbm, wgu, w_sem.at[0]),
        pltpu.make_async_copy(wd_hbm, wd, w_sem.at[1]),
    ]
    for c in loads:
        c.start()

    def head():
        def rows(r):
            mid = block[r].astype(F32) + rms_parts(branch[r])[1] * (1.0 + gains[1:2])
            middle[r] = mid
            ha[r] = (rms_parts(mid)[1] * (1.0 + gains[2:3])).astype(BF)

        by_rows(rows)

    greet(gather[0].near, head)
    gather[0].step(0)
    gain_o[...] = jnp.zeros(gain_o.shape, F32)
    loads[0].wait()

    def gate_up(first, count):
        rows = pl.ds(first, count)

        def column(cols):
            gu[rows, cols] = fold_rows(ha[rows], wgu[:, cols])

        tiles(3, 768, column)

        def finish(i, carry):
            r = pl.ds(pl.multiple_of(first + i * 32, 32), 32)
            act[r] = (gelu_parts(gu[r, 0:UNITS])[0] * gu[r, UNITS : 2 * UNITS]).astype(BF)
            return carry

        lax.fori_loop(0, count // 32, finish, 0)

    def down_part(first, count, dst):
        def column(cols):
            value = fold_rows(act[pl.ds(first, count)], wd[:, cols])
            dst[pl.ds(first, count), cols] = value.astype(dst.dtype)

        tiles(3, 768, column)

    def active_back(first, count):
        rows = pl.ds(first, count)
        for n in range(3):
            cols, up_cols = pl.ds(n * 384, 384), pl.ds(UNITS + n * 384, 384)
            d_active = contract_cols(df[rows], wd[cols])
            value, slope = gelu_parts(gu[rows, cols])
            dgu[rows, cols] = (d_active * gu[rows, up_cols] * slope).astype(BF)
            dgu[rows, up_cols] = (d_active * value).astype(BF)

    def hidden_part(first, count, dst):
        def column(cols):
            value = contract_cols(dgu[pl.ds(first, count)], wgu[cols])
            dst[pl.ds(first, count), cols] = value.astype(dst.dtype)

        tiles(3, 768, column)

    def hidden_near():
        def column(cols):
            value = contract_cols(dgu[0 : 3 * TOK], wgu[cols])
            total[:, cols] = value[0:TOK]
            part[TOK : 3 * TOK, cols] = value[TOK:].astype(BF)

        tiles(3, 768, column)

    n_down = UNITS // TILE
    n_tiles = n_down + ha.shape[1] // TILE

    def grad_out(i):
        slot = i % 2
        if i < n_down:
            return pltpu.make_async_copy(stage.at[slot], wd_grad.at[pl.ds(i * TILE, TILE)], out_sem.at[slot])
        return pltpu.make_async_copy(stage.at[slot], gu_grad.at[pl.ds((i - n_down) * TILE, TILE)], out_sem.at[slot])

    def grad_tiles(first, last):
        for i in range(first, last):
            if i >= 2:
                grad_out(i - 2).wait()
            if i < n_down:
                value = contract_rows(act[:, pl.ds(i * TILE, TILE)], df[...])
            else:
                value = contract_rows(ha[:, pl.ds((i - n_down) * TILE, TILE)], dgu[...])
            stage[i % 2] = value.astype(BF)
            grad_out(i).start()

    gate_up(*OWN)
    for step, pair in enumerate(PAIRS):
        gather[0].step(step + 1)
        if step == 0:
            loads[1].wait()
        gate_up(*pair)
    gather[0].finish()
    gate_up(*LAST)
    down_part(*LAST, part)
    scatter[0].step(0)
    for step, pair in enumerate(PAIRS[::-1]):
        down_part(*pair, part)
        scatter[0].step(step + 1)
    down_part(*OWN, total)
    scatter[0].finish(total)
    gather[0].drain()
    scatter[0].drain()

    def turn(r):
        inverse, normed = rms_parts(total[r])
        df[r] = norm_back(cot[r].astype(F32) * (1.0 + gains[3:4]), normed, inverse).astype(BF)

    def add_gain(i, value):
        gain_o[i : i + 1, 0:D] = gain_o[i : i + 1, 0:D] + jnp.sum(value, axis=0, keepdims=True)

    def outputs(r):
        normed = rms_parts(total[r])[1]
        out_o[r] = (middle[r] + normed * (1.0 + gains[3:4])).astype(BF)
        add_gain(3, cot[r].astype(F32) * normed)

    by_rows(turn)
    gather[1].step(0)
    by_rows(outputs)
    active_back(*OWN)
    for step, pair in enumerate(PAIRS):
        gather[1].step(step + 1)
        active_back(*pair)
    gather[1].finish()
    active_back(*LAST)
    hidden_part(*LAST, part)
    scatter[1].step(0)
    done = 0
    for step, pair in enumerate(PAIRS[::-1]):
        if pair[0] == TOK:
            hidden_near()
        else:
            hidden_part(*pair, part)
        scatter[1].step(step + 1)
        count = (8, 6, n_tiles - 14)[step]
        grad_tiles(done, done + count)
        done += count
    scatter[1].finish(total)

    def tail(r):
        inv_mid, normed_mid = rms_parts(middle[r])
        d_hidden = total[r]
        add_gain(2, d_hidden * normed_mid)
        d_mid = cot[r].astype(F32) + norm_back(d_hidden * (1.0 + gains[2:3]), normed_mid, inv_mid)
        d_mid_o[r] = d_mid
        inv_post, normed_post = rms_parts(branch[r])
        add_gain(1, d_mid * normed_post)
        d_branch_o[r] = norm_back(d_mid * (1.0 + gains[1:2]), normed_post, inv_post).astype(BF)

    by_rows(tail)
    for i in (n_tiles - 2, n_tiles - 1):
        grad_out(i).wait()
    gather[1].drain()
    scatter[1].drain()


def feed_forward(branch, block, gains, out_grad, w_in, w_down, collective_id):
    rows, width = branch.shape
    total = RING * rows

    def full(*shape, dtype=F32):
        return jax.ShapeDtypeStruct(shape, dtype)

    return pl.pallas_call(
        feed_forward_kernel,
        out_shape=[
            full(rows, width, dtype=BF), full(rows, width), full(rows, width, dtype=BF), full(8, PADDED),
            full(UNITS, width, dtype=BF), full(width, 2 * UNITS, dtype=BF),
        ],
        in_specs=[VMEM] * 4 + [HBM] * 2,
        out_specs=[VMEM] * 4 + [HBM] * 2,
        scratch_shapes=[
            pltpu.VMEM((width, 2 * UNITS), BF), pltpu.VMEM((UNITS, width), BF),
            pltpu.VMEM((total, width), BF), pltpu.VMEM((total, 2 * UNITS), F32), pltpu.VMEM((total, UNITS), BF),
            pltpu.VMEM((total, width), BF), pltpu.VMEM((2, 4, rows, width), BF),
            pltpu.VMEM((total, width), BF), pltpu.VMEM((total, 2 * UNITS), BF),
            pltpu.VMEM((rows, width), F32), pltpu.VMEM((rows, width), F32), pltpu.VMEM((2, TILE, width), BF),
            DMA((2,)),
            DMA((2, 2, 4, SUB)), DMA((2, 2, 4, SUB)), DMA((2, 2, 4, SUB)), DMA((2, 2, 4, SUB)),
            DMA((2,)),
        ],
        compiler_params=params(collective_id, 60),
    )(branch, block, gains, out_grad, w_in, w_down)


WIDTHS = (UNITS, UNITS, HD, HD, HD)


SHARD = D // (4 * RING)
PADDED = D + 128
WINDOW = 256


def window(i):
    return pl.ds(pl.multiple_of((SHARD * i) // 128 * 128, 128), WINDOW)


def member_place(t, core, x):
    return device(t // 2, core, t % 2, x)


def slot_of(q, p):
    d = (q - p + RING) % RING
    return jnp.where(d == 0, 0, jnp.where(d < 4, 2 * d, jnp.where(d == 4, 7, 15 - 2 * d)))


def partner(t, j):
    out = 0
    for bit in (1, 2, 4):
        on = (t // bit) % 2
        out = out + bit * (1 - on if j & bit else on)
    return out


def column_start(which, t):
    if which < 2:
        return pl.multiple_of(t * UNITS, 128)
    return pl.multiple_of((t if which == 2 else t // 2) * HD, 128)


def forward_kernel(gate, up, query, key, value, down, out, block, gain_in, cos, sine,
                   w_gu, d_ref, hidden_o, wq_h, q_h, k_h, v_h, att_h, wo, gain_o, inv_o, branch_o,
                   wq, q_o, k_o, v_o, att_o, ring, seq, seq_part, part, buf, wq_in, own, relay, ga, gsum,
                   load, ags, agr, pls, plr, rss, rsr, sws, swr, s1, r1, s2, r2, s3, r3,
                   q1, t1, q2, t2, q3, t3, s4, r4, s5, r5, sg, rg):
    z, core, y, x = my_place()
    t, p = 2 * z + y, ring_index(y, z)
    sibling, across = device(z, 1 - core, y, x), device(z, core, y, 1 - x)
    member = [partner(t, j) for j in range(RING)]
    members = [member_place(tq, core, x) for tq in member]
    plane = []
    for dc in (0, 1):
        for dy in (0, 1):
            for dx in (0, 1):
                if (dc, dx) != (0, 0):
                    plane.append(device(z, (core + dc) % 2, (y + dy) % 2, (x + dx) % 2))
    greet(members[1:] + plane)
    sources = (gate, up, query, key, value)
    pending = []

    def go(*copies):
        for c in copies:
            c.start()
            pending.append(c)

    def owner(tq, corq, xq):
        return (2 * (tq // 2) + corq) * 4 + 2 * (tq % 2) + xq

    me = owner(t, core, x)

    def columns_of(a, tq):
        return sources[a].at[:, pl.ds(column_start(a, tq), WIDTHS[a])]

    def gain_a(j):
        return remote(gain_in, ga.at[j], sg.at[j], rg.at[j], members[j])

    def gain_b(i):
        return remote(gsum.at[i], gsum.at[2 + i], sg.at[RING + i], rg.at[RING + i], (across, sibling)[i])

    def q_first(j, a, wait=False):
        tq = member[j]
        dst = wq_in.at[owner(tq, core, x) if wait else me, :, pl.ds((a - 2) * HD, HD)]
        return remote(columns_of(a, tq), dst, q1.at[j, a - 2], t1.at[j, a - 2], members[j])

    def q_second(j, wait=False):
        i = owner(member[j], core, 1 - x if wait else x)
        return remote(wq_in.at[i], wq_in.at[i], q2.at[j], t2.at[j], across)

    def q_third(j, flip, wait=False):
        i = owner(member[j], 1 - core if wait else core, 1 - x if flip else x)
        return remote(wq_in.at[i], wq_in.at[i], q3.at[j, flip], t3.at[j, flip], sibling)

    def first(j, a, wait=False):
        tq = member[j]
        dst = w_gu.at[owner(tq, core, x) if wait else me, :, pl.ds(a * UNITS, UNITS)]
        return remote(columns_of(a, tq), dst, s1.at[j, a], r1.at[j, a], members[j])

    def second(j, wait=False):
        i = owner(member[j], core, 1 - x if wait else x)
        return remote(own if j == 0 else w_gu.at[i], w_gu.at[i], s2.at[j], r2.at[j], across)

    def third(j, flip, wait=False):
        i = owner(member[j], 1 - core if wait else core, 1 - x if flip else x)
        return remote(own if (j, flip) == (0, 0) else w_gu.at[i], w_gu.at[i], s3.at[j, flip], r3.at[j, flip], sibling)

    def start_round(j):
        go(first(j, 0), first(j, 1))

    def end_round(j):
        first(j, 0, True).wait_recv()
        first(j, 1, True).wait_recv()
        go(second(j), third(j, 0))

    def end_across(j):
        second(j, True).wait_recv()
        go(third(j, 1))

    gather = SlotGather(ring, ags, agr)

    def block_of(slot):
        if slot == 0:
            return p
        if slot == 7:
            return (p + 4) % RING
        s = (slot + 1) // 2
        return (p + (RING - s if slot % 2 else s)) % RING

    def place(slot, act):
        yq, zq = ring_yz(block_of(slot))
        src, dst = ring.at[pl.ds(slot * TOK, TOK)], seq.at[2 * zq + core]

        @pl.when(yq == core)
        def _():
            c = pltpu.make_async_copy(src, dst, load.at[6 + slot])
            c.start() if act == 0 else c.wait()

        @pl.when(yq != core)
        def _():
            c = remote(src, dst, pls.at[zq], plr.at[zq], sibling)
            c.start() if act == 0 else c.wait_send()

    pair = ((down, d_ref), (out, wo))
    mine = 2 * y + x

    def rows_out(xq, a, act):
        src, dst = pair[a][0], pair[a][1].at[mine]
        to_self = (x == core) & (y == core) & (xq == x)

        @pl.when(to_self)
        def _():
            if a == 0:
                c = pltpu.make_async_copy(relay, dst, load.at[5])
            else:
                c = pltpu.make_async_copy(src, dst, load.at[4])
            c.start() if act == 0 else c.wait()

        @pl.when(jnp.logical_not(to_self))
        def _():
            c = remote(src, dst, s4.at[xq, a], r4.at[y, a], device(z, x, core, xq))
            c.start() if act == 0 else c.wait_send()

    def rows_on(yq, a):
        src, dst = pair[a][0], pair[a][1].at[2 * yq + core]
        from_self = (core == y) & (yq == y) & (core == x)

        @pl.when(from_self)
        def _():
            if a == 0:
                pltpu.make_async_copy(relay, dst, load.at[5]).wait()
            else:
                pltpu.make_async_copy(src, dst, load.at[4]).wait()

        @pl.when(jnp.logical_not(from_self))
        def _():
            remote(src, dst, s4.at[0, a], r4.at[yq, a], sibling).wait_recv()

        go(remote(dst, dst, s5.at[yq, a], r5.at[yq, a], sibling))

    locals_ = [pltpu.make_async_copy(columns_of(a, t), wq_in.at[me, :, pl.ds((a - 2) * HD, HD)], load.at[a]) for a in (2, 3)]
    locals_.append(pltpu.make_async_copy(columns_of(4, t), wq_in.at[me, :, pl.ds(2 * HD, HD)], load.at[14]))
    locals_ += [pltpu.make_async_copy(columns_of(a, t), own.at[:, pl.ds(a * UNITS, UNITS)], load.at[a]) for a in (0, 1)]
    relay_load = pltpu.make_async_copy(down, relay, load.at[15])
    for c in locals_:
        c.start()
    relay_load.start()
    ring[0:TOK] = block[...]
    gather.step(0)
    go(*[gain_a(j) for j in range(1, RING)])
    for j in range(1, RING):
        go(*[q_first(j, a) for a in (2, 3, 4)])
    for c in locals_:
        c.wait()
    go(q_second(0), q_third(0, 0))
    for xq in (0, 1):
        rows_out(xq, 1, 0)
    keep_own = pltpu.make_async_copy(own, w_gu.at[me], load.at[16])
    keep_own.start()
    go(second(0), third(0, 0))
    place(0, 0)
    gsum[0] = jnp.zeros(gsum.shape[1:], F32)
    gsum[0, :, window(me)] = gain_in[...]
    for j in range(1, RING):
        gain_a(j).wait_recv()
        lanes = window(owner(member[j], core, x))
        gsum[0, :, lanes] = gsum[0, :, lanes] + ga[j]
    go(gain_b(0))
    gather.step(1)
    place(1, 0)
    place(2, 0)
    gain_b(0).wait_recv()
    gsum[1] = gsum[0] + gsum[2]
    go(gain_b(1))
    for j in range(1, RING):
        for a in (2, 3, 4):
            q_first(j, a, True).wait_recv()
        go(q_second(j), q_third(j, 0))
    for yq in (0, 1):
        rows_on(yq, 1)
    gather.step(2)
    place(3, 0)
    place(4, 0)
    gain_b(1).wait_recv()
    gain_o[...] = (gsum[1] + gsum[3])[:, 0:D]
    for j in range(RING):
        q_second(j, True).wait_recv()
        go(q_third(j, 1))
    gather.step(3)
    place(5, 0)
    place(6, 0)
    for j in (4, 1, 5, 2, 6, 3, 7):
        start_round(j)
    relay_load.wait()
    for xq in (0, 1):
        rows_out(xq, 0, 0)
    end_across(0)
    for j in range(RING):
        for flip in (0, 1):
            q_third(j, flip, True).wait_recv()

    def join(g, carry):
        pieces = [wq_in[4 * g + i].astype(F32) for i in range(4)]
        wq[pl.ds(pl.multiple_of(288 * g, 16), 288)] = jnp.concatenate(pieces, axis=0).astype(BF)
        return carry

    lax.fori_loop(0, 8, join, 0)
    results_out = [pltpu.make_async_copy(wq, wq_h, load.at[22])]
    results_out[0].start()
    gather.finish()
    place(7, 0)
    for zq in range(NZ):
        dst = seq.at[2 * zq + 1 - core]
        remote(dst, dst, pls.at[zq], plr.at[zq], sibling).wait_recv()
    for slot in range(RING):
        place(slot, 1)
    end_round(1)

    factor = 1.0 + gain_o[0:1]

    def norm(c, carry):
        for half in range(2):
            rows = pl.ds(half * 64, 64)
            seq[c, rows] = (rms_parts(seq[c, rows].astype(F32))[1] * factor).astype(BF)
        return carry

    lax.fori_loop(0, RING, norm, 0)
    keep_hidden = pltpu.make_async_copy(seq, hidden_o, load.at[17])
    keep_hidden.start()
    for i in range(4):
        r = pl.ds(i * 256, 256)
        rows = seq[2 * i : 2 * i + 2].reshape(256, -1)
        tabs = (cos[r], sine[r])
        q_o[r] = (rotate(fold_rows(rows, wq[:, 0:HD]), *tabs) * (HD ** (-0.5))).astype(BF)
        k_o[r] = rotate(fold_rows(rows, wq[:, HD : 2 * HD]), *tabs).astype(BF)
        v_o[r] = fold_rows(rows, wq[:, 2 * HD : 3 * HD]).astype(BF)
    for i, (src, dst) in enumerate(((q_o, q_h), (k_o, k_h), (v_o, v_h))):
        results_out.append(pltpu.make_async_copy(src, dst, load.at[23 + i]))
        results_out[-1].start()
    end_round(4)
    end_across(1)

    def swap(zq, kept):
        where = pl.ds(pl.multiple_of(slot_of(ring_index(core, zq), p) * TOK, TOK), TOK)
        if kept:
            return pltpu.make_async_copy(seq_part.at[2 * zq + core], part.at[where], load.at[18 + zq])
        return remote(seq_part.at[2 * zq + 1 - core], part.at[where], sws.at[zq], swr.at[zq], sibling)

    def swapped(zq):
        where = pl.ds(pl.multiple_of(slot_of(ring_index(1 - core, zq), p) * TOK, TOK), TOK)
        return remote(seq_part.at[0], part.at[where], sws.at[zq], swr.at[zq], sibling)

    for yq in (0, 1):
        remote(out, wo.at[2 * yq + 1 - core], s5.at[yq, 1], r5.at[yq, 1], sibling).wait_recv()
    for i in range(4):
        r, upto = pl.ds(i * 256, 256), (i + 1) * 256
        bent = jnp.tanh(contract_cols(q_o[r], k_o[0:upto]) / CAP)
        seen = lax.broadcasted_iota(jnp.int32, bent.shape, 1) <= i * 256 + lax.broadcasted_iota(jnp.int32, bent.shape, 0)
        weights = jnp.where(seen, jnp.exp(CAP * bent), 0.0)
        inverse = 1.0 / jnp.sum(weights, axis=-1, keepdims=True)
        attended = fold_rows(weights.astype(BF), v_o[0:upto]) * inverse
        inv_o[r] = inverse
        att_o[r] = attended
        attended_b = attended.astype(BF)

        def columns(cols):
            sums = fold_rows(attended_b, wo[:, :, cols].reshape(HD, 768))
            seq_part[2 * i, :, cols] = sums[0:TOK].astype(BF)
            seq_part[2 * i + 1, :, cols] = sums[TOK:].astype(BF)

        tiles(3, 768, columns)
        swap(i, True).start()
        swap(i, False).start()
        if i == 0:
            end_round(2)
        if i == 2:
            end_round(5)
            end_across(2)
            for yq in (0, 1):
                rows_on(yq, 0)
    results_out.append(pltpu.make_async_copy(att_o, att_h, load.at[26]))
    results_out[-1].start()
    for zq in range(NZ):
        swap(zq, True).wait()
        swapped(zq).wait_recv()
    scatter = SlotScatter(part, buf, rss, rsr)
    scatter.step(0)
    end_round(3)
    end_across(4)
    scatter.step(1)
    end_round(6)
    end_across(5)
    end_across(3)
    scatter.step(2)
    end_round(7)
    end_across(6)
    scatter.step(3)
    branch_o[...] = part[0:TOK].astype(F32)
    end_across(7)
    scatter.finish(branch_o)

    for j in range(RING):
        for flip in (0, 1):
            third(j, flip, True).wait_recv()
    for yq in (0, 1):
        remote(down, d_ref.at[2 * yq + 1 - core], s5.at[yq, 0], r5.at[yq, 0], sibling).wait_recv()
    for xq in (0, 1):
        for a in (0, 1):
            to_self = (x == core) & (y == core) & (xq == x)

            @pl.when(jnp.logical_not(to_self))
            def _():
                remote(pair[a][0], pair[a][1].at[mine], s4.at[xq, a], r4.at[y, a], device(z, x, core, xq)).wait_send()
    keep_own.wait()
    keep_hidden.wait()
    for c in results_out:
        c.wait()
    for zq in range(NZ):
        swap(zq, False).wait_send()
    gather.drain()
    scatter.drain()
    for c in pending:
        c.wait_send()


def forward(gate, up, query, key, value, down, out, block, gains, cos_tab, sine_tab, collective_id):
    n = 4 * RING
    rows, width = block.shape
    shard, total = gate.shape[0], RING * block.shape[0]

    def full(*shape, dtype=BF):
        return jax.ShapeDtypeStruct(shape, dtype)

    blocks = (RING, rows, width)
    return pl.pallas_call(
        forward_kernel,
        out_shape=[
            full(n, shard, 2 * UNITS), full(4, *down.shape), full(*blocks), full(width, 3 * HD),
            full(total, HD), full(total, HD), full(total, HD), full(total, HD, dtype=F32),
            full(4, *out.shape), full(8, D, dtype=F32), full(total, 1, dtype=F32), full(rows, width, dtype=F32),
        ],
        in_specs=[HBM] * 7 + [VMEM] * 4,
        out_specs=[HBM] * 8 + [VMEM] * 4,
        scratch_shapes=[
            pltpu.VMEM((width, 3 * HD), BF), pltpu.VMEM((total, HD), BF), pltpu.VMEM((total, HD), BF), pltpu.VMEM((total, HD), BF),
            pltpu.VMEM((total, HD), F32),
            pltpu.VMEM((total, width), BF), pltpu.VMEM(blocks, BF), pltpu.VMEM(blocks, BF), pltpu.VMEM((total, width), BF),
            pltpu.VMEM((2, 4, rows, width), BF), pltpu.VMEM((n, shard, 3 * HD), BF),
            pltpu.VMEM((shard, 2 * UNITS), BF), pltpu.VMEM(down.shape, BF),
            pltpu.VMEM((RING,) + gains.shape, F32), pltpu.VMEM((4, 8, PADDED), F32),
            DMA((27,)),
            DMA((2, 4, SUB)), DMA((2, 4, SUB)), DMA((NZ,)), DMA((NZ,)), DMA((2, 4, SUB)), DMA((2, 4, SUB)), DMA((NZ,)), DMA((NZ,)),
            DMA((RING, 2)), DMA((RING, 2)), DMA((RING,)), DMA((RING,)), DMA((RING, 2)), DMA((RING, 2)),
            DMA((RING, 3)), DMA((RING, 3)), DMA((RING,)), DMA((RING,)), DMA((RING, 2)), DMA((RING, 2)),
            DMA((2, 2)), DMA((2, 2)), DMA((2, 2)), DMA((2, 2)), DMA((RING + 2,)), DMA((RING + 2,)),
        ],
        compiler_params=params(collective_id, 60),
    )(gate, up, query, key, value, down, out, block, gains, cos_tab, sine_tab)


ROUNDS = (4, 5, 6, 7, 2, 3, 1, 0)
AHEAD = 2


def backward_kernel(ready, d_branch, gu_in, down_in, hidden, wq, wo, q_in, k_in, v_in, att, inv, cos, sine, block_in, gain_in,
                    d_hid_o, gain_o, c_gu, c_q, down_o, out_o,
                    ring, seq, part, buf, d_att, d_qkv, dk, dv, grad_q, aq, bq,
                    own, a_gu, b_gu, down_own, da, db, og, oa, ob, ga, gsum,
                    load, ags, agr, pls, plr, rss, rsr, sws, swr, s1, r1, s2, r2, s3, r3,
                    q1, t1, q2, t2, q3, t3, sx, rx, sg, rg):
    z, core, y, x = my_place()
    t, p = 2 * z + y, ring_index(y, z)
    sibling, across = device(z, 1 - core, y, x), device(z, core, y, 1 - x)
    diagonal = device(z, 1 - core, 1 - y, x)
    members = [member_place(partner(t, j), core, x) for j in range(RING)]
    order = [partner(t, j) for j in ROUNDS]
    greet(members[1:] + [sibling, across, diagonal])
    pending = []

    def go(*copies):
        for c in copies:
            c.start()
            pending.append(c)

    def owner(tq, corq, xq):
        return (2 * (tq // 2) + corq) * 4 + 2 * (tq % 2) + xq

    side_x = (1 - x, x)

    def gu_a(side, j):
        src = gu_in.at[owner(order[j], 1 - core, side_x[side])]
        return remote(src, a_gu.at[side, j], s1.at[side, j], r1.at[side, j], sibling)

    def gu_own(side, j):
        return pltpu.make_async_copy(gu_in.at[owner(order[j], core, side_x[side])], own.at[j % 2], load.at[j % 2])

    def gu_b(j):
        return remote(a_gu.at[0, j], b_gu.at[j], s2.at[j], r2.at[j], across)

    def gu_c(j, wait=False):
        dst = c_gu.at[order[j] if wait else t]
        if ROUNDS[j] == 0:
            return pltpu.make_async_copy(a_gu.at[1, j], dst, load.at[2])
        return remote(a_gu.at[1, j], dst, s3.at[j], r3.at[j], members[ROUNDS[j]])

    def sum_own(side, j, more=None):
        gu_own(side, j).wait()
        gu_a(side, j).wait_recv()
        total = a_gu[side, j].astype(F32) + own[j % 2].astype(F32)
        if more is not None:
            total = total + more[j].astype(F32)
        a_gu[side, j] = total.astype(BF)

    def pump(first, last):
        for j in range(first, last):
            gu_own(1, j).start()
        for j in range(first, last):
            gu_b(j).wait_recv()
            if j + AHEAD < RING:
                go(gu_b(j + AHEAD))
            sum_own(1, j, b_gu)

    small = ((down_in, down_own, da, db, down_o), (og, None, oa, ob, out_o))

    def small_a(a, xo):
        return remote(small[a][0].at[2 * (1 - core) + xo], small[a][2].at[xo], sx.at[a, xo], rx.at[a, xo], sibling)

    def small_b(a):
        return remote(small[a][2].at[1 - x], small[a][3], sx.at[a, 2], rx.at[a, 2], across)

    def small_c(a, act):
        src, dst = small[a][2].at[x], small[a][4]

        @pl.when(core == y)
        def _():
            c = pltpu.make_async_copy(src, dst, load.at[3 + a])
            c.start() if act == 0 else c.wait()

        @pl.when(core != y)
        def _():
            c = remote(src, dst, sx.at[a, 3], rx.at[a, 3], diagonal)
            c.start() if act == 0 else c.wait()

    def q_a(side, j):
        src = grad_q.at[owner(order[j], 1 - core, side_x[side])]
        return remote(src, aq.at[side, j], q1.at[side, j], t1.at[side, j], sibling)

    def q_b(j):
        return remote(grad_q.at[owner(order[j], core, 1 - x)], bq.at[j], q2.at[j], t2.at[j], across)

    def q_c(j, wait=False):
        src, dst = grad_q.at[owner(order[j], core, x)], c_q.at[order[j] if wait else t]
        if ROUNDS[j] == 0:
            return pltpu.make_async_copy(src, dst, load.at[5])
        return remote(src, dst, q3.at[j], t3.at[j], members[ROUNDS[j]])

    def gain_a():
        return remote(gain_in, gsum.at[2], sg.at[RING], rg.at[RING], sibling)

    def gain_b():
        return remote(gsum.at[0], gsum.at[3], sg.at[RING + 1], rg.at[RING + 1], across)

    def gain_c(j):
        lanes = window(owner(partner(t, j), core, x))
        return remote(gsum.at[1, :, lanes], ga.at[j], sg.at[j], rg.at[j], members[j])

    gather = SlotGather(ring, ags, agr)

    def block(slot):
        if slot == 0:
            return p
        if slot == 7:
            return (p + 4) % RING
        s = (slot + 1) // 2
        return (p + (RING - s if slot % 2 else s)) % RING

    def place(slot, act):
        yq, zq = ring_yz(block(slot))
        src, dst = ring.at[pl.ds(slot * TOK, TOK)], seq.at[2 * zq + core]

        @pl.when(yq == core)
        def _():
            c = pltpu.make_async_copy(src, dst, load.at[6 + slot])
            c.start() if act == 0 else c.wait()

        @pl.when(yq != core)
        def _():
            c = remote(src, dst, pls.at[zq], plr.at[zq], sibling)
            c.start() if act == 0 else c.wait_send()

    first = pltpu.make_async_copy(d_branch, ring.at[pl.ds(0, TOK)], load.at[14])
    first.start()
    first.wait()
    gather.step(0)
    place(0, 0)
    for side in (0, 1):
        go(*[gu_a(side, j) for j in range(RING)])
        if side == 0:
            go(small_a(0, 0), small_a(0, 1))
    for j in range(RING):
        if j < 2:
            gu_own(0, j).start()
        sum_own(0, j)
        if j + 2 < RING:
            gu_own(0, j + 2).start()
        if j < AHEAD:
            go(gu_b(j))

    def down_sum(xo):
        c = pltpu.make_async_copy(down_in.at[2 * core + xo], down_own, load.at[16])
        c.start()
        small_a(0, xo).wait_recv()
        c.wait()
        da[xo] = (da[xo].astype(F32) + down_own[...].astype(F32)).astype(BF)

    down_sum(0)
    gather.step(1)
    place(1, 0)
    place(2, 0)
    pump(0, 1)
    down_sum(1)
    pump(1, 2)
    gather.step(2)
    place(3, 0)
    place(4, 0)
    pump(2, 4)
    gather.step(3)
    place(5, 0)
    place(6, 0)
    pump(4, 5)
    gather.finish()
    place(7, 0)
    for j in range(5):
        go(gu_c(j))
    for zq in range(NZ):
        dst = seq.at[2 * zq + 1 - core]
        remote(dst, dst, pls.at[zq], plr.at[zq], sibling).wait_recv()
    for slot in range(RING):
        place(slot, 1)
    gather.drain()
    hidden_load = pltpu.make_async_copy(hidden, ring, load.at[14])
    hidden_load.start()
    ready()

    for c in range(0, RING, 2):
        rows = pl.ds(c * TOK, 2 * TOK)
        d_att[rows] = contract_cols(seq[c : c + 2].reshape(2 * TOK, -1), wo[...]).astype(BF)

    def out_columns(cols):
        value = contract_rows(att[...].astype(BF), seq[:, :, cols].reshape(RING * TOK, 768))
        for f in range(4):
            og[f, :, cols] = value[64 * f : 64 * (f + 1)].astype(BF)

    tiles(3, 768, out_columns)
    go(small_a(1, 0), small_a(1, 1))
    pump(5, 6)
    go(gu_c(5))
    dk[...] = jnp.zeros_like(dk)
    dv[...] = jnp.zeros_like(dv)
    for i in range(4):
        r, upto = pl.ds(i * 256, 256), (i + 1) * 256
        keys, vals, query = k_in[0:upto], v_in[0:upto], q_in[r]
        bent = jnp.tanh(contract_cols(query, keys) / CAP)
        seen = lax.broadcasted_iota(jnp.int32, bent.shape, 1) <= i * 256 + lax.broadcasted_iota(jnp.int32, bent.shape, 0)
        weights = jnp.where(seen, jnp.exp(CAP * bent), 0.0)
        grad = d_att[r].astype(F32)
        delta = jnp.sum(grad * att[r], axis=-1, keepdims=True)
        d_probs = contract_cols(d_att[r], vals)
        d_raw = (weights * inv[r] * (d_probs - delta) * (1.0 - bent * bent)).astype(BF)
        dq = fold_rows(d_raw, keys) * (HD ** (-0.5))
        d_qkv[r, 0:HD] = unrotate(dq, cos[r], sine[r]).astype(BF)
        dk[0:upto] = dk[0:upto] + contract_rows(d_raw, query)
        scaled = grad * inv[r]
        high = scaled.astype(BF)
        rest = (scaled - high.astype(F32)).astype(BF)
        weights_b = weights.astype(BF)
        dv[0:upto] = dv[0:upto] + contract_rows(weights_b, high) + contract_rows(weights_b, rest)
        if i == 1:
            pump(6, 7)
            go(gu_c(6))
            go(small_b(0))
        if i == 3:
            pump(7, 8)
            go_self = gu_c(7)
            go_self.start()
    d_qkv[:, HD : 2 * HD] = unrotate(dk[...], cos[...], sine[...]).astype(BF)
    d_qkv[:, 2 * HD : 3 * HD] = dv[...].astype(BF)

    scatter = SlotScatter(part, buf, rss, rsr)

    def swap(zq, kept):
        where = pl.ds(pl.multiple_of(slot_of(ring_index(core, zq), p) * TOK, TOK), TOK)
        if kept:
            return pltpu.make_async_copy(seq.at[2 * zq + core], part.at[where], load.at[17 + zq])
        return remote(seq.at[2 * zq + 1 - core], part.at[where], sws.at[zq], swr.at[zq], sibling)

    def swapped(zq):
        where = pl.ds(pl.multiple_of(slot_of(ring_index(1 - core, zq), p) * TOK, TOK), TOK)
        return remote(seq.at[0], part.at[where], sws.at[zq], swr.at[zq], sibling)

    for zq in range(NZ):
        rows = d_qkv[2 * zq * TOK : (2 * zq + 2) * TOK]

        def columns(cols):
            value = contract_cols(rows, wq[cols])
            seq[2 * zq, :, cols] = value[0:TOK].astype(BF)
            seq[2 * zq + 1, :, cols] = value[TOK:].astype(BF)

        tiles(3, 768, columns)
        swap(zq, True).start()
        swap(zq, False).start()
    for zq in range(NZ):
        swap(zq, True).wait()
        swapped(zq).wait_recv()
    scatter.step(0)

    hidden_load.wait()

    def grad_half(half):
        def columns(cols):
            value = contract_rows(ring[:, pl.ds(half * 1152, 1152)], d_qkv[:, cols])
            for i in range(16):
                grad_q[half * 16 + i, :, cols] = value[72 * i : 72 * (i + 1)].astype(BF)

        tiles(3, 256, columns)

    grad_half(0)
    scatter.step(1)
    grad_half(1)
    for side in (0, 1):
        go(*[q_a(side, j) for j in range(RING)])
    for xo in (0, 1):
        small_a(1, xo).wait_recv()
        oa[xo] = (oa[xo].astype(F32) + og[2 * core + xo].astype(F32)).astype(BF)
    go(small_b(1))
    scatter.step(2)

    def q_sum(side, j):
        i = owner(order[j], core, side_x[side])
        q_a(side, j).wait_recv()
        total = grad_q[i].astype(F32) + aq[side, j].astype(F32)
        if side == 1:
            q_b(j).wait_recv()
            total = total + bq[j].astype(F32)
        grad_q[i] = total.astype(BF)

    for j in range(RING):
        q_sum(0, j)
        if j < AHEAD:
            go(q_b(j))
    small_b(0).wait_recv()
    da[x] = (da[x].astype(F32) + db[...].astype(F32)).astype(BF)
    small_c(0, 0)
    scatter.step(3)

    def q_round(j):
        q_sum(1, j)
        if j + AHEAD < RING:
            go(q_b(j + AHEAD))
        if ROUNDS[j] == 0:
            q_c(j).start()
        else:
            go(q_c(j))

    for j in range(4):
        q_round(j)
    small_b(1).wait_recv()
    oa[x] = (oa[x].astype(F32) + ob[...].astype(F32)).astype(BF)
    small_c(1, 0)

    def own_part(cols):
        slot = part[0:TOK, cols]
        d_hid_o[:, cols] = slot.astype(F32)

    tiles(3, 768, own_part)
    for j in range(4, RING):
        q_round(j)
    scatter.finish(d_hid_o)
    def pre_gain(r):
        value = d_hid_o[r] * rms_parts(block_in[r].astype(F32))[1]
        gain_in[0:1, 0:D] = gain_in[0:1, 0:D] + jnp.sum(value, axis=0, keepdims=True)

    by_rows(pre_gain)
    go(gain_a())
    gain_a().wait_recv()
    gsum[0] = gain_in[...] + gsum[2]
    go(gain_b())
    gain_b().wait_recv()
    gsum[1] = gsum[0] + gsum[3]
    go(*[gain_c(j) for j in range(1, RING)])
    total = gsum[1, :, window(owner(t, core, x))]
    for j in range(1, RING):
        gain_c(j).wait_recv()
        total = total + ga[j]
    gain_o[...] = total

    for j in range(RING):
        if ROUNDS[j] == 0:
            gu_c(j).wait()
            q_c(j).wait()
        else:
            gu_c(j, True).wait_recv()
            q_c(j, True).wait_recv()
    small_c(0, 1)
    small_c(1, 1)
    for zq in range(NZ):
        swap(zq, False).wait_send()
    scatter.drain()
    for c in pending:
        c.wait_send()


def backward(d_branch, gu, down, hidden, w_qkv, w_out, queries, keys, values, attended, inv_total, cos_tab, sine_tab,
             block, gain_parts, collective_id):
    n = 4 * RING
    rows, width = d_branch.shape
    shard = gu.shape[0] // n
    gu = gu.reshape(n, shard, 2 * UNITS)
    down = down.reshape(4, -1, width)
    total, down_rows, out_rows = RING * rows, down.shape[1], w_out.shape[0] // 4
    gain_shape = (8, PADDED)

    def out(*shape, dtype=BF):
        return jax.ShapeDtypeStruct(shape, dtype)

    def body(*refs):
        ins, rest = refs[:14], refs[14:]
        gains_ref, rest = rest[0], rest[1:]
        outs, scr = rest[:6], rest[6:]
        gain_scr, loaded, sems, scr = scr[0], scr[1:8], scr[8], scr[9:]
        gain_scr[...] = gains_ref[...]
        ins = list(ins)
        copies = []
        for i, place in enumerate((4, 6, 7, 8, 9, 11, 12)):
            copies.append(pltpu.make_async_copy(ins[place], loaded[i], sems.at[i]))
            copies[-1].start()
            ins[place] = loaded[i]

        def ready():
            for c in copies:
                c.wait()

        backward_kernel(ready, *ins, gain_scr, *outs, *scr)

    return pl.pallas_call(
        body,
        out_shape=[
            out(rows, width, dtype=F32), out(8, WINDOW, dtype=F32),
            out(RING, shard, 2 * UNITS), out(RING, shard, 3 * HD),
            out(down_rows, width), out(out_rows, width),
        ],
        in_specs=[HBM] * 5 + [VMEM] + [HBM] * 4 + [VMEM] + [HBM] * 2 + [VMEM] * 2,
        out_specs=[VMEM] * 2 + [HBM] * 4,
        scratch_shapes=[
            pltpu.VMEM(gain_shape, F32),
            pltpu.VMEM((width, 3 * HD), BF), pltpu.VMEM((total, HD), BF), pltpu.VMEM((total, HD), BF), pltpu.VMEM((total, HD), BF),
            pltpu.VMEM((total, HD), F32), pltpu.VMEM((total, HD // 2), F32), pltpu.VMEM((total, HD // 2), F32),
            DMA((7,)),
            pltpu.VMEM((total, width), BF), pltpu.VMEM((RING, rows, width), BF), pltpu.VMEM((total, width), BF),
            pltpu.VMEM((2, 4, rows, width), BF),
            pltpu.VMEM((total, HD), BF), pltpu.VMEM((total, 3 * HD), BF),
            pltpu.VMEM((total, HD), F32), pltpu.VMEM((total, HD), F32),
            pltpu.VMEM((n, shard, 3 * HD), BF), pltpu.VMEM((2, RING, shard, 3 * HD), BF), pltpu.VMEM((RING, shard, 3 * HD), BF),
            pltpu.VMEM((2, shard, 2 * UNITS), BF), pltpu.VMEM((2, RING, shard, 2 * UNITS), BF), pltpu.VMEM((RING, shard, 2 * UNITS), BF),
            pltpu.VMEM((down_rows, width), BF), pltpu.VMEM((2, down_rows, width), BF), pltpu.VMEM((down_rows, width), BF),
            pltpu.VMEM((4, out_rows, width), BF), pltpu.VMEM((2, out_rows, width), BF), pltpu.VMEM((out_rows, width), BF),
            pltpu.VMEM((RING, 8, WINDOW), F32), pltpu.VMEM((4,) + gain_shape, F32),
            DMA((21,)),
            DMA((2, 4, SUB)), DMA((2, 4, SUB)), DMA((NZ,)), DMA((NZ,)), DMA((2, 4, SUB)), DMA((2, 4, SUB)), DMA((NZ,)), DMA((NZ,)),
            DMA((2, RING)), DMA((2, RING)), DMA((RING,)), DMA((RING,)), DMA((RING,)), DMA((RING,)),
            DMA((2, RING)), DMA((2, RING)), DMA((RING,)), DMA((RING,)), DMA((RING,)), DMA((RING,)),
            DMA((2, 4)), DMA((2, 4)), DMA((RING + 2,)), DMA((RING + 2,)),
        ],
        compiler_params=params(collective_id, 60),
    )(d_branch, gu, down, hidden, w_qkv, w_out, queries, keys, values, attended, inv_total, cos_tab, sine_tab, block, gain_parts)


def results_kernel(gu, qkv, down, out, d_hidden, d_middle, block, gains,
                   gate_o, up_o, query_o, key_o, value_o, down_o, out_o, token_o):
    for i in range(2):
        units, heads = pl.ds(i * UNITS, UNITS), pl.ds(i * HD, HD)
        gate_o[:, units] = gu[i, :, 0:UNITS].astype(F32)
        up_o[:, units] = gu[i, :, UNITS : 2 * UNITS].astype(F32)
        query_o[:, heads] = qkv[i, :, 0:HD].astype(F32)
    key_o[...] = qkv[0, :, HD : 2 * HD].astype(F32) + qkv[1, :, HD : 2 * HD].astype(F32)
    value_o[...] = qkv[0, :, 2 * HD :].astype(F32) + qkv[1, :, 2 * HD :].astype(F32)
    down_o[...] = down[...].astype(F32)
    out_o[...] = out[...].astype(F32)
    inverse, normed = rms_parts(block[...].astype(F32))
    back = norm_back(d_hidden[...] * (1.0 + gains[0:1]), normed, inverse)
    token_o[...] = (d_middle[...] + back).astype(BF)


def results(gu, qkv, down, out, d_hidden, d_middle, block, gains):
    steps = RING // 2
    shard, width = gu.shape[1], down.shape[1]
    tok, down_rows, out_rows = d_hidden.shape[0] // steps, down.shape[0] // steps, out.shape[0] // steps

    def rows(n, wide):
        return pl.BlockSpec((n, wide), lambda i: (i, 0))

    def columns(wide):
        return pl.BlockSpec((shard, wide), lambda i: (0, i))

    def full(*shape):
        return jax.ShapeDtypeStruct(shape, F32)

    return pl.pallas_call(
        results_kernel,
        grid=(steps,),
        out_shape=[
            full(shard, FF), full(shard, FF), full(shard, H * HD), full(shard, KVH * HD), full(shard, KVH * HD),
            full(*down.shape), full(*out.shape), jax.ShapeDtypeStruct(d_hidden.shape, BF),
        ],
        in_specs=[
            pl.BlockSpec((2, shard, 2 * UNITS), lambda i: (i, 0, 0)), pl.BlockSpec((2, shard, 3 * HD), lambda i: (i, 0, 0)),
            rows(down_rows, width), rows(out_rows, width), rows(tok, width), rows(tok, width), rows(tok, width),
            pl.BlockSpec(gains.shape, lambda i: (0, 0)),
        ],
        out_specs=[
            columns(2 * UNITS), columns(2 * UNITS), columns(2 * HD), columns(HD), columns(HD),
            rows(down_rows, width), rows(out_rows, width), rows(tok, width),
        ],
        compiler_params=pltpu.CompilerParams(vmem_limit_bytes=60 * 2**20),
    )(gu, qkv, down, out, d_hidden, d_middle, block, gains)


def on_ring(
    tokens, w_query, w_key, w_value, w_out, w_gate, w_up, w_down,
    pre_gain, post_gain, pre_ffn_gain, post_ffn_gain, out_grad,
):
    ids = iter(range(32))
    length = RING * tokens.shape[1]
    shard_gain = pre_gain.shape[0]
    mine = lax.axis_index("ctx") * 4 + lax.axis_index("fsdp")
    gains = jnp.stack([pre_gain, post_gain, pre_ffn_gain, post_ffn_gain]).astype(F32)
    gains = lax.dynamic_update_slice(jnp.zeros((8, WINDOW), F32), gains, (0, (mine * shard_gain) % 128))
    cos_tab, sine_tab = (jnp.asarray(table) for table in constant_tables(length, HD))
    w_gu, down_in, hidden, w_qkv, queries, keys, values, attended, out_in, gains, inv_total, branch = forward(
        w_gate, w_up, w_query, w_key, w_value, w_down, w_out, tokens[0], gains, cos_tab, sine_tab, next(ids)
    )
    w_gu, hidden = w_gu.reshape(D, 2 * UNITS), hidden.reshape(length, D)
    w_dn = down_in.reshape(UNITS, D)
    w_ot = out_in.reshape(HD, D)
    output, d_middle, d_branch, gain_parts, down_part, gu_part = feed_forward(
        branch, tokens[0], gains, out_grad[0], w_gu, w_dn, next(ids)
    )
    d_hidden, gain_g, gu_g, qkv_g, down_g, out_g = backward(
        d_branch, gu_part, down_part, hidden, w_qkv, w_ot, queries, keys, values, attended, inv_total,
        cos_tab, sine_tab, tokens[0], gain_parts, next(ids),
    )
    gate_g, up_g, query_g, key_g, value_g, down_g, out_g, token_grad = results(
        gu_g, qkv_g, down_g, out_g, d_hidden, d_middle, tokens[0], gains
    )
    gain_g = lax.dynamic_slice(gain_g, (0, (mine * shard_gain) % 128), (4, shard_gain))
    return (
        output[None], token_grad[None],
        query_g, key_g, value_g, out_g, gate_g, up_g, down_g,
        gain_g[0], gain_g[1], gain_g[2], gain_g[3],
    )


ROW_FOLD = 4


def head_tables(positions, width):
    half_width = width // 2
    inv_freqs = ROPE_BASE ** (-jnp.arange(half_width, dtype=jnp.float32) * 2.0 / width)
    angles = positions.astype(jnp.float32)[:, None] * inv_freqs[None, :]
    return (jnp.cos(angles)[:, None, :], jnp.sin(angles)[:, None, :])


def rotate_heads(heads_in, cos_tab, sine_tab):
    half_width = heads_in.shape[-1] // 2
    front_half = heads_in[..., :half_width]
    back_half = heads_in[..., half_width:]
    return jnp.concatenate(
        [front_half * cos_tab - back_half * sine_tab, back_half * cos_tab + front_half * sine_tab],
        axis=-1,
    )


def unrotate_heads(grad_in, cos_tab, sine_tab):
    half_width = grad_in.shape[-1] // 2
    front_half = grad_in[..., :half_width]
    back_half = grad_in[..., half_width:]
    return jnp.concatenate(
        [front_half * cos_tab + back_half * sine_tab, back_half * cos_tab - front_half * sine_tab],
        axis=-1,
    )


def to_groups(flat_heads, tok_rows, q_group):
    shaped = flat_heads.reshape(tok_rows, KVH, q_group, HD)
    return jnp.transpose(shaped, (1, 2, 0, 3)).reshape(KVH, q_group * tok_rows, HD)


def from_groups(grouped, tok_rows, q_group):
    shaped = grouped.reshape(KVH, q_group, tok_rows, HD)
    return jnp.transpose(shaped, (2, 0, 1, 3)).reshape(tok_rows, KVH * q_group * HD)


def grad_rows(left, right, folding, count):
    block = contract_rows(left, right)
    return block.reshape(count, right.shape[1] // folding)


def blockwise(step_fn, carry, piece, width):
    key_count = piece[0].shape[0]
    n_steps = key_count // width
    stacked = tuple((member.reshape(n_steps, width, member.shape[1]) for member in piece))

    def one_step(partial_value, block_item):
        block_index, members = block_item
        return (step_fn(partial_value, members, block_index * width), None)

    carry, unused = lax.scan(one_step, carry, (jnp.arange(n_steps, dtype=jnp.int32), stacked))
    return carry


def block_grads(query_g, query_pos, d_att_g, delta, inv_tot, key_block, value_block, key_first):
    key_count = key_block.shape[0]
    key_grp = key_block.reshape(key_count, KVH, HD)
    value_grp = value_block.reshape(key_count, KVH, HD)
    raw_scores = jnp.einsum("grd,ngd->grn", query_g, key_grp, preferred_element_type=jnp.float32)
    capped = CAP * jnp.tanh(raw_scores / CAP)
    key_pos = key_first + jnp.arange(key_count, dtype=jnp.int32)
    allowed = key_pos[None, None, :] <= query_pos[None, :, None]
    weights = jnp.where(allowed, jnp.exp(capped), 0.0)
    prob_rows = weights * inv_tot[..., None]
    d_probs = jnp.einsum("grd,ngd->grn", d_att_g, value_grp, preferred_element_type=jnp.float32)
    slope = 1.0 - capped / CAP * (capped / CAP)
    d_raw = (prob_rows * (d_probs - delta[..., None]) * slope).astype(jnp.bfloat16)
    d_query = jnp.einsum("grn,ngd->grd", d_raw, key_grp, preferred_element_type=jnp.float32)
    d_key = jnp.einsum("grn,grd->ngd", d_raw, query_g, preferred_element_type=jnp.float32)
    weights_b = weights.astype(jnp.bfloat16)
    d_scaled = d_att_g.astype(jnp.float32) * inv_tot[..., None]
    scaled_high = d_scaled.astype(jnp.bfloat16)
    scaled_rest = (d_scaled - scaled_high.astype(jnp.float32)).astype(jnp.bfloat16)
    d_value = jnp.einsum("grn,grd->ngd", weights_b, scaled_high, preferred_element_type=jnp.float32)
    d_value = d_value + jnp.einsum(
        "grn,grd->ngd", weights_b, scaled_rest, preferred_element_type=jnp.float32
    )
    return (d_query, d_key.reshape(key_count, KVH * HD), d_value.reshape(key_count, KVH * HD))


def on_any_mesh(
    tokens,
    w_query,
    w_key,
    w_value,
    w_out,
    w_gate,
    w_up,
    w_down,
    pre_gain,
    post_gain,
    pre_ffn_gain,
    post_ffn_gain,
    out_grad,
):
    tok_rows = tokens.shape[1]
    q_group = H // KVH
    q_scale = HD ** (-0.5)
    width_q = H * HD
    width_kv = KVH * HD
    width_qkv = width_q + 2 * width_kv
    n_ctx = lax.axis_size("ctx")
    my_block = lax.axis_index("ctx")
    my_start = my_block * tok_rows
    positions = my_start + jnp.arange(tok_rows, dtype=jnp.int32)
    cos_tab, sine_tab = head_tables(positions, HD)
    row_pos = jnp.tile(positions, q_group)
    last_pos = my_start + tok_rows - 1
    resid_in = tokens[0].astype(jnp.float32)
    qkv_shard = jnp.concatenate([w_query, w_key, w_value], axis=1)
    gateup_shard = jnp.concatenate([w_gate, w_up], axis=1)
    shard_rows = qkv_shard.shape[0]
    gains_shard = jnp.stack([pre_gain, post_gain, pre_ffn_gain, post_ffn_gain])
    full_gains, full_qkv, full_out = (
        lax.all_gather(gains_shard, ("ctx", "fsdp"), axis=1, tiled=True),
        lax.all_gather(qkv_shard, ("ctx", "fsdp"), axis=0, tiled=True),
        lax.all_gather(w_out, ("ctx", "fsdp"), axis=0, tiled=True),
    )
    factors = 1.0 + full_gains.astype(jnp.float32)
    pre_factor, post_factor, pre_ffn_factor, post_ffn_factor = (
        factors[0],
        factors[1],
        factors[2],
        factors[3],
    )
    inv_pre, normed_pre = rms_parts(resid_in)
    hidden = (normed_pre * pre_factor).astype(jnp.bfloat16)
    projected = jnp.dot(hidden, full_qkv, preferred_element_type=jnp.float32)
    query_lin = projected[:, :width_q].reshape(tok_rows, H, HD)
    queries = (
        (rotate_heads(query_lin, cos_tab, sine_tab) * q_scale)
        .astype(jnp.bfloat16)
        .reshape(tok_rows, width_q)
    )
    query_grp = to_groups(queries, tok_rows, q_group)
    key_lin = projected[:, width_q : width_q + width_kv].reshape(tok_rows, KVH, HD)
    key_rows = rotate_heads(key_lin, cos_tab, sine_tab).astype(jnp.bfloat16).reshape(tok_rows, width_kv)
    value_rows = projected[:, width_q + width_kv :].astype(jnp.bfloat16)

    def add_block(partial_value, piece, first_row):
        key_block, value_block = piece

        def add_compute_block(state):
            row_total, weighted = state
            key_count = key_block.shape[0]
            key_grp = key_block.reshape(key_count, KVH, HD)
            raw_scores = jnp.einsum(
                "grd,ngd->grn", query_grp, key_grp, preferred_element_type=jnp.float32
            )
            capped = CAP * jnp.tanh(raw_scores / CAP)
            key_pos = first_row + jnp.arange(key_count, dtype=jnp.int32)
            allowed = key_pos[None, None, :] <= row_pos[None, :, None]
            weights = jnp.where(allowed, jnp.exp(capped), 0.0)
            value_grp = value_block.reshape(key_count, KVH, HD)
            weighted = weighted + jnp.einsum(
                "grn,ngd->grd",
                weights.astype(jnp.bfloat16),
                value_grp,
                preferred_element_type=jnp.float32,
            )
            return (row_total + jnp.sum(weights, axis=-1), weighted)

        def add_skip_block(state):
            return state

        return lax.cond(first_row <= last_pos, add_compute_block, add_skip_block, partial_value)

    start_state = (
        jnp.zeros((KVH, q_group * tok_rows), jnp.float32),
        jnp.zeros((KVH, q_group * tok_rows, HD), jnp.float32),
    )
    row_total, weighted = blockwise(
        add_block,
        start_state,
        (
            lax.all_gather(key_rows, "ctx", axis=0, tiled=True),
            lax.all_gather(value_rows, "ctx", axis=0, tiled=True),
        ),
        512,
    )
    inv_total = 1.0 / row_total
    attended_grp = weighted * inv_total[..., None]
    attended_b = from_groups(attended_grp, tok_rows, q_group).astype(jnp.bfloat16)
    branch = jnp.dot(attended_b, full_out, preferred_element_type=jnp.float32)
    inv_post, normed_post = rms_parts(branch)
    middle = resid_in + normed_post * post_factor
    inv_mid, normed_mid = rms_parts(middle)
    hidden_ffn = (normed_mid * pre_ffn_factor).astype(jnp.bfloat16)
    gate_up = fold_rows(
        hidden_ffn, lax.all_gather(gateup_shard, ("ctx", "fsdp"), axis=0, tiled=True)
    )
    gate_lin = gate_up[:, :FF]
    up_lin = gate_up[:, FF:]
    active = gated(gate_lin, up_lin).astype(jnp.bfloat16)
    ffn_branch = fold_rows(active, lax.all_gather(w_down, ("ctx", "fsdp"), axis=0, tiled=True))
    inv_ffn, normed_ffn = rms_parts(ffn_branch)
    output = (middle + normed_ffn * post_ffn_factor).astype(jnp.bfloat16)
    out_cot = out_grad[0].astype(jnp.float32)
    post_ffn_part = jnp.sum(out_cot * normed_ffn, axis=0)
    d_ffn_b = norm_back(out_cot * post_ffn_factor, normed_ffn, inv_ffn).astype(jnp.bfloat16)
    down_total = lax.psum_scatter(
        grad_rows(active, d_ffn_b, 1, lax.axis_size(("ctx", "fsdp")) * w_down.shape[0]),
        ("ctx", "fsdp"),
        scatter_dimension=0,
        tiled=True,
    )
    d_active = contract_cols(d_ffn_b, lax.all_gather(w_down, ("ctx", "fsdp"), axis=0, tiled=True))
    unused_value, gate_pull = jax.vjp(gated, gate_lin, up_lin)
    d_gate, d_up = gate_pull(d_active)
    d_gateup_b = jnp.concatenate([d_gate.astype(jnp.bfloat16), d_up.astype(jnp.bfloat16)], axis=1)
    gateup_folded = lax.psum_scatter(
        grad_rows(
            hidden_ffn,
            d_gateup_b,
            ROW_FOLD,
            lax.axis_size(("ctx", "fsdp")) * (ROW_FOLD * shard_rows),
        ),
        ("ctx", "fsdp"),
        scatter_dimension=0,
        tiled=True,
    )
    gateup_total = gateup_folded.reshape(shard_rows, 2 * FF)
    d_hidden_ffn = contract_cols(
        d_gateup_b, lax.all_gather(gateup_shard, ("ctx", "fsdp"), axis=0, tiled=True)
    )
    pre_ffn_part = jnp.sum(d_hidden_ffn * normed_mid, axis=0)
    d_middle = out_cot + norm_back(d_hidden_ffn * pre_ffn_factor, normed_mid, inv_mid)
    back_qkv, back_out = (
        lax.all_gather(qkv_shard, ("ctx", "fsdp"), axis=0, tiled=True),
        lax.all_gather(w_out, ("ctx", "fsdp"), axis=0, tiled=True),
    )
    post_gain_part = jnp.sum(d_middle * normed_post, axis=0)
    d_branch_b = norm_back(d_middle * post_factor, normed_post, inv_post).astype(jnp.bfloat16)
    w_out_part = contract_rows(attended_b, d_branch_b)
    d_attended = contract_cols(d_branch_b, back_out).astype(jnp.bfloat16)
    d_att_grp = to_groups(d_attended, tok_rows, q_group)
    row_delta = jnp.sum(d_att_grp.astype(jnp.float32) * attended_grp, axis=-1)
    zero_rows = jnp.zeros((tok_rows, width_kv), jnp.float32)
    zero_query = jnp.zeros((KVH, q_group * tok_rows, HD), jnp.float32)
    block_ids = jnp.arange(n_ctx, dtype=jnp.int32)
    all_keys, all_values = (
        lax.all_gather(key_rows, "ctx", axis=0, tiled=True),
        lax.all_gather(value_rows, "ctx", axis=0, tiled=True),
    )

    def returned_step(acc_query, block_item):
        block_index, key_block, value_block = block_item
        first_row = block_index * tok_rows

        def returned_compute_block(acc_in):
            d_query, d_key, d_value = block_grads(
                query_grp,
                row_pos,
                d_att_grp,
                row_delta,
                inv_total,
                key_block,
                value_block,
                first_row,
            )
            return (acc_in + d_query, (d_key, d_value))

        def returned_skip_block(acc_in):
            return (acc_in, (zero_rows, zero_rows))

        return lax.cond(
            first_row <= last_pos, returned_compute_block, returned_skip_block, acc_query
        )

    key_blocks = all_keys.reshape(n_ctx, tok_rows, width_kv)
    value_blocks = all_values.reshape(n_ctx, tok_rows, width_kv)
    d_query_grp, key_terms = lax.scan(
        returned_step, zero_query, (block_ids, key_blocks, value_blocks)
    )
    key_term_rows = key_terms[0].reshape(n_ctx * tok_rows, width_kv)
    value_term_rows = key_terms[1].reshape(n_ctx * tok_rows, width_kv)
    d_keys, d_values = (
        lax.psum_scatter(
            key_term_rows.astype(jnp.bfloat16), "ctx", scatter_dimension=0, tiled=True
        ).astype(jnp.float32),
        lax.psum_scatter(
            value_term_rows.astype(jnp.bfloat16), "ctx", scatter_dimension=0, tiled=True
        ).astype(jnp.float32),
    )
    d_query_flat = from_groups(d_query_grp, tok_rows, q_group).reshape(tok_rows, H, HD) * q_scale
    dq_lin = (
        unrotate_heads(d_query_flat, cos_tab, sine_tab).astype(jnp.bfloat16).reshape(tok_rows, width_q)
    )
    dk_lin = (
        unrotate_heads(d_keys.reshape(tok_rows, KVH, HD), cos_tab, sine_tab)
        .astype(jnp.bfloat16)
        .reshape(tok_rows, width_kv)
    )
    dv_lin = d_values.astype(jnp.bfloat16)
    dqkv_b = jnp.concatenate([dq_lin, dk_lin, dv_lin], axis=1)
    d_hidden = contract_cols(dqkv_b, back_qkv)
    qkv_part = contract_rows(hidden, dqkv_b).reshape(ROW_FOLD * D, width_qkv // ROW_FOLD)
    pre_gain_part = jnp.sum(d_hidden * normed_pre, axis=0)
    token_grad = d_middle + norm_back(d_hidden * pre_factor, normed_pre, inv_pre)
    gain_parts = jnp.stack([pre_gain_part, post_gain_part, pre_ffn_part, post_ffn_part])
    qkv_folded, out_total, gain_totals = (
        lax.psum_scatter(qkv_part, ("ctx", "fsdp"), scatter_dimension=0, tiled=True),
        lax.psum_scatter(w_out_part, ("ctx", "fsdp"), scatter_dimension=0, tiled=True),
        lax.psum_scatter(gain_parts, ("ctx", "fsdp"), scatter_dimension=1, tiled=True),
    )
    qkv_total = qkv_folded.reshape(shard_rows, width_qkv)
    return (
        output[None],
        token_grad.astype(jnp.bfloat16)[None],
        qkv_total[:, :width_q],
        qkv_total[:, width_q : width_q + width_kv],
        qkv_total[:, width_q + width_kv :],
        out_total,
        gateup_total[:, :FF],
        gateup_total[:, FF:],
        down_total,
        gain_totals[0],
        gain_totals[1],
        gain_totals[2],
        gain_totals[3],
    )


def solution(mesh):
    ring = mesh.shape["ctx"] == RING and mesh.shape["fsdp"] == 4
    tokens, rows, gains = P("fsdp", "ctx", None), P(("ctx", "fsdp"), None), P(("ctx", "fsdp"))
    return jax.shard_map(
        on_ring if ring else on_any_mesh,
        mesh=mesh,
        in_specs=(tokens,) + (rows,) * 7 + (gains,) * 4 + (tokens,),
        out_specs=(tokens, tokens) + (rows,) * 7 + (gains,) * 4,
        check_vma=False,
    )
```
